32 devices in a mesh: dp: 4 (over y, x), seq: 8 (over z, core).
Axes of the slice: x: 2, y: 2, z: 4, core: 2. Of those that a mesh axis runs over, the one named last changes fastest.
Arguments:
- tokens: bfloat16 [4, 4096, 1024], P('dp', 'seq'), may hold values from -6 to 6
- starts: int32 [4, 13], P('dp'), may hold values from 0 to 4048, as said below
- query_key_value_weight: bfloat16 [1024, 3072], P(('dp', 'seq')), may hold values from -0.1875 to 0.1875
- attention_output_weight: bfloat16 [1024, 1024], P(('dp', 'seq')), may hold values from -0.75 to 0.75
- up_projection_weight: bfloat16 [1024, 4096], P(('dp', 'seq')), may hold values from -0.1875 to 0.1875
- down_projection_weight: bfloat16 [4096, 1024], P(('dp', 'seq')), may hold values from -0.09375 to 0.09375
- first_gain: bfloat16 [1024], P(('dp', 'seq')), may hold values from 0.5 to 1.5
- first_shift: bfloat16 [1024], P(('dp', 'seq')), may hold values from -0.5 to 0.5
- second_gain: bfloat16 [1024], P(('dp', 'seq')), may hold values from 0.5 to 1.5
- second_shift: bfloat16 [1024], P(('dp', 'seq')), may hold values from -0.5 to 0.5
- cotangent: bfloat16 [4, 4096, 1024], P('dp', 'seq'), may hold values from -6 to 6
Outputs:
- result_tokens: bfloat16 [4, 4096, 1024], P('dp', 'seq')
- grad_tokens: float32 [4, 4096, 1024], P('dp', 'seq')
- grad_input_weight: float32 [1024, 3072], P(('dp', 'seq'))
- grad_output_weight: float32 [1024, 1024], P(('dp', 'seq'))
- grad_upward_weight: float32 [1024, 4096], P(('dp', 'seq'))
- grad_downward_weight: float32 [4096, 1024], P(('dp', 'seq'))
- grad_first_gain: float32 [1024], P(('dp', 'seq'))
- grad_first_shift: float32 [1024], P(('dp', 'seq'))
- grad_second_gain: float32 [1024], P(('dp', 'seq'))
- grad_second_shift: float32 [1024], P(('dp', 'seq'))
The draws below stay inside these ranges and needn't reach their ends.
Inputs may be any that keep to these rules, and one draw needn't show every extreme that they name: In each packed sequence starts[0] = 0 and the first image holds 64 positions; the other 12 images follow back to end, 4 of 768 positions, 4 of 192 and 4 of 48, in an order drawn from the seed except that the last is always one of 48 positions; the last ends at the sequence's end.
All inputs are finite; a program needn't handle non-finite values.
Results may differ from the reference program's by a relative error of at most 0.008.
Values may be sent and summed in bfloat16 or wider, within the bound.
A program may use at most 192 MiB of HBM per device.

```python
from functools import partial
import jax
import jax.numpy as jnp
from jax import lax

D = 1024
FF = 4096
HEADS = 16
HEAD = 64
BLOCK = 512
PACKS = 4
PACK_LEN = 4096


def draw_starts(key, part):
    key = jax.random.fold_in(key, 7)
    largest = 3 * PACK_LEN // 16
    opening = PACK_LEN // 64
    kinds = jnp.array([0, 0, 0, 0, 1, 1, 1, 1, 2, 2, 2], jnp.int32)

    def draw_pack(pack_key):
        order = jnp.concatenate([jax.random.permutation(pack_key, kinds), jnp.array([2], jnp.int32)])
        sizes = jnp.where(order == 0, largest, jnp.where(order == 1, largest // 4, largest // 16)).astype(jnp.int32)
        ends = jnp.cumsum(sizes).astype(jnp.int32)
        later = opening + ends[:-1] - ends[0] + sizes[0]
        firsts = jnp.concatenate([jnp.array([opening], jnp.int32), later.astype(jnp.int32)])
        return jnp.concatenate([jnp.zeros((1,), jnp.int32), firsts])
    return jax.vmap(draw_pack)(jax.random.split(key, PACKS))


def steps_of(rng, shape, cuts, least, top_value):
    factor_of, own = 1.0, jax.random.fold_in(rng, 6)
    for position, blocks in cuts:
        heights = jnp.exp(jax.random.uniform(jax.random.fold_in(own, position), (blocks,), jnp.float32, least / len(cuts), top_value / len(cuts)))
        factor_of = factor_of * jnp.repeat(heights, shape[position] // blocks).reshape([-1 if axis == position else 1 for axis in range(len(shape))])
    return factor_of


def bell_draw(own_key, extent, scale, most, cuts=(), kind=jnp.bfloat16):
    factor_of = steps_of(own_key, extent, cuts, -0.22, 0.18) if cuts else 1.0
    values = jax.random.normal(own_key, extent, jnp.float32) * scale * factor_of
    return jnp.minimum(jnp.maximum(values, -most), most).astype(kind)


def setup_inputs(seed: int = 0) -> dict:
    seeds = jax.random.split(jax.random.key(seed), 12)
    return {
        "tokens": bell_draw(seeds[0], (PACKS, PACK_LEN, D), 1.0, 6.0, ((0, 4), (1, 8))),
        "starts": draw_starts(jax.random.fold_in(seeds[11], 71), 0),
        "query_key_value_weight": bell_draw(seeds[2], (D, 3 * D), D ** -0.5, 0.1875, ((0, 32),)),
        "attention_output_weight": bell_draw(seeds[3], (D, D), (D // 16) ** -0.5, 0.75, ((0, 32),)),
        "up_projection_weight": bell_draw(seeds[4], (D, FF), D ** -0.5, 0.1875, ((0, 32),)),
        "down_projection_weight": bell_draw(seeds[5], (FF, D), FF ** -0.5, 0.09375, ((0, 32),)),
        "first_gain": jnp.clip(1.0 + 0.1 * jax.random.normal(seeds[6], (D,), jnp.float32), 0.5, 1.5).astype(jnp.bfloat16),
        "first_shift": jnp.clip(jax.random.uniform(seeds[7], (D,), jnp.float32, -0.5, 0.5) * steps_of(seeds[7], (D,), ((0, 32),), -0.4, 0.0), -0.5, 0.5).astype(jnp.bfloat16),
        "second_gain": jnp.clip(1.0 + 0.1 * jax.random.normal(seeds[8], (D,), jnp.float32), 0.5, 1.5).astype(jnp.bfloat16),
        "second_shift": jnp.clip(jax.random.uniform(seeds[9], (D,), jnp.float32, -0.5, 0.5) * steps_of(seeds[9], (D,), ((0, 32),), -0.4, 0.0), -0.5, 0.5).astype(jnp.bfloat16),
        "cotangent": bell_draw(seeds[10], (PACKS, PACK_LEN, D), 1.0, 6.0, ((0, 4), (1, 8))),
    }


@jax.custom_vjp
def low(v):
    return lax.optimization_barrier(v.astype(jnp.bfloat16)).astype(jnp.float32)

@jax.custom_vjp
def low_back(v):
    return v

def low_keep(v):
    return (low(v), None)

def low_pass(kept, grad):
    return (grad,)

def back_keep(v):
    return (v, None)

def back_low(kept, grad):
    return (low(grad),)
low.defvjp(low_keep, low_pass)
low_back.defvjp(back_keep, back_low)
HIGH_PRECISION = lax.Precision.HIGHEST

def layer_norm(values, norm_gain, norm_shift):
    average = lax.optimization_barrier(jnp.mean(values, axis=-1, keepdims=True))
    centred = values - average
    spread = lax.optimization_barrier(jnp.mean(centred * centred, axis=-1, keepdims=True))
    return centred * lax.rsqrt(spread + 1e-05) * norm_gain + norm_shift

def feature(values):
    return jax.nn.elu(values) + 1.0

def attention(feat_query, feat_key, value_low, image_ids):
    pack_count, length, model_width = feat_query.shape
    blocks = length // BLOCK

    def to_blocks(values):
        return jnp.moveaxis(values.reshape(pack_count, blocks, BLOCK, HEADS, HEAD), 1, 0)
    block_ids_all = jnp.moveaxis(image_ids.reshape(pack_count, blocks, BLOCK), 1, 0).astype(jnp.int32)
    causal = jnp.arange(BLOCK)[:, None] >= jnp.arange(BLOCK)[None, :]

    def block_step(carried_in, pieces):
        memory, key_sum, previous = carried_in
        block_query, block_key, block_value, block_ids = pieces
        keep_mask = (block_ids == previous[:, None]).astype(jnp.float32)
        same_image = (causal[None] & (block_ids[:, :, None] == block_ids[:, None, :])).astype(jnp.float32)
        raw_scores = jnp.einsum('sthe,sjhe->shtj', block_query, block_key, precision=HIGH_PRECISION)
        scores = low_back(raw_scores * same_image[:, None])
        carried = jnp.einsum('sthe,shef->sthf', block_query, low(memory), precision=HIGH_PRECISION) * keep_mask[:, :, None, None]
        numerator = low_back(jnp.einsum('shtj,sjhf->sthf', low(scores), block_value, precision=HIGH_PRECISION) + carried)
        denominator = jnp.moveaxis(lax.optimization_barrier(jnp.sum(scores, axis=3)), 1, 2) + keep_mask[:, :, None] * lax.optimization_barrier(jnp.sum(block_query * key_sum[:, None], axis=3))
        ratio = numerator / denominator[..., None]
        last_id = block_ids[:, -1].astype(jnp.int32)
        tail_mask = (block_ids == last_id[:, None]).astype(jnp.float32)
        tail_key = block_key * tail_mask[:, :, None, None]
        update = low_back(jnp.einsum('sjhe,sjhf->shef', tail_key, block_value, precision=HIGH_PRECISION))
        carry_flag = (last_id == previous).astype(jnp.float32)
        memory = carry_flag[:, None, None, None] * memory + update
        key_sum = carry_flag[:, None, None] * key_sum + lax.optimization_barrier(jnp.sum(tail_key, axis=1))
        return ((memory, key_sum, last_id), ratio)
    initial = (jnp.zeros((pack_count, HEADS, HEAD, HEAD), jnp.float32), jnp.zeros((pack_count, HEADS, HEAD), jnp.float32), jnp.full((pack_count,), -1, jnp.int32))
    final_state, results = lax.scan(jax.checkpoint(block_step), initial, (to_blocks(feat_query), to_blocks(feat_key), to_blocks(value_low), block_ids_all))
    return jnp.moveaxis(results, 0, 1).reshape(pack_count, length, model_width)

def forward(input_tokens, query_key_value_weight, attention_output_weight, up_projection_weight, down_projection_weight, first_gain, first_shift, second_gain, second_shift, image_ids=None):
    first_normed_tokens = low(layer_norm(input_tokens, first_gain, first_shift))
    projected_tokens = low_back(jnp.einsum('kmn,nx->kmx', first_normed_tokens, query_key_value_weight, precision=HIGH_PRECISION))
    queries = projected_tokens[..., :D]
    keys_raw = projected_tokens[..., D:2 * D]
    values_raw = projected_tokens[..., 2 * D:]
    mixed_tokens = low(attention(low(feature(queries)), low(feature(keys_raw)), low(values_raw), image_ids))
    middle_tokens = input_tokens + low_back(jnp.einsum('kmn,nx->kmx', mixed_tokens, attention_output_weight, precision=HIGH_PRECISION))
    second_normed_tokens = low(layer_norm(middle_tokens, second_gain, second_shift))
    upper_hidden = low_back(jnp.einsum('kmn,nx->kmx', second_normed_tokens, up_projection_weight, precision=HIGH_PRECISION))
    active_hidden = low(jax.nn.gelu(upper_hidden))
    return middle_tokens + low_back(jnp.einsum('kmn,nx->kmx', active_hidden, down_projection_weight, precision=HIGH_PRECISION))

def reference(tokens, starts, query_key_value_weight, attention_output_weight, up_projection_weight, down_projection_weight, first_gain, first_shift, second_gain, second_shift, cotangent):
    positions = jnp.arange(PACK_LEN, dtype=jnp.int32)
    image_ids = (lax.optimization_barrier(jnp.sum((starts[:, None, :] <= positions[None, :, None]).astype(jnp.int32), axis=2)) - 1).astype(jnp.int32)
    floats = [item.astype(jnp.float32) for item in (tokens, query_key_value_weight, attention_output_weight, up_projection_weight, down_projection_weight, first_gain, first_shift, second_gain, second_shift)]
    result, pullback = jax.vjp(partial(forward, image_ids=image_ids), *floats)
    gradients = pullback(cotangent.astype(jnp.float32))
    return (result.astype(jnp.bfloat16), gradients[0], gradients[1], gradients[2], gradients[3], gradients[4], gradients[5], gradients[6], gradients[7], gradients[8])
```

```python
import jax
import jax.numpy as jnp
from jax import lax
from jax.experimental import pallas as pl
from jax.experimental.pallas import tpu as pltpu
from jax.sharding import PartitionSpec as P

HEAD = 64
BLOCK = 512


def prefix(value, axis, combine, identity, reverse):
    size, mine = (lax.axis_size(axis), lax.axis_index(axis))
    everything = jax.tree.map(
        lambda part, kind: lax.all_gather(part.astype(kind), axis),
        value,
        jax.tree.map(lambda a: jnp.bfloat16 if a.dtype == jnp.float32 else a.dtype, value),
    )
    start = jax.tree.map(
        lambda part, zero: jnp.broadcast_to(jnp.asarray(zero, part.dtype), part.shape),
        value,
        identity,
    )

    def lap(k, before):
        at = size - 1 - k if reverse else k
        reached = at > mine if reverse else at < mine
        new = combine(
            before, jax.tree.map(lambda part, own: part[at].astype(own.dtype), everything, value)
        )
        return jax.tree.map(lambda a, b: jnp.where(reached, a, b), new, before)

    return lax.fori_loop(0, size, lap, start)


def layer_norm(values, norm_gain, norm_shift):
    average = jnp.mean(values, axis=-1, keepdims=True)
    centred = values - average
    spread = jnp.mean(centred * centred, axis=-1, keepdims=True)
    return centred * lax.rsqrt(spread + 1e-05) * norm_gain + norm_shift


def feature(values):
    return jax.nn.elu(values) + 1.0


def combine(former, latter):
    return (
        former[0] * latter[0],
        latter[0] * former[1] + latter[1],
        latter[0] * former[2] + latter[2],
    )


def rows_product(factor_one, factor_two):
    return lax.dot_general(
        factor_one, factor_two, (((0,), (0,)), ((), ())), preferred_element_type=jnp.float32
    )


def cols_product(factor_one, factor_two):
    return lax.dot_general(
        factor_one, factor_two, (((1,), (1,)), ((), ())), preferred_element_type=jnp.float32
    )


def on_device_general(
    tokens,
    starts,
    query_key_value_weight,
    attention_output_weight,
    up_projection_weight,
    down_projection_weight,
    first_gain,
    first_shift,
    second_gain,
    second_shift,
    cotangent,
):
    local_len = tokens.shape[1]
    model_width = tokens.shape[2]
    head_count = model_width // HEAD
    block_count = local_len // BLOCK
    block_shape = (block_count, BLOCK, head_count, HEAD)
    zero_low = jnp.zeros((), jnp.bfloat16)
    input_tokens = tokens[0].astype(jnp.float32)
    first_pos = lax.axis_index("seq") * local_len
    positions = first_pos + jnp.arange(local_len, dtype=jnp.int32)
    pack_starts = starts[0]
    image_ids = jnp.sum((pack_starts[None, :] <= positions[:, None]).astype(jnp.int32), axis=1) - 1
    before_id = jnp.sum((pack_starts <= first_pos - 1).astype(jnp.int32)) - 1
    causal = jnp.arange(BLOCK)[:, None] >= jnp.arange(BLOCK)[None, :]
    attn_set = (
        lax.all_gather(query_key_value_weight, ("dp", "seq"), axis=0, tiled=True),
        lax.all_gather(attention_output_weight, ("dp", "seq"), axis=0, tiled=True),
        lax.all_gather(first_gain, ("dp", "seq"), axis=0, tiled=True),
        lax.all_gather(first_shift, ("dp", "seq"), axis=0, tiled=True),
    )
    in_full = attn_set[0]
    out_full = attn_set[1]
    gain_one = attn_set[2].astype(jnp.float32)
    shift_one = attn_set[3].astype(jnp.float32)
    first_normed_tokens = layer_norm(input_tokens, gain_one, shift_one)
    normed_low = first_normed_tokens.astype(jnp.bfloat16)
    projected_tokens = jnp.dot(normed_low, in_full, preferred_element_type=jnp.float32)
    queries = projected_tokens[:, :model_width]
    keys_raw = projected_tokens[:, model_width : 2 * model_width]
    values_raw = projected_tokens[:, 2 * model_width :]
    feat_query = feature(queries).astype(jnp.bfloat16).reshape(block_shape)
    feat_key = feature(keys_raw).astype(jnp.bfloat16).reshape(block_shape)
    value_low = values_raw.astype(jnp.bfloat16).reshape(block_shape)
    block_number = 0
    last_id = image_ids[-1]
    tail_mask = image_ids == last_id
    tail_key = jnp.where(tail_mask[:, None, None], feat_key[block_number], zero_low)
    keep_list = [image_ids == before_id]
    tail_list = [tail_mask]
    flag_list = [(last_id == before_id).astype(jnp.float32)]
    same_list = [causal & (image_ids[:, None] == image_ids[None, :])]
    update_list = [
        jnp.einsum(
            "jhe,jhf->hef", tail_key, value_low[block_number], preferred_element_type=jnp.float32
        )
    ]
    total_list = [jnp.sum(tail_key.astype(jnp.float32), axis=0)]
    identity = (
        jnp.ones((), jnp.float32),
        jnp.zeros((head_count, HEAD, HEAD), jnp.float32),
        jnp.zeros((head_count, HEAD), jnp.float32),
    )
    combined = identity
    block_number = 0
    combined = combine(
        combined, (flag_list[block_number], update_list[block_number], total_list[block_number])
    )
    entering = prefix(combined, "seq", combine, identity, False)
    memory = entering[1]
    key_sum = entering[2]
    block_number = 0
    query_block = feat_query[block_number]
    keep_float = keep_list[block_number].astype(jnp.float32)
    memory_low = memory.astype(jnp.bfloat16)
    raw_scores = jnp.einsum(
        "the,jhe->htj", query_block, feat_key[block_number], preferred_element_type=jnp.float32
    )
    masked = jnp.where(same_list[block_number][None], raw_scores, 0.0)
    scores_low = masked.astype(jnp.bfloat16)
    carried = (
        jnp.einsum("the,hef->thf", query_block, memory_low, preferred_element_type=jnp.float32)
        * keep_float[:, None, None]
    )
    numerator = (
        jnp.einsum(
            "htj,jhf->thf", scores_low, value_low[block_number], preferred_element_type=jnp.float32
        )
        + carried
    )
    denominator = jnp.transpose(jnp.sum(masked, axis=2)) + keep_float[:, None] * jnp.sum(
        query_block.astype(jnp.float32) * key_sum[None], axis=2
    )
    memory_list = [memory_low]
    keysum_list = [key_sum]
    numer_list = [numerator]
    denom_list = [denominator]
    ratio_list = numerator / denominator[:, :, None]
    mixed_low = ratio_list.reshape(local_len, model_width).astype(jnp.bfloat16)
    middle_tokens = input_tokens + jnp.dot(mixed_low, out_full, preferred_element_type=jnp.float32)
    mlp_set = (
        lax.all_gather(up_projection_weight, ("dp", "seq"), axis=0, tiled=True),
        lax.all_gather(down_projection_weight, ("dp", "seq"), axis=0, tiled=True),
        lax.all_gather(second_gain, ("dp", "seq"), axis=0, tiled=True),
        lax.all_gather(second_shift, ("dp", "seq"), axis=0, tiled=True),
    )
    up_full = mlp_set[0]
    down_full = mlp_set[1]
    gain_two = mlp_set[2].astype(jnp.float32)
    shift_two = mlp_set[3].astype(jnp.float32)
    normed_two_low = layer_norm(middle_tokens, gain_two, shift_two).astype(jnp.bfloat16)
    upper_hidden = jnp.dot(normed_two_low, up_full, preferred_element_type=jnp.float32)
    active_low = jax.nn.gelu(upper_hidden).astype(jnp.bfloat16)
    result = middle_tokens + jnp.dot(active_low, down_full, preferred_element_type=jnp.float32)
    result_tokens = result.astype(jnp.bfloat16).reshape(1, local_len, model_width)
    grad_out = cotangent[0].astype(jnp.float32)
    mlp_again = (
        lax.all_gather(up_projection_weight, ("dp", "seq"), axis=0, tiled=True),
        lax.all_gather(down_projection_weight, ("dp", "seq"), axis=0, tiled=True),
        lax.all_gather(second_gain, ("dp", "seq"), axis=0, tiled=True),
        lax.all_gather(second_shift, ("dp", "seq"), axis=0, tiled=True),
    )
    up_back = mlp_again[0]
    down_back = mlp_again[1]
    grad_out_low = cotangent[0]
    grad_down = rows_product(active_low, grad_out_low)
    d_active = cols_product(grad_out_low, down_back)
    gelu_value, gelu_back = jax.vjp(jax.nn.gelu, upper_hidden)
    g_upper = gelu_back(d_active)[0].astype(jnp.bfloat16)
    grad_up = rows_product(normed_two_low, g_upper)
    d_normed_two = cols_product(g_upper, up_back)
    norm_value, norm_back = jax.vjp(layer_norm, middle_tokens, gain_two, shift_two)
    middle_part, grad_gain_two, grad_shift_two = norm_back(d_normed_two)
    g_middle = grad_out + middle_part
    attn_again = (
        lax.all_gather(query_key_value_weight, ("dp", "seq"), axis=0, tiled=True),
        lax.all_gather(attention_output_weight, ("dp", "seq"), axis=0, tiled=True),
        lax.all_gather(first_gain, ("dp", "seq"), axis=0, tiled=True),
        lax.all_gather(first_shift, ("dp", "seq"), axis=0, tiled=True),
    )
    in_back = attn_again[0]
    out_back = attn_again[1]
    g_middle_low = g_middle.astype(jnp.bfloat16)
    grad_out_weight = rows_product(mixed_low, g_middle_low)
    d_mixed = cols_product(g_middle_low, out_back).reshape(block_shape)
    block_number = 0
    query_block = feat_query[block_number]
    denominator = denom_list[block_number]
    g_numerator = (d_mixed[block_number] / denominator[:, :, None]).astype(jnp.bfloat16)
    g_denominator = -jnp.sum(d_mixed[block_number] * numer_list[block_number], axis=2) / (
        denominator * denominator
    )
    kept_query = jnp.where(keep_list[block_number][:, None, None], query_block, zero_low)
    gnum_list = [g_numerator]
    gden_list = [g_denominator]
    local_list = [
        jnp.einsum("the,thf->hef", kept_query, g_numerator, preferred_element_type=jnp.float32)
    ]
    localkey_list = [jnp.sum(kept_query.astype(jnp.float32) * g_denominator[:, :, None], axis=0)]
    combined = identity
    for block_number in reversed(range(block_count)):
        combined = combine(
            combined,
            (flag_list[block_number], local_list[block_number], localkey_list[block_number]),
        )
    leaving = prefix(combined, "seq", combine, identity, True)
    g_memory = leaving[1]
    g_key_sum = leaving[2]
    gq_list = []
    gk_list = []
    gv_list = []
    for block_number in reversed(range(block_count)):
        query_block = feat_query[block_number]
        key_block = feat_key[block_number]
        value_block = value_low[block_number]
        keep_float = keep_list[block_number].astype(jnp.float32)
        tail_float = tail_list[block_number].astype(jnp.float32)
        g_numerator = gnum_list[block_number]
        g_denominator = gden_list[block_number]
        g_update = g_memory.astype(jnp.bfloat16)
        raw_scores = jnp.einsum(
            "the,jhe->htj", query_block, key_block, preferred_element_type=jnp.float32
        )
        scores_low = jnp.where(same_list[block_number][None], raw_scores, 0.0).astype(jnp.bfloat16)
        g_scores = (
            jnp.einsum("thf,jhf->htj", g_numerator, value_block, preferred_element_type=jnp.float32)
            + jnp.transpose(g_denominator)[:, :, None]
        )
        g_scores_low = jnp.where(
            same_list[block_number][None], g_scores.astype(jnp.bfloat16), zero_low
        )
        query_grad = jnp.einsum(
            "htj,jhe->the", g_scores_low, key_block, preferred_element_type=jnp.float32
        )
        query_grad = query_grad + keep_float[:, None, None] * (
            jnp.einsum(
                "thf,hef->the",
                g_numerator,
                memory_list[block_number],
                preferred_element_type=jnp.float32,
            )
            + g_denominator[:, :, None] * keysum_list[block_number][None]
        )
        key_grad = jnp.einsum(
            "htj,the->jhe", g_scores_low, query_block, preferred_element_type=jnp.float32
        )
        key_grad = key_grad + tail_float[:, None, None] * (
            jnp.einsum("jhf,hef->jhe", value_block, g_update, preferred_element_type=jnp.float32)
            + g_key_sum[None]
        )
        tail_key = jnp.where(tail_list[block_number][:, None, None], key_block, zero_low)
        value_grad = jnp.einsum(
            "htj,thf->jhf", scores_low, g_numerator, preferred_element_type=jnp.float32
        )
        value_grad = value_grad + jnp.einsum(
            "jhe,hef->jhf", tail_key, g_update, preferred_element_type=jnp.float32
        )
        gq_list.append(query_grad)
        gk_list.append(key_grad)
        gv_list.append(value_grad)
        g_memory = local_list[block_number] + flag_list[block_number] * g_memory
        g_key_sum = localkey_list[block_number] + flag_list[block_number] * g_key_sum
    d_feat_query = jnp.concatenate(gq_list[::-1], axis=0).reshape(local_len, model_width)
    d_feat_key = jnp.concatenate(gk_list[::-1], axis=0).reshape(local_len, model_width)
    d_value = jnp.concatenate(gv_list[::-1], axis=0).reshape(local_len, model_width)
    query_value, query_back = jax.vjp(feature, queries)
    key_value, key_back = jax.vjp(feature, keys_raw)
    g_projected = jnp.concatenate(
        [query_back(d_feat_query)[0], key_back(d_feat_key)[0], d_value], axis=1
    ).astype(jnp.bfloat16)
    grad_in_weight = rows_product(normed_low, g_projected)
    d_normed = cols_product(g_projected, in_back)
    first_value, first_back = jax.vjp(layer_norm, input_tokens, gain_one, shift_one)
    input_part, grad_gain_one, grad_shift_one = first_back(d_normed)
    grad_tokens = (g_middle + input_part).reshape(1, local_len, model_width)
    summed = (
        lax.psum_scatter(grad_in_weight, ("dp", "seq"), scatter_dimension=0, tiled=True),
        lax.psum_scatter(grad_out_weight, ("dp", "seq"), scatter_dimension=0, tiled=True),
        lax.psum_scatter(grad_up, ("dp", "seq"), scatter_dimension=0, tiled=True),
        lax.psum_scatter(grad_down, ("dp", "seq"), scatter_dimension=0, tiled=True),
        lax.psum_scatter(grad_gain_one, ("dp", "seq"), scatter_dimension=0, tiled=True),
        lax.psum_scatter(grad_shift_one, ("dp", "seq"), scatter_dimension=0, tiled=True),
        lax.psum_scatter(grad_gain_two, ("dp", "seq"), scatter_dimension=0, tiled=True),
        lax.psum_scatter(grad_shift_two, ("dp", "seq"), scatter_dimension=0, tiled=True),
    )
    return (
        result_tokens,
        grad_tokens,
        summed[0],
        summed[1],
        summed[2],
        summed[3],
        summed[4],
        summed[5],
        summed[6],
        summed[7],
    )


MESH = pl.DeviceIdType.MESH
LOW = jnp.bfloat16
FULL = jnp.float32


class Place:
    def __init__(self):
        dp, seq = lax.axis_index("dp"), lax.axis_index("seq")
        self.y, self.x = dp // 2, dp % 2
        self.z, self.c = seq // 2, seq % 2
        self.dp, self.seq = dp, seq
        self.over_x = (self.y * 2 + 1 - self.x, seq)
        self.over_y = ((1 - self.y) * 2 + self.x, seq)
        self.sibling = (dp, self.z * 2 + 1 - self.c)
        self.along_z = [(dp, (self.z + d) % 4 * 2 + self.c) for d in (1, 2, 3)]

    def meet(self):
        barrier = pltpu.get_barrier_semaphore()
        everyone = [self.over_x, self.over_y, self.sibling, *self.along_z]
        for device in everyone:
            pl.semaphore_signal(barrier, inc=1, device_id=device, device_id_type=MESH)
        pl.semaphore_wait(barrier, len(everyone))


def remote(source, target, send, recv, device):
    return pltpu.make_async_remote_copy(
        src_ref=source,
        dst_ref=target,
        send_sem=send,
        recv_sem=recv,
        device_id=device,
        device_id_type=MESH,
    )


class Gather:
    def __init__(self, place, full, send, recv):
        p = place
        half = full.shape[4] // 2
        low, high = pl.ds(0, half), pl.ds(half, half)
        own = full.at[p.y, p.x, p.z, p.c]
        parts = [(own, device) for device in p.along_z]
        parts.append((full.at[p.y, p.x, :, p.c, low], p.over_x))
        parts.append((full.at[p.y, p.x, :, p.c, high], p.over_y))
        parts.append((full.at[p.y, :, :, p.c, low], p.over_y))
        parts.append((full.at[:, p.x, :, p.c, high], p.over_x))
        for y, x in ((p.y, p.x), (p.y, 1 - p.x), (1 - p.y, p.x), (1 - p.y, 1 - p.x)):
            parts.append((full.at[y, x, :, p.c], p.sibling))
        self.copies = [
            remote(ref, ref, send.at[i], recv.at[i], device)
            for i, (ref, device) in enumerate(parts)
        ]

    def start(self, *which):
        for i in which:
            self.copies[i].start()

    def arrive(self, *which):
        for i in which:
            self.copies[i].wait_recv()

    def step(self, number):
        if number == 0:
            self.start(0, 1, 2)
        elif number == 1:
            self.arrive(0, 1, 2)
            self.start(3, 4, 7)
        elif number == 2:
            self.arrive(3, 4)
            self.start(5, 6)
        elif number == 3:
            self.arrive(5, 6)
            self.start(8, 9, 10)
        else:
            self.arrive(7, 8, 9, 10)

    def finish(self):
        for copy in self.copies:
            copy.wait_send()


class Scatter:
    def __init__(self, place, own, total, pair, first_a, first_b, second_a, second_b, last, send, recv):
        p = place
        half = own.shape[4] // 2
        self.place, self.half = p, half
        self.own, self.total, self.pair = own, total, pair
        self.first_a, self.first_b = first_a, first_b
        self.second_a, self.second_b = second_a, second_b
        self.last = last
        low, high = pl.ds(0, half), pl.ds(half, half)
        parts = [
            (own.at[:, :, :, 1 - p.c], pair, p.sibling),
            (total.at[1 - p.y, :, :, low], first_a, p.over_y),
            (total.at[:, 1 - p.x, :, high], first_b, p.over_x),
            (total.at[p.y, 1 - p.x, :, low], second_a, p.over_x),
            (total.at[1 - p.y, p.x, :, high], second_b, p.over_y),
        ]
        self.keep = pltpu.make_async_copy(own.at[:, :, :, p.c], total, send.at[8])
        for d in (1, 2, 3):
            parts.append((total.at[p.y, p.x, (p.z + d) % 4], last.at[d - 1], p.along_z[d - 1]))
        self.copies = [
            remote(source, target, send.at[i], recv.at[i], device)
            for i, (source, target, device) in enumerate(parts)
        ]

    def step(self, number):
        p, half = self.place, self.half
        low, high = slice(0, half), slice(half, 2 * half)
        total = self.total
        if number == 0:
            self.copies[0].start()
            self.keep.start()
        elif number == 1:
            self.keep.wait()
            self.copies[0].wait_recv()

            @pl.loop(0, 4)
            def _(i):
                y, x = i // 2, i % 2
                total[y, x] = total[y, x] + self.pair[y, x]

            self.copies[1].start()
            self.copies[2].start()
        elif number == 2:
            self.copies[1].wait_recv()
            self.copies[2].wait_recv()
            for i in range(2):
                total[p.y, i, :, low] += self.first_a[i]
                total[i, p.x, :, high] += self.first_b[i]
            self.copies[3].start()
            self.copies[4].start()
        elif number == 3:
            self.copies[3].wait_recv()
            self.copies[4].wait_recv()
            total[p.y, p.x, :, low] += self.second_a[...]
            total[p.y, p.x, :, high] += self.second_b[...]
            for i in (5, 6, 7):
                self.copies[i].start()

    def result(self):
        for i in (5, 6, 7):
            self.copies[i].wait_recv()
        p = self.place
        value = total = self.total[p.y, p.x, p.z].astype(FULL)
        for d in range(3):
            value = value + self.last[d].astype(FULL)
        return value

    def finish(self):
        for copy in self.copies:
            copy.wait_send()


def gather_kernel(inputs, outputs, wide, tall, pack, send, recv, sends, recvs, local):
    p = Place()
    for j in range(8):
        source = inputs[min(j // 3, 2) if j < 4 else 2] if j != 3 else inputs[1]
        column = j if j < 3 else (0 if j == 3 else j - 4)
        wide[j, p.y, p.x, p.z, p.c] = source[:, column * 1024 : column * 1024 + 1024]
    for j in range(4):
        tall[j, p.y, p.x, p.z, p.c] = inputs[3][:, 256 * j : 256 * j + 256]
    pack[p.y, p.x, p.z, p.c] = inputs[4][...]
    p.meet()
    small = SmallGather(p, pack, sends, recvs)
    chunks = [Gather(p, wide.at[j], send.at[j], recv.at[j]) for j in range(8)]
    chunks += [Gather(p, tall.at[j], send.at[8 + j], recv.at[8 + j]) for j in range(4)]
    outs = []
    for j in range(8):
        target = outputs[0] if j < 3 else (outputs[1] if j == 3 else outputs[2])
        column = j if j < 3 else (0 if j == 3 else j - 4)
        outs.append(
            pltpu.make_async_copy(
                wide.at[j], target.at[:, :, :, :, :, pl.ds(column * 1024, 1024)], local.at[j]
            )
        )
    for j in range(4):
        outs.append(
            pltpu.make_async_copy(
                tall.at[j], outputs[3].at[:, :, :, :, :, pl.ds(256 * j, 256)], local.at[8 + j]
            )
        )
    for tick in range(12 + 4):
        for number in range(5):
            j = tick - number
            if 0 <= j < 12:
                chunks[j].step(number)
                if number == 4:
                    outs[j].start()
        if tick < 5:
            small.step(tick)
    outputs[4][...] = pack[...]
    small.finish()
    for chunk in chunks:
        chunk.finish()
    for copy in outs:
        copy.wait()


def gather_all(in_weight, out_weight, up_weight, down_weight, pack):
    block = lambda rows, columns: jax.ShapeDtypeStruct((2, 2, 4, 2, rows, columns), LOW)

    def body(*refs):
        gather_kernel(refs[:5], refs[5:10], *refs[10:])

    return pl.pallas_call(
        body,
        out_shape=[block(32, 3072), block(32, 1024), block(32, 4096), block(128, 1024), block(16, 128)],
        in_specs=[pl.BlockSpec(memory_space=pltpu.VMEM)] * 5,
        out_specs=[pl.BlockSpec(memory_space=pl.ANY)] * 4 + [pl.BlockSpec(memory_space=pltpu.VMEM)],
        scratch_shapes=[
            pltpu.VMEM((8, 2, 2, 4, 2, 32, 1024), LOW),
            pltpu.VMEM((4, 2, 2, 4, 2, 128, 256), LOW),
            pltpu.VMEM((2, 2, 4, 2, 16, 128), LOW),
            pltpu.SemaphoreType.DMA((12, 11)),
            pltpu.SemaphoreType.DMA((12, 11)),
            pltpu.SemaphoreType.DMA((9,)),
            pltpu.SemaphoreType.DMA((9,)),
            pltpu.SemaphoreType.DMA((12,)),
        ],
        compiler_params=pltpu.CompilerParams(
            collective_id=0, has_side_effects=True, vmem_limit_bytes=60 << 20
        ),
        name="gather_weights",
    )(in_weight, out_weight, up_weight, down_weight, pack)


def scatter_kernel(inputs, outputs, wide, tall, send, recv):
    p = Place()
    p.meet()
    order = [8, 9, 10, 11, 4, 5, 6, 7, 3, 0, 1, 2]
    chunks = []
    places = []
    for j in range(12):
        if j < 8:
            source = 0 if j < 3 else (1 if j == 3 else 2)
            column = j if j < 3 else (0 if j == 3 else j - 4)
            columns = pl.ds(column * 1024, 1024)
            own, buffers, at = inputs[source].at[:, :, :, :, :, columns], wide, j
        else:
            source, columns, buffers, at = 3, pl.ds((j - 8) * 256, 256), tall, j - 8
            own = inputs[3].at[:, :, :, :, :, columns]
        chunks.append(Scatter(p, own, *[ref.at[at] for ref in buffers], send.at[j], recv.at[j]))
        places.append((source, columns))
    for tick in range(12 + 4):
        for number in range(5):
            if 0 <= tick - number < 12:
                j = order[tick - number]
                if number < 4:
                    chunks[j].step(number)
                else:
                    source, columns = places[j]
                    outputs[source][:, columns] = chunks[j].result()
    for chunk in chunks:
        chunk.finish()


def scatter_buffers(count, rows, columns):
    half = rows // 2
    shapes = [
        (2, 2, 4, rows, columns),
        (2, 2, 4, rows, columns),
        (2, 4, half, columns),
        (2, 4, half, columns),
        (4, half, columns),
        (4, half, columns),
        (3, rows, columns),
    ]
    return [pltpu.VMEM((count, *shape), LOW) for shape in shapes]


def scatter_all(*grads):
    def body(*refs):
        scatter_kernel(refs[:4], refs[4:8], refs[8:15], refs[15:22], *refs[22:])

    return pl.pallas_call(
        body,
        out_shape=[
            jax.ShapeDtypeStruct(shape, FULL)
            for shape in ((32, 3072), (32, 1024), (32, 4096), (128, 1024))
        ],
        in_specs=[pl.BlockSpec(memory_space=pl.ANY)] * 4,
        out_specs=[pl.BlockSpec(memory_space=pltpu.VMEM)] * 4,
        scratch_shapes=scatter_buffers(8, 32, 1024)
        + scatter_buffers(4, 128, 256)
        + [pltpu.SemaphoreType.DMA((12, 9)), pltpu.SemaphoreType.DMA((12, 8))],
        compiler_params=pltpu.CompilerParams(
            collective_id=1, has_side_effects=True, vmem_limit_bytes=60 << 20
        ),
        name="scatter_gradients",
    )(*[grad.reshape(2, 2, 4, 2, grad.shape[0] // 32, grad.shape[1]) for grad in grads])


class SmallGather(Gather):
    def __init__(self, place, full, send, recv):
        p = place
        own = full.at[p.y, p.x, p.z, p.c]
        parts = [(own, device) for device in p.along_z]
        parts.append((full.at[p.y, p.x, :, p.c], p.over_x))
        parts.append((full.at[p.y, :, :, p.c], p.over_y))
        for y in range(2):
            for x in range(2):
                parts.append((full.at[y, x, :, p.c], p.sibling))
        self.copies = [
            remote(ref, ref, send.at[i], recv.at[i], device)
            for i, (ref, device) in enumerate(parts)
        ]

    def step(self, number):
        if number == 0:
            self.start(0, 1, 2)
        elif number == 1:
            self.arrive(0, 1, 2)
            self.start(3)
        elif number == 2:
            self.arrive(3)
            self.start(4)
        elif number == 3:
            self.arrive(4)
            self.start(5, 6, 7, 8)
        else:
            self.arrive(5, 6, 7, 8)


def on_device(
    tokens,
    starts,
    query_key_value_weight,
    attention_output_weight,
    up_projection_weight,
    down_projection_weight,
    first_gain,
    first_shift,
    second_gain,
    second_shift,
    cotangent,
):
    local_len = tokens.shape[1]
    model_width = tokens.shape[2]
    head_count = model_width // HEAD
    block_count = local_len // BLOCK
    block_shape = (block_count, BLOCK, head_count, HEAD)
    zero_low = jnp.zeros((), jnp.bfloat16)
    input_tokens = tokens[0].astype(jnp.float32)
    first_pos = lax.axis_index("seq") * local_len
    positions = first_pos + jnp.arange(local_len, dtype=jnp.int32)
    pack_starts = starts[0]
    image_ids = jnp.sum((pack_starts[None, :] <= positions[:, None]).astype(jnp.int32), axis=1) - 1
    before_id = jnp.sum((pack_starts <= first_pos - 1).astype(jnp.int32)) - 1
    causal = jnp.arange(BLOCK)[:, None] >= jnp.arange(BLOCK)[None, :]
    mine = lax.axis_index("dp") * 8 + lax.axis_index("seq")
    pack = jnp.stack([first_gain, first_shift, second_gain, second_shift]).astype(FULL)
    pack = jnp.roll(jnp.pad(pack, ((0, 12), (0, 96))), 32 * (mine % 4), axis=1).astype(LOW)
    in_full, out_full, up_full, down_full, packs = gather_all(
        query_key_value_weight,
        attention_output_weight,
        up_projection_weight,
        down_projection_weight,
        pack,
    )
    in_full, out_full = in_full.reshape(1024, 3072), out_full.reshape(1024, 1024)
    up_full, down_full = up_full.reshape(1024, 4096), down_full.reshape(4096, 1024)
    packs = jnp.sum(packs.reshape(8, 4, 16, 128).astype(FULL), axis=1)
    packs = jnp.transpose(packs[:, :4], (1, 0, 2)).reshape(4, 1024)
    gain_one, shift_one, gain_two, shift_two = packs[0], packs[1], packs[2], packs[3]
    first_normed_tokens = layer_norm(input_tokens, gain_one, shift_one)
    normed_low = first_normed_tokens.astype(jnp.bfloat16)
    projected_tokens = jnp.dot(normed_low, in_full, preferred_element_type=jnp.float32)
    queries = projected_tokens[:, :model_width]
    keys_raw = projected_tokens[:, model_width : 2 * model_width]
    values_raw = projected_tokens[:, 2 * model_width :]
    feat_query = feature(queries).astype(jnp.bfloat16).reshape(block_shape)
    feat_key = feature(keys_raw).astype(jnp.bfloat16).reshape(block_shape)
    value_low = values_raw.astype(jnp.bfloat16).reshape(block_shape)
    block_number = 0
    last_id = image_ids[-1]
    tail_mask = image_ids == last_id
    tail_key = jnp.where(tail_mask[:, None, None], feat_key[block_number], zero_low)
    keep_list = [image_ids == before_id]
    tail_list = [tail_mask]
    flag_list = [(last_id == before_id).astype(jnp.float32)]
    same_list = [causal & (image_ids[:, None] == image_ids[None, :])]
    update_list = [
        jnp.einsum(
            "jhe,jhf->hef", tail_key, value_low[block_number], preferred_element_type=jnp.float32
        )
    ]
    total_list = [jnp.sum(tail_key.astype(jnp.float32), axis=0)]
    identity = (
        jnp.ones((), jnp.float32),
        jnp.zeros((head_count, HEAD, HEAD), jnp.float32),
        jnp.zeros((head_count, HEAD), jnp.float32),
    )
    combined = identity
    block_number = 0
    combined = combine(
        combined, (flag_list[block_number], update_list[block_number], total_list[block_number])
    )
    entering = prefix(combined, "seq", combine, identity, False)
    memory = entering[1]
    key_sum = entering[2]
    block_number = 0
    query_block = feat_query[block_number]
    keep_float = keep_list[block_number].astype(jnp.float32)
    memory_low = memory.astype(jnp.bfloat16)
    raw_scores = jnp.einsum(
        "the,jhe->htj", query_block, feat_key[block_number], preferred_element_type=jnp.float32
    )
    masked = jnp.where(same_list[block_number][None], raw_scores, 0.0)
    scores_low = masked.astype(jnp.bfloat16)
    carried = (
        jnp.einsum("the,hef->thf", query_block, memory_low, preferred_element_type=jnp.float32)
        * keep_float[:, None, None]
    )
    numerator = (
        jnp.einsum(
            "htj,jhf->thf", scores_low, value_low[block_number], preferred_element_type=jnp.float32
        )
        + carried
    )
    denominator = jnp.transpose(jnp.sum(masked, axis=2)) + keep_float[:, None] * jnp.sum(
        query_block.astype(jnp.float32) * key_sum[None], axis=2
    )
    memory_list = [memory_low]
    keysum_list = [key_sum]
    numer_list = [numerator]
    denom_list = [denominator]
    ratio_list = numerator / denominator[:, :, None]
    mixed_low = ratio_list.reshape(local_len, model_width).astype(jnp.bfloat16)
    middle_tokens = input_tokens + jnp.dot(mixed_low, out_full, preferred_element_type=jnp.float32)
    normed_two_low = layer_norm(middle_tokens, gain_two, shift_two).astype(jnp.bfloat16)
    upper_hidden = jnp.dot(normed_two_low, up_full, preferred_element_type=jnp.float32)
    active_low = jax.nn.gelu(upper_hidden).astype(jnp.bfloat16)
    result = middle_tokens + jnp.dot(active_low, down_full, preferred_element_type=jnp.float32)
    result_tokens = result.astype(jnp.bfloat16).reshape(1, local_len, model_width)
    grad_out = cotangent[0].astype(jnp.float32)
    grad_out_low = cotangent[0]
    grad_down = rows_product(active_low, grad_out_low)
    d_active = cols_product(grad_out_low, down_full)
    gelu_value, gelu_back = jax.vjp(jax.nn.gelu, upper_hidden)
    g_upper = gelu_back(d_active)[0].astype(jnp.bfloat16)
    grad_up = rows_product(normed_two_low, g_upper)
    d_normed_two = cols_product(g_upper, up_full)
    norm_value, norm_back = jax.vjp(layer_norm, middle_tokens, gain_two, shift_two)
    middle_part, grad_gain_two, grad_shift_two = norm_back(d_normed_two)
    g_middle = grad_out + middle_part
    g_middle_low = g_middle.astype(jnp.bfloat16)
    grad_out_weight = rows_product(mixed_low, g_middle_low)
    d_mixed = cols_product(g_middle_low, out_full).reshape(block_shape)
    block_number = 0
    query_block = feat_query[block_number]
    denominator = denom_list[block_number]
    g_numerator = (d_mixed[block_number] / denominator[:, :, None]).astype(jnp.bfloat16)
    g_denominator = -jnp.sum(d_mixed[block_number] * numer_list[block_number], axis=2) / (
        denominator * denominator
    )
    kept_query = jnp.where(keep_list[block_number][:, None, None], query_block, zero_low)
    gnum_list = [g_numerator]
    gden_list = [g_denominator]
    local_list = [
        jnp.einsum("the,thf->hef", kept_query, g_numerator, preferred_element_type=jnp.float32)
    ]
    localkey_list = [jnp.sum(kept_query.astype(jnp.float32) * g_denominator[:, :, None], axis=0)]
    combined = identity
    for block_number in reversed(range(block_count)):
        combined = combine(
            combined,
            (flag_list[block_number], local_list[block_number], localkey_list[block_number]),
        )
    leaving = prefix(combined, "seq", combine, identity, True)
    g_memory = leaving[1]
    g_key_sum = leaving[2]
    gq_list = []
    gk_list = []
    gv_list = []
    for block_number in reversed(range(block_count)):
        query_block = feat_query[block_number]
        key_block = feat_key[block_number]
        value_block = value_low[block_number]
        keep_float = keep_list[block_number].astype(jnp.float32)
        tail_float = tail_list[block_number].astype(jnp.float32)
        g_numerator = gnum_list[block_number]
        g_denominator = gden_list[block_number]
        g_update = g_memory.astype(jnp.bfloat16)
        raw_scores = jnp.einsum(
            "the,jhe->htj", query_block, key_block, preferred_element_type=jnp.float32
        )
        scores_low = jnp.where(same_list[block_number][None], raw_scores, 0.0).astype(jnp.bfloat16)
        g_scores = (
            jnp.einsum("thf,jhf->htj", g_numerator, value_block, preferred_element_type=jnp.float32)
            + jnp.transpose(g_denominator)[:, :, None]
        )
        g_scores_low = jnp.where(
            same_list[block_number][None], g_scores.astype(jnp.bfloat16), zero_low
        )
        query_grad = jnp.einsum(
            "htj,jhe->the", g_scores_low, key_block, preferred_element_type=jnp.float32
        )
        query_grad = query_grad + keep_float[:, None, None] * (
            jnp.einsum(
                "thf,hef->the",
                g_numerator,
                memory_list[block_number],
                preferred_element_type=jnp.float32,
            )
            + g_denominator[:, :, None] * keysum_list[block_number][None]
        )
        key_grad = jnp.einsum(
            "htj,the->jhe", g_scores_low, query_block, preferred_element_type=jnp.float32
        )
        key_grad = key_grad + tail_float[:, None, None] * (
            jnp.einsum("jhf,hef->jhe", value_block, g_update, preferred_element_type=jnp.float32)
            + g_key_sum[None]
        )
        tail_key = jnp.where(tail_list[block_number][:, None, None], key_block, zero_low)
        value_grad = jnp.einsum(
            "htj,thf->jhf", scores_low, g_numerator, preferred_element_type=jnp.float32
        )
        value_grad = value_grad + jnp.einsum(
            "jhe,hef->jhf", tail_key, g_update, preferred_element_type=jnp.float32
        )
        gq_list.append(query_grad)
        gk_list.append(key_grad)
        gv_list.append(value_grad)
        g_memory = local_list[block_number] + flag_list[block_number] * g_memory
        g_key_sum = localkey_list[block_number] + flag_list[block_number] * g_key_sum
    d_feat_query = jnp.concatenate(gq_list[::-1], axis=0).reshape(local_len, model_width)
    d_feat_key = jnp.concatenate(gk_list[::-1], axis=0).reshape(local_len, model_width)
    d_value = jnp.concatenate(gv_list[::-1], axis=0).reshape(local_len, model_width)
    query_value, query_back = jax.vjp(feature, queries)
    key_value, key_back = jax.vjp(feature, keys_raw)
    g_projected = jnp.concatenate(
        [query_back(d_feat_query)[0], key_back(d_feat_key)[0], d_value], axis=1
    ).astype(jnp.bfloat16)
    grad_in_weight = rows_product(normed_low, g_projected)
    d_normed = cols_product(g_projected, in_full)
    first_value, first_back = jax.vjp(layer_norm, input_tokens, gain_one, shift_one)
    input_part, grad_gain_one, grad_shift_one = first_back(d_normed)
    grad_tokens = (g_middle + input_part).reshape(1, local_len, model_width)
    weights = scatter_all(
        grad_in_weight.astype(LOW),
        grad_out_weight.astype(LOW),
        grad_up.astype(LOW),
        grad_down.astype(LOW),
    )
    summed = (
        *weights,
        lax.psum_scatter(grad_gain_one, ("dp", "seq"), scatter_dimension=0, tiled=True),
        lax.psum_scatter(grad_shift_one, ("dp", "seq"), scatter_dimension=0, tiled=True),
        lax.psum_scatter(grad_gain_two, ("dp", "seq"), scatter_dimension=0, tiled=True),
        lax.psum_scatter(grad_shift_two, ("dp", "seq"), scatter_dimension=0, tiled=True),
    )
    return (
        result_tokens,
        grad_tokens,
        summed[0],
        summed[1],
        summed[2],
        summed[3],
        summed[4],
        summed[5],
        summed[6],
        summed[7],
    )


def solution(mesh):

    fast = dict(mesh.shape) == {"dp": 4, "seq": 8}
    return jax.shard_map(
        on_device if fast else on_device_general,
        mesh=mesh,
        in_specs=(
            P("dp", "seq", None),
            P("dp", None),
            P(("dp", "seq"), None),
            P(("dp", "seq"), None),
            P(("dp", "seq"), None),
            P(("dp", "seq"), None),
            P(("dp", "seq")),
            P(("dp", "seq")),
            P(("dp", "seq")),
            P(("dp", "seq")),
            P("dp", "seq", None),
        ),
        out_specs=(
            P("dp", "seq", None),
            P("dp", "seq", None),
            P(("dp", "seq"), None),
            P(("dp", "seq"), None),
            P(("dp", "seq"), None),
            P(("dp", "seq"), None),
            P(("dp", "seq")),
            P(("dp", "seq")),
            P(("dp", "seq")),
            P(("dp", "seq")),
        ),
        check_vma=False,
    )
```

```python
import functools

import jax
import jax.numpy as jnp
from jax import lax
from jax.experimental import pallas as pl
from jax.experimental.pallas import tpu as pltpu
from jax.sharding import PartitionSpec as P

HEAD = 64
BLOCK = 512


def prefix(value, axis, combine, identity, reverse):
    size, mine = (lax.axis_size(axis), lax.axis_index(axis))
    everything = jax.tree.map(
        lambda part, kind: lax.all_gather(part.astype(kind), axis),
        value,
        jax.tree.map(lambda a: jnp.bfloat16 if a.dtype == jnp.float32 else a.dtype, value),
    )
    start = jax.tree.map(
        lambda part, zero: jnp.broadcast_to(jnp.asarray(zero, part.dtype), part.shape),
        value,
        identity,
    )

    def lap(k, before):
        at = size - 1 - k if reverse else k
        reached = at > mine if reverse else at < mine
        new = combine(
            before, jax.tree.map(lambda part, own: part[at].astype(own.dtype), everything, value)
        )
        return jax.tree.map(lambda a, b: jnp.where(reached, a, b), new, before)

    return lax.fori_loop(0, size, lap, start)


def layer_norm(values, norm_gain, norm_shift):
    average = jnp.mean(values, axis=-1, keepdims=True)
    centred = values - average
    spread = jnp.mean(centred * centred, axis=-1, keepdims=True)
    return centred * lax.rsqrt(spread + 1e-05) * norm_gain + norm_shift


def feature(values):
    return jax.nn.elu(values) + 1.0


def combine(former, latter):
    return (
        former[0] * latter[0],
        latter[0] * former[1] + latter[1],
        latter[0] * former[2] + latter[2],
    )


def rows_product(factor_one, factor_two):
    return lax.dot_general(
        factor_one, factor_two, (((0,), (0,)), ((), ())), preferred_element_type=jnp.float32
    )


def cols_product(factor_one, factor_two):
    return lax.dot_general(
        factor_one, factor_two, (((1,), (1,)), ((), ())), preferred_element_type=jnp.float32
    )


def on_device_general(
    tokens,
    starts,
    query_key_value_weight,
    attention_output_weight,
    up_projection_weight,
    down_projection_weight,
    first_gain,
    first_shift,
    second_gain,
    second_shift,
    cotangent,
):
    local_len = tokens.shape[1]
    model_width = tokens.shape[2]
    head_count = model_width // HEAD
    block_count = local_len // BLOCK
    block_shape = (block_count, BLOCK, head_count, HEAD)
    zero_low = jnp.zeros((), jnp.bfloat16)
    input_tokens = tokens[0].astype(jnp.float32)
    first_pos = lax.axis_index("seq") * local_len
    positions = first_pos + jnp.arange(local_len, dtype=jnp.int32)
    pack_starts = starts[0]
    image_ids = jnp.sum((pack_starts[None, :] <= positions[:, None]).astype(jnp.int32), axis=1) - 1
    before_id = jnp.sum((pack_starts <= first_pos - 1).astype(jnp.int32)) - 1
    causal = jnp.arange(BLOCK)[:, None] >= jnp.arange(BLOCK)[None, :]
    attn_set = (
        lax.all_gather(query_key_value_weight, ("dp", "seq"), axis=0, tiled=True),
        lax.all_gather(attention_output_weight, ("dp", "seq"), axis=0, tiled=True),
        lax.all_gather(first_gain, ("dp", "seq"), axis=0, tiled=True),
        lax.all_gather(first_shift, ("dp", "seq"), axis=0, tiled=True),
    )
    in_full = attn_set[0]
    out_full = attn_set[1]
    gain_one = attn_set[2].astype(jnp.float32)
    shift_one = attn_set[3].astype(jnp.float32)
    first_normed_tokens = layer_norm(input_tokens, gain_one, shift_one)
    normed_low = first_normed_tokens.astype(jnp.bfloat16)
    projected_tokens = jnp.dot(normed_low, in_full, preferred_element_type=jnp.float32)
    queries = projected_tokens[:, :model_width]
    keys_raw = projected_tokens[:, model_width : 2 * model_width]
    values_raw = projected_tokens[:, 2 * model_width :]
    feat_query = feature(queries).astype(jnp.bfloat16).reshape(block_shape)
    feat_key = feature(keys_raw).astype(jnp.bfloat16).reshape(block_shape)
    value_low = values_raw.astype(jnp.bfloat16).reshape(block_shape)
    block_number = 0
    last_id = image_ids[-1]
    tail_mask = image_ids == last_id
    tail_key = jnp.where(tail_mask[:, None, None], feat_key[block_number], zero_low)
    keep_list = [image_ids == before_id]
    tail_list = [tail_mask]
    flag_list = [(last_id == before_id).astype(jnp.float32)]
    same_list = [causal & (image_ids[:, None] == image_ids[None, :])]
    update_list = [
        jnp.einsum(
            "jhe,jhf->hef", tail_key, value_low[block_number], preferred_element_type=jnp.float32
        )
    ]
    total_list = [jnp.sum(tail_key.astype(jnp.float32), axis=0)]
    identity = (
        jnp.ones((), jnp.float32),
        jnp.zeros((head_count, HEAD, HEAD), jnp.float32),
        jnp.zeros((head_count, HEAD), jnp.float32),
    )
    combined = identity
    block_number = 0
    combined = combine(
        combined, (flag_list[block_number], update_list[block_number], total_list[block_number])
    )
    entering = prefix(combined, "seq", combine, identity, False)
    memory = entering[1]
    key_sum = entering[2]
    block_number = 0
    query_block = feat_query[block_number]
    keep_float = keep_list[block_number].astype(jnp.float32)
    memory_low = memory.astype(jnp.bfloat16)
    raw_scores = jnp.einsum(
        "the,jhe->htj", query_block, feat_key[block_number], preferred_element_type=jnp.float32
    )
    masked = jnp.where(same_list[block_number][None], raw_scores, 0.0)
    scores_low = masked.astype(jnp.bfloat16)
    carried = (
        jnp.einsum("the,hef->thf", query_block, memory_low, preferred_element_type=jnp.float32)
        * keep_float[:, None, None]
    )
    numerator = (
        jnp.einsum(
            "htj,jhf->thf", scores_low, value_low[block_number], preferred_element_type=jnp.float32
        )
        + carried
    )
    denominator = jnp.transpose(jnp.sum(masked, axis=2)) + keep_float[:, None] * jnp.sum(
        query_block.astype(jnp.float32) * key_sum[None], axis=2
    )
    memory_list = [memory_low]
    keysum_list = [key_sum]
    numer_list = [numerator]
    denom_list = [denominator]
    ratio_list = numerator / denominator[:, :, None]
    mixed_low = ratio_list.reshape(local_len, model_width).astype(jnp.bfloat16)
    middle_tokens = input_tokens + jnp.dot(mixed_low, out_full, preferred_element_type=jnp.float32)
    mlp_set = (
        lax.all_gather(up_projection_weight, ("dp", "seq"), axis=0, tiled=True),
        lax.all_gather(down_projection_weight, ("dp", "seq"), axis=0, tiled=True),
        lax.all_gather(second_gain, ("dp", "seq"), axis=0, tiled=True),
        lax.all_gather(second_shift, ("dp", "seq"), axis=0, tiled=True),
    )
    up_full = mlp_set[0]
    down_full = mlp_set[1]
    gain_two = mlp_set[2].astype(jnp.float32)
    shift_two = mlp_set[3].astype(jnp.float32)
    normed_two_low = layer_norm(middle_tokens, gain_two, shift_two).astype(jnp.bfloat16)
    upper_hidden = jnp.dot(normed_two_low, up_full, preferred_element_type=jnp.float32)
    active_low = jax.nn.gelu(upper_hidden).astype(jnp.bfloat16)
    result = middle_tokens + jnp.dot(active_low, down_full, preferred_element_type=jnp.float32)
    result_tokens = result.astype(jnp.bfloat16).reshape(1, local_len, model_width)
    grad_out = cotangent[0].astype(jnp.float32)
    mlp_again = (
        lax.all_gather(up_projection_weight, ("dp", "seq"), axis=0, tiled=True),
        lax.all_gather(down_projection_weight, ("dp", "seq"), axis=0, tiled=True),
        lax.all_gather(second_gain, ("dp", "seq"), axis=0, tiled=True),
        lax.all_gather(second_shift, ("dp", "seq"), axis=0, tiled=True),
    )
    up_back = mlp_again[0]
    down_back = mlp_again[1]
    grad_out_low = cotangent[0]
    grad_down = rows_product(active_low, grad_out_low)
    d_active = cols_product(grad_out_low, down_back)
    gelu_value, gelu_back = jax.vjp(jax.nn.gelu, upper_hidden)
    g_upper = gelu_back(d_active)[0].astype(jnp.bfloat16)
    grad_up = rows_product(normed_two_low, g_upper)
    d_normed_two = cols_product(g_upper, up_back)
    norm_value, norm_back = jax.vjp(layer_norm, middle_tokens, gain_two, shift_two)
    middle_part, grad_gain_two, grad_shift_two = norm_back(d_normed_two)
    g_middle = grad_out + middle_part
    attn_again = (
        lax.all_gather(query_key_value_weight, ("dp", "seq"), axis=0, tiled=True),
        lax.all_gather(attention_output_weight, ("dp", "seq"), axis=0, tiled=True),
        lax.all_gather(first_gain, ("dp", "seq"), axis=0, tiled=True),
        lax.all_gather(first_shift, ("dp", "seq"), axis=0, tiled=True),
    )
    in_back = attn_again[0]
    out_back = attn_again[1]
    g_middle_low = g_middle.astype(jnp.bfloat16)
    grad_out_weight = rows_product(mixed_low, g_middle_low)
    d_mixed = cols_product(g_middle_low, out_back).reshape(block_shape)
    block_number = 0
    query_block = feat_query[block_number]
    denominator = denom_list[block_number]
    g_numerator = (d_mixed[block_number] / denominator[:, :, None]).astype(jnp.bfloat16)
    g_denominator = -jnp.sum(d_mixed[block_number] * numer_list[block_number], axis=2) / (
        denominator * denominator
    )
    kept_query = jnp.where(keep_list[block_number][:, None, None], query_block, zero_low)
    gnum_list = [g_numerator]
    gden_list = [g_denominator]
    local_list = [
        jnp.einsum("the,thf->hef", kept_query, g_numerator, preferred_element_type=jnp.float32)
    ]
    localkey_list = [jnp.sum(kept_query.astype(jnp.float32) * g_denominator[:, :, None], axis=0)]
    combined = identity
    for block_number in reversed(range(block_count)):
        combined = combine(
            combined,
            (flag_list[block_number], local_list[block_number], localkey_list[block_number]),
        )
    leaving = prefix(combined, "seq", combine, identity, True)
    g_memory = leaving[1]
    g_key_sum = leaving[2]
    gq_list = []
    gk_list = []
    gv_list = []
    for block_number in reversed(range(block_count)):
        query_block = feat_query[block_number]
        key_block = feat_key[block_number]
        value_block = value_low[block_number]
        keep_float = keep_list[block_number].astype(jnp.float32)
        tail_float = tail_list[block_number].astype(jnp.float32)
        g_numerator = gnum_list[block_number]
        g_denominator = gden_list[block_number]
        g_update = g_memory.astype(jnp.bfloat16)
        raw_scores = jnp.einsum(
            "the,jhe->htj", query_block, key_block, preferred_element_type=jnp.float32
        )
        scores_low = jnp.where(same_list[block_number][None], raw_scores, 0.0).astype(jnp.bfloat16)
        g_scores = (
            jnp.einsum("thf,jhf->htj", g_numerator, value_block, preferred_element_type=jnp.float32)
            + jnp.transpose(g_denominator)[:, :, None]
        )
        g_scores_low = jnp.where(
            same_list[block_number][None], g_scores.astype(jnp.bfloat16), zero_low
        )
        query_grad = jnp.einsum(
            "htj,jhe->the", g_scores_low, key_block, preferred_element_type=jnp.float32
        )
        query_grad = query_grad + keep_float[:, None, None] * (
            jnp.einsum(
                "thf,hef->the",
                g_numerator,
                memory_list[block_number],
                preferred_element_type=jnp.float32,
            )
            + g_denominator[:, :, None] * keysum_list[block_number][None]
        )
        key_grad = jnp.einsum(
            "htj,the->jhe", g_scores_low, query_block, preferred_element_type=jnp.float32
        )
        key_grad = key_grad + tail_float[:, None, None] * (
            jnp.einsum("jhf,hef->jhe", value_block, g_update, preferred_element_type=jnp.float32)
            + g_key_sum[None]
        )
        tail_key = jnp.where(tail_list[block_number][:, None, None], key_block, zero_low)
        value_grad = jnp.einsum(
            "htj,thf->jhf", scores_low, g_numerator, preferred_element_type=jnp.float32
        )
        value_grad = value_grad + jnp.einsum(
            "jhe,hef->jhf", tail_key, g_update, preferred_element_type=jnp.float32
        )
        gq_list.append(query_grad)
        gk_list.append(key_grad)
        gv_list.append(value_grad)
        g_memory = local_list[block_number] + flag_list[block_number] * g_memory
        g_key_sum = localkey_list[block_number] + flag_list[block_number] * g_key_sum
    d_feat_query = jnp.concatenate(gq_list[::-1], axis=0).reshape(local_len, model_width)
    d_feat_key = jnp.concatenate(gk_list[::-1], axis=0).reshape(local_len, model_width)
    d_value = jnp.concatenate(gv_list[::-1], axis=0).reshape(local_len, model_width)
    query_value, query_back = jax.vjp(feature, queries)
    key_value, key_back = jax.vjp(feature, keys_raw)
    g_projected = jnp.concatenate(
        [query_back(d_feat_query)[0], key_back(d_feat_key)[0], d_value], axis=1
    ).astype(jnp.bfloat16)
    grad_in_weight = rows_product(normed_low, g_projected)
    d_normed = cols_product(g_projected, in_back)
    first_value, first_back = jax.vjp(layer_norm, input_tokens, gain_one, shift_one)
    input_part, grad_gain_one, grad_shift_one = first_back(d_normed)
    grad_tokens = (g_middle + input_part).reshape(1, local_len, model_width)
    summed = (
        lax.psum_scatter(grad_in_weight, ("dp", "seq"), scatter_dimension=0, tiled=True),
        lax.psum_scatter(grad_out_weight, ("dp", "seq"), scatter_dimension=0, tiled=True),
        lax.psum_scatter(grad_up, ("dp", "seq"), scatter_dimension=0, tiled=True),
        lax.psum_scatter(grad_down, ("dp", "seq"), scatter_dimension=0, tiled=True),
        lax.psum_scatter(grad_gain_one, ("dp", "seq"), scatter_dimension=0, tiled=True),
        lax.psum_scatter(grad_shift_one, ("dp", "seq"), scatter_dimension=0, tiled=True),
        lax.psum_scatter(grad_gain_two, ("dp", "seq"), scatter_dimension=0, tiled=True),
        lax.psum_scatter(grad_shift_two, ("dp", "seq"), scatter_dimension=0, tiled=True),
    )
    return (
        result_tokens,
        grad_tokens,
        summed[0],
        summed[1],
        summed[2],
        summed[3],
        summed[4],
        summed[5],
        summed[6],
        summed[7],
    )


MESH = pl.DeviceIdType.MESH
LOW = jnp.bfloat16
FULL = jnp.float32


class Place:
    def __init__(self):
        dp, seq = lax.axis_index("dp"), lax.axis_index("seq")
        self.y, self.x = dp // 2, dp % 2
        self.z, self.c = seq // 2, seq % 2
        self.dp, self.seq = dp, seq
        self.over_x = (self.y * 2 + 1 - self.x, seq)
        self.over_y = ((1 - self.y) * 2 + self.x, seq)
        self.sibling = (dp, self.z * 2 + 1 - self.c)
        self.following = [(dp, (seq + 1) % 8), (dp, (seq + 2) % 8)]
        self.preceding = [(dp, (seq + 7) % 8), (dp, (seq + 6) % 8)]
        self.over_end = (dp, (seq + 2 * self.c + 7) % 8)
        self.along_z = [(dp, (self.z + d) % 4 * 2 + self.c) for d in (1, 2, 3)]

    def meet(self):
        barrier = pltpu.get_barrier_semaphore()
        everyone = [self.over_x, self.over_y, self.sibling, self.over_end, *self.along_z]
        for device in everyone:
            pl.semaphore_signal(barrier, inc=1, device_id=device, device_id_type=MESH)
        pl.semaphore_wait(barrier, len(everyone))


def remote(source, target, send, recv, device):
    return pltpu.make_async_remote_copy(
        src_ref=source,
        dst_ref=target,
        send_sem=send,
        recv_sem=recv,
        device_id=device,
        device_id_type=MESH,
    )


class Gather:
    def __init__(self, place, full, send, recv):
        p = place
        half = full.shape[4] // 2
        low, high = pl.ds(0, half), pl.ds(half, half)
        own = full.at[p.y, p.x, p.z, p.c]
        parts = [(own, device) for device in p.along_z]
        parts.append((full.at[p.y, p.x, :, p.c, low], p.over_x))
        parts.append((full.at[p.y, p.x, :, p.c, high], p.over_y))
        parts.append((full.at[p.y, :, :, p.c, low], p.over_y))
        parts.append((full.at[:, p.x, :, p.c, high], p.over_x))
        for y, x in ((p.y, p.x), (p.y, 1 - p.x), (1 - p.y, p.x), (1 - p.y, 1 - p.x)):
            parts.append((full.at[y, x, :, p.c], p.sibling))
        self.copies = [
            remote(ref, ref, send.at[i], recv.at[i], device)
            for i, (ref, device) in enumerate(parts)
        ]

    def start(self, *which):
        for i in which:
            self.copies[i].start()

    def arrive(self, *which):
        for i in which:
            self.copies[i].wait_recv()

    def step(self, number):
        if number == 0:
            self.start(0, 1, 2)
        elif number == 1:
            self.arrive(0, 1, 2)
            self.start(3, 4, 7)
        elif number == 2:
            self.arrive(3, 4)
            self.start(5, 6)
        elif number == 3:
            self.arrive(5, 6)
            self.start(8, 9, 10)
        else:
            self.arrive(7, 8, 9, 10)

    def finish(self):
        for copy in self.copies:
            copy.wait_send()


class Scatter:
    def __init__(self, place, own, total, pair, first_a, first_b, second_a, second_b, last, send, recv):
        p = place
        half = own.shape[4] // 2
        self.place, self.half = p, half
        self.own, self.total, self.pair = own, total, pair
        self.first_a, self.first_b = first_a, first_b
        self.second_a, self.second_b = second_a, second_b
        self.last = last
        low, high = pl.ds(0, half), pl.ds(half, half)
        parts = [
            (own.at[:, :, :, 1 - p.c], pair, p.sibling),
            (total.at[1 - p.y, :, :, low], first_a, p.over_y),
            (total.at[:, 1 - p.x, :, high], first_b, p.over_x),
            (total.at[p.y, 1 - p.x, :, low], second_a, p.over_x),
            (total.at[1 - p.y, p.x, :, high], second_b, p.over_y),
        ]
        self.keep = pltpu.make_async_copy(own.at[:, :, :, p.c], total, send.at[8])
        for d in (1, 2, 3):
            parts.append((total.at[p.y, p.x, (p.z + d) % 4], last.at[d - 1], p.along_z[d - 1]))
        self.copies = [
            remote(source, target, send.at[i], recv.at[i], device)
            for i, (source, target, device) in enumerate(parts)
        ]

    def step(self, number):
        p, half = self.place, self.half
        low, high = slice(0, half), slice(half, 2 * half)
        total = self.total
        if number == 0:
            self.copies[0].start()
            self.keep.start()
        elif number == 1:
            self.keep.wait()
            self.copies[0].wait_recv()

            @pl.loop(0, 4)
            def _(i):
                y, x = i // 2, i % 2
                total[y, x] = total[y, x] + self.pair[y, x]

            self.copies[1].start()
            self.copies[2].start()
        elif number == 2:
            self.copies[1].wait_recv()
            self.copies[2].wait_recv()
            for i in range(2):
                total[p.y, i, :, low] += self.first_a[i]
                total[i, p.x, :, high] += self.first_b[i]
            self.copies[3].start()
            self.copies[4].start()
        elif number == 3:
            self.copies[3].wait_recv()
            self.copies[4].wait_recv()
            total[p.y, p.x, :, low] += self.second_a[...]
            total[p.y, p.x, :, high] += self.second_b[...]
            for i in (5, 6, 7):
                self.copies[i].start()

    def result(self):
        for i in (5, 6, 7):
            self.copies[i].wait_recv()
        p = self.place
        value = total = self.total[p.y, p.x, p.z].astype(FULL)
        for d in range(3):
            value = value + self.last[d].astype(FULL)
        return value

    def finish(self):
        for copy in self.copies:
            copy.wait_send()


class SmallGather(Gather):
    def __init__(self, place, full, send, recv):
        p = place
        own = full.at[p.y, p.x, p.z, p.c]
        parts = [(own, device) for device in p.along_z]
        parts.append((full.at[p.y, p.x, :, p.c], p.over_x))
        parts.append((full.at[p.y, :, :, p.c], p.over_y))
        for y in range(2):
            for x in range(2):
                parts.append((full.at[y, x, :, p.c], p.sibling))
        self.copies = [
            remote(ref, ref, send.at[i], recv.at[i], device)
            for i, (ref, device) in enumerate(parts)
        ]

    def step(self, number):
        if number == 0:
            self.start(0, 1, 2)
        elif number == 1:
            self.arrive(0, 1, 2)
            self.start(3)
        elif number == 2:
            self.arrive(3)
            self.start(4)
        elif number == 3:
            self.arrive(4)
            self.start(5, 6, 7, 8)
        else:
            self.arrive(5, 6, 7, 8)


def product(one, two):
    return jnp.dot(one, two, preferred_element_type=FULL)


def across(one, two):
    return lax.dot_general(one, two, (((1,), (1,)), ((), ())), preferred_element_type=FULL)


def down_rows(one, two):
    return lax.dot_general(one, two, (((0,), (0,)), ((), ())), preferred_element_type=FULL)


def tile(i, size):
    return pl.ds(pl.multiple_of(i * size, size), size)


def image_count(starts, at):
    total = jnp.where(starts[0, 0] <= at, 1, 0)
    for k in range(1, starts.shape[1]):
        total = total + jnp.where(starts[0, k] <= at, 1, 0)
    return total


class Images:
    def __init__(self, starts, seq, length):
        first = seq * length
        self.length = length
        self.column = image_count(starts, first + lax.broadcasted_iota(jnp.int32, (length, 128), 0))
        self.row = image_count(starts, first + lax.broadcasted_iota(jnp.int32, (8, length), 1))
        before = image_count(starts, first - 1)
        last = image_count(starts, first + length - 1)
        earlier = image_count(starts, first - length - 1)
        later = image_count(starts, first + 2 * length - 1)
        self.keep = jnp.where(self.column == before, 1.0, 0.0)
        self.tail = jnp.where(self.column == last, 1.0, 0.0)
        self.flag_before = jnp.where(before == earlier, 1.0, 0.0)
        self.flag_after = jnp.where(later == last, 1.0, 0.0)


def same_mask(images, rows, columns, transposed):
    shape = (images.length, images.length)
    down = lax.broadcasted_iota(jnp.int32, shape, 0)
    along = lax.broadcasted_iota(jnp.int32, shape, 1)
    order = down <= along if transposed else down >= along
    equal = images.column[:, :1] == images.row[:1, :]
    return jnp.where(order & equal, 1.0, 0.0).astype(LOW)


def head_lanes(rows):
    return lax.broadcasted_iota(jnp.int32, (rows, 128), 1) < HEAD


def own_block():
    return jnp.where(
        (lax.broadcasted_iota(jnp.int32, (128, 128), 0) < HEAD)
        == (lax.broadcasted_iota(jnp.int32, (128, 128), 1) < HEAD),
        1.0,
        0.0,
    ).astype(LOW)


def pack_pair(square):
    return jnp.where(head_lanes(HEAD), square[:HEAD], square[HEAD:])


def unpack_pair(packed):
    lanes = head_lanes(HEAD)
    zero = jnp.zeros_like(packed)
    return jnp.concatenate([jnp.where(lanes, packed, zero), jnp.where(lanes, zero, packed)], axis=0)


def statistics(values):
    average = jnp.mean(values, axis=-1, keepdims=True)
    centred = values - average
    spread = jnp.mean(centred * centred, axis=-1, keepdims=True)
    scale = lax.rsqrt(spread + 1e-05)
    return centred * scale, scale


def gelu_both(values):
    root = 0.7978845608028654
    square = values * values
    angle = jnp.tanh(root * values * (1.0 + 0.044715 * square))
    half = 0.5 + 0.5 * angle
    slope = half + 0.5 * values * (1.0 - angle * angle) * (root * (1.0 + 0.134145 * square))
    return values * half, slope


def forward_kernel(inputs, outputs, scratch):
    tokens_in, cotangent_in, starts, in_weight, out_weight, up_weight, down_weight, pack_in = inputs
    (
        in_full,
        out_full,
        up_full,
        down_full,
        grad_down_out,
        result_out,
        heads_out,
        mixed_out,
        inverse_out,
        middle_out,
        slope_out,
        memory_out,
        sums_out,
        gains_out,
    ) = outputs
    (
        wide,
        tall,
        pack,
        tokens,
        cotangent,
        gains,
        normed,
        heads,
        mask,
        mixed,
        mixed_low,
        inverse,
        middle,
        active,
        slope,
        grad_down,
        result,
        outgoing,
        incoming,
        memory,
        sums,
        send,
        recv,
        small_send,
        small_recv,
        state_send,
        state_recv,
        local,
        store,
    ) = scratch
    p = Place()
    length, width = tokens.shape
    loads = []
    for j in range(8):
        source = in_weight if j < 3 else (out_weight if j == 3 else up_weight)
        column = j if j < 3 else (0 if j == 3 else j - 4)
        loads.append((source.at[:, pl.ds(column * 1024, 1024)], wide.at[j, p.y, p.x, p.z, p.c]))
    for j in range(4):
        loads.append((down_weight.at[:, pl.ds(256 * j, 256)], tall.at[j, p.y, p.x, p.z, p.c]))
    loads.append((pack_in, pack.at[p.y, p.x, p.z, p.c]))
    loads.append((tokens_in, tokens))
    loads.append((cotangent_in, cotangent))
    loads = [pltpu.make_async_copy(a, b, local.at[i]) for i, (a, b) in enumerate(loads)]
    for i in (12, 0, 1, 2, 13, 3, 4, 5, 6, 7, 8, 9, 10, 11, 14):
        loads[i].start()
    stores = []

    def save(source, target):
        copy = pltpu.make_async_copy(source, target, store.at[len(stores)])
        copy.start()
        stores.append(copy)

    p.meet()
    small = SmallGather(p, pack, small_send, small_recv)
    chunks = [Gather(p, wide.at[j], send.at[j], recv.at[j]) for j in range(8)]
    chunks += [Gather(p, tall.at[j], send.at[8 + j], recv.at[8 + j]) for j in range(4)]

    def event(j, number):
        if not 0 <= j < 12:
            return
        if number == 0:
            loads[j].wait()
        chunks[j].step(number)
        if number == 4:
            if j < 8:
                target = in_full if j < 3 else (out_full if j == 3 else up_full)
                column = j if j < 3 else (0 if j == 3 else j - 4)
                save(wide.at[j], target.at[:, :, :, :, :, pl.ds(column * 1024, 1024)])
            else:
                save(tall.at[j - 8], down_full.at[:, :, :, :, :, pl.ds(256 * (j - 8), 256)])

    def weight(j, columns):
        return wide[j, :, :, :, :, :, columns].reshape(width, columns.size)

    images = Images(starts, p.seq, length)

    def first_norm():
        for y in range(2):
            for x in range(2):
                for k in range(2):
                    value = pack[y, x, 2 * k : 2 * k + 2].astype(FULL)
                    value = (value[0, 0] + value[0, 1]) + (value[1, 0] + value[1, 1])
                    at = 128 * ((y * 2 + x) * 2 + k)
                    gains[:, at : at + 128] = value
        save(gains, gains_out)
        loads[13].wait()

        @pl.loop(0, length // 128)
        def _(i):
            rows = tile(i, 128)
            value, _ = statistics(tokens[rows, :].astype(FULL))
            normed[rows, :] = (value * gains[0:1, :] + gains[1:2, :]).astype(LOW)

        mask[...] = same_mask(images, length, length, False)

    def project(j):
        @pl.loop(0, 2)
        def _(i):
            value = product(normed[...], weight(j, tile(i, 512)))
            if j < 2:
                value = jnp.where(value > 0, value + 1.0, jnp.exp(jnp.minimum(value, 0.0)))
            heads[j, :, tile(i, 512)] = value.astype(LOW)

    def update():
        tail = images.tail.astype(LOW)

        @pl.loop(0, 8)
        def _(i):
            lanes = tile(i, 128)
            key = heads[1, :, lanes] * tail
            square = down_rows(key, heads[2, :, lanes])
            outgoing[i, 0:HEAD] = pack_pair(square).astype(LOW)
            total = product(jnp.ones((16, length), LOW), key)
            outgoing[i, HEAD : HEAD + 16] = total.astype(LOW)

        save(heads, heads_out)
        for copy in state:
            copy.start()

    state = [
        remote(outgoing, incoming.at[d], state_send.at[d], state_recv.at[d], device)
        for d, device in enumerate(p.following)
    ]

    def enter():
        for copy in state:
            copy.wait_recv()

        @pl.loop(0, 8)
        def _(i):
            value = incoming[0, i].astype(FULL) + images.flag_before * incoming[1, i].astype(FULL)
            memory[i] = value[0:HEAD].astype(LOW)
            sums[i] = value[HEAD : HEAD + 8]

        save(memory, memory_out)
        save(sums, sums_out)

    def attend(begin, end):
        lanes_column = head_lanes(length)
        blocks = own_block()
        keep = images.keep.astype(LOW)
        half = length // 2
        identity = jnp.where(
            lax.broadcasted_iota(jnp.int32, (128, 128), 0)
            == lax.broadcasted_iota(jnp.int32, (128, 128), 1),
            1.0,
            0.0,
        )
        ones = jnp.ones((length, 128), LOW)

        @pl.loop(begin, end)
        def _(i):
            lanes = tile(i, 128)
            query, key, value = heads[0, :, lanes], heads[1, :, lanes], heads[2, :, lanes]
            wider = jnp.concatenate([value, ones], axis=1)
            parts = []
            for h in range(2):
                mine = lanes_column if h == 0 else ~lanes_column
                own = jnp.where(mine, query, jnp.zeros_like(query))
                upper = across(own[:half], key[:half]).astype(LOW) * mask[:half, :half]
                lower = across(own[half:], key).astype(LOW) * mask[half:, :]
                parts.append(
                    jnp.concatenate([product(upper, wider[:half]), product(lower, wider)], axis=0)
                )
            diagonal = (identity * sums[i, 0:1]).astype(LOW)
            right = jnp.concatenate(
                [unpack_pair(memory[i]), product(diagonal, blocks).astype(LOW)], axis=1
            )
            carried = product(query * keep, right)
            numerator = jnp.where(lanes_column, parts[0][:, :128], parts[1][:, :128])
            denominator = jnp.where(lanes_column, parts[0][:, 128:], parts[1][:, 128:])
            over = 1.0 / (denominator + carried[:, 128:])
            value = (numerator + carried[:, :128]) * over
            inverse[:, lanes] = over
            mixed[:, lanes] = value
            mixed_low[:, lanes] = value.astype(LOW)

    def join():
        save(mixed, mixed_out)
        save(inverse, inverse_out)

        @pl.loop(0, 2)
        def _(i):
            columns = tile(i, 512)
            middle[:, columns] = tokens[:, columns].astype(FULL) + product(
                mixed_low[...], weight(3, columns)
            )

        save(middle, middle_out)

    def second_norm():
        @pl.loop(0, length // 128)
        def _(i):
            rows = tile(i, 128)
            value, _ = statistics(middle[rows, :])
            normed[rows, :] = (value * gains[2:3, :] + gains[3:4, :]).astype(LOW)

    def raise_up(j):
        @pl.loop(0, 4)
        def _(i):
            value = product(normed[...], weight(4 + j, tile(i, 256)))
            columns = pl.ds(pl.multiple_of(j * 1024 + i * 256, 256), 256)
            value, steep = gelu_both(value)
            active[:, columns] = value.astype(LOW)
            slope[:, columns] = steep.astype(LOW)

        if j == 3:
            save(slope, slope_out)

    def down_gradient(begin, end):
        if begin == 0:
            loads[14].wait()

        @pl.loop(begin, end)
        def _(i):
            value = down_rows(active[:, tile(i, 512)], cotangent[...]).astype(LOW)
            y, x, z = i // 4, i // 2 % 2, i % 2 * 2
            for j in range(4):
                part = value[:, 256 * j : 256 * j + 256].reshape(2, 2, 128, 256)
                grad_down[j, y, x, pl.ds(z, 2)] = part

        if end == 8:
            save(grad_down, grad_down_out)

    def lower(j):
        columns = slice(256 * j, 256 * j + 256)

        @pl.loop(0, 2)
        def _(i):
            rows = tile(i, 256)
            value = product(active[rows, :], tall[j].reshape(4 * width, 256))
            result[rows, columns] = (middle[rows, columns] + value).astype(LOW)

        save(result.at[:, pl.ds(256 * j, 256)], result_out.at[:, pl.ds(256 * j, 256)])

    work = {
        5: [functools.partial(project, 0)],
        6: [functools.partial(project, 1)],
        7: [functools.partial(project, 2), update],
        8: [enter, functools.partial(attend, 0, 2), functools.partial(attend, 2, 4)],
        9: [
            functools.partial(attend, 4, 6),
            functools.partial(attend, 6, 8),
            join,
        ],
        10: [second_norm, functools.partial(raise_up, 0), functools.partial(raise_up, 1)],
        11: [functools.partial(raise_up, 2)],
        12: [
            functools.partial(raise_up, 3),
            functools.partial(down_gradient, 0, 4),
            functools.partial(down_gradient, 4, 8),
        ],
        13: [functools.partial(lower, 0)],
        14: [functools.partial(lower, 1)],
        15: [functools.partial(lower, 2)],
    }
    for tick in range(12 + 4):
        todo = work.get(tick, []) + [lambda: None] * 3
        if tick == 0:
            event(0, 0)
            loads[12].wait()
            small.step(0)
            event(1, 0)
            for number in range(1, 5):
                small.step(number)
            first_norm()
            continue
        if tick > 1:
            event(tick, 0)
        event(tick - 1, 1)
        todo[0]()
        event(tick - 2, 2)
        todo[1]()
        event(tick - 3, 3)
        event(tick - 4, 4)
        todo[2]()
    lower(3)
    small.finish()
    for copy in state:
        copy.wait_send()
    for chunk in chunks:
        chunk.finish()
    for copy in stores:
        copy.wait()


def forward_pass(tokens, cotangent, starts, in_weight, out_weight, up_weight, down_weight, pack):
    length, width = tokens.shape
    block = lambda rows, columns: jax.ShapeDtypeStruct((2, 2, 4, 2, rows, columns), LOW)
    shape = jax.ShapeDtypeStruct

    def body(*refs):
        forward_kernel(refs[:8], refs[8:22], refs[22:])

    return pl.pallas_call(
        body,
        out_shape=[
            block(32, 3072),
            block(32, 1024),
            block(32, 4096),
            block(128, 1024),
            shape((4, 2, 2, 4, 2, 128, 256), LOW),
            shape((length, width), LOW),
            shape((3, length, width), LOW),
            shape((length, width), FULL),
            shape((length, width), FULL),
            shape((length, width), FULL),
            shape((length, 4 * width), LOW),
            shape((8, HEAD, 128), LOW),
            shape((8, 8, 128), FULL),
            shape((16, width), FULL),
        ],
        in_specs=[
            pl.BlockSpec(memory_space=pltpu.SMEM if i == 2 else pl.ANY) for i in range(8)
        ],
        out_specs=[pl.BlockSpec(memory_space=pl.ANY)] * 14,
        scratch_shapes=[
            pltpu.VMEM((8, 2, 2, 4, 2, 32, 1024), LOW),
            pltpu.VMEM((4, 2, 2, 4, 2, 128, 256), LOW),
            pltpu.VMEM((2, 2, 4, 2, 16, 128), LOW),
            pltpu.VMEM((length, width), LOW),
            pltpu.VMEM((length, width), LOW),
            pltpu.VMEM((16, width), FULL),
            pltpu.VMEM((length, width), LOW),
            pltpu.VMEM((3, length, width), LOW),
            pltpu.VMEM((length, length), LOW),
            pltpu.VMEM((length, width), FULL),
            pltpu.VMEM((length, width), LOW),
            pltpu.VMEM((length, width), FULL),
            pltpu.VMEM((length, width), FULL),
            pltpu.VMEM((length, 4 * width), LOW),
            pltpu.VMEM((length, 4 * width), LOW),
            pltpu.VMEM((4, 2, 2, 4, 2, 128, 256), LOW),
            pltpu.VMEM((length, width), LOW),
            pltpu.VMEM((8, HEAD + 16, 128), LOW),
            pltpu.VMEM((2, 8, HEAD + 16, 128), LOW),
            pltpu.VMEM((8, HEAD, 128), LOW),
            pltpu.VMEM((8, 8, 128), FULL),
            pltpu.SemaphoreType.DMA((12, 11)),
            pltpu.SemaphoreType.DMA((12, 11)),
            pltpu.SemaphoreType.DMA((9,)),
            pltpu.SemaphoreType.DMA((9,)),
            pltpu.SemaphoreType.DMA((2,)),
            pltpu.SemaphoreType.DMA((2,)),
            pltpu.SemaphoreType.DMA((15,)),
            pltpu.SemaphoreType.DMA((26,)),
        ],
        compiler_params=pltpu.CompilerParams(
            collective_id=0, has_side_effects=True, vmem_limit_bytes=62 << 20
        ),
        name="forward_pass",
    )(tokens, cotangent, starts, in_weight, out_weight, up_weight, down_weight, pack)


def scatter_kernel(inputs, outputs, wide, tall, send, recv):
    p = Place()
    p.meet()
    order = [8, 9, 10, 11, 4, 5, 6, 7, 3, 0, 1, 2]
    chunks = []
    places = []
    for j in range(12):
        if j < 8:
            source = 0 if j < 3 else (1 if j == 3 else 2)
            column = j if j < 3 else (0 if j == 3 else j - 4)
            columns = pl.ds(column * 1024, 1024)
            own, buffers, at = inputs[source].at[:, :, :, :, :, columns], wide, j
        else:
            source, columns, buffers, at = 3, pl.ds((j - 8) * 256, 256), tall, j - 8
            own = inputs[3].at[:, :, :, :, :, columns]
        chunks.append(Scatter(p, own, *[ref.at[at] for ref in buffers], send.at[j], recv.at[j]))
        places.append((source, columns))
    for tick in range(12 + 4):
        for number in range(5):
            if 0 <= tick - number < 12:
                j = order[tick - number]
                if number < 4:
                    chunks[j].step(number)
                else:
                    source, columns = places[j]
                    outputs[source][:, columns] = chunks[j].result()
    for chunk in chunks:
        chunk.finish()


def scatter_buffers(count, rows, columns):
    half = rows // 2
    shapes = [
        (2, 2, 4, rows, columns),
        (2, 2, 4, rows, columns),
        (2, 4, half, columns),
        (2, 4, half, columns),
        (4, half, columns),
        (4, half, columns),
        (3, rows, columns),
    ]
    return [pltpu.VMEM((count, *shape), LOW) for shape in shapes]


def scatter_all(*grads):
    def body(*refs):
        scatter_kernel(refs[:4], refs[4:8], refs[8:15], refs[15:22], *refs[22:])

    return pl.pallas_call(
        body,
        out_shape=[
            jax.ShapeDtypeStruct(shape, FULL)
            for shape in ((32, 3072), (32, 1024), (32, 4096), (128, 1024))
        ],
        in_specs=[pl.BlockSpec(memory_space=pl.ANY)] * 4,
        out_specs=[pl.BlockSpec(memory_space=pltpu.VMEM)] * 4,
        scratch_shapes=scatter_buffers(8, 32, 1024)
        + scatter_buffers(4, 128, 256)
        + [pltpu.SemaphoreType.DMA((12, 9)), pltpu.SemaphoreType.DMA((12, 8))],
        compiler_params=pltpu.CompilerParams(
            collective_id=1, has_side_effects=True, vmem_limit_bytes=60 << 20
        ),
        name="scatter_gradients",
    )(*[grad.reshape(2, 2, 4, 2, grad.shape[0] // 32, grad.shape[1]) for grad in grads])


def on_device(
    tokens,
    starts,
    query_key_value_weight,
    attention_output_weight,
    up_projection_weight,
    down_projection_weight,
    first_gain,
    first_shift,
    second_gain,
    second_shift,
    cotangent,
):
    local_len = tokens.shape[1]
    model_width = tokens.shape[2]
    head_count = model_width // HEAD
    block_count = local_len // BLOCK
    block_shape = (block_count, BLOCK, head_count, HEAD)
    zero_low = jnp.zeros((), jnp.bfloat16)
    input_tokens = tokens[0].astype(jnp.float32)
    first_pos = lax.axis_index("seq") * local_len
    positions = first_pos + jnp.arange(local_len, dtype=jnp.int32)
    pack_starts = starts[0]
    image_ids = jnp.sum((pack_starts[None, :] <= positions[:, None]).astype(jnp.int32), axis=1) - 1
    before_id = jnp.sum((pack_starts <= first_pos - 1).astype(jnp.int32)) - 1
    causal = jnp.arange(BLOCK)[:, None] >= jnp.arange(BLOCK)[None, :]
    mine = lax.axis_index("dp") * 8 + lax.axis_index("seq")
    pack = jnp.stack([first_gain, first_shift, second_gain, second_shift]).astype(FULL)
    pack = jnp.roll(jnp.pad(pack, ((0, 12), (0, 96))), 32 * (mine % 4), axis=1).astype(LOW)
    (
        in_full,
        out_full,
        up_full,
        down_full,
        grad_down,
        result,
        heads,
        mixed,
        inverse,
        middle_tokens,
        slope,
        memory,
        sums,
        gains,
    ) = forward_pass(
        tokens[0],
        cotangent[0],
        starts,
        query_key_value_weight,
        attention_output_weight,
        up_projection_weight,
        down_projection_weight,
        pack,
    )
    result_tokens = result.reshape(1, local_len, model_width)
    in_full, out_full = in_full.reshape(1024, 3072), out_full.reshape(1024, 1024)
    up_full, down_full = up_full.reshape(1024, 4096), down_full.reshape(4096, 1024)
    gain_one, shift_one, gain_two, shift_two = gains[0], gains[1], gains[2], gains[3]
    normed_low = layer_norm(input_tokens, gain_one, shift_one).astype(LOW)
    projected_tokens = jnp.dot(normed_low, in_full, preferred_element_type=jnp.float32)
    queries = projected_tokens[:, :model_width]
    keys_raw = projected_tokens[:, model_width : 2 * model_width]
    feat_query, feat_key, value_low = heads[0].reshape(block_shape), heads[1].reshape(block_shape), heads[2].reshape(block_shape)
    last_id = image_ids[-1]
    tail_mask = image_ids == last_id
    keep_list = [image_ids == before_id]
    tail_list = [tail_mask]
    flag_list = [(last_id == before_id).astype(jnp.float32)]
    same_list = [causal & (image_ids[:, None] == image_ids[None, :])]
    identity = (
        jnp.ones((), jnp.float32),
        jnp.zeros((head_count, HEAD, HEAD), jnp.float32),
        jnp.zeros((head_count, HEAD), jnp.float32),
    )
    memory_list = [jnp.transpose(memory.reshape(8, HEAD, 2, HEAD), (0, 2, 1, 3)).reshape(16, HEAD, HEAD)]
    keysum_list = [sums[:, 0].reshape(16, HEAD)]
    denominator = 1.0 / inverse.reshape(512, 16, 64)
    numer_list = [mixed.reshape(512, 16, 64) * denominator]
    denom_list = [denominator[:, :, 0]]
    mixed_low = mixed.astype(LOW)
    normed_two_low = layer_norm(middle_tokens, gain_two, shift_two).astype(jnp.bfloat16)
    grad_out = cotangent[0].astype(jnp.float32)
    grad_out_low = cotangent[0]
    d_active = cols_product(grad_out_low, down_full)
    g_upper = (slope.astype(FULL) * d_active).astype(jnp.bfloat16)
    grad_up = rows_product(normed_two_low, g_upper)
    d_normed_two = cols_product(g_upper, up_full)
    norm_value, norm_back = jax.vjp(layer_norm, middle_tokens, gain_two, shift_two)
    middle_part, grad_gain_two, grad_shift_two = norm_back(d_normed_two)
    g_middle = grad_out + middle_part
    g_middle_low = g_middle.astype(jnp.bfloat16)
    grad_out_weight = rows_product(mixed_low, g_middle_low)
    d_mixed = cols_product(g_middle_low, out_full).reshape(block_shape)
    block_number = 0
    query_block = feat_query[block_number]
    denominator = denom_list[block_number]
    g_numerator = (d_mixed[block_number] / denominator[:, :, None]).astype(jnp.bfloat16)
    g_denominator = -jnp.sum(d_mixed[block_number] * numer_list[block_number], axis=2) / (
        denominator * denominator
    )
    kept_query = jnp.where(keep_list[block_number][:, None, None], query_block, zero_low)
    gnum_list = [g_numerator]
    gden_list = [g_denominator]
    local_list = [
        jnp.einsum("the,thf->hef", kept_query, g_numerator, preferred_element_type=jnp.float32)
    ]
    localkey_list = [jnp.sum(kept_query.astype(jnp.float32) * g_denominator[:, :, None], axis=0)]
    combined = identity
    for block_number in reversed(range(block_count)):
        combined = combine(
            combined,
            (flag_list[block_number], local_list[block_number], localkey_list[block_number]),
        )
    leaving = prefix(combined, "seq", combine, identity, True)
    g_memory = leaving[1]
    g_key_sum = leaving[2]
    gq_list = []
    gk_list = []
    gv_list = []
    for block_number in reversed(range(block_count)):
        query_block = feat_query[block_number]
        key_block = feat_key[block_number]
        value_block = value_low[block_number]
        keep_float = keep_list[block_number].astype(jnp.float32)
        tail_float = tail_list[block_number].astype(jnp.float32)
        g_numerator = gnum_list[block_number]
        g_denominator = gden_list[block_number]
        g_update = g_memory.astype(jnp.bfloat16)
        raw_scores = jnp.einsum(
            "the,jhe->htj", query_block, key_block, preferred_element_type=jnp.float32
        )
        scores_low = jnp.where(same_list[block_number][None], raw_scores, 0.0).astype(jnp.bfloat16)
        g_scores = (
            jnp.einsum("thf,jhf->htj", g_numerator, value_block, preferred_element_type=jnp.float32)
            + jnp.transpose(g_denominator)[:, :, None]
        )
        g_scores_low = jnp.where(
            same_list[block_number][None], g_scores.astype(jnp.bfloat16), zero_low
        )
        query_grad = jnp.einsum(
            "htj,jhe->the", g_scores_low, key_block, preferred_element_type=jnp.float32
        )
        query_grad = query_grad + keep_float[:, None, None] * (
            jnp.einsum(
                "thf,hef->the",
                g_numerator,
                memory_list[block_number],
                preferred_element_type=jnp.float32,
            )
            + g_denominator[:, :, None] * keysum_list[block_number][None]
        )
        key_grad = jnp.einsum(
            "htj,the->jhe", g_scores_low, query_block, preferred_element_type=jnp.float32
        )
        key_grad = key_grad + tail_float[:, None, None] * (
            jnp.einsum("jhf,hef->jhe", value_block, g_update, preferred_element_type=jnp.float32)
            + g_key_sum[None]
        )
        tail_key = jnp.where(tail_list[block_number][:, None, None], key_block, zero_low)
        value_grad = jnp.einsum(
            "htj,thf->jhf", scores_low, g_numerator, preferred_element_type=jnp.float32
        )
        value_grad = value_grad + jnp.einsum(
            "jhe,hef->jhf", tail_key, g_update, preferred_element_type=jnp.float32
        )
        gq_list.append(query_grad)
        gk_list.append(key_grad)
        gv_list.append(value_grad)
        g_memory = local_list[block_number] + flag_list[block_number] * g_memory
        g_key_sum = localkey_list[block_number] + flag_list[block_number] * g_key_sum
    d_feat_query = jnp.concatenate(gq_list[::-1], axis=0).reshape(local_len, model_width)
    d_feat_key = jnp.concatenate(gk_list[::-1], axis=0).reshape(local_len, model_width)
    d_value = jnp.concatenate(gv_list[::-1], axis=0).reshape(local_len, model_width)
    query_value, query_back = jax.vjp(feature, queries)
    key_value, key_back = jax.vjp(feature, keys_raw)
    g_projected = jnp.concatenate(
        [query_back(d_feat_query)[0], key_back(d_feat_key)[0], d_value], axis=1
    ).astype(jnp.bfloat16)
    grad_in_weight = rows_product(normed_low, g_projected)
    d_normed = cols_product(g_projected, in_full)
    first_value, first_back = jax.vjp(layer_norm, input_tokens, gain_one, shift_one)
    input_part, grad_gain_one, grad_shift_one = first_back(d_normed)
    grad_tokens = (g_middle + input_part).reshape(1, local_len, model_width)
    weights = scatter_all(
        grad_in_weight.astype(LOW),
        grad_out_weight.astype(LOW),
        grad_up.astype(LOW),
        jnp.moveaxis(grad_down, 0, 5).reshape(4096, 1024),
    )
    summed = (
        *weights,
        lax.psum_scatter(grad_gain_one, ("dp", "seq"), scatter_dimension=0, tiled=True),
        lax.psum_scatter(grad_shift_one, ("dp", "seq"), scatter_dimension=0, tiled=True),
        lax.psum_scatter(grad_gain_two, ("dp", "seq"), scatter_dimension=0, tiled=True),
        lax.psum_scatter(grad_shift_two, ("dp", "seq"), scatter_dimension=0, tiled=True),
    )
    return (
        result_tokens,
        grad_tokens,
        summed[0],
        summed[1],
        summed[2],
        summed[3],
        summed[4],
        summed[5],
        summed[6],
        summed[7],
    )


def solution(mesh):

    fast = dict(mesh.shape) == {"dp": 4, "seq": 8}
    return jax.shard_map(
        on_device if fast else on_device_general,
        mesh=mesh,
        in_specs=(
            P("dp", "seq", None),
            P("dp", None),
            P(("dp", "seq"), None),
            P(("dp", "seq"), None),
            P(("dp", "seq"), None),
            P(("dp", "seq"), None),
            P(("dp", "seq")),
            P(("dp", "seq")),
            P(("dp", "seq")),
            P(("dp", "seq")),
            P("dp", "seq", None),
        ),
        out_specs=(
            P("dp", "seq", None),
            P("dp", "seq", None),
            P(("dp", "seq"), None),
            P(("dp", "seq"), None),
            P(("dp", "seq"), None),
            P(("dp", "seq"), None),
            P(("dp", "seq")),
            P(("dp", "seq")),
            P(("dp", "seq")),
            P(("dp", "seq")),
        ),
        check_vma=False,
    )
```

```python
import functools

import jax
import jax.numpy as jnp
from jax import lax
from jax.experimental import pallas as pl
from jax.experimental.pallas import tpu as pltpu
from jax.sharding import PartitionSpec as P

HEAD = 64
BLOCK = 512


def prefix(value, axis, combine, identity, reverse):
    size, mine = (lax.axis_size(axis), lax.axis_index(axis))
    everything = jax.tree.map(
        lambda part, kind: lax.all_gather(part.astype(kind), axis),
        value,
        jax.tree.map(lambda a: jnp.bfloat16 if a.dtype == jnp.float32 else a.dtype, value),
    )
    start = jax.tree.map(
        lambda part, zero: jnp.broadcast_to(jnp.asarray(zero, part.dtype), part.shape),
        value,
        identity,
    )

    def lap(k, before):
        at = size - 1 - k if reverse else k
        reached = at > mine if reverse else at < mine
        new = combine(
            before, jax.tree.map(lambda part, own: part[at].astype(own.dtype), everything, value)
        )
        return jax.tree.map(lambda a, b: jnp.where(reached, a, b), new, before)

    return lax.fori_loop(0, size, lap, start)


def layer_norm(values, norm_gain, norm_shift):
    average = jnp.mean(values, axis=-1, keepdims=True)
    centred = values - average
    spread = jnp.mean(centred * centred, axis=-1, keepdims=True)
    return centred * lax.rsqrt(spread + 1e-05) * norm_gain + norm_shift


def feature(values):
    return jax.nn.elu(values) + 1.0


def combine(former, latter):
    return (
        former[0] * latter[0],
        latter[0] * former[1] + latter[1],
        latter[0] * former[2] + latter[2],
    )


def rows_product(factor_one, factor_two):
    return lax.dot_general(
        factor_one, factor_two, (((0,), (0,)), ((), ())), preferred_element_type=jnp.float32
    )


def cols_product(factor_one, factor_two):
    return lax.dot_general(
        factor_one, factor_two, (((1,), (1,)), ((), ())), preferred_element_type=jnp.float32
    )


def on_device_general(
    tokens,
    starts,
    query_key_value_weight,
    attention_output_weight,
    up_projection_weight,
    down_projection_weight,
    first_gain,
    first_shift,
    second_gain,
    second_shift,
    cotangent,
):
    local_len = tokens.shape[1]
    model_width = tokens.shape[2]
    head_count = model_width // HEAD
    block_count = local_len // BLOCK
    block_shape = (block_count, BLOCK, head_count, HEAD)
    zero_low = jnp.zeros((), jnp.bfloat16)
    input_tokens = tokens[0].astype(jnp.float32)
    first_pos = lax.axis_index("seq") * local_len
    positions = first_pos + jnp.arange(local_len, dtype=jnp.int32)
    pack_starts = starts[0]
    image_ids = jnp.sum((pack_starts[None, :] <= positions[:, None]).astype(jnp.int32), axis=1) - 1
    before_id = jnp.sum((pack_starts <= first_pos - 1).astype(jnp.int32)) - 1
    causal = jnp.arange(BLOCK)[:, None] >= jnp.arange(BLOCK)[None, :]
    attn_set = (
        lax.all_gather(query_key_value_weight, ("dp", "seq"), axis=0, tiled=True),
        lax.all_gather(attention_output_weight, ("dp", "seq"), axis=0, tiled=True),
        lax.all_gather(first_gain, ("dp", "seq"), axis=0, tiled=True),
        lax.all_gather(first_shift, ("dp", "seq"), axis=0, tiled=True),
    )
    in_full = attn_set[0]
    out_full = attn_set[1]
    gain_one = attn_set[2].astype(jnp.float32)
    shift_one = attn_set[3].astype(jnp.float32)
    first_normed_tokens = layer_norm(input_tokens, gain_one, shift_one)
    normed_low = first_normed_tokens.astype(jnp.bfloat16)
    projected_tokens = jnp.dot(normed_low, in_full, preferred_element_type=jnp.float32)
    queries = projected_tokens[:, :model_width]
    keys_raw = projected_tokens[:, model_width : 2 * model_width]
    values_raw = projected_tokens[:, 2 * model_width :]
    feat_query = feature(queries).astype(jnp.bfloat16).reshape(block_shape)
    feat_key = feature(keys_raw).astype(jnp.bfloat16).reshape(block_shape)
    value_low = values_raw.astype(jnp.bfloat16).reshape(block_shape)
    block_number = 0
    last_id = image_ids[-1]
    tail_mask = image_ids == last_id
    tail_key = jnp.where(tail_mask[:, None, None], feat_key[block_number], zero_low)
    keep_list = [image_ids == before_id]
    tail_list = [tail_mask]
    flag_list = [(last_id == before_id).astype(jnp.float32)]
    same_list = [causal & (image_ids[:, None] == image_ids[None, :])]
    update_list = [
        jnp.einsum(
            "jhe,jhf->hef", tail_key, value_low[block_number], preferred_element_type=jnp.float32
        )
    ]
    total_list = [jnp.sum(tail_key.astype(jnp.float32), axis=0)]
    identity = (
        jnp.ones((), jnp.float32),
        jnp.zeros((head_count, HEAD, HEAD), jnp.float32),
        jnp.zeros((head_count, HEAD), jnp.float32),
    )
    combined = identity
    block_number = 0
    combined = combine(
        combined, (flag_list[block_number], update_list[block_number], total_list[block_number])
    )
    entering = prefix(combined, "seq", combine, identity, False)
    memory = entering[1]
    key_sum = entering[2]
    block_number = 0
    query_block = feat_query[block_number]
    keep_float = keep_list[block_number].astype(jnp.float32)
    memory_low = memory.astype(jnp.bfloat16)
    raw_scores = jnp.einsum(
        "the,jhe->htj", query_block, feat_key[block_number], preferred_element_type=jnp.float32
    )
    masked = jnp.where(same_list[block_number][None], raw_scores, 0.0)
    scores_low = masked.astype(jnp.bfloat16)
    carried = (
        jnp.einsum("the,hef->thf", query_block, memory_low, preferred_element_type=jnp.float32)
        * keep_float[:, None, None]
    )
    numerator = (
        jnp.einsum(
            "htj,jhf->thf", scores_low, value_low[block_number], preferred_element_type=jnp.float32
        )
        + carried
    )
    denominator = jnp.transpose(jnp.sum(masked, axis=2)) + keep_float[:, None] * jnp.sum(
        query_block.astype(jnp.float32) * key_sum[None], axis=2
    )
    memory_list = [memory_low]
    keysum_list = [key_sum]
    numer_list = [numerator]
    denom_list = [denominator]
    ratio_list = numerator / denominator[:, :, None]
    mixed_low = ratio_list.reshape(local_len, model_width).astype(jnp.bfloat16)
    middle_tokens = input_tokens + jnp.dot(mixed_low, out_full, preferred_element_type=jnp.float32)
    mlp_set = (
        lax.all_gather(up_projection_weight, ("dp", "seq"), axis=0, tiled=True),
        lax.all_gather(down_projection_weight, ("dp", "seq"), axis=0, tiled=True),
        lax.all_gather(second_gain, ("dp", "seq"), axis=0, tiled=True),
        lax.all_gather(second_shift, ("dp", "seq"), axis=0, tiled=True),
    )
    up_full = mlp_set[0]
    down_full = mlp_set[1]
    gain_two = mlp_set[2].astype(jnp.float32)
    shift_two = mlp_set[3].astype(jnp.float32)
    normed_two_low = layer_norm(middle_tokens, gain_two, shift_two).astype(jnp.bfloat16)
    upper_hidden = jnp.dot(normed_two_low, up_full, preferred_element_type=jnp.float32)
    active_low = jax.nn.gelu(upper_hidden).astype(jnp.bfloat16)
    result = middle_tokens + jnp.dot(active_low, down_full, preferred_element_type=jnp.float32)
    result_tokens = result.astype(jnp.bfloat16).reshape(1, local_len, model_width)
    grad_out = cotangent[0].astype(jnp.float32)
    mlp_again = (
        lax.all_gather(up_projection_weight, ("dp", "seq"), axis=0, tiled=True),
        lax.all_gather(down_projection_weight, ("dp", "seq"), axis=0, tiled=True),
        lax.all_gather(second_gain, ("dp", "seq"), axis=0, tiled=True),
        lax.all_gather(second_shift, ("dp", "seq"), axis=0, tiled=True),
    )
    up_back = mlp_again[0]
    down_back = mlp_again[1]
    grad_out_low = cotangent[0]
    grad_down = rows_product(active_low, grad_out_low)
    d_active = cols_product(grad_out_low, down_back)
    gelu_value, gelu_back = jax.vjp(jax.nn.gelu, upper_hidden)
    g_upper = gelu_back(d_active)[0].astype(jnp.bfloat16)
    grad_up = rows_product(normed_two_low, g_upper)
    d_normed_two = cols_product(g_upper, up_back)
    norm_value, norm_back = jax.vjp(layer_norm, middle_tokens, gain_two, shift_two)
    middle_part, grad_gain_two, grad_shift_two = norm_back(d_normed_two)
    g_middle = grad_out + middle_part
    attn_again = (
        lax.all_gather(query_key_value_weight, ("dp", "seq"), axis=0, tiled=True),
        lax.all_gather(attention_output_weight, ("dp", "seq"), axis=0, tiled=True),
        lax.all_gather(first_gain, ("dp", "seq"), axis=0, tiled=True),
        lax.all_gather(first_shift, ("dp", "seq"), axis=0, tiled=True),
    )
    in_back = attn_again[0]
    out_back = attn_again[1]
    g_middle_low = g_middle.astype(jnp.bfloat16)
    grad_out_weight = rows_product(mixed_low, g_middle_low)
    d_mixed = cols_product(g_middle_low, out_back).reshape(block_shape)
    block_number = 0
    query_block = feat_query[block_number]
    denominator = denom_list[block_number]
    g_numerator = (d_mixed[block_number] / denominator[:, :, None]).astype(jnp.bfloat16)
    g_denominator = -jnp.sum(d_mixed[block_number] * numer_list[block_number], axis=2) / (
        denominator * denominator
    )
    kept_query = jnp.where(keep_list[block_number][:, None, None], query_block, zero_low)
    gnum_list = [g_numerator]
    gden_list = [g_denominator]
    local_list = [
        jnp.einsum("the,thf->hef", kept_query, g_numerator, preferred_element_type=jnp.float32)
    ]
    localkey_list = [jnp.sum(kept_query.astype(jnp.float32) * g_denominator[:, :, None], axis=0)]
    combined = identity
    for block_number in reversed(range(block_count)):
        combined = combine(
            combined,
            (flag_list[block_number], local_list[block_number], localkey_list[block_number]),
        )
    leaving = prefix(combined, "seq", combine, identity, True)
    g_memory = leaving[1]
    g_key_sum = leaving[2]
    gq_list = []
    gk_list = []
    gv_list = []
    for block_number in reversed(range(block_count)):
        query_block = feat_query[block_number]
        key_block = feat_key[block_number]
        value_block = value_low[block_number]
        keep_float = keep_list[block_number].astype(jnp.float32)
        tail_float = tail_list[block_number].astype(jnp.float32)
        g_numerator = gnum_list[block_number]
        g_denominator = gden_list[block_number]
        g_update = g_memory.astype(jnp.bfloat16)
        raw_scores = jnp.einsum(
            "the,jhe->htj", query_block, key_block, preferred_element_type=jnp.float32
        )
        scores_low = jnp.where(same_list[block_number][None], raw_scores, 0.0).astype(jnp.bfloat16)
        g_scores = (
            jnp.einsum("thf,jhf->htj", g_numerator, value_block, preferred_element_type=jnp.float32)
            + jnp.transpose(g_denominator)[:, :, None]
        )
        g_scores_low = jnp.where(
            same_list[block_number][None], g_scores.astype(jnp.bfloat16), zero_low
        )
        query_grad = jnp.einsum(
            "htj,jhe->the", g_scores_low, key_block, preferred_element_type=jnp.float32
        )
        query_grad = query_grad + keep_float[:, None, None] * (
            jnp.einsum(
                "thf,hef->the",
                g_numerator,
                memory_list[block_number],
                preferred_element_type=jnp.float32,
            )
            + g_denominator[:, :, None] * keysum_list[block_number][None]
        )
        key_grad = jnp.einsum(
            "htj,the->jhe", g_scores_low, query_block, preferred_element_type=jnp.float32
        )
        key_grad = key_grad + tail_float[:, None, None] * (
            jnp.einsum("jhf,hef->jhe", value_block, g_update, preferred_element_type=jnp.float32)
            + g_key_sum[None]
        )
        tail_key = jnp.where(tail_list[block_number][:, None, None], key_block, zero_low)
        value_grad = jnp.einsum(
            "htj,thf->jhf", scores_low, g_numerator, preferred_element_type=jnp.float32
        )
        value_grad = value_grad + jnp.einsum(
            "jhe,hef->jhf", tail_key, g_update, preferred_element_type=jnp.float32
        )
        gq_list.append(query_grad)
        gk_list.append(key_grad)
        gv_list.append(value_grad)
        g_memory = local_list[block_number] + flag_list[block_number] * g_memory
        g_key_sum = localkey_list[block_number] + flag_list[block_number] * g_key_sum
    d_feat_query = jnp.concatenate(gq_list[::-1], axis=0).reshape(local_len, model_width)
    d_feat_key = jnp.concatenate(gk_list[::-1], axis=0).reshape(local_len, model_width)
    d_value = jnp.concatenate(gv_list[::-1], axis=0).reshape(local_len, model_width)
    query_value, query_back = jax.vjp(feature, queries)
    key_value, key_back = jax.vjp(feature, keys_raw)
    g_projected = jnp.concatenate(
        [query_back(d_feat_query)[0], key_back(d_feat_key)[0], d_value], axis=1
    ).astype(jnp.bfloat16)
    grad_in_weight = rows_product(normed_low, g_projected)
    d_normed = cols_product(g_projected, in_back)
    first_value, first_back = jax.vjp(layer_norm, input_tokens, gain_one, shift_one)
    input_part, grad_gain_one, grad_shift_one = first_back(d_normed)
    grad_tokens = (g_middle + input_part).reshape(1, local_len, model_width)
    summed = (
        lax.psum_scatter(grad_in_weight, ("dp", "seq"), scatter_dimension=0, tiled=True),
        lax.psum_scatter(grad_out_weight, ("dp", "seq"), scatter_dimension=0, tiled=True),
        lax.psum_scatter(grad_up, ("dp", "seq"), scatter_dimension=0, tiled=True),
        lax.psum_scatter(grad_down, ("dp", "seq"), scatter_dimension=0, tiled=True),
        lax.psum_scatter(grad_gain_one, ("dp", "seq"), scatter_dimension=0, tiled=True),
        lax.psum_scatter(grad_shift_one, ("dp", "seq"), scatter_dimension=0, tiled=True),
        lax.psum_scatter(grad_gain_two, ("dp", "seq"), scatter_dimension=0, tiled=True),
        lax.psum_scatter(grad_shift_two, ("dp", "seq"), scatter_dimension=0, tiled=True),
    )
    return (
        result_tokens,
        grad_tokens,
        summed[0],
        summed[1],
        summed[2],
        summed[3],
        summed[4],
        summed[5],
        summed[6],
        summed[7],
    )


MESH = pl.DeviceIdType.MESH
LOW = jnp.bfloat16
FULL = jnp.float32


class Place:
    def __init__(self):
        dp, seq = lax.axis_index("dp"), lax.axis_index("seq")
        self.y, self.x = dp // 2, dp % 2
        self.z, self.c = seq // 2, seq % 2
        self.dp, self.seq = dp, seq
        self.over_x = (self.y * 2 + 1 - self.x, seq)
        self.over_y = ((1 - self.y) * 2 + self.x, seq)
        self.sibling = (dp, self.z * 2 + 1 - self.c)
        self.following = [(dp, (seq + 1) % 8), (dp, (seq + 2) % 8)]
        self.preceding = [(dp, (seq + 7) % 8), (dp, (seq + 6) % 8)]
        self.over_end = (dp, (seq + 2 * self.c + 7) % 8)
        self.along_z = [(dp, (self.z + d) % 4 * 2 + self.c) for d in (1, 2, 3)]

    def meet(self):
        barrier = pltpu.get_barrier_semaphore()
        everyone = [self.over_x, self.over_y, self.sibling, self.over_end, *self.along_z]
        for device in everyone:
            pl.semaphore_signal(barrier, inc=1, device_id=device, device_id_type=MESH)
        pl.semaphore_wait(barrier, len(everyone))


def remote(source, target, send, recv, device):
    return pltpu.make_async_remote_copy(
        src_ref=source,
        dst_ref=target,
        send_sem=send,
        recv_sem=recv,
        device_id=device,
        device_id_type=MESH,
    )


class Gather:
    def __init__(self, place, full, send, recv):
        p = place
        half = full.shape[4] // 2
        low, high = pl.ds(0, half), pl.ds(half, half)
        own = full.at[p.y, p.x, p.z, p.c]
        parts = [(own, device) for device in p.along_z]
        parts.append((full.at[p.y, p.x, :, p.c, low], p.over_x))
        parts.append((full.at[p.y, p.x, :, p.c, high], p.over_y))
        parts.append((full.at[p.y, :, :, p.c, low], p.over_y))
        parts.append((full.at[:, p.x, :, p.c, high], p.over_x))
        for y, x in ((p.y, p.x), (p.y, 1 - p.x), (1 - p.y, p.x), (1 - p.y, 1 - p.x)):
            parts.append((full.at[y, x, :, p.c], p.sibling))
        self.copies = [
            remote(ref, ref, send.at[i], recv.at[i], device)
            for i, (ref, device) in enumerate(parts)
        ]

    def start(self, *which):
        for i in which:
            self.copies[i].start()

    def arrive(self, *which):
        for i in which:
            self.copies[i].wait_recv()

    def step(self, number):
        if number == 0:
            self.start(0, 1, 2)
        elif number == 1:
            self.arrive(0, 1, 2)
            self.start(3, 4, 7)
        elif number == 2:
            self.arrive(3, 4)
            self.start(5, 6)
        elif number == 3:
            self.arrive(5, 6)
            self.start(8, 9, 10)
        else:
            self.arrive(7, 8, 9, 10)

    def finish(self):
        for copy in self.copies:
            copy.wait_send()


class Scatter:
    def __init__(self, place, own, total, pair, first_a, first_b, second_a, second_b, last, send, recv, outside):
        p = place
        self.outside, self.released = outside, False
        half = own.shape[4] // 2
        self.place, self.half = p, half
        self.own, self.total, self.pair = own, total, pair
        self.first_a, self.first_b = first_a, first_b
        self.second_a, self.second_b = second_a, second_b
        self.last = last
        low, high = pl.ds(0, half), pl.ds(half, half)
        parts = [
            (own.at[:, :, :, 1 - p.c], pair, p.sibling),
            (total.at[1 - p.y, :, :, low], first_a, p.over_y),
            (total.at[:, 1 - p.x, :, high], first_b, p.over_x),
            (total.at[p.y, 1 - p.x, :, low], second_a, p.over_x),
            (total.at[1 - p.y, p.x, :, high], second_b, p.over_y),
        ]
        if outside:
            self.keep = pltpu.make_async_copy(own.at[:, :, :, p.c], total, send.at[8])
        for d in (1, 2, 3):
            parts.append((total.at[p.y, p.x, (p.z + d) % 4], last.at[d - 1], p.along_z[d - 1]))
        self.copies = [
            remote(source, target, send.at[i], recv.at[i], device)
            for i, (source, target, device) in enumerate(parts)
        ]

    def step(self, number):
        p, half = self.place, self.half
        low, high = slice(0, half), slice(half, 2 * half)
        total = self.total
        if number == 0:
            self.copies[0].start()
            if self.outside:
                self.keep.start()
        elif number == 1:
            if self.outside:
                self.keep.wait()
            self.copies[0].wait_recv()

            @pl.loop(0, 4)
            def _(i):
                y, x = i // 2, i % 2
                mine = total[y, x] if self.outside else self.own[y, x, :, p.c]
                total[y, x] = mine + self.pair[y, x]

            self.copies[1].start()
            self.copies[2].start()
        elif number == 2:
            self.copies[1].wait_recv()
            self.copies[2].wait_recv()
            for i in range(2):
                total[p.y, i, :, low] += self.first_a[i]
                total[i, p.x, :, high] += self.first_b[i]
            self.copies[3].start()
            self.copies[4].start()
        elif number == 3:
            self.copies[3].wait_recv()
            self.copies[4].wait_recv()
            total[p.y, p.x, :, low] += self.second_a[...]
            total[p.y, p.x, :, high] += self.second_b[...]
            for i in (5, 6, 7):
                self.copies[i].start()

    def result(self):
        for i in (5, 6, 7):
            self.copies[i].wait_recv()
        p = self.place
        value = self.total[p.y, p.x, p.z].astype(FULL)
        for d in range(3):
            value = value + self.last[d].astype(FULL)
        return value

    def release(self):
        self.copies[0].wait_send()
        self.released = True

    def finish(self):
        for copy in self.copies[1 if self.released else 0 :]:
            copy.wait_send()


class SmallGather(Gather):
    def __init__(self, place, full, send, recv):
        p = place
        own = full.at[p.y, p.x, p.z, p.c]
        parts = [(own, device) for device in p.along_z]
        parts.append((full.at[p.y, p.x, :, p.c], p.over_x))
        parts.append((full.at[p.y, :, :, p.c], p.over_y))
        for y in range(2):
            for x in range(2):
                parts.append((full.at[y, x, :, p.c], p.sibling))
        self.copies = [
            remote(ref, ref, send.at[i], recv.at[i], device)
            for i, (ref, device) in enumerate(parts)
        ]

    def step(self, number):
        if number == 0:
            self.start(0, 1, 2)
        elif number == 1:
            self.arrive(0, 1, 2)
            self.start(3)
        elif number == 2:
            self.arrive(3)
            self.start(4)
        elif number == 3:
            self.arrive(4)
            self.start(5, 6, 7, 8)
        else:
            self.arrive(5, 6, 7, 8)


def product(one, two):
    return jnp.dot(one, two, preferred_element_type=FULL)


def across(one, two):
    return lax.dot_general(one, two, (((1,), (1,)), ((), ())), preferred_element_type=FULL)


def down_rows(one, two):
    return lax.dot_general(one, two, (((0,), (0,)), ((), ())), preferred_element_type=FULL)


def tile(i, size):
    return pl.ds(pl.multiple_of(i * size, size), size)


def image_count(starts, at):
    total = jnp.where(starts[0, 0] <= at, 1, 0)
    for k in range(1, starts.shape[1]):
        total = total + jnp.where(starts[0, k] <= at, 1, 0)
    return total


class Images:
    def __init__(self, starts, seq, length):
        first = seq * length
        self.length = length
        self.column = image_count(starts, first + lax.broadcasted_iota(jnp.int32, (length, 128), 0))
        self.row = image_count(starts, first + lax.broadcasted_iota(jnp.int32, (8, length), 1))
        before = image_count(starts, first - 1)
        last = image_count(starts, first + length - 1)
        earlier = image_count(starts, first - length - 1)
        later = image_count(starts, first + 2 * length - 1)
        self.keep = jnp.where(self.column == before, 1.0, 0.0)
        self.tail = jnp.where(self.column == last, 1.0, 0.0)
        self.flag_before = jnp.where(before == earlier, 1.0, 0.0)
        self.flag_after = jnp.where(later == last, 1.0, 0.0)


def same_mask(images, rows, columns, transposed):
    shape = (images.length, images.length)
    down = lax.broadcasted_iota(jnp.int32, shape, 0)
    along = lax.broadcasted_iota(jnp.int32, shape, 1)
    order = down <= along if transposed else down >= along
    equal = images.column[:, :1] == images.row[:1, :]
    return jnp.where(order & equal, 1.0, 0.0).astype(LOW)


def head_lanes(rows):
    return lax.broadcasted_iota(jnp.int32, (rows, 128), 1) < HEAD


def own_block():
    return jnp.where(
        (lax.broadcasted_iota(jnp.int32, (128, 128), 0) < HEAD)
        == (lax.broadcasted_iota(jnp.int32, (128, 128), 1) < HEAD),
        1.0,
        0.0,
    ).astype(LOW)


def pack_pair(square):
    return jnp.where(head_lanes(HEAD), square[:HEAD], square[HEAD:])


def unpack_pair(packed):
    lanes = head_lanes(HEAD)
    zero = jnp.zeros_like(packed)
    return jnp.concatenate([jnp.where(lanes, packed, zero), jnp.where(lanes, zero, packed)], axis=0)


def statistics(values):
    average = jnp.mean(values, axis=-1, keepdims=True)
    centred = values - average
    spread = jnp.mean(centred * centred, axis=-1, keepdims=True)
    scale = lax.rsqrt(spread + 1e-05)
    return centred * scale, scale


def gelu_both(values):
    root = 0.7978845608028654
    square = values * values
    angle = jnp.tanh(root * values * (1.0 + 0.044715 * square))
    half = 0.5 + 0.5 * angle
    slope = half + 0.5 * values * (1.0 - angle * angle) * (root * (1.0 + 0.134145 * square))
    return values * half, slope


def forward_kernel(inputs, outputs, scratch):
    tokens_in, cotangent_in, starts, in_weight, out_weight, up_weight, down_weight, pack_in = inputs
    (
        in_full,
        out_full,
        up_full,
        down_full,
        grad_down_out,
        result_out,
        heads_out,
        mixed_out,
        inverse_out,
        middle_out,
        slope_out,
        memory_out,
        sums_out,
        gains_out,
    ) = outputs
    (
        wide,
        tall,
        pack,
        tokens,
        cotangent,
        gains,
        normed,
        heads,
        mask,
        mixed,
        mixed_low,
        inverse,
        middle,
        active,
        slope,
        grad_down,
        result,
        outgoing,
        incoming,
        memory,
        sums,
        send,
        recv,
        small_send,
        small_recv,
        state_send,
        state_recv,
        local,
        store,
    ) = scratch
    p = Place()
    length, width = tokens.shape
    loads = []
    for j in range(8):
        source = in_weight if j < 3 else (out_weight if j == 3 else up_weight)
        column = j if j < 3 else (0 if j == 3 else j - 4)
        loads.append((source.at[:, pl.ds(column * 1024, 1024)], wide.at[j, p.y, p.x, p.z, p.c]))
    for j in range(4):
        loads.append((down_weight.at[:, pl.ds(256 * j, 256)], tall.at[j, p.y, p.x, p.z, p.c]))
    loads.append((pack_in, pack.at[p.y, p.x, p.z, p.c]))
    loads.append((tokens_in, tokens))
    loads.append((cotangent_in, cotangent))
    loads = [pltpu.make_async_copy(a, b, local.at[i]) for i, (a, b) in enumerate(loads)]
    for i in (12, 0, 1, 2, 13, 3, 4, 5, 6, 7, 8, 9, 10, 11, 14):
        loads[i].start()
    stores = []

    def save(source, target):
        copy = pltpu.make_async_copy(source, target, store.at[len(stores)])
        copy.start()
        stores.append(copy)

    p.meet()
    small = SmallGather(p, pack, small_send, small_recv)
    chunks = [Gather(p, wide.at[j], send.at[j], recv.at[j]) for j in range(8)]
    chunks += [Gather(p, tall.at[j], send.at[8 + j], recv.at[8 + j]) for j in range(4)]

    def event(j, number):
        if not 0 <= j < 12:
            return
        if number == 0:
            loads[j].wait()
        chunks[j].step(number)
        if number == 4:
            if j < 8:
                target = in_full if j < 3 else (out_full if j == 3 else up_full)
                column = j if j < 3 else (0 if j == 3 else j - 4)
                save(wide.at[j], target.at[:, :, :, :, :, pl.ds(column * 1024, 1024)])
            else:
                save(tall.at[j - 8], down_full.at[:, :, :, :, :, pl.ds(256 * (j - 8), 256)])

    def weight(j, columns):
        return wide[j, :, :, :, :, :, columns].reshape(width, columns.size)

    images = Images(starts, p.seq, length)

    def first_norm():
        for y in range(2):
            for x in range(2):
                for k in range(2):
                    value = pack[y, x, 2 * k : 2 * k + 2].astype(FULL)
                    value = (value[0, 0] + value[0, 1]) + (value[1, 0] + value[1, 1])
                    at = 128 * ((y * 2 + x) * 2 + k)
                    gains[:, at : at + 128] = value
        save(gains, gains_out)
        loads[13].wait()

        @pl.loop(0, length // 128)
        def _(i):
            rows = tile(i, 128)
            value, _ = statistics(tokens[rows, :].astype(FULL))
            normed[rows, :] = (value * gains[0:1, :] + gains[1:2, :]).astype(LOW)

        mask[...] = same_mask(images, length, length, False)

    def project(j):
        @pl.loop(0, 2)
        def _(i):
            value = product(normed[...], weight(j, tile(i, 512)))
            if j < 2:
                value = jnp.where(value > 0, value + 1.0, jnp.exp(jnp.minimum(value, 0.0)))
            heads[j, :, tile(i, 512)] = value.astype(LOW)

    def update():
        tail = images.tail.astype(LOW)

        @pl.loop(0, 8)
        def _(i):
            lanes = tile(i, 128)
            key = heads[1, :, lanes] * tail
            square = down_rows(key, heads[2, :, lanes])
            outgoing[i, 0:HEAD] = pack_pair(square).astype(LOW)
            total = product(jnp.ones((16, length), LOW), key)
            outgoing[i, HEAD : HEAD + 16] = total.astype(LOW)

        save(heads, heads_out)
        for copy in state:
            copy.start()

    state = [
        remote(outgoing, incoming.at[d], state_send.at[d], state_recv.at[d], device)
        for d, device in enumerate(p.following)
    ]

    def enter():
        for copy in state:
            copy.wait_recv()

        @pl.loop(0, 8)
        def _(i):
            value = incoming[0, i].astype(FULL) + images.flag_before * incoming[1, i].astype(FULL)
            memory[i] = value[0:HEAD].astype(LOW)
            sums[i] = value[HEAD : HEAD + 8]

        save(memory, memory_out)
        save(sums, sums_out)

    def attend(begin, end):
        lanes_column = head_lanes(length)
        blocks = own_block()
        keep = images.keep.astype(LOW)
        half = length // 2
        identity = jnp.where(
            lax.broadcasted_iota(jnp.int32, (128, 128), 0)
            == lax.broadcasted_iota(jnp.int32, (128, 128), 1),
            1.0,
            0.0,
        )
        ones = jnp.ones((length, 128), LOW)

        @pl.loop(begin, end)
        def _(i):
            lanes = tile(i, 128)
            query, key, value = heads[0, :, lanes], heads[1, :, lanes], heads[2, :, lanes]
            wider = jnp.concatenate([value, ones], axis=1)
            parts = []
            for h in range(2):
                mine = lanes_column if h == 0 else ~lanes_column
                own = jnp.where(mine, query, jnp.zeros_like(query))
                upper = across(own[:half], key[:half]).astype(LOW) * mask[:half, :half]
                lower = across(own[half:], key).astype(LOW) * mask[half:, :]
                parts.append(
                    jnp.concatenate([product(upper, wider[:half]), product(lower, wider)], axis=0)
                )
            diagonal = (identity * sums[i, 0:1]).astype(LOW)
            right = jnp.concatenate(
                [unpack_pair(memory[i]), product(diagonal, blocks).astype(LOW)], axis=1
            )
            carried = product(query * keep, right)
            numerator = jnp.where(lanes_column, parts[0][:, :128], parts[1][:, :128])
            denominator = jnp.where(lanes_column, parts[0][:, 128:], parts[1][:, 128:])
            over = 1.0 / (denominator + carried[:, 128:])
            value = (numerator + carried[:, :128]) * over
            inverse[:, lanes] = over
            mixed[:, lanes] = value
            mixed_low[:, lanes] = value.astype(LOW)

    def join():
        save(mixed, mixed_out)
        save(inverse, inverse_out)

        @pl.loop(0, 2)
        def _(i):
            columns = tile(i, 512)
            middle[:, columns] = tokens[:, columns].astype(FULL) + product(
                mixed_low[...], weight(3, columns)
            )

        save(middle, middle_out)

    def second_norm():
        @pl.loop(0, length // 128)
        def _(i):
            rows = tile(i, 128)
            value, _ = statistics(middle[rows, :])
            normed[rows, :] = (value * gains[2:3, :] + gains[3:4, :]).astype(LOW)

    def raise_up(j):
        @pl.loop(0, 4)
        def _(i):
            value = product(normed[...], weight(4 + j, tile(i, 256)))
            columns = pl.ds(pl.multiple_of(j * 1024 + i * 256, 256), 256)
            value, steep = gelu_both(value)
            active[:, columns] = value.astype(LOW)
            slope[:, columns] = steep.astype(LOW)

        if j == 3:
            save(slope, slope_out)

    def down_gradient(begin, end):
        if begin == 0:
            loads[14].wait()

        @pl.loop(begin, end)
        def _(i):
            value = down_rows(active[:, tile(i, 512)], cotangent[...]).astype(LOW)
            y, x, z = i // 4, i // 2 % 2, i % 2 * 2
            for j in range(4):
                part = value[:, 256 * j : 256 * j + 256].reshape(2, 2, 128, 256)
                grad_down[j, y, x, pl.ds(z, 2)] = part

        if end == 8:
            save(grad_down, grad_down_out)

    def lower(j):
        columns = slice(256 * j, 256 * j + 256)

        @pl.loop(0, 2)
        def _(i):
            rows = tile(i, 256)
            value = product(active[rows, :], tall[j].reshape(4 * width, 256))
            result[rows, columns] = (middle[rows, columns] + value).astype(LOW)

        save(result.at[:, pl.ds(256 * j, 256)], result_out.at[:, pl.ds(256 * j, 256)])

    work = {
        5: [functools.partial(project, 0)],
        6: [functools.partial(project, 1)],
        7: [functools.partial(project, 2), update],
        8: [enter, functools.partial(attend, 0, 2), functools.partial(attend, 2, 4)],
        9: [
            functools.partial(attend, 4, 6),
            functools.partial(attend, 6, 8),
            join,
        ],
        10: [second_norm, functools.partial(raise_up, 0), functools.partial(raise_up, 1)],
        11: [functools.partial(raise_up, 2)],
        12: [
            functools.partial(raise_up, 3),
            functools.partial(down_gradient, 0, 4),
            functools.partial(down_gradient, 4, 8),
        ],
        13: [functools.partial(lower, 0)],
        14: [functools.partial(lower, 1)],
        15: [functools.partial(lower, 2)],
    }
    for tick in range(12 + 4):
        todo = work.get(tick, []) + [lambda: None] * 3
        if tick == 0:
            event(0, 0)
            loads[12].wait()
            small.step(0)
            event(1, 0)
            for number in range(1, 5):
                small.step(number)
            first_norm()
            continue
        if tick > 1:
            event(tick, 0)
        event(tick - 1, 1)
        todo[0]()
        event(tick - 2, 2)
        todo[1]()
        event(tick - 3, 3)
        event(tick - 4, 4)
        todo[2]()
    lower(3)
    small.finish()
    for copy in state:
        copy.wait_send()
    for chunk in chunks:
        chunk.finish()
    for copy in stores:
        copy.wait()


def forward_pass(tokens, cotangent, starts, in_weight, out_weight, up_weight, down_weight, pack):
    length, width = tokens.shape
    block = lambda rows, columns: jax.ShapeDtypeStruct((2, 2, 4, 2, rows, columns), LOW)
    shape = jax.ShapeDtypeStruct

    def body(*refs):
        forward_kernel(refs[:8], refs[8:22], refs[22:])

    return pl.pallas_call(
        body,
        out_shape=[
            block(32, 3072),
            block(32, 1024),
            block(32, 4096),
            block(128, 1024),
            shape((4, 2, 2, 4, 2, 128, 256), LOW),
            shape((length, width), LOW),
            shape((3, length, width), LOW),
            shape((length, width), FULL),
            shape((length, width), FULL),
            shape((length, width), FULL),
            shape((length, 4 * width), LOW),
            shape((8, HEAD, 128), LOW),
            shape((8, 8, 128), FULL),
            shape((16, width), FULL),
        ],
        in_specs=[
            pl.BlockSpec(memory_space=pltpu.SMEM if i == 2 else pl.ANY) for i in range(8)
        ],
        out_specs=[pl.BlockSpec(memory_space=pl.ANY)] * 14,
        scratch_shapes=[
            pltpu.VMEM((8, 2, 2, 4, 2, 32, 1024), LOW),
            pltpu.VMEM((4, 2, 2, 4, 2, 128, 256), LOW),
            pltpu.VMEM((2, 2, 4, 2, 16, 128), LOW),
            pltpu.VMEM((length, width), LOW),
            pltpu.VMEM((length, width), LOW),
            pltpu.VMEM((16, width), FULL),
            pltpu.VMEM((length, width), LOW),
            pltpu.VMEM((3, length, width), LOW),
            pltpu.VMEM((length, length), LOW),
            pltpu.VMEM((length, width), FULL),
            pltpu.VMEM((length, width), LOW),
            pltpu.VMEM((length, width), FULL),
            pltpu.VMEM((length, width), FULL),
            pltpu.VMEM((length, 4 * width), LOW),
            pltpu.VMEM((length, 4 * width), LOW),
            pltpu.VMEM((4, 2, 2, 4, 2, 128, 256), LOW),
            pltpu.VMEM((length, width), LOW),
            pltpu.VMEM((8, HEAD + 16, 128), LOW),
            pltpu.VMEM((2, 8, HEAD + 16, 128), LOW),
            pltpu.VMEM((8, HEAD, 128), LOW),
            pltpu.VMEM((8, 8, 128), FULL),
            pltpu.SemaphoreType.DMA((12, 11)),
            pltpu.SemaphoreType.DMA((12, 11)),
            pltpu.SemaphoreType.DMA((9,)),
            pltpu.SemaphoreType.DMA((9,)),
            pltpu.SemaphoreType.DMA((2,)),
            pltpu.SemaphoreType.DMA((2,)),
            pltpu.SemaphoreType.DMA((15,)),
            pltpu.SemaphoreType.DMA((26,)),
        ],
        compiler_params=pltpu.CompilerParams(
            collective_id=0, has_side_effects=True, vmem_limit_bytes=62 << 20
        ),
        name="forward_pass",
    )(tokens, cotangent, starts, in_weight, out_weight, up_weight, down_weight, pack)


def scatter_buffers(count, rows, columns):
    half = rows // 2
    shapes = [
        (2, 2, 4, rows, columns),
        (2, 2, 4, rows, columns),
        (2, 4, half, columns),
        (2, 4, half, columns),
        (4, half, columns),
        (4, half, columns),
        (3, rows, columns),
    ]
    return [pltpu.VMEM((count, *shape), LOW) for shape in shapes]


class Sum:
    def __init__(self, place, stages, landed, send, recv):
        p = place
        devices = [p.sibling, p.over_x, p.over_y, *p.along_z]
        self.stages, self.landed = stages, landed
        self.copies = [
            remote(stages.at[min(i, 3)], landed.at[i], send.at[i], recv.at[i], device)
            for i, device in enumerate(devices)
        ]

    def step(self, number):
        stages, landed = self.stages, self.landed
        if 1 <= number <= 3:
            self.copies[number - 1].wait_recv()
            stages[number] = stages[number - 1] + landed[number - 1]
        if number < 3:
            self.copies[number].start()
        elif number == 3:
            for i in (3, 4, 5):
                self.copies[i].start()

    def result(self):
        for i in (3, 4, 5):
            self.copies[i].wait_recv()
        return (self.stages[3] + self.landed[3]) + (self.landed[4] + self.landed[5])

    def finish(self):
        for copy in self.copies:
            copy.wait_send()


def backward_kernel(inputs, outputs, tall, wide, scratch):
    (
        tokens_in,
        cotangent_in,
        starts,
        in_full,
        out_full,
        up_full,
        down_full,
        grad_down_in,
        heads_in,
        mixed_in,
        inverse_in,
        middle_in,
        slope_in,
        memory_in,
        sums_in,
        gains_in,
    ) = inputs
    (
        cotangent,
        normed,
        slab,
        broad,
        grad_middle,
        inner,
        mixed,
        inverse,
        memory,
        sums,
        gains,
        mask,
        mask_back,
        parts,
        done_in,
        done_out,
        done_up,
        done_down,
        stages,
        landed,
        outgoing,
        incoming,
        update,
        key_update,
        send,
        recv,
        sum_send,
        sum_recv,
        state_send,
        state_recv,
        local,
        stream,
        store,
    ) = scratch
    p = Place()
    length, width = cotangent.shape

    pairs = [
        (cotangent_in, cotangent),
        (slope_in, broad),
        (middle_in, grad_middle),
        (gains_in, gains),
        (memory_in, memory),
        (sums_in, sums),
        (mixed_in, mixed),
        (inverse_in, inverse),
        (tokens_in, cotangent),
    ]
    pairs += [(heads_in.at[k], broad.at[:, pl.ds(1024 * k, 1024)]) for k in range(3)]
    loads = [pltpu.make_async_copy(a, b, local.at[i]) for i, (a, b) in enumerate(pairs)]
    slabs = [down_full.at[pl.ds(1024 * j, 1024), :] for j in range(4)]
    slabs += [up_full.at[:, pl.ds(1024 * j, 1024)] for j in range(4)]
    slabs += [out_full]
    slabs += [in_full.at[:, pl.ds(1024 * j, 1024)] for j in range(3)]
    slabs = [
        pltpu.make_async_copy(source, slab.at[i % 2], stream.at[i]) for i, source in enumerate(slabs)
    ]
    order = [8, 9, 10, 11, 4, 5, 6, 7, 3, 0, 1, 2]
    room = {4: 0, 5: 1, 6: 2, 7: 0, 3: 1, 0: 2, 1: 0, 2: 1}
    chunks = []
    for j in range(12):
        if j < 8:
            first, *others = [ref.at[j] for ref in wide]
            buffers = [first, first, *others]
            own = parts.at[room[j]]
        else:
            buffers = [ref.at[j - 8] for ref in tall]
            own = grad_down_in.at[j - 8]
        chunks.append(Scatter(p, own, *buffers, send.at[j], recv.at[j], j >= 8))

    p.meet()
    chunks[8].step(0)
    for i in range(4):
        loads[i].start()
    slabs[0].start()
    slabs[1].start()
    for i in range(4, 8):
        loads[i].start()
    stores = []

    def save(source, target):
        copy = pltpu.make_async_copy(source, target, store.at[len(stores)])
        copy.start()
        stores.append(copy)

    def event(position, number):
        if not 0 <= position < 12:
            return
        j = order[position]
        if number < 4:
            if (j, number) != (8, 0):
                chunks[j].step(number)
            return
        if j < 8:
            target, k = (done_in, j) if j < 3 else ((done_out, 0) if j == 3 else (done_up, j - 4))
            size = 1024
        else:
            target, k, size = done_down, j - 8, 256
        where = outputs[0 if j < 3 else 1 if j == 3 else 2 if j < 8 else 3]
        target[:, size * k : size * k + size] = chunks[j].result()
        save(target.at[:, pl.ds(size * k, size)], where.at[:, pl.ds(size * k, size)])

    images = Images(starts, p.seq, length)

    def second_norm():
        loads[2].wait()
        loads[3].wait()

        @pl.loop(0, length // 128)
        def _(i):
            rows = tile(i, 128)
            value, _ = statistics(grad_middle[rows, :])
            normed[rows, :] = (value * gains[2:3, :] + gains[3:4, :]).astype(LOW)

    def active_gradient(j):
        if j == 0:
            loads[0].wait()
            loads[1].wait()
        slabs[j].wait()

        @pl.loop(0, 4)
        def _(i):
            columns = pl.ds(pl.multiple_of(1024 * j + 256 * i, 256), 256)
            value = across(cotangent[...], slab[j % 2, tile(i, 256), :])
            broad[:, columns] = (value * broad[:, columns].astype(FULL)).astype(LOW)

        slabs[j + 2].start()

    def weight_gradient(j, left, right):
        at = room[j]

        @pl.loop(0, 4)
        def _(i):
            value = down_rows(left(tile(i, 256)), right()).astype(LOW)
            parts[at, i // 2, i % 2] = value.reshape(4, 2, 32, 1024)

    def up_gradient(j):
        if j == 3:
            chunks[4].release()
        weight_gradient(
            4 + j,
            lambda columns: normed[:, columns],
            lambda: broad[:, 1024 * j : 1024 * j + 1024],
        )
        if j == 3:
            for k in range(9, 12):
                loads[k].start()

    def inner_gradient(first, j):
        slabs[first + j].wait()

        @pl.loop(0, 4)
        def _(i):
            columns = tile(i, 256)
            value = across(
                broad[:, 1024 * j : 1024 * j + 1024], slab[(first + j) % 2, columns, :]
            )
            if j > 0:
                value = value + inner[:, columns]
            inner[:, columns] = value

        if first + j + 2 < 12:
            slabs[first + j + 2].start()

    def norm_gradient(rows, values, gain):
        unit, scale = statistics(values)
        given = inner[rows, :]
        scaled = given * gain
        one = jnp.mean(scaled, axis=-1, keepdims=True)
        two = jnp.mean(scaled * unit, axis=-1, keepdims=True)
        return scale * (scaled - one - unit * two), given * unit, given

    def fold(values):
        return jnp.sum(values, axis=0, keepdims=True)

    def middle_gradient():
        stages[0] = jnp.zeros((8, width), FULL)

        @pl.loop(0, length // 128)
        def _(i):
            rows = tile(i, 128)
            value, gain, shift = norm_gradient(rows, grad_middle[rows, :], gains[2:3, :])
            stages[0, 2:3, :] += fold(gain)
            stages[0, 3:4, :] += fold(shift)
            value = value + cotangent[rows, :].astype(FULL)
            grad_middle[rows, :] = value
            cotangent[rows, :] = value.astype(LOW)

    def output_gradient():
        loads[6].wait()
        chunks[5].release()
        weight_gradient(
            3, lambda columns: mixed[:, columns].astype(LOW), lambda: cotangent[...]
        )
        loads[8].start()

    def mixed_gradient():
        slabs[8].wait()

        @pl.loop(0, 4)
        def _(i):
            columns = tile(i, 256)
            inner[:, columns] = across(cotangent[...], slab[0, columns, :])

        slabs[10].start()

    state = [
        remote(outgoing, incoming.at[d], state_send.at[d], state_recv.at[d], device)
        for d, device in enumerate(p.preceding)
    ]

    def numerator_gradient():
        for i in (4, 5, 7, 9, 10, 11):
            loads[i].wait()
        blocks = own_block()
        doubled = jnp.concatenate([blocks, blocks], axis=0)

        @pl.loop(0, 8)
        def _(i):
            lanes = tile(i, 128)
            given, over = inner[:, lanes], inverse[:, lanes]
            numerator = (given * over).astype(LOW)
            each = given * mixed[:, lanes]
            high = each.astype(LOW)
            rest = (each - high.astype(FULL)).astype(LOW)
            slant = product(jnp.concatenate([high, rest], axis=1), doubled) * over * -1.0
            mixed[:, lanes] = slant
            broad[:, pl.ds(pl.multiple_of(3072 + 128 * i, 128), 128)] = numerator
            kept = broad[:, lanes].astype(FULL) * images.keep
            square = down_rows(kept.astype(LOW), numerator)
            outgoing[i, 0:HEAD] = pack_pair(square).astype(LOW)
            total = fold(kept * slant)
            outgoing[i, HEAD : HEAD + 16] = jnp.broadcast_to(total, (16, 128)).astype(LOW)

        for copy in state:
            copy.start()
        mask[...] = same_mask(images, length, length, False)
        mask_back[...] = same_mask(images, length, length, True)

    def enter():
        for copy in state:
            copy.wait_recv()
        flag = jnp.where(p.seq == 7, 0.0, images.flag_after)

        @pl.loop(0, 8)
        def _(i):
            value = incoming[0, i].astype(FULL) + flag * incoming[1, i].astype(FULL)
            update[i] = value[0:HEAD].astype(LOW)
            key_update[i] = value[HEAD : HEAD + 8]

    def attend(begin, end):
        if begin == 0:
            enter()
        if end == 8:
            first_norm()
        first = head_lanes(length)
        lane = lax.broadcasted_iota(jnp.int32, (length, 128), 1)
        ones = jnp.ones((length, 128), LOW)
        zero = jnp.zeros((length, 128), LOW)
        half = length // 2

        @pl.loop(begin, end)
        def _(i):
            at = [pl.ds(pl.multiple_of(1024 * k + 128 * i, 128), 128) for k in range(4)]
            query, key, value, numerator = [broad[:, lanes] for lanes in at]
            slant = mixed[:, at[0]]
            high = slant.astype(LOW)
            rest = (slant - high.astype(FULL)).astype(LOW)
            right = jnp.concatenate([value, ones], axis=1)
            grads = []
            for h in range(2):
                mine = first if h == 0 else ~first
                own_query = jnp.where(mine, query, zero)
                left = jnp.concatenate(
                    [
                        jnp.where(mine, numerator, zero),
                        jnp.where(
                            lane == HEAD * h, high, jnp.where(lane == HEAD * h + 1, rest, zero)
                        ),
                    ],
                    axis=1,
                )
                upper = across(left[:half], right[:half]).astype(LOW) * mask[:half, :half]
                lower = across(left[half:], right).astype(LOW) * mask[half:, :]
                for_query = jnp.concatenate([product(upper, key[:half]), product(lower, key)], axis=0)
                upper = across(right[:half], left).astype(LOW) * mask_back[:half, :]
                lower = across(right[half:], left[half:]).astype(LOW) * mask_back[half:, half:]
                for_key = jnp.concatenate(
                    [product(upper, query), product(lower, query[half:])], axis=0
                )
                upper = across(key[:half], own_query).astype(LOW) * mask_back[:half, :]
                lower = across(key[half:], own_query[half:]).astype(LOW) * mask_back[half:, half:]
                for_value = jnp.concatenate(
                    [product(upper, numerator), product(lower, numerator[half:])], axis=0
                )
                grads.append((for_query, for_key, for_value))
            for_query, for_key, for_value = [
                jnp.where(first, one, two) for one, two in zip(*grads, strict=True)
            ]
            keep, tail = images.keep, images.tail
            for_query = for_query + keep * (
                across(numerator, unpack_pair(memory[i])) + slant * sums[i, 0:1]
            )
            square = unpack_pair(update[i])
            for_key = for_key + tail * (across(value, square) + key_update[i, 0:1])
            for_value = for_value + product(key * tail.astype(LOW), square)
            broad[:, at[0]] = (for_query * jnp.minimum(query.astype(FULL), 1.0)).astype(LOW)
            broad[:, at[1]] = (for_key * jnp.minimum(key.astype(FULL), 1.0)).astype(LOW)
            broad[:, at[2]] = for_value.astype(LOW)

    def first_norm():
        loads[8].wait()

        @pl.loop(0, length // 128)
        def _(i):
            rows = tile(i, 128)
            value, _ = statistics(cotangent[rows, :].astype(FULL))
            normed[rows, :] = (value * gains[0:1, :] + gains[1:2, :]).astype(LOW)

    def in_gradient(j):
        chunks[(6, 7, 3)[j]].release()
        weight_gradient(
            j,
            lambda columns: normed[:, columns],
            lambda: broad[:, 1024 * j : 1024 * j + 1024],
        )

    total = Sum(p, stages, landed, sum_send, sum_recv)

    def token_gradient():
        @pl.loop(0, length // 128)
        def _(i):
            rows = tile(i, 128)
            value, gain, shift = norm_gradient(rows, cotangent[rows, :].astype(FULL), gains[0:1, :])
            stages[0, 0:1, :] += fold(gain)
            stages[0, 1:2, :] += fold(shift)
            grad_middle[rows, :] += value

        save(grad_middle, outputs[4])
        total.step(0)

    do = functools.partial
    work = {
        0: [second_norm],
        1: [do(active_gradient, 0), do(active_gradient, 1), do(active_gradient, 2)],
        2: [do(active_gradient, 3), do(up_gradient, 0), do(up_gradient, 1)],
        3: [do(up_gradient, 2), do(inner_gradient, 4, 0), do(inner_gradient, 4, 1)],
        4: [do(inner_gradient, 4, 2), do(inner_gradient, 4, 3), middle_gradient],
        5: [do(up_gradient, 3), mixed_gradient],
        6: [output_gradient, numerator_gradient],
        7: [do(attend, 0, 2), do(attend, 2, 4), do(attend, 4, 5)],
        8: [do(attend, 5, 7), do(attend, 7, 8), do(in_gradient, 0)],
        9: [do(in_gradient, 1), do(in_gradient, 2), do(inner_gradient, 9, 0)],
        10: [
            do(inner_gradient, 9, 1),
            do(inner_gradient, 9, 2),
            token_gradient,
        ],
        11: [do(total.step, 1), do(total.step, 2), do(total.step, 3)],
    }
    for tick in range(12 + 4):
        todo = work.get(tick, []) + [lambda: None] * 3
        event(tick, 0)
        event(tick - 1, 1)
        todo[0]()
        event(tick - 2, 2)
        todo[1]()
        event(tick - 3, 3)
        event(tick - 4, 4)
        todo[2]()
    total_value = total.result()
    landed[0] = total_value
    group = (p.dp * 8 + p.seq) // 4
    mine = landed[0, :, tile(group, 128)]
    mine = pltpu.roll(mine, (128 - 32 * (p.seq % 4)) % 128, 1)
    for k in range(4):
        outputs[5 + k][...] = mine[k : k + 1, 0:32]
    total.finish()
    for copy in state:
        copy.wait_send()
    for chunk in chunks:
        chunk.finish()
    for copy in stores:
        copy.wait()


def backward_pass(*inputs):
    length, width = inputs[0].shape
    shape = jax.ShapeDtypeStruct
    vmem = pltpu.VMEM
    tall = scatter_buffers(4, 128, 256)
    wide = scatter_buffers(8, 32, 1024)[1:]

    def body(*refs):
        backward_kernel(refs[:16], refs[16:25], refs[25:32], refs[32:38], refs[38:])

    return pl.pallas_call(
        body,
        out_shape=[
            shape((32, 3072), FULL),
            shape((32, 1024), FULL),
            shape((32, 4096), FULL),
            shape((128, 1024), FULL),
            shape((length, width), FULL),
            *[shape((1, 32), FULL)] * 4,
        ],
        in_specs=[
            pl.BlockSpec(memory_space=pltpu.SMEM if i == 2 else pl.ANY) for i in range(16)
        ],
        out_specs=[pl.BlockSpec(memory_space=pl.ANY)] * 5
        + [pl.BlockSpec(memory_space=pltpu.VMEM)] * 4,
        scratch_shapes=[
            *tall,
            *wide,
            vmem((length, width), LOW),
            vmem((length, width), LOW),
            vmem((2, width, width), LOW),
            vmem((length, 4 * width), LOW),
            vmem((length, width), FULL),
            vmem((length, width), FULL),
            vmem((length, width), FULL),
            vmem((length, width), FULL),
            vmem((8, HEAD, 128), LOW),
            vmem((8, 8, 128), FULL),
            vmem((16, width), FULL),
            vmem((length, length), LOW),
            vmem((length, length), LOW),
            vmem((3, 2, 2, 4, 2, 32, 1024), LOW),
            vmem((32, 3072), FULL),
            vmem((32, 1024), FULL),
            vmem((32, 4096), FULL),
            vmem((128, 1024), FULL),
            vmem((4, 8, width), FULL),
            vmem((6, 8, width), FULL),
            vmem((8, HEAD + 16, 128), LOW),
            vmem((2, 8, HEAD + 16, 128), LOW),
            vmem((8, HEAD, 128), LOW),
            vmem((8, 8, 128), FULL),
            pltpu.SemaphoreType.DMA((12, 9)),
            pltpu.SemaphoreType.DMA((12, 8)),
            pltpu.SemaphoreType.DMA((6,)),
            pltpu.SemaphoreType.DMA((6,)),
            pltpu.SemaphoreType.DMA((2,)),
            pltpu.SemaphoreType.DMA((2,)),
            pltpu.SemaphoreType.DMA((12,)),
            pltpu.SemaphoreType.DMA((12,)),
            pltpu.SemaphoreType.DMA((13,)),
        ],
        compiler_params=pltpu.CompilerParams(
            collective_id=1, has_side_effects=True, vmem_limit_bytes=62 << 20
        ),
        name="backward_pass",
    )(*inputs)


def on_device(
    tokens,
    starts,
    query_key_value_weight,
    attention_output_weight,
    up_projection_weight,
    down_projection_weight,
    first_gain,
    first_shift,
    second_gain,
    second_shift,
    cotangent,
):
    mine = lax.axis_index("dp") * 8 + lax.axis_index("seq")
    pack = jnp.stack([first_gain, first_shift, second_gain, second_shift]).astype(FULL)
    pack = jnp.roll(jnp.pad(pack, ((0, 12), (0, 96))), 32 * (mine % 4), axis=1).astype(LOW)
    in_full, out_full, up_full, down_full, grad_down, result, *saved = forward_pass(
        tokens[0],
        cotangent[0],
        starts,
        query_key_value_weight,
        attention_output_weight,
        up_projection_weight,
        down_projection_weight,
        pack,
    )
    grads = backward_pass(
        tokens[0],
        cotangent[0],
        starts,
        in_full.reshape(1024, 3072),
        out_full.reshape(1024, 1024),
        up_full.reshape(1024, 4096),
        down_full.reshape(4096, 1024),
        grad_down,
        *saved,
    )
    vectors = [grad.reshape(32) for grad in grads[5:]]
    return (result[None], grads[4][None], *grads[:4], *vectors)


def solution(mesh):

    fast = dict(mesh.shape) == {"dp": 4, "seq": 8}
    return jax.shard_map(
        on_device if fast else on_device_general,
        mesh=mesh,
        in_specs=(
            P("dp", "seq", None),
            P("dp", None),
            P(("dp", "seq"), None),
            P(("dp", "seq"), None),
            P(("dp", "seq"), None),
            P(("dp", "seq"), None),
            P(("dp", "seq")),
            P(("dp", "seq")),
            P(("dp", "seq")),
            P(("dp", "seq")),
            P("dp", "seq", None),
        ),
        out_specs=(
            P("dp", "seq", None),
            P("dp", "seq", None),
            P(("dp", "seq"), None),
            P(("dp", "seq"), None),
            P(("dp", "seq"), None),
            P(("dp", "seq"), None),
            P(("dp", "seq")),
            P(("dp", "seq")),
            P(("dp", "seq")),
            P(("dp", "seq")),
        ),
        check_vma=False,
    )
```

```python
import functools

import jax
import jax.numpy as jnp
from jax import lax
from jax.experimental import pallas as pl
from jax.experimental.pallas import tpu as pltpu
from jax.sharding import PartitionSpec as P

HEAD = 64
BLOCK = 512


def prefix(value, axis, combine, identity, reverse):
    size, mine = (lax.axis_size(axis), lax.axis_index(axis))
    everything = jax.tree.map(
        lambda part, kind: lax.all_gather(part.astype(kind), axis),
        value,
        jax.tree.map(lambda a: jnp.bfloat16 if a.dtype == jnp.float32 else a.dtype, value),
    )
    start = jax.tree.map(
        lambda part, zero: jnp.broadcast_to(jnp.asarray(zero, part.dtype), part.shape),
        value,
        identity,
    )

    def lap(k, before):
        at = size - 1 - k if reverse else k
        reached = at > mine if reverse else at < mine
        new = combine(
            before, jax.tree.map(lambda part, own: part[at].astype(own.dtype), everything, value)
        )
        return jax.tree.map(lambda a, b: jnp.where(reached, a, b), new, before)

    return lax.fori_loop(0, size, lap, start)


def layer_norm(values, norm_gain, norm_shift):
    average = jnp.mean(values, axis=-1, keepdims=True)
    centred = values - average
    spread = jnp.mean(centred * centred, axis=-1, keepdims=True)
    return centred * lax.rsqrt(spread + 1e-05) * norm_gain + norm_shift


def feature(values):
    return jax.nn.elu(values) + 1.0


def combine(former, latter):
    return (
        former[0] * latter[0],
        latter[0] * former[1] + latter[1],
        latter[0] * former[2] + latter[2],
    )


def rows_product(factor_one, factor_two):
    return lax.dot_general(
        factor_one, factor_two, (((0,), (0,)), ((), ())), preferred_element_type=jnp.float32
    )


def cols_product(factor_one, factor_two):
    return lax.dot_general(
        factor_one, factor_two, (((1,), (1,)), ((), ())), preferred_element_type=jnp.float32
    )


def on_device_general(
    tokens,
    starts,
    query_key_value_weight,
    attention_output_weight,
    up_projection_weight,
    down_projection_weight,
    first_gain,
    first_shift,
    second_gain,
    second_shift,
    cotangent,
):
    local_len = tokens.shape[1]
    model_width = tokens.shape[2]
    head_count = model_width // HEAD
    block_count = local_len // BLOCK
    block_shape = (block_count, BLOCK, head_count, HEAD)
    zero_low = jnp.zeros((), jnp.bfloat16)
    input_tokens = tokens[0].astype(jnp.float32)
    first_pos = lax.axis_index("seq") * local_len
    positions = first_pos + jnp.arange(local_len, dtype=jnp.int32)
    pack_starts = starts[0]
    image_ids = jnp.sum((pack_starts[None, :] <= positions[:, None]).astype(jnp.int32), axis=1) - 1
    before_id = jnp.sum((pack_starts <= first_pos - 1).astype(jnp.int32)) - 1
    causal = jnp.arange(BLOCK)[:, None] >= jnp.arange(BLOCK)[None, :]
    attn_set = (
        lax.all_gather(query_key_value_weight, ("dp", "seq"), axis=0, tiled=True),
        lax.all_gather(attention_output_weight, ("dp", "seq"), axis=0, tiled=True),
        lax.all_gather(first_gain, ("dp", "seq"), axis=0, tiled=True),
        lax.all_gather(first_shift, ("dp", "seq"), axis=0, tiled=True),
    )
    in_full = attn_set[0]
    out_full = attn_set[1]
    gain_one = attn_set[2].astype(jnp.float32)
    shift_one = attn_set[3].astype(jnp.float32)
    first_normed_tokens = layer_norm(input_tokens, gain_one, shift_one)
    normed_low = first_normed_tokens.astype(jnp.bfloat16)
    projected_tokens = jnp.dot(normed_low, in_full, preferred_element_type=jnp.float32)
    queries = projected_tokens[:, :model_width]
    keys_raw = projected_tokens[:, model_width : 2 * model_width]
    values_raw = projected_tokens[:, 2 * model_width :]
    feat_query = feature(queries).astype(jnp.bfloat16).reshape(block_shape)
    feat_key = feature(keys_raw).astype(jnp.bfloat16).reshape(block_shape)
    value_low = values_raw.astype(jnp.bfloat16).reshape(block_shape)
    block_number = 0
    last_id = image_ids[-1]
    tail_mask = image_ids == last_id
    tail_key = jnp.where(tail_mask[:, None, None], feat_key[block_number], zero_low)
    keep_list = [image_ids == before_id]
    tail_list = [tail_mask]
    flag_list = [(last_id == before_id).astype(jnp.float32)]
    same_list = [causal & (image_ids[:, None] == image_ids[None, :])]
    update_list = [
        jnp.einsum(
            "jhe,jhf->hef", tail_key, value_low[block_number], preferred_element_type=jnp.float32
        )
    ]
    total_list = [jnp.sum(tail_key.astype(jnp.float32), axis=0)]
    identity = (
        jnp.ones((), jnp.float32),
        jnp.zeros((head_count, HEAD, HEAD), jnp.float32),
        jnp.zeros((head_count, HEAD), jnp.float32),
    )
    combined = identity
    block_number = 0
    combined = combine(
        combined, (flag_list[block_number], update_list[block_number], total_list[block_number])
    )
    entering = prefix(combined, "seq", combine, identity, False)
    memory = entering[1]
    key_sum = entering[2]
    block_number = 0
    query_block = feat_query[block_number]
    keep_float = keep_list[block_number].astype(jnp.float32)
    memory_low = memory.astype(jnp.bfloat16)
    raw_scores = jnp.einsum(
        "the,jhe->htj", query_block, feat_key[block_number], preferred_element_type=jnp.float32
    )
    masked = jnp.where(same_list[block_number][None], raw_scores, 0.0)
    scores_low = masked.astype(jnp.bfloat16)
    carried = (
        jnp.einsum("the,hef->thf", query_block, memory_low, preferred_element_type=jnp.float32)
        * keep_float[:, None, None]
    )
    numerator = (
        jnp.einsum(
            "htj,jhf->thf", scores_low, value_low[block_number], preferred_element_type=jnp.float32
        )
        + carried
    )
    denominator = jnp.transpose(jnp.sum(masked, axis=2)) + keep_float[:, None] * jnp.sum(
        query_block.astype(jnp.float32) * key_sum[None], axis=2
    )
    memory_list = [memory_low]
    keysum_list = [key_sum]
    numer_list = [numerator]
    denom_list = [denominator]
    ratio_list = numerator / denominator[:, :, None]
    mixed_low = ratio_list.reshape(local_len, model_width).astype(jnp.bfloat16)
    middle_tokens = input_tokens + jnp.dot(mixed_low, out_full, preferred_element_type=jnp.float32)
    mlp_set = (
        lax.all_gather(up_projection_weight, ("dp", "seq"), axis=0, tiled=True),
        lax.all_gather(down_projection_weight, ("dp", "seq"), axis=0, tiled=True),
        lax.all_gather(second_gain, ("dp", "seq"), axis=0, tiled=True),
        lax.all_gather(second_shift, ("dp", "seq"), axis=0, tiled=True),
    )
    up_full = mlp_set[0]
    down_full = mlp_set[1]
    gain_two = mlp_set[2].astype(jnp.float32)
    shift_two = mlp_set[3].astype(jnp.float32)
    normed_two_low = layer_norm(middle_tokens, gain_two, shift_two).astype(jnp.bfloat16)
    upper_hidden = jnp.dot(normed_two_low, up_full, preferred_element_type=jnp.float32)
    active_low = jax.nn.gelu(upper_hidden).astype(jnp.bfloat16)
    result = middle_tokens + jnp.dot(active_low, down_full, preferred_element_type=jnp.float32)
    result_tokens = result.astype(jnp.bfloat16).reshape(1, local_len, model_width)
    grad_out = cotangent[0].astype(jnp.float32)
    mlp_again = (
        lax.all_gather(up_projection_weight, ("dp", "seq"), axis=0, tiled=True),
        lax.all_gather(down_projection_weight, ("dp", "seq"), axis=0, tiled=True),
        lax.all_gather(second_gain, ("dp", "seq"), axis=0, tiled=True),
        lax.all_gather(second_shift, ("dp", "seq"), axis=0, tiled=True),
    )
    up_back = mlp_again[0]
    down_back = mlp_again[1]
    grad_out_low = cotangent[0]
    grad_down = rows_product(active_low, grad_out_low)
    d_active = cols_product(grad_out_low, down_back)
    gelu_value, gelu_back = jax.vjp(jax.nn.gelu, upper_hidden)
    g_upper = gelu_back(d_active)[0].astype(jnp.bfloat16)
    grad_up = rows_product(normed_two_low, g_upper)
    d_normed_two = cols_product(g_upper, up_back)
    norm_value, norm_back = jax.vjp(layer_norm, middle_tokens, gain_two, shift_two)
    middle_part, grad_gain_two, grad_shift_two = norm_back(d_normed_two)
    g_middle = grad_out + middle_part
    attn_again = (
        lax.all_gather(query_key_value_weight, ("dp", "seq"), axis=0, tiled=True),
        lax.all_gather(attention_output_weight, ("dp", "seq"), axis=0, tiled=True),
        lax.all_gather(first_gain, ("dp", "seq"), axis=0, tiled=True),
        lax.all_gather(first_shift, ("dp", "seq"), axis=0, tiled=True),
    )
    in_back = attn_again[0]
    out_back = attn_again[1]
    g_middle_low = g_middle.astype(jnp.bfloat16)
    grad_out_weight = rows_product(mixed_low, g_middle_low)
    d_mixed = cols_product(g_middle_low, out_back).reshape(block_shape)
    block_number = 0
    query_block = feat_query[block_number]
    denominator = denom_list[block_number]
    g_numerator = (d_mixed[block_number] / denominator[:, :, None]).astype(jnp.bfloat16)
    g_denominator = -jnp.sum(d_mixed[block_number] * numer_list[block_number], axis=2) / (
        denominator * denominator
    )
    kept_query = jnp.where(keep_list[block_number][:, None, None], query_block, zero_low)
    gnum_list = [g_numerator]
    gden_list = [g_denominator]
    local_list = [
        jnp.einsum("the,thf->hef", kept_query, g_numerator, preferred_element_type=jnp.float32)
    ]
    localkey_list = [jnp.sum(kept_query.astype(jnp.float32) * g_denominator[:, :, None], axis=0)]
    combined = identity
    for block_number in reversed(range(block_count)):
        combined = combine(
            combined,
            (flag_list[block_number], local_list[block_number], localkey_list[block_number]),
        )
    leaving = prefix(combined, "seq", combine, identity, True)
    g_memory = leaving[1]
    g_key_sum = leaving[2]
    gq_list = []
    gk_list = []
    gv_list = []
    for block_number in reversed(range(block_count)):
        query_block = feat_query[block_number]
        key_block = feat_key[block_number]
        value_block = value_low[block_number]
        keep_float = keep_list[block_number].astype(jnp.float32)
        tail_float = tail_list[block_number].astype(jnp.float32)
        g_numerator = gnum_list[block_number]
        g_denominator = gden_list[block_number]
        g_update = g_memory.astype(jnp.bfloat16)
        raw_scores = jnp.einsum(
            "the,jhe->htj", query_block, key_block, preferred_element_type=jnp.float32
        )
        scores_low = jnp.where(same_list[block_number][None], raw_scores, 0.0).astype(jnp.bfloat16)
        g_scores = (
            jnp.einsum("thf,jhf->htj", g_numerator, value_block, preferred_element_type=jnp.float32)
            + jnp.transpose(g_denominator)[:, :, None]
        )
        g_scores_low = jnp.where(
            same_list[block_number][None], g_scores.astype(jnp.bfloat16), zero_low
        )
        query_grad = jnp.einsum(
            "htj,jhe->the", g_scores_low, key_block, preferred_element_type=jnp.float32
        )
        query_grad = query_grad + keep_float[:, None, None] * (
            jnp.einsum(
                "thf,hef->the",
                g_numerator,
                memory_list[block_number],
                preferred_element_type=jnp.float32,
            )
            + g_denominator[:, :, None] * keysum_list[block_number][None]
        )
        key_grad = jnp.einsum(
            "htj,the->jhe", g_scores_low, query_block, preferred_element_type=jnp.float32
        )
        key_grad = key_grad + tail_float[:, None, None] * (
            jnp.einsum("jhf,hef->jhe", value_block, g_update, preferred_element_type=jnp.float32)
            + g_key_sum[None]
        )
        tail_key = jnp.where(tail_list[block_number][:, None, None], key_block, zero_low)
        value_grad = jnp.einsum(
            "htj,thf->jhf", scores_low, g_numerator, preferred_element_type=jnp.float32
        )
        value_grad = value_grad + jnp.einsum(
            "jhe,hef->jhf", tail_key, g_update, preferred_element_type=jnp.float32
        )
        gq_list.append(query_grad)
        gk_list.append(key_grad)
        gv_list.append(value_grad)
        g_memory = local_list[block_number] + flag_list[block_number] * g_memory
        g_key_sum = localkey_list[block_number] + flag_list[block_number] * g_key_sum
    d_feat_query = jnp.concatenate(gq_list[::-1], axis=0).reshape(local_len, model_width)
    d_feat_key = jnp.concatenate(gk_list[::-1], axis=0).reshape(local_len, model_width)
    d_value = jnp.concatenate(gv_list[::-1], axis=0).reshape(local_len, model_width)
    query_value, query_back = jax.vjp(feature, queries)
    key_value, key_back = jax.vjp(feature, keys_raw)
    g_projected = jnp.concatenate(
        [query_back(d_feat_query)[0], key_back(d_feat_key)[0], d_value], axis=1
    ).astype(jnp.bfloat16)
    grad_in_weight = rows_product(normed_low, g_projected)
    d_normed = cols_product(g_projected, in_back)
    first_value, first_back = jax.vjp(layer_norm, input_tokens, gain_one, shift_one)
    input_part, grad_gain_one, grad_shift_one = first_back(d_normed)
    grad_tokens = (g_middle + input_part).reshape(1, local_len, model_width)
    summed = (
        lax.psum_scatter(grad_in_weight, ("dp", "seq"), scatter_dimension=0, tiled=True),
        lax.psum_scatter(grad_out_weight, ("dp", "seq"), scatter_dimension=0, tiled=True),
        lax.psum_scatter(grad_up, ("dp", "seq"), scatter_dimension=0, tiled=True),
        lax.psum_scatter(grad_down, ("dp", "seq"), scatter_dimension=0, tiled=True),
        lax.psum_scatter(grad_gain_one, ("dp", "seq"), scatter_dimension=0, tiled=True),
        lax.psum_scatter(grad_shift_one, ("dp", "seq"), scatter_dimension=0, tiled=True),
        lax.psum_scatter(grad_gain_two, ("dp", "seq"), scatter_dimension=0, tiled=True),
        lax.psum_scatter(grad_shift_two, ("dp", "seq"), scatter_dimension=0, tiled=True),
    )
    return (
        result_tokens,
        grad_tokens,
        summed[0],
        summed[1],
        summed[2],
        summed[3],
        summed[4],
        summed[5],
        summed[6],
        summed[7],
    )


MESH = pl.DeviceIdType.MESH
LOW = jnp.bfloat16
FULL = jnp.float32


class Place:
    def __init__(self):
        dp, seq = lax.axis_index("dp"), lax.axis_index("seq")
        self.y, self.x = dp // 2, dp % 2
        self.z, self.c = seq // 2, seq % 2
        self.dp, self.seq = dp, seq
        self.over_x = (self.y * 2 + 1 - self.x, seq)
        self.over_y = ((1 - self.y) * 2 + self.x, seq)
        self.sibling = (dp, self.z * 2 + 1 - self.c)
        self.following = [(dp, (seq + 1) % 8), (dp, (seq + 2) % 8)]
        self.preceding = [(dp, (seq + 7) % 8), (dp, (seq + 6) % 8)]
        self.over_end = (dp, (seq + 2 * self.c + 7) % 8)
        self.along_z = [(dp, (self.z + d) % 4 * 2 + self.c) for d in (1, 2, 3)]

    def meet(self):
        barrier = pltpu.get_barrier_semaphore()
        everyone = [self.over_x, self.over_y, self.sibling, self.over_end, *self.along_z]
        for device in everyone:
            pl.semaphore_signal(barrier, inc=1, device_id=device, device_id_type=MESH)
        pl.semaphore_wait(barrier, len(everyone))


def remote(source, target, send, recv, device):
    return pltpu.make_async_remote_copy(
        src_ref=source,
        dst_ref=target,
        send_sem=send,
        recv_sem=recv,
        device_id=device,
        device_id_type=MESH,
    )


class Gather:
    def __init__(self, place, full, send, recv):
        p = place
        half = full.shape[4] // 2
        low, high = pl.ds(0, half), pl.ds(half, half)
        own = full.at[p.y, p.x, p.z, p.c]
        parts = [(own, device) for device in p.along_z]
        parts.append((full.at[p.y, p.x, :, p.c, low], p.over_x))
        parts.append((full.at[p.y, p.x, :, p.c, high], p.over_y))
        parts.append((full.at[p.y, :, :, p.c, low], p.over_y))
        parts.append((full.at[:, p.x, :, p.c, high], p.over_x))
        for y, x in ((p.y, p.x), (p.y, 1 - p.x), (1 - p.y, p.x), (1 - p.y, 1 - p.x)):
            parts.append((full.at[y, x, :, p.c], p.sibling))
        self.copies = [
            remote(ref, ref, send.at[i], recv.at[i], device)
            for i, (ref, device) in enumerate(parts)
        ]

    def start(self, *which):
        for i in which:
            self.copies[i].start()

    def arrive(self, *which):
        for i in which:
            self.copies[i].wait_recv()

    def step(self, number):
        if number == 0:
            self.start(0, 1, 2)
        elif number == 1:
            self.arrive(0, 1, 2)
            self.start(3, 4, 7)
        elif number == 2:
            self.arrive(3, 4)
            self.start(5, 6)
        elif number == 3:
            self.arrive(5, 6)
            self.start(8, 9, 10)
        else:
            self.arrive(7, 8, 9, 10)

    def finish(self):
        for copy in self.copies:
            copy.wait_send()


class Scatter:
    def __init__(self, place, own, total, pair, first_a, first_b, second_a, second_b, last, send, recv, outside):
        p = place
        self.outside, self.released = outside, False
        half = own.shape[4] // 2
        self.place, self.half = p, half
        self.own, self.total, self.pair = own, total, pair
        self.first_a, self.first_b = first_a, first_b
        self.second_a, self.second_b = second_a, second_b
        self.last = last
        low, high = pl.ds(0, half), pl.ds(half, half)
        parts = [
            (own.at[:, :, :, 1 - p.c], pair, p.sibling),
            (total.at[1 - p.y, :, :, low], first_a, p.over_y),
            (total.at[:, 1 - p.x, :, high], first_b, p.over_x),
            (total.at[p.y, 1 - p.x, :, low], second_a, p.over_x),
            (total.at[1 - p.y, p.x, :, high], second_b, p.over_y),
        ]
        if outside:
            self.keep = pltpu.make_async_copy(own.at[:, :, :, p.c], total, send.at[8])
        for d in (1, 2, 3):
            parts.append((total.at[p.y, p.x, (p.z + d) % 4], last.at[d - 1], p.along_z[d - 1]))
        self.copies = [
            remote(source, target, send.at[i], recv.at[i], device)
            for i, (source, target, device) in enumerate(parts)
        ]

    def step(self, number):
        p, half = self.place, self.half
        low, high = slice(0, half), slice(half, 2 * half)
        total = self.total
        if number == 0:
            self.copies[0].start()
            if self.outside:
                self.keep.start()
        elif number == 1:
            if self.outside:
                self.keep.wait()
            self.copies[0].wait_recv()

            @pl.loop(0, 4)
            def _(i):
                y, x = i // 2, i % 2
                mine = total[y, x] if self.outside else self.own[y, x, :, p.c]
                total[y, x] = mine + self.pair[y, x]

            self.copies[1].start()
            self.copies[2].start()
        elif number == 2:
            self.copies[1].wait_recv()
            self.copies[2].wait_recv()
            for i in range(2):
                total[p.y, i, :, low] += self.first_a[i]
                total[i, p.x, :, high] += self.first_b[i]
            self.copies[3].start()
            self.copies[4].start()
        elif number == 3:
            self.copies[3].wait_recv()
            self.copies[4].wait_recv()
            total[p.y, p.x, :, low] += self.second_a[...]
            total[p.y, p.x, :, high] += self.second_b[...]
            for i in (5, 6, 7):
                self.copies[i].start()

    def result(self):
        for i in (5, 6, 7):
            self.copies[i].wait_recv()
        p = self.place
        value = self.total[p.y, p.x, p.z].astype(FULL)
        for d in range(3):
            value = value + self.last[d].astype(FULL)
        return value

    def release(self):
        self.copies[0].wait_send()
        self.released = True

    def finish(self):
        for copy in self.copies[1 if self.released else 0 :]:
            copy.wait_send()


class SmallGather(Gather):
    def __init__(self, place, full, send, recv):
        p = place
        own = full.at[p.y, p.x, p.z, p.c]
        parts = [(own, device) for device in p.along_z]
        parts.append((full.at[p.y, p.x, :, p.c], p.over_x))
        parts.append((full.at[p.y, :, :, p.c], p.over_y))
        for y in range(2):
            for x in range(2):
                parts.append((full.at[y, x, :, p.c], p.sibling))
        self.copies = [
            remote(ref, ref, send.at[i], recv.at[i], device)
            for i, (ref, device) in enumerate(parts)
        ]

    def step(self, number):
        if number == 0:
            self.start(0, 1, 2)
        elif number == 1:
            self.arrive(0, 1, 2)
            self.start(3)
        elif number == 2:
            self.arrive(3)
            self.start(4)
        elif number == 3:
            self.arrive(4)
            self.start(5, 6, 7, 8)
        else:
            self.arrive(5, 6, 7, 8)


def product(one, two):
    return jnp.dot(one, two, preferred_element_type=FULL)


def across(one, two):
    return lax.dot_general(one, two, (((1,), (1,)), ((), ())), preferred_element_type=FULL)


def down_rows(one, two):
    return lax.dot_general(one, two, (((0,), (0,)), ((), ())), preferred_element_type=FULL)


def tile(i, size):
    return pl.ds(pl.multiple_of(i * size, size), size)


def image_count(starts, at):
    total = jnp.where(starts[0, 0] <= at, 1, 0)
    for k in range(1, starts.shape[1]):
        total = total + jnp.where(starts[0, k] <= at, 1, 0)
    return total


class Images:
    def __init__(self, starts, seq, length):
        first = seq * length
        self.length = length
        self.column = image_count(starts, first + lax.broadcasted_iota(jnp.int32, (length, 128), 0))
        self.row = image_count(starts, first + lax.broadcasted_iota(jnp.int32, (8, length), 1))
        before = image_count(starts, first - 1)
        last = image_count(starts, first + length - 1)
        earlier = image_count(starts, first - length - 1)
        later = image_count(starts, first + 2 * length - 1)
        self.keep = jnp.where(self.column == before, 1.0, 0.0)
        self.tail = jnp.where(self.column == last, 1.0, 0.0)
        self.flag_before = jnp.where(before == earlier, 1.0, 0.0)
        self.flag_after = jnp.where(later == last, 1.0, 0.0)


def same_mask(images, rows, columns, transposed):
    shape = (images.length, images.length)
    down = lax.broadcasted_iota(jnp.int32, shape, 0)
    along = lax.broadcasted_iota(jnp.int32, shape, 1)
    order = down <= along if transposed else down >= along
    equal = images.column[:, :1] == images.row[:1, :]
    return jnp.where(order & equal, 1.0, 0.0).astype(LOW)


def head_lanes(rows):
    return lax.broadcasted_iota(jnp.int32, (rows, 128), 1) < HEAD


def own_block():
    return jnp.where(
        (lax.broadcasted_iota(jnp.int32, (128, 128), 0) < HEAD)
        == (lax.broadcasted_iota(jnp.int32, (128, 128), 1) < HEAD),
        1.0,
        0.0,
    ).astype(LOW)


def pack_pair(square):
    return jnp.where(head_lanes(HEAD), square[:HEAD], square[HEAD:])


def unpack_pair(packed):
    lanes = head_lanes(HEAD)
    zero = jnp.zeros_like(packed)
    return jnp.concatenate([jnp.where(lanes, packed, zero), jnp.where(lanes, zero, packed)], axis=0)


def statistics(values):
    average = jnp.mean(values, axis=-1, keepdims=True)
    centred = values - average
    spread = jnp.mean(centred * centred, axis=-1, keepdims=True)
    scale = lax.rsqrt(spread + 1e-05)
    return centred * scale, scale


def gelu_both(values):
    root = 0.7978845608028654
    square = values * values
    angle = jnp.tanh(root * values * (1.0 + 0.044715 * square))
    half = 0.5 + 0.5 * angle
    slope = half + 0.5 * values * (1.0 - angle * angle) * (root * (1.0 + 0.134145 * square))
    return values * half, slope


def forward_kernel(inputs, outputs, scratch):
    tokens_in, cotangent_in, starts, in_weight, out_weight, up_weight, down_weight, pack_in = inputs
    (
        in_full,
        out_full,
        up_full,
        down_full,
        grad_down_out,
        result_out,
        heads_out,
        mixed_out,
        inverse_out,
        middle_out,
        slope_out,
        memory_out,
        sums_out,
        gains_out,
    ) = outputs
    (
        wide,
        tall,
        pack,
        tokens,
        cotangent,
        gains,
        normed,
        heads,
        mask,
        mixed,
        mixed_low,
        inverse,
        middle,
        active,
        slope,
        grad_down,
        result,
        outgoing,
        incoming,
        memory,
        sums,
        send,
        recv,
        small_send,
        small_recv,
        state_send,
        state_recv,
        local,
        store,
    ) = scratch
    p = Place()
    length, width = tokens.shape
    loads = []
    for j in range(8):
        source = in_weight if j < 3 else (out_weight if j == 3 else up_weight)
        column = j if j < 3 else (0 if j == 3 else j - 4)
        loads.append((source.at[:, pl.ds(column * 1024, 1024)], wide.at[j, p.y, p.x, p.z, p.c]))
    for j in range(4):
        loads.append((down_weight.at[:, pl.ds(256 * j, 256)], tall.at[j, p.y, p.x, p.z, p.c]))
    loads.append((pack_in, pack.at[p.y, p.x, p.z, p.c]))
    loads.append((tokens_in, tokens))
    loads.append((cotangent_in, cotangent))
    loads = [pltpu.make_async_copy(a, b, local.at[i]) for i, (a, b) in enumerate(loads)]
    for i in (12, 0, 1, 2, 13, 3, 4, 5, 6, 7, 8, 9, 10, 11, 14):
        loads[i].start()
    stores = []

    def save(source, target):
        copy = pltpu.make_async_copy(source, target, store.at[len(stores)])
        copy.start()
        stores.append(copy)

    p.meet()
    small = SmallGather(p, pack, small_send, small_recv)
    chunks = [Gather(p, wide.at[j], send.at[j], recv.at[j]) for j in range(8)]
    chunks += [Gather(p, tall.at[j], send.at[8 + j], recv.at[8 + j]) for j in range(4)]

    def event(j, number):
        if not 0 <= j < 12:
            return
        if number == 0:
            loads[j].wait()
        chunks[j].step(number)
        if number == 4:
            if j < 8:
                target = in_full if j < 3 else (out_full if j == 3 else up_full)
                column = j if j < 3 else (0 if j == 3 else j - 4)
                save(wide.at[j], target.at[:, :, :, :, :, pl.ds(column * 1024, 1024)])
            else:
                save(tall.at[j - 8], down_full.at[:, :, :, :, :, pl.ds(256 * (j - 8), 256)])

    def weight(j, columns):
        return wide[j, :, :, :, :, :, columns].reshape(width, columns.size)

    images = Images(starts, p.seq, length)

    def first_norm():
        for y in range(2):
            for x in range(2):
                for k in range(2):
                    value = pack[y, x, 2 * k : 2 * k + 2].astype(FULL)
                    value = (value[0, 0] + value[0, 1]) + (value[1, 0] + value[1, 1])
                    at = 128 * ((y * 2 + x) * 2 + k)
                    gains[:, at : at + 128] = value
        save(gains, gains_out)
        loads[13].wait()

        @pl.loop(0, length // 128, unroll=2)
        def _(i):
            rows = tile(i, 128)
            value, _ = statistics(tokens[rows, :].astype(FULL))
            normed[rows, :] = (value * gains[0:1, :] + gains[1:2, :]).astype(LOW)

        mask[...] = same_mask(images, length, length, False)

    def project(j):
        @pl.loop(0, 2, unroll=2)
        def _(i):
            value = product(normed[...], weight(j, tile(i, 512)))
            if j < 2:
                value = jnp.where(value > 0, value + 1.0, jnp.exp(jnp.minimum(value, 0.0)))
            heads[j, :, tile(i, 512)] = value.astype(LOW)

    def update():
        tail = images.tail.astype(LOW)

        @pl.loop(0, 8, unroll=2)
        def _(i):
            lanes = tile(i, 128)
            key = heads[1, :, lanes] * tail
            square = down_rows(key, heads[2, :, lanes])
            outgoing[i, 0:HEAD] = pack_pair(square).astype(LOW)
            total = product(jnp.ones((16, length), LOW), key)
            outgoing[i, HEAD : HEAD + 16] = total.astype(LOW)

        save(heads, heads_out)
        for copy in state:
            copy.start()

    state = [
        remote(outgoing, incoming.at[d], state_send.at[d], state_recv.at[d], device)
        for d, device in enumerate(p.following)
    ]

    def enter():
        for copy in state:
            copy.wait_recv()

        @pl.loop(0, 8, unroll=2)
        def _(i):
            value = incoming[0, i].astype(FULL) + images.flag_before * incoming[1, i].astype(FULL)
            memory[i] = value[0:HEAD].astype(LOW)
            sums[i] = value[HEAD : HEAD + 8]

        save(memory, memory_out)
        save(sums, sums_out)

    def attend(begin, end):
        lanes_column = head_lanes(length)
        blocks = own_block()
        keep = images.keep.astype(LOW)
        half = length // 2
        identity = jnp.where(
            lax.broadcasted_iota(jnp.int32, (128, 128), 0)
            == lax.broadcasted_iota(jnp.int32, (128, 128), 1),
            1.0,
            0.0,
        )
        ones = jnp.ones((length, 128), LOW)

        @pl.loop(begin, end, unroll=2)
        def _(i):
            lanes = tile(i, 128)
            query, key, value = heads[0, :, lanes], heads[1, :, lanes], heads[2, :, lanes]
            wider = jnp.concatenate([value, ones], axis=1)
            parts = []
            for h in range(2):
                mine = lanes_column if h == 0 else ~lanes_column
                own = jnp.where(mine, query, jnp.zeros_like(query))
                upper = across(own[:half], key[:half]).astype(LOW) * mask[:half, :half]
                lower = across(own[half:], key).astype(LOW) * mask[half:, :]
                parts.append(
                    jnp.concatenate([product(upper, wider[:half]), product(lower, wider)], axis=0)
                )
            diagonal = (identity * sums[i, 0:1]).astype(LOW)
            right = jnp.concatenate(
                [unpack_pair(memory[i]), product(diagonal, blocks).astype(LOW)], axis=1
            )
            carried = product(query * keep, right)
            numerator = jnp.where(lanes_column, parts[0][:, :128], parts[1][:, :128])
            denominator = jnp.where(lanes_column, parts[0][:, 128:], parts[1][:, 128:])
            over = 1.0 / (denominator + carried[:, 128:])
            value = (numerator + carried[:, :128]) * over
            inverse[:, lanes] = over
            mixed[:, lanes] = value
            mixed_low[:, lanes] = value.astype(LOW)

    def join():
        save(mixed, mixed_out)
        save(inverse, inverse_out)

        @pl.loop(0, 2, unroll=2)
        def _(i):
            columns = tile(i, 512)
            middle[:, columns] = tokens[:, columns].astype(FULL) + product(
                mixed_low[...], weight(3, columns)
            )

        save(middle, middle_out)

    def second_norm():
        @pl.loop(0, length // 128, unroll=2)
        def _(i):
            rows = tile(i, 128)
            value, _ = statistics(middle[rows, :])
            normed[rows, :] = (value * gains[2:3, :] + gains[3:4, :]).astype(LOW)

    def raise_up(j):
        @pl.loop(0, 4, unroll=4)
        def _(i):
            value = product(normed[...], weight(4 + j, tile(i, 256)))
            columns = pl.ds(pl.multiple_of(j * 1024 + i * 256, 256), 256)
            value, steep = gelu_both(value)
            active[:, columns] = value.astype(LOW)
            slope[:, columns] = steep.astype(LOW)

        if j == 3:
            save(slope, slope_out)

    def down_gradient(begin, end):
        if begin == 0:
            loads[14].wait()

        @pl.loop(begin, end, unroll=4)
        def _(i):
            value = down_rows(active[:, tile(i, 512)], cotangent[...]).astype(LOW)
            y, x, z = i // 4, i // 2 % 2, i % 2 * 2
            for j in range(4):
                part = value[:, 256 * j : 256 * j + 256].reshape(2, 2, 128, 256)
                grad_down[j, y, x, pl.ds(z, 2)] = part

        if end == 8:
            save(grad_down, grad_down_out)

    def lower(j):
        columns = slice(256 * j, 256 * j + 256)

        @pl.loop(0, 2, unroll=2)
        def _(i):
            rows = tile(i, 256)
            value = product(active[rows, :], tall[j].reshape(4 * width, 256))
            result[rows, columns] = (middle[rows, columns] + value).astype(LOW)

        save(result.at[:, pl.ds(256 * j, 256)], result_out.at[:, pl.ds(256 * j, 256)])

    work = {
        5: [functools.partial(project, 0)],
        6: [functools.partial(project, 1)],
        7: [functools.partial(project, 2), update],
        8: [enter, functools.partial(attend, 0, 2), functools.partial(attend, 2, 4)],
        9: [
            functools.partial(attend, 4, 6),
            functools.partial(attend, 6, 8),
            join,
        ],
        10: [second_norm, functools.partial(raise_up, 0), functools.partial(raise_up, 1)],
        11: [functools.partial(raise_up, 2)],
        12: [
            functools.partial(raise_up, 3),
            functools.partial(down_gradient, 0, 4),
            functools.partial(down_gradient, 4, 8),
        ],
        13: [functools.partial(lower, 0)],
        14: [functools.partial(lower, 1)],
        15: [functools.partial(lower, 2)],
    }
    for tick in range(12 + 4):
        todo = work.get(tick, []) + [lambda: None] * 3
        if tick == 0:
            event(0, 0)
            loads[12].wait()
            small.step(0)
            event(1, 0)
            for number in range(1, 5):
                small.step(number)
            first_norm()
            continue
        if tick > 1:
            event(tick, 0)
        event(tick - 1, 1)
        todo[0]()
        event(tick - 2, 2)
        todo[1]()
        event(tick - 3, 3)
        event(tick - 4, 4)
        todo[2]()
    lower(3)
    small.finish()
    for copy in state:
        copy.wait_send()
    for chunk in chunks:
        chunk.finish()
    for copy in stores:
        copy.wait()


def forward_pass(tokens, cotangent, starts, in_weight, out_weight, up_weight, down_weight, pack):
    length, width = tokens.shape
    block = lambda rows, columns: jax.ShapeDtypeStruct((2, 2, 4, 2, rows, columns), LOW)
    shape = jax.ShapeDtypeStruct

    def body(*refs):
        forward_kernel(refs[:8], refs[8:22], refs[22:])

    return pl.pallas_call(
        body,
        out_shape=[
            block(32, 3072),
            block(32, 1024),
            block(32, 4096),
            block(128, 1024),
            shape((4, 2, 2, 4, 2, 128, 256), LOW),
            shape((length, width), LOW),
            shape((3, length, width), LOW),
            shape((length, width), FULL),
            shape((length, width), FULL),
            shape((length, width), FULL),
            shape((length, 4 * width), LOW),
            shape((8, HEAD, 128), LOW),
            shape((8, 8, 128), FULL),
            shape((16, width), FULL),
        ],
        in_specs=[
            pl.BlockSpec(memory_space=pltpu.SMEM if i == 2 else pl.ANY) for i in range(8)
        ],
        out_specs=[pl.BlockSpec(memory_space=pl.ANY)] * 14,
        scratch_shapes=[
            pltpu.VMEM((8, 2, 2, 4, 2, 32, 1024), LOW),
            pltpu.VMEM((4, 2, 2, 4, 2, 128, 256), LOW),
            pltpu.VMEM((2, 2, 4, 2, 16, 128), LOW),
            pltpu.VMEM((length, width), LOW),
            pltpu.VMEM((length, width), LOW),
            pltpu.VMEM((16, width), FULL),
            pltpu.VMEM((length, width), LOW),
            pltpu.VMEM((3, length, width), LOW),
            pltpu.VMEM((length, length), LOW),
            pltpu.VMEM((length, width), FULL),
            pltpu.VMEM((length, width), LOW),
            pltpu.VMEM((length, width), FULL),
            pltpu.VMEM((length, width), FULL),
            pltpu.VMEM((length, 4 * width), LOW),
            pltpu.VMEM((length, 4 * width), LOW),
            pltpu.VMEM((4, 2, 2, 4, 2, 128, 256), LOW),
            pltpu.VMEM((length, width), LOW),
            pltpu.VMEM((8, HEAD + 16, 128), LOW),
            pltpu.VMEM((2, 8, HEAD + 16, 128), LOW),
            pltpu.VMEM((8, HEAD, 128), LOW),
            pltpu.VMEM((8, 8, 128), FULL),
            pltpu.SemaphoreType.DMA((12, 11)),
            pltpu.SemaphoreType.DMA((12, 11)),
            pltpu.SemaphoreType.DMA((9,)),
            pltpu.SemaphoreType.DMA((9,)),
            pltpu.SemaphoreType.DMA((2,)),
            pltpu.SemaphoreType.DMA((2,)),
            pltpu.SemaphoreType.DMA((15,)),
            pltpu.SemaphoreType.DMA((26,)),
        ],
        compiler_params=pltpu.CompilerParams(
            collective_id=0, has_side_effects=True, vmem_limit_bytes=62 << 20
        ),
        name="forward_pass",
    )(tokens, cotangent, starts, in_weight, out_weight, up_weight, down_weight, pack)


def scatter_buffers(count, rows, columns):
    half = rows // 2
    shapes = [
        (2, 2, 4, rows, columns),
        (2, 2, 4, rows, columns),
        (2, 4, half, columns),
        (2, 4, half, columns),
        (4, half, columns),
        (4, half, columns),
        (3, rows, columns),
    ]
    return [pltpu.VMEM((count, *shape), LOW) for shape in shapes]


class Sum:
    def __init__(self, place, stages, landed, send, recv):
        p = place
        devices = [p.sibling, p.over_x, p.over_y, *p.along_z]
        self.stages, self.landed = stages, landed
        self.copies = [
            remote(stages.at[min(i, 3)], landed.at[i], send.at[i], recv.at[i], device)
            for i, device in enumerate(devices)
        ]

    def step(self, number):
        stages, landed = self.stages, self.landed
        if 1 <= number <= 3:
            self.copies[number - 1].wait_recv()
            stages[number] = stages[number - 1] + landed[number - 1]
        if number < 3:
            self.copies[number].start()
        elif number == 3:
            for i in (3, 4, 5):
                self.copies[i].start()

    def result(self):
        for i in (3, 4, 5):
            self.copies[i].wait_recv()
        return (self.stages[3] + self.landed[3]) + (self.landed[4] + self.landed[5])

    def finish(self):
        for copy in self.copies:
            copy.wait_send()


def backward_kernel(inputs, outputs, tall, wide, scratch):
    (
        tokens_in,
        cotangent_in,
        starts,
        in_full,
        out_full,
        up_full,
        down_full,
        grad_down_in,
        heads_in,
        mixed_in,
        inverse_in,
        middle_in,
        slope_in,
        memory_in,
        sums_in,
        gains_in,
    ) = inputs
    (
        cotangent,
        normed,
        slab,
        broad,
        grad_middle,
        inner,
        mixed,
        inverse,
        memory,
        sums,
        gains,
        mask,
        mask_back,
        parts,
        done_in,
        done_out,
        done_up,
        done_down,
        stages,
        landed,
        outgoing,
        incoming,
        update,
        key_update,
        send,
        recv,
        sum_send,
        sum_recv,
        state_send,
        state_recv,
        local,
        stream,
        store,
    ) = scratch
    p = Place()
    length, width = cotangent.shape

    pairs = [
        (cotangent_in, cotangent),
        (slope_in, broad),
        (middle_in, grad_middle),
        (gains_in, gains),
        (memory_in, memory),
        (sums_in, sums),
        (mixed_in, mixed),
        (inverse_in, inverse),
        (tokens_in, cotangent),
    ]
    pairs += [(heads_in.at[k], broad.at[:, pl.ds(1024 * k, 1024)]) for k in range(3)]
    loads = [pltpu.make_async_copy(a, b, local.at[i]) for i, (a, b) in enumerate(pairs)]
    slabs = [down_full.at[pl.ds(1024 * j, 1024), :] for j in range(4)]
    slabs += [up_full.at[:, pl.ds(1024 * j, 1024)] for j in range(4)]
    slabs += [out_full]
    slabs += [in_full.at[:, pl.ds(1024 * j, 1024)] for j in range(3)]
    slabs = [
        pltpu.make_async_copy(source, slab.at[i % 2], stream.at[i]) for i, source in enumerate(slabs)
    ]
    order = [8, 9, 10, 11, 4, 5, 6, 7, 3, 0, 1, 2]
    room = {4: 0, 5: 1, 6: 2, 7: 0, 3: 1, 0: 2, 1: 0, 2: 1}
    chunks = []
    for j in range(12):
        if j < 8:
            first, *others = [ref.at[j] for ref in wide]
            buffers = [first, first, *others]
            own = parts.at[room[j]]
        else:
            buffers = [ref.at[j - 8] for ref in tall]
            own = grad_down_in.at[j - 8]
        chunks.append(Scatter(p, own, *buffers, send.at[j], recv.at[j], j >= 8))

    p.meet()
    chunks[8].step(0)
    for i in range(4):
        loads[i].start()
    slabs[0].start()
    slabs[1].start()
    for i in range(4, 8):
        loads[i].start()
    stores = []

    def save(source, target):
        copy = pltpu.make_async_copy(source, target, store.at[len(stores)])
        copy.start()
        stores.append(copy)

    def event(position, number):
        if not 0 <= position < 12:
            return
        j = order[position]
        if number < 4:
            if (j, number) != (8, 0):
                chunks[j].step(number)
            return
        if j < 8:
            target, k = (done_in, j) if j < 3 else ((done_out, 0) if j == 3 else (done_up, j - 4))
            size = 1024
        else:
            target, k, size = done_down, j - 8, 256
        where = outputs[0 if j < 3 else 1 if j == 3 else 2 if j < 8 else 3]
        target[:, size * k : size * k + size] = chunks[j].result()
        save(target.at[:, pl.ds(size * k, size)], where.at[:, pl.ds(size * k, size)])

    images = Images(starts, p.seq, length)

    def second_norm():
        loads[2].wait()
        loads[3].wait()

        @pl.loop(0, length // 128, unroll=2)
        def _(i):
            rows = tile(i, 128)
            value, _ = statistics(grad_middle[rows, :])
            normed[rows, :] = (value * gains[2:3, :] + gains[3:4, :]).astype(LOW)

    def active_gradient(j):
        if j == 0:
            loads[0].wait()
            loads[1].wait()
        slabs[j].wait()

        @pl.loop(0, 4, unroll=4)
        def _(i):
            columns = pl.ds(pl.multiple_of(1024 * j + 256 * i, 256), 256)
            value = across(cotangent[...], slab[j % 2, tile(i, 256), :])
            broad[:, columns] = (value * broad[:, columns].astype(FULL)).astype(LOW)

        slabs[j + 2].start()

    def weight_gradient(j, left, right):
        at = room[j]

        @pl.loop(0, 4, unroll=4)
        def _(i):
            value = down_rows(left(tile(i, 256)), right()).astype(LOW)
            parts[at, i // 2, i % 2] = value.reshape(4, 2, 32, 1024)

    def up_gradient(j):
        if j == 3:
            chunks[4].release()
        weight_gradient(
            4 + j,
            lambda columns: normed[:, columns],
            lambda: broad[:, 1024 * j : 1024 * j + 1024],
        )
        if j == 3:
            for k in range(9, 12):
                loads[k].start()

    def inner_gradient(first, j):
        slabs[first + j].wait()

        @pl.loop(0, 4, unroll=4)
        def _(i):
            columns = tile(i, 256)
            value = across(
                broad[:, 1024 * j : 1024 * j + 1024], slab[(first + j) % 2, columns, :]
            )
            if j > 0:
                value = value + inner[:, columns]
            inner[:, columns] = value

        if first + j + 2 < 12:
            slabs[first + j + 2].start()

    def norm_gradient(rows, values, gain):
        unit, scale = statistics(values)
        given = inner[rows, :]
        scaled = given * gain
        one = jnp.mean(scaled, axis=-1, keepdims=True)
        two = jnp.mean(scaled * unit, axis=-1, keepdims=True)
        return scale * (scaled - one - unit * two), given * unit, given

    def fold(values):
        return jnp.sum(values, axis=0, keepdims=True)

    def middle_gradient():
        stages[0] = jnp.zeros((8, width), FULL)

        @pl.loop(0, length // 128, unroll=2)
        def _(i):
            rows = tile(i, 128)
            value, gain, shift = norm_gradient(rows, grad_middle[rows, :], gains[2:3, :])
            stages[0, 2:3, :] += fold(gain)
            stages[0, 3:4, :] += fold(shift)
            value = value + cotangent[rows, :].astype(FULL)
            grad_middle[rows, :] = value
            cotangent[rows, :] = value.astype(LOW)

    def output_gradient():
        loads[6].wait()
        chunks[5].release()
        weight_gradient(
            3, lambda columns: mixed[:, columns].astype(LOW), lambda: cotangent[...]
        )
        loads[8].start()

    def mixed_gradient():
        slabs[8].wait()

        @pl.loop(0, 4, unroll=4)
        def _(i):
            columns = tile(i, 256)
            inner[:, columns] = across(cotangent[...], slab[0, columns, :])

        slabs[10].start()

    state = [
        remote(outgoing, incoming.at[d], state_send.at[d], state_recv.at[d], device)
        for d, device in enumerate(p.preceding)
    ]

    def numerator_gradient():
        for i in (4, 5, 7, 9, 10, 11):
            loads[i].wait()
        blocks = own_block()
        doubled = jnp.concatenate([blocks, blocks], axis=0)

        @pl.loop(0, 8, unroll=2)
        def _(i):
            lanes = tile(i, 128)
            given, over = inner[:, lanes], inverse[:, lanes]
            numerator = (given * over).astype(LOW)
            each = given * mixed[:, lanes]
            high = each.astype(LOW)
            rest = (each - high.astype(FULL)).astype(LOW)
            slant = product(jnp.concatenate([high, rest], axis=1), doubled) * over * -1.0
            mixed[:, lanes] = slant
            broad[:, pl.ds(pl.multiple_of(3072 + 128 * i, 128), 128)] = numerator
            kept = broad[:, lanes].astype(FULL) * images.keep
            square = down_rows(kept.astype(LOW), numerator)
            outgoing[i, 0:HEAD] = pack_pair(square).astype(LOW)
            total = fold(kept * slant)
            outgoing[i, HEAD : HEAD + 16] = jnp.broadcast_to(total, (16, 128)).astype(LOW)

        for copy in state:
            copy.start()
        mask[...] = same_mask(images, length, length, False)
        mask_back[...] = same_mask(images, length, length, True)

    def enter():
        for copy in state:
            copy.wait_recv()
        flag = jnp.where(p.seq == 7, 0.0, images.flag_after)

        @pl.loop(0, 8, unroll=2)
        def _(i):
            value = incoming[0, i].astype(FULL) + flag * incoming[1, i].astype(FULL)
            update[i] = value[0:HEAD].astype(LOW)
            key_update[i] = value[HEAD : HEAD + 8]

    def attend(begin, end):
        if begin == 0:
            enter()
        if end == 8:
            first_norm()
        first = head_lanes(length)
        lane = lax.broadcasted_iota(jnp.int32, (length, 128), 1)
        ones = jnp.ones((length, 128), LOW)
        zero = jnp.zeros((length, 128), LOW)
        half = length // 2

        @pl.loop(begin, end)
        def _(i):
            at = [pl.ds(pl.multiple_of(1024 * k + 128 * i, 128), 128) for k in range(4)]
            query, key, value, numerator = [broad[:, lanes] for lanes in at]
            slant = mixed[:, at[0]]
            high = slant.astype(LOW)
            rest = (slant - high.astype(FULL)).astype(LOW)
            right = jnp.concatenate([value, ones], axis=1)
            grads = []
            for h in range(2):
                mine = first if h == 0 else ~first
                own_query = jnp.where(mine, query, zero)
                left = jnp.concatenate(
                    [
                        jnp.where(mine, numerator, zero),
                        jnp.where(
                            lane == HEAD * h, high, jnp.where(lane == HEAD * h + 1, rest, zero)
                        ),
                    ],
                    axis=1,
                )
                upper = across(left[:half], right[:half]).astype(LOW) * mask[:half, :half]
                lower = across(left[half:], right).astype(LOW) * mask[half:, :]
                for_query = jnp.concatenate([product(upper, key[:half]), product(lower, key)], axis=0)
                upper = across(right[:half], left).astype(LOW) * mask_back[:half, :]
                lower = across(right[half:], left[half:]).astype(LOW) * mask_back[half:, half:]
                for_key = jnp.concatenate(
                    [product(upper, query), product(lower, query[half:])], axis=0
                )
                upper = across(key[:half], own_query).astype(LOW) * mask_back[:half, :]
                lower = across(key[half:], own_query[half:]).astype(LOW) * mask_back[half:, half:]
                for_value = jnp.concatenate(
                    [product(upper, numerator), product(lower, numerator[half:])], axis=0
                )
                grads.append((for_query, for_key, for_value))
            for_query, for_key, for_value = [
                jnp.where(first, one, two) for one, two in zip(*grads, strict=True)
            ]
            keep, tail = images.keep, images.tail
            for_query = for_query + keep * (
                across(numerator, unpack_pair(memory[i])) + slant * sums[i, 0:1]
            )
            square = unpack_pair(update[i])
            for_key = for_key + tail * (across(value, square) + key_update[i, 0:1])
            for_value = for_value + product(key * tail.astype(LOW), square)
            broad[:, at[0]] = (for_query * jnp.minimum(query.astype(FULL), 1.0)).astype(LOW)
            broad[:, at[1]] = (for_key * jnp.minimum(key.astype(FULL), 1.0)).astype(LOW)
            broad[:, at[2]] = for_value.astype(LOW)

    def first_norm():
        loads[8].wait()

        @pl.loop(0, length // 128, unroll=2)
        def _(i):
            rows = tile(i, 128)
            value, _ = statistics(cotangent[rows, :].astype(FULL))
            normed[rows, :] = (value * gains[0:1, :] + gains[1:2, :]).astype(LOW)

    def in_gradient(j):
        chunks[(6, 7, 3)[j]].release()
        weight_gradient(
            j,
            lambda columns: normed[:, columns],
            lambda: broad[:, 1024 * j : 1024 * j + 1024],
        )

    total = Sum(p, stages, landed, sum_send, sum_recv)

    def token_gradient():
        @pl.loop(0, length // 128, unroll=2)
        def _(i):
            rows = tile(i, 128)
            value, gain, shift = norm_gradient(rows, cotangent[rows, :].astype(FULL), gains[0:1, :])
            stages[0, 0:1, :] += fold(gain)
            stages[0, 1:2, :] += fold(shift)
            grad_middle[rows, :] += value

        save(grad_middle, outputs[4])
        total.step(0)

    do = functools.partial
    work = {
        0: [second_norm],
        1: [do(active_gradient, 0), do(active_gradient, 1), do(active_gradient, 2)],
        2: [do(active_gradient, 3), do(up_gradient, 0), do(up_gradient, 1)],
        3: [do(up_gradient, 2), do(inner_gradient, 4, 0), do(inner_gradient, 4, 1)],
        4: [do(inner_gradient, 4, 2), do(inner_gradient, 4, 3), middle_gradient],
        5: [do(up_gradient, 3), mixed_gradient],
        6: [output_gradient, numerator_gradient],
        7: [do(attend, 0, 2), do(attend, 2, 4), do(attend, 4, 5)],
        8: [do(attend, 5, 7), do(attend, 7, 8), do(in_gradient, 0)],
        9: [do(in_gradient, 1), do(in_gradient, 2), do(inner_gradient, 9, 0)],
        10: [
            do(inner_gradient, 9, 1),
            do(inner_gradient, 9, 2),
            token_gradient,
        ],
        11: [do(total.step, 1), do(total.step, 2), do(total.step, 3)],
    }
    for tick in range(12 + 6):
        todo = work.get(tick, []) + [lambda: None] * 3
        event(tick - 0, 0)
        event(tick - 1, 1)
        todo[0]()
        event(tick - 2, 2)
        todo[1]()
        event(tick - 3, 3)
        event(tick - 6, 4)
        todo[2]()
    total_value = total.result()
    landed[0] = total_value
    group = (p.dp * 8 + p.seq) // 4
    mine = landed[0, :, tile(group, 128)]
    mine = pltpu.roll(mine, (128 - 32 * (p.seq % 4)) % 128, 1)
    outputs[5][...] = mine
    total.finish()
    for copy in state:
        copy.wait_send()
    for chunk in chunks:
        chunk.finish()
    for copy in stores:
        copy.wait()


def backward_pass(*inputs):
    length, width = inputs[0].shape
    shape = jax.ShapeDtypeStruct
    vmem = pltpu.VMEM
    tall = scatter_buffers(4, 128, 256)
    wide = scatter_buffers(8, 32, 1024)[1:]

    def body(*refs):
        backward_kernel(refs[:16], refs[16:22], refs[22:29], refs[29:35], refs[35:])

    return pl.pallas_call(
        body,
        out_shape=[
            shape((32, 3072), FULL),
            shape((32, 1024), FULL),
            shape((32, 4096), FULL),
            shape((128, 1024), FULL),
            shape((length, width), FULL),
            shape((8, 128), FULL),
        ],
        in_specs=[
            pl.BlockSpec(memory_space=pltpu.SMEM if i == 2 else pl.ANY) for i in range(16)
        ],
        out_specs=[pl.BlockSpec(memory_space=pl.ANY)] * 5
        + [pl.BlockSpec(memory_space=pltpu.VMEM)],
        scratch_shapes=[
            *tall,
            *wide,
            vmem((length, width), LOW),
            vmem((length, width), LOW),
            vmem((2, width, width), LOW),
            vmem((length, 4 * width), LOW),
            vmem((length, width), FULL),
            vmem((length, width), FULL),
            vmem((length, width), FULL),
            vmem((length, width), FULL),
            vmem((8, HEAD, 128), LOW),
            vmem((8, 8, 128), FULL),
            vmem((16, width), FULL),
            vmem((length, length), LOW),
            vmem((length, length), LOW),
            vmem((3, 2, 2, 4, 2, 32, 1024), LOW),
            vmem((32, 3072), FULL),
            vmem((32, 1024), FULL),
            vmem((32, 4096), FULL),
            vmem((128, 1024), FULL),
            vmem((4, 8, width), FULL),
            vmem((6, 8, width), FULL),
            vmem((8, HEAD + 16, 128), LOW),
            vmem((2, 8, HEAD + 16, 128), LOW),
            vmem((8, HEAD, 128), LOW),
            vmem((8, 8, 128), FULL),
            pltpu.SemaphoreType.DMA((12, 9)),
            pltpu.SemaphoreType.DMA((12, 8)),
            pltpu.SemaphoreType.DMA((6,)),
            pltpu.SemaphoreType.DMA((6,)),
            pltpu.SemaphoreType.DMA((2,)),
            pltpu.SemaphoreType.DMA((2,)),
            pltpu.SemaphoreType.DMA((12,)),
            pltpu.SemaphoreType.DMA((12,)),
            pltpu.SemaphoreType.DMA((13,)),
        ],
        compiler_params=pltpu.CompilerParams(
            collective_id=1, has_side_effects=True, vmem_limit_bytes=62 << 20
        ),
        name="backward_pass",
    )(*inputs)


def hand_over(*values):
    large = len(values) - 1

    def body(*refs):
        inputs, vectors, outputs = refs[:large], refs[large], refs[large + 1 : 2 * large + 1]
        small, held, sems = refs[2 * large + 1 : 2 * large + 5], refs[2 * large + 5 : -1], refs[-1]
        copies = [
            (
                pltpu.make_async_copy(inputs[i], held[i], sems.at[0, i]),
                pltpu.make_async_copy(held[i], outputs[i], sems.at[1, i]),
            )
            for i in range(large)
        ]
        for load, _ in copies:
            load.start()
        for k in range(4):
            small[k][...] = vectors[k : k + 1, 0:32]
        for load, store in copies:
            load.wait()
            store.start()
        for _, store in copies:
            store.wait()

    anywhere, near = pl.BlockSpec(memory_space=pl.ANY), pl.BlockSpec(memory_space=pltpu.VMEM)
    return pl.pallas_call(
        body,
        out_shape=[jax.ShapeDtypeStruct(value.shape, value.dtype) for value in values[:large]]
        + [jax.ShapeDtypeStruct((1, 32), FULL)] * 4,
        in_specs=[anywhere] * large + [near],
        out_specs=[anywhere] * large + [near] * 4,
        scratch_shapes=[pltpu.VMEM(value.shape, value.dtype) for value in values[:large]]
        + [pltpu.SemaphoreType.DMA((2, large))],
        name="hand_over",
    )(*values)


def on_device(
    tokens,
    starts,
    query_key_value_weight,
    attention_output_weight,
    up_projection_weight,
    down_projection_weight,
    first_gain,
    first_shift,
    second_gain,
    second_shift,
    cotangent,
):
    mine = lax.axis_index("dp") * 8 + lax.axis_index("seq")
    pack = jnp.stack([first_gain, first_shift, second_gain, second_shift]).astype(FULL)
    pack = jnp.roll(jnp.pad(pack, ((0, 12), (0, 96))), 32 * (mine % 4), axis=1).astype(LOW)
    in_full, out_full, up_full, down_full, grad_down, result, *saved = forward_pass(
        tokens[0],
        cotangent[0],
        starts,
        query_key_value_weight,
        attention_output_weight,
        up_projection_weight,
        down_projection_weight,
        pack,
    )
    grads = backward_pass(
        tokens[0],
        cotangent[0],
        starts,
        in_full.reshape(1024, 3072),
        out_full.reshape(1024, 1024),
        up_full.reshape(1024, 4096),
        down_full.reshape(4096, 1024),
        grad_down,
        *saved,
    )
    result, *grads = hand_over(result, *grads)
    vectors = [grad.reshape(32) for grad in grads[5:]]
    return (result[None], grads[4][None], *grads[:4], *vectors)


def solution(mesh):

    fast = dict(mesh.shape) == {"dp": 4, "seq": 8}
    return jax.shard_map(
        on_device if fast else on_device_general,
        mesh=mesh,
        in_specs=(
            P("dp", "seq", None),
            P("dp", None),
            P(("dp", "seq"), None),
            P(("dp", "seq"), None),
            P(("dp", "seq"), None),
            P(("dp", "seq"), None),
            P(("dp", "seq")),
            P(("dp", "seq")),
            P(("dp", "seq")),
            P(("dp", "seq")),
            P("dp", "seq", None),
        ),
        out_specs=(
            P("dp", "seq", None),
            P("dp", "seq", None),
            P(("dp", "seq"), None),
            P(("dp", "seq"), None),
            P(("dp", "seq"), None),
            P(("dp", "seq"), None),
            P(("dp", "seq")),
            P(("dp", "seq")),
            P(("dp", "seq")),
            P(("dp", "seq")),
        ),
        check_vma=False,
    )
```

```python
import functools

import jax
import jax.numpy as jnp
from jax import lax
from jax.experimental import pallas as pl
from jax.experimental.pallas import tpu as pltpu
from jax.sharding import PartitionSpec as P

HEAD = 64
BLOCK = 512


def prefix(value, axis, combine, identity, reverse):
    size, mine = (lax.axis_size(axis), lax.axis_index(axis))
    everything = jax.tree.map(
        lambda part, kind: lax.all_gather(part.astype(kind), axis),
        value,
        jax.tree.map(lambda a: jnp.bfloat16 if a.dtype == jnp.float32 else a.dtype, value),
    )
    start = jax.tree.map(
        lambda part, zero: jnp.broadcast_to(jnp.asarray(zero, part.dtype), part.shape),
        value,
        identity,
    )

    def lap(k, before):
        at = size - 1 - k if reverse else k
        reached = at > mine if reverse else at < mine
        new = combine(
            before, jax.tree.map(lambda part, own: part[at].astype(own.dtype), everything, value)
        )
        return jax.tree.map(lambda a, b: jnp.where(reached, a, b), new, before)

    return lax.fori_loop(0, size, lap, start)


def layer_norm(values, norm_gain, norm_shift):
    average = jnp.mean(values, axis=-1, keepdims=True)
    centred = values - average
    spread = jnp.mean(centred * centred, axis=-1, keepdims=True)
    return centred * lax.rsqrt(spread + 1e-05) * norm_gain + norm_shift


def feature(values):
    return jax.nn.elu(values) + 1.0


def combine(former, latter):
    return (
        former[0] * latter[0],
        latter[0] * former[1] + latter[1],
        latter[0] * former[2] + latter[2],
    )


def rows_product(factor_one, factor_two):
    return lax.dot_general(
        factor_one, factor_two, (((0,), (0,)), ((), ())), preferred_element_type=jnp.float32
    )


def cols_product(factor_one, factor_two):
    return lax.dot_general(
        factor_one, factor_two, (((1,), (1,)), ((), ())), preferred_element_type=jnp.float32
    )


def on_device_general(
    tokens,
    starts,
    query_key_value_weight,
    attention_output_weight,
    up_projection_weight,
    down_projection_weight,
    first_gain,
    first_shift,
    second_gain,
    second_shift,
    cotangent,
):
    local_len = tokens.shape[1]
    model_width = tokens.shape[2]
    head_count = model_width // HEAD
    block_count = local_len // BLOCK
    block_shape = (block_count, BLOCK, head_count, HEAD)
    zero_low = jnp.zeros((), jnp.bfloat16)
    input_tokens = tokens[0].astype(jnp.float32)
    first_pos = lax.axis_index("seq") * local_len
    positions = first_pos + jnp.arange(local_len, dtype=jnp.int32)
    pack_starts = starts[0]
    image_ids = jnp.sum((pack_starts[None, :] <= positions[:, None]).astype(jnp.int32), axis=1) - 1
    before_id = jnp.sum((pack_starts <= first_pos - 1).astype(jnp.int32)) - 1
    causal = jnp.arange(BLOCK)[:, None] >= jnp.arange(BLOCK)[None, :]
    attn_set = (
        lax.all_gather(query_key_value_weight, ("dp", "seq"), axis=0, tiled=True),
        lax.all_gather(attention_output_weight, ("dp", "seq"), axis=0, tiled=True),
        lax.all_gather(first_gain, ("dp", "seq"), axis=0, tiled=True),
        lax.all_gather(first_shift, ("dp", "seq"), axis=0, tiled=True),
    )
    in_full = attn_set[0]
    out_full = attn_set[1]
    gain_one = attn_set[2].astype(jnp.float32)
    shift_one = attn_set[3].astype(jnp.float32)
    first_normed_tokens = layer_norm(input_tokens, gain_one, shift_one)
    normed_low = first_normed_tokens.astype(jnp.bfloat16)
    projected_tokens = jnp.dot(normed_low, in_full, preferred_element_type=jnp.float32)
    queries = projected_tokens[:, :model_width]
    keys_raw = projected_tokens[:, model_width : 2 * model_width]
    values_raw = projected_tokens[:, 2 * model_width :]
    feat_query = feature(queries).astype(jnp.bfloat16).reshape(block_shape)
    feat_key = feature(keys_raw).astype(jnp.bfloat16).reshape(block_shape)
    value_low = values_raw.astype(jnp.bfloat16).reshape(block_shape)
    block_number = 0
    last_id = image_ids[-1]
    tail_mask = image_ids == last_id
    tail_key = jnp.where(tail_mask[:, None, None], feat_key[block_number], zero_low)
    keep_list = [image_ids == before_id]
    tail_list = [tail_mask]
    flag_list = [(last_id == before_id).astype(jnp.float32)]
    same_list = [causal & (image_ids[:, None] == image_ids[None, :])]
    update_list = [
        jnp.einsum(
            "jhe,jhf->hef", tail_key, value_low[block_number], preferred_element_type=jnp.float32
        )
    ]
    total_list = [jnp.sum(tail_key.astype(jnp.float32), axis=0)]
    identity = (
        jnp.ones((), jnp.float32),
        jnp.zeros((head_count, HEAD, HEAD), jnp.float32),
        jnp.zeros((head_count, HEAD), jnp.float32),
    )
    combined = identity
    block_number = 0
    combined = combine(
        combined, (flag_list[block_number], update_list[block_number], total_list[block_number])
    )
    entering = prefix(combined, "seq", combine, identity, False)
    memory = entering[1]
    key_sum = entering[2]
    block_number = 0
    query_block = feat_query[block_number]
    keep_float = keep_list[block_number].astype(jnp.float32)
    memory_low = memory.astype(jnp.bfloat16)
    raw_scores = jnp.einsum(
        "the,jhe->htj", query_block, feat_key[block_number], preferred_element_type=jnp.float32
    )
    masked = jnp.where(same_list[block_number][None], raw_scores, 0.0)
    scores_low = masked.astype(jnp.bfloat16)
    carried = (
        jnp.einsum("the,hef->thf", query_block, memory_low, preferred_element_type=jnp.float32)
        * keep_float[:, None, None]
    )
    numerator = (
        jnp.einsum(
            "htj,jhf->thf", scores_low, value_low[block_number], preferred_element_type=jnp.float32
        )
        + carried
    )
    denominator = jnp.transpose(jnp.sum(masked, axis=2)) + keep_float[:, None] * jnp.sum(
        query_block.astype(jnp.float32) * key_sum[None], axis=2
    )
    memory_list = [memory_low]
    keysum_list = [key_sum]
    numer_list = [numerator]
    denom_list = [denominator]
    ratio_list = numerator / denominator[:, :, None]
    mixed_low = ratio_list.reshape(local_len, model_width).astype(jnp.bfloat16)
    middle_tokens = input_tokens + jnp.dot(mixed_low, out_full, preferred_element_type=jnp.float32)
    mlp_set = (
        lax.all_gather(up_projection_weight, ("dp", "seq"), axis=0, tiled=True),
        lax.all_gather(down_projection_weight, ("dp", "seq"), axis=0, tiled=True),
        lax.all_gather(second_gain, ("dp", "seq"), axis=0, tiled=True),
        lax.all_gather(second_shift, ("dp", "seq"), axis=0, tiled=True),
    )
    up_full = mlp_set[0]
    down_full = mlp_set[1]
    gain_two = mlp_set[2].astype(jnp.float32)
    shift_two = mlp_set[3].astype(jnp.float32)
    normed_two_low = layer_norm(middle_tokens, gain_two, shift_two).astype(jnp.bfloat16)
    upper_hidden = jnp.dot(normed_two_low, up_full, preferred_element_type=jnp.float32)
    active_low = jax.nn.gelu(upper_hidden).astype(jnp.bfloat16)
    result = middle_tokens + jnp.dot(active_low, down_full, preferred_element_type=jnp.float32)
    result_tokens = result.astype(jnp.bfloat16).reshape(1, local_len, model_width)
    grad_out = cotangent[0].astype(jnp.float32)
    mlp_again = (
        lax.all_gather(up_projection_weight, ("dp", "seq"), axis=0, tiled=True),
        lax.all_gather(down_projection_weight, ("dp", "seq"), axis=0, tiled=True),
        lax.all_gather(second_gain, ("dp", "seq"), axis=0, tiled=True),
        lax.all_gather(second_shift, ("dp", "seq"), axis=0, tiled=True),
    )
    up_back = mlp_again[0]
    down_back = mlp_again[1]
    grad_out_low = cotangent[0]
    grad_down = rows_product(active_low, grad_out_low)
    d_active = cols_product(grad_out_low, down_back)
    gelu_value, gelu_back = jax.vjp(jax.nn.gelu, upper_hidden)
    g_upper = gelu_back(d_active)[0].astype(jnp.bfloat16)
    grad_up = rows_product(normed_two_low, g_upper)
    d_normed_two = cols_product(g_upper, up_back)
    norm_value, norm_back = jax.vjp(layer_norm, middle_tokens, gain_two, shift_two)
    middle_part, grad_gain_two, grad_shift_two = norm_back(d_normed_two)
    g_middle = grad_out + middle_part
    attn_again = (
        lax.all_gather(query_key_value_weight, ("dp", "seq"), axis=0, tiled=True),
        lax.all_gather(attention_output_weight, ("dp", "seq"), axis=0, tiled=True),
        lax.all_gather(first_gain, ("dp", "seq"), axis=0, tiled=True),
        lax.all_gather(first_shift, ("dp", "seq"), axis=0, tiled=True),
    )
    in_back = attn_again[0]
    out_back = attn_again[1]
    g_middle_low = g_middle.astype(jnp.bfloat16)
    grad_out_weight = rows_product(mixed_low, g_middle_low)
    d_mixed = cols_product(g_middle_low, out_back).reshape(block_shape)
    block_number = 0
    query_block = feat_query[block_number]
    denominator = denom_list[block_number]
    g_numerator = (d_mixed[block_number] / denominator[:, :, None]).astype(jnp.bfloat16)
    g_denominator = -jnp.sum(d_mixed[block_number] * numer_list[block_number], axis=2) / (
        denominator * denominator
    )
    kept_query = jnp.where(keep_list[block_number][:, None, None], query_block, zero_low)
    gnum_list = [g_numerator]
    gden_list = [g_denominator]
    local_list = [
        jnp.einsum("the,thf->hef", kept_query, g_numerator, preferred_element_type=jnp.float32)
    ]
    localkey_list = [jnp.sum(kept_query.astype(jnp.float32) * g_denominator[:, :, None], axis=0)]
    combined = identity
    for block_number in reversed(range(block_count)):
        combined = combine(
            combined,
            (flag_list[block_number], local_list[block_number], localkey_list[block_number]),
        )
    leaving = prefix(combined, "seq", combine, identity, True)
    g_memory = leaving[1]
    g_key_sum = leaving[2]
    gq_list = []
    gk_list = []
    gv_list = []
    for block_number in reversed(range(block_count)):
        query_block = feat_query[block_number]
        key_block = feat_key[block_number]
        value_block = value_low[block_number]
        keep_float = keep_list[block_number].astype(jnp.float32)
        tail_float = tail_list[block_number].astype(jnp.float32)
        g_numerator = gnum_list[block_number]
        g_denominator = gden_list[block_number]
        g_update = g_memory.astype(jnp.bfloat16)
        raw_scores = jnp.einsum(
            "the,jhe->htj", query_block, key_block, preferred_element_type=jnp.float32
        )
        scores_low = jnp.where(same_list[block_number][None], raw_scores, 0.0).astype(jnp.bfloat16)
        g_scores = (
            jnp.einsum("thf,jhf->htj", g_numerator, value_block, preferred_element_type=jnp.float32)
            + jnp.transpose(g_denominator)[:, :, None]
        )
        g_scores_low = jnp.where(
            same_list[block_number][None], g_scores.astype(jnp.bfloat16), zero_low
        )
        query_grad = jnp.einsum(
            "htj,jhe->the", g_scores_low, key_block, preferred_element_type=jnp.float32
        )
        query_grad = query_grad + keep_float[:, None, None] * (
            jnp.einsum(
                "thf,hef->the",
                g_numerator,
                memory_list[block_number],
                preferred_element_type=jnp.float32,
            )
            + g_denominator[:, :, None] * keysum_list[block_number][None]
        )
        key_grad = jnp.einsum(
            "htj,the->jhe", g_scores_low, query_block, preferred_element_type=jnp.float32
        )
        key_grad = key_grad + tail_float[:, None, None] * (
            jnp.einsum("jhf,hef->jhe", value_block, g_update, preferred_element_type=jnp.float32)
            + g_key_sum[None]
        )
        tail_key = jnp.where(tail_list[block_number][:, None, None], key_block, zero_low)
        value_grad = jnp.einsum(
            "htj,thf->jhf", scores_low, g_numerator, preferred_element_type=jnp.float32
        )
        value_grad = value_grad + jnp.einsum(
            "jhe,hef->jhf", tail_key, g_update, preferred_element_type=jnp.float32
        )
        gq_list.append(query_grad)
        gk_list.append(key_grad)
        gv_list.append(value_grad)
        g_memory = local_list[block_number] + flag_list[block_number] * g_memory
        g_key_sum = localkey_list[block_number] + flag_list[block_number] * g_key_sum
    d_feat_query = jnp.concatenate(gq_list[::-1], axis=0).reshape(local_len, model_width)
    d_feat_key = jnp.concatenate(gk_list[::-1], axis=0).reshape(local_len, model_width)
    d_value = jnp.concatenate(gv_list[::-1], axis=0).reshape(local_len, model_width)
    query_value, query_back = jax.vjp(feature, queries)
    key_value, key_back = jax.vjp(feature, keys_raw)
    g_projected = jnp.concatenate(
        [query_back(d_feat_query)[0], key_back(d_feat_key)[0], d_value], axis=1
    ).astype(jnp.bfloat16)
    grad_in_weight = rows_product(normed_low, g_projected)
    d_normed = cols_product(g_projected, in_back)
    first_value, first_back = jax.vjp(layer_norm, input_tokens, gain_one, shift_one)
    input_part, grad_gain_one, grad_shift_one = first_back(d_normed)
    grad_tokens = (g_middle + input_part).reshape(1, local_len, model_width)
    summed = (
        lax.psum_scatter(grad_in_weight, ("dp", "seq"), scatter_dimension=0, tiled=True),
        lax.psum_scatter(grad_out_weight, ("dp", "seq"), scatter_dimension=0, tiled=True),
        lax.psum_scatter(grad_up, ("dp", "seq"), scatter_dimension=0, tiled=True),
        lax.psum_scatter(grad_down, ("dp", "seq"), scatter_dimension=0, tiled=True),
        lax.psum_scatter(grad_gain_one, ("dp", "seq"), scatter_dimension=0, tiled=True),
        lax.psum_scatter(grad_shift_one, ("dp", "seq"), scatter_dimension=0, tiled=True),
        lax.psum_scatter(grad_gain_two, ("dp", "seq"), scatter_dimension=0, tiled=True),
        lax.psum_scatter(grad_shift_two, ("dp", "seq"), scatter_dimension=0, tiled=True),
    )
    return (
        result_tokens,
        grad_tokens,
        summed[0],
        summed[1],
        summed[2],
        summed[3],
        summed[4],
        summed[5],
        summed[6],
        summed[7],
    )


MESH = pl.DeviceIdType.MESH
LOW = jnp.bfloat16
FULL = jnp.float32


class Place:
    def __init__(self):
        dp, seq = lax.axis_index("dp"), lax.axis_index("seq")
        self.y, self.x = dp // 2, dp % 2
        self.z, self.c = seq // 2, seq % 2
        self.dp, self.seq = dp, seq
        self.over_x = (self.y * 2 + 1 - self.x, seq)
        self.over_y = ((1 - self.y) * 2 + self.x, seq)
        self.sibling = (dp, self.z * 2 + 1 - self.c)
        self.following = [(dp, (seq + 1) % 8), (dp, (seq + 2) % 8)]
        self.preceding = [(dp, (seq + 7) % 8), (dp, (seq + 6) % 8)]
        self.over_end = (dp, (seq + 2 * self.c + 7) % 8)
        self.along_z = [(dp, (self.z + d) % 4 * 2 + self.c) for d in (1, 2, 3)]

    def meet(self):
        barrier = pltpu.get_barrier_semaphore()
        everyone = [self.over_x, self.over_y, self.sibling, self.over_end, *self.along_z]
        for device in everyone:
            pl.semaphore_signal(barrier, inc=1, device_id=device, device_id_type=MESH)
        pl.semaphore_wait(barrier, len(everyone))


def remote(source, target, send, recv, device):
    return pltpu.make_async_remote_copy(
        src_ref=source,
        dst_ref=target,
        send_sem=send,
        recv_sem=recv,
        device_id=device,
        device_id_type=MESH,
    )


class Gather:
    def __init__(self, place, full, send, recv):
        p = place
        half = full.shape[4] // 2
        low, high = pl.ds(0, half), pl.ds(half, half)
        own = full.at[p.y, p.x, p.z, p.c]
        parts = [(own, device) for device in p.along_z]
        parts.append((full.at[p.y, p.x, :, p.c, low], p.over_x))
        parts.append((full.at[p.y, p.x, :, p.c, high], p.over_y))
        parts.append((full.at[p.y, :, :, p.c, low], p.over_y))
        parts.append((full.at[:, p.x, :, p.c, high], p.over_x))
        for y, x in ((p.y, p.x), (p.y, 1 - p.x), (1 - p.y, p.x), (1 - p.y, 1 - p.x)):
            parts.append((full.at[y, x, :, p.c], p.sibling))
        self.copies = [
            remote(ref, ref, send.at[i], recv.at[i], device)
            for i, (ref, device) in enumerate(parts)
        ]

    def start(self, *which):
        for i in which:
            self.copies[i].start()

    def arrive(self, *which):
        for i in which:
            self.copies[i].wait_recv()

    def step(self, number):
        if number == 0:
            self.start(0, 1, 2)
        elif number == 1:
            self.arrive(0, 1, 2)
            self.start(3, 4, 7)
        elif number == 2:
            self.arrive(3, 4)
            self.start(5, 6)
        elif number == 3:
            self.arrive(5, 6)
            self.start(8, 9, 10)
        else:
            self.arrive(7, 8, 9, 10)

    def finish(self):
        for copy in self.copies:
            copy.wait_send()


class Scatter:
    def __init__(self, place, own, total, pair, first_a, first_b, second_a, second_b, last, send, recv, outside):
        p = place
        self.outside, self.released = outside, False
        half = own.shape[4] // 2
        self.place, self.half = p, half
        self.own, self.total, self.pair = own, total, pair
        self.first_a, self.first_b = first_a, first_b
        self.second_a, self.second_b = second_a, second_b
        self.last = last
        low, high = pl.ds(0, half), pl.ds(half, half)
        parts = [
            (own.at[:, :, :, 1 - p.c], pair, p.sibling),
            (total.at[1 - p.y, :, :, low], first_a, p.over_y),
            (total.at[:, 1 - p.x, :, high], first_b, p.over_x),
            (total.at[p.y, 1 - p.x, :, low], second_a, p.over_x),
            (total.at[1 - p.y, p.x, :, high], second_b, p.over_y),
        ]
        if outside:
            self.keep = pltpu.make_async_copy(own.at[:, :, :, p.c], total, send.at[8])
        for d in (1, 2, 3):
            parts.append((total.at[p.y, p.x, (p.z + d) % 4], last.at[d - 1], p.along_z[d - 1]))
        self.copies = [
            remote(source, target, send.at[i], recv.at[i], device)
            for i, (source, target, device) in enumerate(parts)
        ]

    def step(self, number):
        p, half = self.place, self.half
        low, high = slice(0, half), slice(half, 2 * half)
        total = self.total
        if number == 0:
            self.copies[0].start()
            if self.outside:
                self.keep.start()
        elif number == 1:
            if self.outside:
                self.keep.wait()
            self.copies[0].wait_recv()

            @pl.loop(0, 4)
            def _(i):
                y, x = i // 2, i % 2
                mine = total[y, x] if self.outside else self.own[y, x, :, p.c]
                total[y, x] = mine + self.pair[y, x]

            self.copies[1].start()
            self.copies[2].start()
        elif number == 2:
            self.copies[1].wait_recv()
            self.copies[2].wait_recv()
            for i in range(2):
                total[p.y, i, :, low] += self.first_a[i]
                total[i, p.x, :, high] += self.first_b[i]
            self.copies[3].start()
            self.copies[4].start()
        elif number == 3:
            self.copies[3].wait_recv()
            self.copies[4].wait_recv()
            total[p.y, p.x, :, low] += self.second_a[...]
            total[p.y, p.x, :, high] += self.second_b[...]
            for i in (5, 6, 7):
                self.copies[i].start()

    def result(self):
        for i in (5, 6, 7):
            self.copies[i].wait_recv()
        p = self.place
        value = self.total[p.y, p.x, p.z].astype(FULL)
        for d in range(3):
            value = value + self.last[d].astype(FULL)
        return value

    def release(self):
        self.copies[0].wait_send()
        self.released = True

    def finish(self):
        for copy in self.copies[1 if self.released else 0 :]:
            copy.wait_send()


class SmallGather(Gather):
    def __init__(self, place, full, send, recv):
        p = place
        own = full.at[p.y, p.x, p.z, p.c]
        parts = [(own, device) for device in p.along_z]
        parts.append((full.at[p.y, p.x, :, p.c], p.over_x))
        parts.append((full.at[p.y, :, :, p.c], p.over_y))
        for y in range(2):
            for x in range(2):
                parts.append((full.at[y, x, :, p.c], p.sibling))
        self.copies = [
            remote(ref, ref, send.at[i], recv.at[i], device)
            for i, (ref, device) in enumerate(parts)
        ]

    def step(self, number):
        if number == 0:
            self.start(0, 1, 2)
        elif number == 1:
            self.arrive(0, 1, 2)
            self.start(3)
        elif number == 2:
            self.arrive(3)
            self.start(4)
        elif number == 3:
            self.arrive(4)
            self.start(5, 6, 7, 8)
        else:
            self.arrive(5, 6, 7, 8)


def product(one, two):
    return jnp.dot(one, two, preferred_element_type=FULL)


def across(one, two):
    return lax.dot_general(one, two, (((1,), (1,)), ((), ())), preferred_element_type=FULL)


def down_rows(one, two):
    return lax.dot_general(one, two, (((0,), (0,)), ((), ())), preferred_element_type=FULL)


def tile(i, size):
    return pl.ds(pl.multiple_of(i * size, size), size)


def image_count(starts, at):
    total = jnp.where(starts[0, 0] <= at, 1, 0)
    for k in range(1, starts.shape[1]):
        total = total + jnp.where(starts[0, k] <= at, 1, 0)
    return total


class Images:
    def __init__(self, starts, seq, length):
        first = seq * length
        self.length = length
        self.column = image_count(starts, first + lax.broadcasted_iota(jnp.int32, (length, 128), 0))
        self.row = image_count(starts, first + lax.broadcasted_iota(jnp.int32, (8, length), 1))
        before = image_count(starts, first - 1)
        last = image_count(starts, first + length - 1)
        earlier = image_count(starts, first - length - 1)
        later = image_count(starts, first + 2 * length - 1)
        self.keep = jnp.where(self.column == before, 1.0, 0.0)
        self.tail = jnp.where(self.column == last, 1.0, 0.0)
        self.flag_before = jnp.where(before == earlier, 1.0, 0.0)
        self.flag_after = jnp.where(later == last, 1.0, 0.0)


def same_mask(images, rows, columns, transposed):
    shape = (images.length, images.length)
    down = lax.broadcasted_iota(jnp.int32, shape, 0)
    along = lax.broadcasted_iota(jnp.int32, shape, 1)
    order = down <= along if transposed else down >= along
    equal = images.column[:, :1] == images.row[:1, :]
    return jnp.where(order & equal, 1.0, 0.0).astype(LOW)


def head_lanes(rows):
    return lax.broadcasted_iota(jnp.int32, (rows, 128), 1) < HEAD


def own_block():
    return jnp.where(
        (lax.broadcasted_iota(jnp.int32, (128, 128), 0) < HEAD)
        == (lax.broadcasted_iota(jnp.int32, (128, 128), 1) < HEAD),
        1.0,
        0.0,
    ).astype(LOW)


def pack_pair(square):
    return jnp.where(head_lanes(HEAD), square[:HEAD], square[HEAD:])


def unpack_pair(packed):
    lanes = head_lanes(HEAD)
    zero = jnp.zeros_like(packed)
    return jnp.concatenate([jnp.where(lanes, packed, zero), jnp.where(lanes, zero, packed)], axis=0)


def statistics(values):
    average = jnp.mean(values, axis=-1, keepdims=True)
    centred = values - average
    spread = jnp.mean(centred * centred, axis=-1, keepdims=True)
    scale = lax.rsqrt(spread + 1e-05)
    return centred * scale, scale


def gelu_both(values):
    root = 0.7978845608028654
    square = values * values
    angle = jnp.tanh(root * values * (1.0 + 0.044715 * square))
    half = 0.5 + 0.5 * angle
    slope = half + 0.5 * values * (1.0 - angle * angle) * (root * (1.0 + 0.134145 * square))
    return values * half, slope


def forward_kernel(inputs, outputs, scratch):
    tokens_in, cotangent_in, starts, in_weight, out_weight, up_weight, down_weight, pack_in = inputs
    (
        in_full,
        out_full,
        up_full,
        down_full,
        grad_down_out,
        result_out,
        heads_out,
        mixed_out,
        inverse_out,
        middle_out,
        slope_out,
        memory_out,
        sums_out,
        gains_out,
    ) = outputs
    (
        wide,
        tall,
        pack,
        tokens,
        cotangent,
        gains,
        normed,
        heads,
        mask,
        mixed,
        mixed_low,
        inverse,
        middle,
        active,
        slope,
        grad_down,
        result,
        outgoing,
        incoming,
        memory,
        sums,
        send,
        recv,
        small_send,
        small_recv,
        state_send,
        state_recv,
        local,
        store,
    ) = scratch
    p = Place()
    length, width = tokens.shape
    loads = []
    for j in range(8):
        source = in_weight if j < 3 else (out_weight if j == 3 else up_weight)
        column = j if j < 3 else (0 if j == 3 else j - 4)
        loads.append((source.at[:, pl.ds(column * 1024, 1024)], wide.at[j, p.y, p.x, p.z, p.c]))
    for j in range(4):
        loads.append((down_weight.at[:, pl.ds(256 * j, 256)], tall.at[j, p.y, p.x, p.z, p.c]))
    loads.append((pack_in, pack.at[p.y, p.x, p.z, p.c]))
    loads.append((tokens_in, tokens))
    loads.append((cotangent_in, cotangent))
    loads = [pltpu.make_async_copy(a, b, local.at[i]) for i, (a, b) in enumerate(loads)]
    for i in (12, 0, 1, 2, 13, 3, 4, 5, 6, 7, 8, 9, 10, 11, 14):
        loads[i].start()
    stores = []

    def save(source, target):
        copy = pltpu.make_async_copy(source, target, store.at[len(stores)])
        copy.start()
        stores.append(copy)

    p.meet()
    small = SmallGather(p, pack, small_send, small_recv)
    chunks = [Gather(p, wide.at[j], send.at[j], recv.at[j]) for j in range(8)]
    chunks += [Gather(p, tall.at[j], send.at[8 + j], recv.at[8 + j]) for j in range(4)]

    def event(j, number):
        if not 0 <= j < 12:
            return
        if number == 0:
            loads[j].wait()
        chunks[j].step(number)
        if number == 4:
            if j < 8:
                target = in_full if j < 3 else (out_full if j == 3 else up_full)
                column = j if j < 3 else (0 if j == 3 else j - 4)
                save(wide.at[j], target.at[:, :, :, :, :, pl.ds(column * 1024, 1024)])
            else:
                save(tall.at[j - 8], down_full.at[:, :, :, :, :, pl.ds(256 * (j - 8), 256)])

    def weight(j, columns):
        return wide[j, :, :, :, :, :, columns].reshape(width, columns.size)

    images = Images(starts, p.seq, length)

    def first_norm():
        for y in range(2):
            for x in range(2):
                for k in range(2):
                    value = pack[y, x, 2 * k : 2 * k + 2].astype(FULL)
                    value = (value[0, 0] + value[0, 1]) + (value[1, 0] + value[1, 1])
                    at = 128 * ((y * 2 + x) * 2 + k)
                    gains[:, at : at + 128] = value
        save(gains, gains_out)
        loads[13].wait()

        @pl.loop(0, length // 128, unroll=2)
        def _(i):
            rows = tile(i, 128)
            value, _ = statistics(tokens[rows, :].astype(FULL))
            normed[rows, :] = (value * gains[0:1, :] + gains[1:2, :]).astype(LOW)

        mask[...] = same_mask(images, length, length, False)

    def project(j):
        @pl.loop(0, 2, unroll=2)
        def _(i):
            value = product(normed[...], weight(j, tile(i, 512)))
            if j < 2:
                value = jnp.where(value > 0, value + 1.0, jnp.exp(jnp.minimum(value, 0.0)))
            heads[j, :, tile(i, 512)] = value.astype(LOW)

    def update():
        tail = images.tail.astype(LOW)

        @pl.loop(0, 8, unroll=2)
        def _(i):
            lanes = tile(i, 128)
            key = heads[1, :, lanes] * tail
            square = down_rows(key, heads[2, :, lanes])
            outgoing[i, 0:HEAD] = pack_pair(square).astype(LOW)
            total = product(jnp.ones((16, length), LOW), key)
            outgoing[i, HEAD : HEAD + 16] = total.astype(LOW)

        save(heads, heads_out)
        for copy in state:
            copy.start()

    state = [
        remote(outgoing, incoming.at[d], state_send.at[d], state_recv.at[d], device)
        for d, device in enumerate(p.following)
    ]

    def enter():
        for copy in state:
            copy.wait_recv()

        @pl.loop(0, 8, unroll=2)
        def _(i):
            value = incoming[0, i].astype(FULL) + images.flag_before * incoming[1, i].astype(FULL)
            memory[i] = value[0:HEAD].astype(LOW)
            sums[i] = value[HEAD : HEAD + 8]

        save(memory, memory_out)
        save(sums, sums_out)

    def attend(begin, end):
        lanes_column = head_lanes(length)
        blocks = own_block()
        keep = images.keep.astype(LOW)
        half = length // 2
        identity = jnp.where(
            lax.broadcasted_iota(jnp.int32, (128, 128), 0)
            == lax.broadcasted_iota(jnp.int32, (128, 128), 1),
            1.0,
            0.0,
        )
        ones = jnp.ones((length, 128), LOW)

        @pl.loop(begin, end, unroll=2)
        def _(i):
            lanes = tile(i, 128)
            query, key, value = heads[0, :, lanes], heads[1, :, lanes], heads[2, :, lanes]
            wider = jnp.concatenate([value, ones], axis=1)
            parts = []
            for h in range(2):
                mine = lanes_column if h == 0 else ~lanes_column
                own = jnp.where(mine, query, jnp.zeros_like(query))
                upper = across(own[:half], key[:half]).astype(LOW) * mask[:half, :half]
                lower = across(own[half:], key).astype(LOW) * mask[half:, :]
                parts.append(
                    jnp.concatenate([product(upper, wider[:half]), product(lower, wider)], axis=0)
                )
            diagonal = (identity * sums[i, 0:1]).astype(LOW)
            right = jnp.concatenate(
                [unpack_pair(memory[i]), product(diagonal, blocks).astype(LOW)], axis=1
            )
            carried = product(query * keep, right)
            numerator = jnp.where(lanes_column, parts[0][:, :128], parts[1][:, :128])
            denominator = jnp.where(lanes_column, parts[0][:, 128:], parts[1][:, 128:])
            over = 1.0 / (denominator + carried[:, 128:])
            value = (numerator + carried[:, :128]) * over
            inverse[:, lanes] = over
            mixed[:, lanes] = value
            mixed_low[:, lanes] = value.astype(LOW)

    def join():
        save(mixed, mixed_out)
        save(inverse, inverse_out)

        @pl.loop(0, 2, unroll=2)
        def _(i):
            columns = tile(i, 512)
            middle[:, columns] = tokens[:, columns].astype(FULL) + product(
                mixed_low[...], weight(3, columns)
            )

        save(middle, middle_out)

    def second_norm():
        @pl.loop(0, length // 128, unroll=2)
        def _(i):
            rows = tile(i, 128)
            value, _ = statistics(middle[rows, :])
            normed[rows, :] = (value * gains[2:3, :] + gains[3:4, :]).astype(LOW)

    def raise_up(j):
        @pl.loop(0, 4, unroll=4)
        def _(i):
            value = product(normed[...], weight(4 + j, tile(i, 256)))
            columns = pl.ds(pl.multiple_of(j * 1024 + i * 256, 256), 256)
            value, steep = gelu_both(value)
            active[:, columns] = value.astype(LOW)
            slope[:, columns] = steep.astype(LOW)

        if j == 3:
            save(slope, slope_out)

    def down_gradient(begin, end):
        if begin == 0:
            loads[14].wait()

        @pl.loop(begin, end, unroll=4)
        def _(i):
            value = down_rows(active[:, tile(i, 512)], cotangent[...]).astype(LOW)
            y, x, z = i // 4, i // 2 % 2, i % 2 * 2
            for j in range(4):
                part = value[:, 256 * j : 256 * j + 256].reshape(2, 2, 128, 256)
                grad_down[j, y, x, pl.ds(z, 2)] = part

        if end == 8:
            save(grad_down, grad_down_out)

    def lower(j):
        columns = slice(256 * j, 256 * j + 256)

        @pl.loop(0, 2, unroll=2)
        def _(i):
            rows = tile(i, 256)
            value = product(active[rows, :], tall[j].reshape(4 * width, 256))
            result[rows, columns] = (middle[rows, columns] + value).astype(LOW)

        save(result.at[:, pl.ds(256 * j, 256)], result_out.at[:, pl.ds(256 * j, 256)])

    do = functools.partial
    work = {
        4: [lambda: None, first_norm],
        5: [do(project, 0)],
        6: [do(project, 1)],
        7: [do(project, 2), update],
        8: [lambda: None, lambda: None, enter],
        9: [do(attend, 0, 4), do(attend, 4, 6), do(attend, 6, 8)],
        10: [join, second_norm, do(raise_up, 0)],
        11: [do(raise_up, 1), do(raise_up, 2)],
        12: [do(raise_up, 3), do(down_gradient, 0, 4), do(down_gradient, 4, 8)],
        13: [do(lower, 0)],
        14: [do(lower, 1)],
        15: [do(lower, 2)],
    }
    loads[12].wait()
    small.step(0)
    for tick in range(12 + 4):
        todo = work.get(tick, []) + [lambda: None] * 3
        event(tick, 0)
        event(tick - 1, 1)
        if 1 <= tick < 5:
            small.step(tick)
        todo[0]()
        event(tick - 2, 2)
        todo[1]()
        event(tick - 3, 3)
        event(tick - 4, 4)
        todo[2]()
    lower(3)
    small.finish()
    for copy in state:
        copy.wait_send()
    for chunk in chunks:
        chunk.finish()
    for copy in stores:
        copy.wait()


def forward_pass(tokens, cotangent, starts, in_weight, out_weight, up_weight, down_weight, pack):
    length, width = tokens.shape
    block = lambda rows, columns: jax.ShapeDtypeStruct((2, 2, 4, 2, rows, columns), LOW)
    shape = jax.ShapeDtypeStruct

    def body(*refs):
        forward_kernel(refs[:8], refs[8:22], refs[22:])

    return pl.pallas_call(
        body,
        out_shape=[
            block(32, 3072),
            block(32, 1024),
            block(32, 4096),
            block(128, 1024),
            shape((4, 2, 2, 4, 2, 128, 256), LOW),
            shape((length, width), LOW),
            shape((3, length, width), LOW),
            shape((length, width), FULL),
            shape((length, width), FULL),
            shape((length, width), FULL),
            shape((length, 4 * width), LOW),
            shape((8, HEAD, 128), LOW),
            shape((8, 8, 128), FULL),
            shape((16, width), FULL),
        ],
        in_specs=[
            pl.BlockSpec(memory_space=pltpu.SMEM if i == 2 else pl.ANY) for i in range(8)
        ],
        out_specs=[pl.BlockSpec(memory_space=pl.ANY)] * 14,
        scratch_shapes=[
            pltpu.VMEM((8, 2, 2, 4, 2, 32, 1024), LOW),
            pltpu.VMEM((4, 2, 2, 4, 2, 128, 256), LOW),
            pltpu.VMEM((2, 2, 4, 2, 16, 128), LOW),
            pltpu.VMEM((length, width), LOW),
            pltpu.VMEM((length, width), LOW),
            pltpu.VMEM((16, width), FULL),
            pltpu.VMEM((length, width), LOW),
            pltpu.VMEM((3, length, width), LOW),
            pltpu.VMEM((length, length), LOW),
            pltpu.VMEM((length, width), FULL),
            pltpu.VMEM((length, width), LOW),
            pltpu.VMEM((length, width), FULL),
            pltpu.VMEM((length, width), FULL),
            pltpu.VMEM((length, 4 * width), LOW),
            pltpu.VMEM((length, 4 * width), LOW),
            pltpu.VMEM((4, 2, 2, 4, 2, 128, 256), LOW),
            pltpu.VMEM((length, width), LOW),
            pltpu.VMEM((8, HEAD + 16, 128), LOW),
            pltpu.VMEM((2, 8, HEAD + 16, 128), LOW),
            pltpu.VMEM((8, HEAD, 128), LOW),
            pltpu.VMEM((8, 8, 128), FULL),
            pltpu.SemaphoreType.DMA((12, 11)),
            pltpu.SemaphoreType.DMA((12, 11)),
            pltpu.SemaphoreType.DMA((9,)),
            pltpu.SemaphoreType.DMA((9,)),
            pltpu.SemaphoreType.DMA((2,)),
            pltpu.SemaphoreType.DMA((2,)),
            pltpu.SemaphoreType.DMA((15,)),
            pltpu.SemaphoreType.DMA((26,)),
        ],
        compiler_params=pltpu.CompilerParams(
            collective_id=0, has_side_effects=True, vmem_limit_bytes=62 << 20
        ),
        name="forward_pass",
    )(tokens, cotangent, starts, in_weight, out_weight, up_weight, down_weight, pack)


def scatter_buffers(count, rows, columns):
    half = rows // 2
    shapes = [
        (2, 2, 4, rows, columns),
        (2, 2, 4, rows, columns),
        (2, 4, half, columns),
        (2, 4, half, columns),
        (4, half, columns),
        (4, half, columns),
        (3, rows, columns),
    ]
    return [pltpu.VMEM((count, *shape), LOW) for shape in shapes]


class Sum:
    def __init__(self, place, stages, landed, send, recv):
        p = place
        devices = [p.sibling, p.over_x, p.over_y, *p.along_z]
        self.stages, self.landed = stages, landed
        self.copies = [
            remote(stages.at[min(i, 3)], landed.at[i], send.at[i], recv.at[i], device)
            for i, device in enumerate(devices)
        ]

    def step(self, number):
        stages, landed = self.stages, self.landed
        if 1 <= number <= 3:
            self.copies[number - 1].wait_recv()
            stages[number] = stages[number - 1] + landed[number - 1]
        if number < 3:
            self.copies[number].start()
        elif number == 3:
            for i in (3, 4, 5):
                self.copies[i].start()

    def result(self):
        for i in (3, 4, 5):
            self.copies[i].wait_recv()
        return (self.stages[3] + self.landed[3]) + (self.landed[4] + self.landed[5])

    def finish(self):
        for copy in self.copies:
            copy.wait_send()


def backward_kernel(inputs, outputs, tall, wide, scratch):
    (
        tokens_in,
        cotangent_in,
        starts,
        in_full,
        out_full,
        up_full,
        down_full,
        grad_down_in,
        heads_in,
        mixed_in,
        inverse_in,
        middle_in,
        slope_in,
        memory_in,
        sums_in,
        gains_in,
    ) = inputs
    (
        cotangent,
        normed,
        slab,
        broad,
        grad_middle,
        inner,
        mixed,
        inverse,
        memory,
        sums,
        gains,
        mask,
        mask_back,
        parts,
        done_in,
        done_out,
        done_up,
        done_down,
        stages,
        landed,
        outgoing,
        incoming,
        update,
        key_update,
        send,
        recv,
        sum_send,
        sum_recv,
        state_send,
        state_recv,
        local,
        stream,
        store,
    ) = scratch
    p = Place()
    length, width = cotangent.shape

    pairs = [
        (cotangent_in, cotangent),
        (slope_in, broad),
        (middle_in, grad_middle),
        (gains_in, gains),
        (memory_in, memory),
        (sums_in, sums),
        (mixed_in, mixed),
        (inverse_in, inverse),
        (tokens_in, cotangent),
    ]
    pairs += [(heads_in.at[k], broad.at[:, pl.ds(1024 * k, 1024)]) for k in range(3)]
    loads = [pltpu.make_async_copy(a, b, local.at[i]) for i, (a, b) in enumerate(pairs)]
    slabs = [down_full.at[pl.ds(1024 * j, 1024), :] for j in range(4)]
    slabs += [up_full.at[:, pl.ds(1024 * j, 1024)] for j in range(4)]
    slabs += [out_full]
    slabs += [in_full.at[:, pl.ds(1024 * j, 1024)] for j in range(3)]
    slabs = [
        pltpu.make_async_copy(source, slab.at[i % 2], stream.at[i]) for i, source in enumerate(slabs)
    ]
    order = [8, 9, 10, 11, 4, 5, 6, 7, 3, 0, 1, 2]
    room = {4: 0, 5: 1, 6: 2, 7: 0, 3: 1, 0: 2, 1: 0, 2: 1}
    chunks = []
    for j in range(12):
        if j < 8:
            first, *others = [ref.at[j] for ref in wide]
            buffers = [first, first, *others]
            own = parts.at[room[j]]
        else:
            buffers = [ref.at[j - 8] for ref in tall]
            own = grad_down_in.at[j - 8]
        chunks.append(Scatter(p, own, *buffers, send.at[j], recv.at[j], j >= 8))

    p.meet()
    chunks[8].step(0)
    for i in range(4):
        loads[i].start()
    slabs[0].start()
    slabs[1].start()
    for i in range(4, 8):
        loads[i].start()
    stores = []

    def save(source, target):
        copy = pltpu.make_async_copy(source, target, store.at[len(stores)])
        copy.start()
        stores.append(copy)

    def event(position, number):
        if not 0 <= position < 12:
            return
        j = order[position]
        if number < 4:
            if (j, number) != (8, 0):
                chunks[j].step(number)
            return
        if j < 8:
            target, k = (done_in, j) if j < 3 else ((done_out, 0) if j == 3 else (done_up, j - 4))
            size = 1024
        else:
            target, k, size = done_down, j - 8, 256
        where = outputs[0 if j < 3 else 1 if j == 3 else 2 if j < 8 else 3]
        target[:, size * k : size * k + size] = chunks[j].result()
        save(target.at[:, pl.ds(size * k, size)], where.at[:, pl.ds(size * k, size)])

    images = Images(starts, p.seq, length)

    def second_norm():
        loads[2].wait()
        loads[3].wait()

        @pl.loop(0, length // 128, unroll=2)
        def _(i):
            rows = tile(i, 128)
            value, _ = statistics(grad_middle[rows, :])
            normed[rows, :] = (value * gains[2:3, :] + gains[3:4, :]).astype(LOW)

    def active_gradient(j):
        if j == 0:
            loads[0].wait()
            loads[1].wait()
        slabs[j].wait()

        @pl.loop(0, 4, unroll=4)
        def _(i):
            columns = pl.ds(pl.multiple_of(1024 * j + 256 * i, 256), 256)
            value = across(cotangent[...], slab[j % 2, tile(i, 256), :])
            broad[:, columns] = (value * broad[:, columns].astype(FULL)).astype(LOW)

        slabs[j + 2].start()

    def weight_gradient(j, left, right):
        at = room[j]

        @pl.loop(0, 4, unroll=4)
        def _(i):
            value = down_rows(left(tile(i, 256)), right()).astype(LOW)
            parts[at, i // 2, i % 2] = value.reshape(4, 2, 32, 1024)

    def up_gradient(j):
        if j == 3:
            chunks[4].release()
        weight_gradient(
            4 + j,
            lambda columns: normed[:, columns],
            lambda: broad[:, 1024 * j : 1024 * j + 1024],
        )
        if j == 3:
            for k in range(9, 12):
                loads[k].start()

    def inner_gradient(first, j):
        slabs[first + j].wait()

        @pl.loop(0, 4, unroll=4)
        def _(i):
            columns = tile(i, 256)
            value = across(
                broad[:, 1024 * j : 1024 * j + 1024], slab[(first + j) % 2, columns, :]
            )
            if j > 0:
                value = value + inner[:, columns]
            inner[:, columns] = value

        if first + j + 2 < 12:
            slabs[first + j + 2].start()

    def norm_gradient(rows, values, gain):
        unit, scale = statistics(values)
        given = inner[rows, :]
        scaled = given * gain
        one = jnp.mean(scaled, axis=-1, keepdims=True)
        two = jnp.mean(scaled * unit, axis=-1, keepdims=True)
        return scale * (scaled - one - unit * two), given * unit, given

    def fold(values):
        return jnp.sum(values, axis=0, keepdims=True)

    def middle_gradient():
        stages[0] = jnp.zeros((8, width), FULL)

        @pl.loop(0, length // 128, unroll=2)
        def _(i):
            rows = tile(i, 128)
            value, gain, shift = norm_gradient(rows, grad_middle[rows, :], gains[2:3, :])
            stages[0, 2:3, :] += fold(gain)
            stages[0, 3:4, :] += fold(shift)
            value = value + cotangent[rows, :].astype(FULL)
            grad_middle[rows, :] = value
            cotangent[rows, :] = value.astype(LOW)

    def output_gradient():
        loads[6].wait()
        chunks[5].release()
        weight_gradient(
            3, lambda columns: mixed[:, columns].astype(LOW), lambda: cotangent[...]
        )
        loads[8].start()

    def mixed_gradient():
        slabs[8].wait()

        @pl.loop(0, 4, unroll=4)
        def _(i):
            columns = tile(i, 256)
            inner[:, columns] = across(cotangent[...], slab[0, columns, :])

        slabs[10].start()

    state = [
        remote(outgoing, incoming.at[d], state_send.at[d], state_recv.at[d], device)
        for d, device in enumerate(p.preceding)
    ]

    def numerator_gradient():
        for i in (4, 5, 7, 9, 10, 11):
            loads[i].wait()
        blocks = own_block()
        doubled = jnp.concatenate([blocks, blocks], axis=0)

        @pl.loop(0, 8, unroll=2)
        def _(i):
            lanes = tile(i, 128)
            given, over = inner[:, lanes], inverse[:, lanes]
            numerator = (given * over).astype(LOW)
            each = given * mixed[:, lanes]
            high = each.astype(LOW)
            rest = (each - high.astype(FULL)).astype(LOW)
            slant = product(jnp.concatenate([high, rest], axis=1), doubled) * over * -1.0
            mixed[:, lanes] = slant
            broad[:, pl.ds(pl.multiple_of(3072 + 128 * i, 128), 128)] = numerator
            kept = broad[:, lanes].astype(FULL) * images.keep
            square = down_rows(kept.astype(LOW), numerator)
            outgoing[i, 0:HEAD] = pack_pair(square).astype(LOW)
            total = fold(kept * slant)
            outgoing[i, HEAD : HEAD + 16] = jnp.broadcast_to(total, (16, 128)).astype(LOW)

        for copy in state:
            copy.start()
        mask[...] = same_mask(images, length, length, False)
        mask_back[...] = same_mask(images, length, length, True)

    def enter():
        for copy in state:
            copy.wait_recv()
        flag = jnp.where(p.seq == 7, 0.0, images.flag_after)

        @pl.loop(0, 8, unroll=2)
        def _(i):
            value = incoming[0, i].astype(FULL) + flag * incoming[1, i].astype(FULL)
            update[i] = value[0:HEAD].astype(LOW)
            key_update[i] = value[HEAD : HEAD + 8]

    def attend(begin, end):
        if begin == 0:
            enter()
        if end == 8:
            first_norm()
        first = head_lanes(length)
        lane = lax.broadcasted_iota(jnp.int32, (length, 128), 1)
        ones = jnp.ones((length, 128), LOW)
        zero = jnp.zeros((length, 128), LOW)
        half = length // 2

        @pl.loop(begin, end)
        def _(i):
            at = [pl.ds(pl.multiple_of(1024 * k + 128 * i, 128), 128) for k in range(4)]
            query, key, value, numerator = [broad[:, lanes] for lanes in at]
            slant = mixed[:, at[0]]
            high = slant.astype(LOW)
            rest = (slant - high.astype(FULL)).astype(LOW)
            right = jnp.concatenate([value, ones], axis=1)
            grads = []
            for h in range(2):
                mine = first if h == 0 else ~first
                own_query = jnp.where(mine, query, zero)
                left = jnp.concatenate(
                    [
                        jnp.where(mine, numerator, zero),
                        jnp.where(
                            lane == HEAD * h, high, jnp.where(lane == HEAD * h + 1, rest, zero)
                        ),
                    ],
                    axis=1,
                )
                upper = across(left[:half], right[:half]).astype(LOW) * mask[:half, :half]
                lower = across(left[half:], right).astype(LOW) * mask[half:, :]
                for_query = jnp.concatenate([product(upper, key[:half]), product(lower, key)], axis=0)
                upper = across(right[:half], left).astype(LOW) * mask_back[:half, :]
                lower = across(right[half:], left[half:]).astype(LOW) * mask_back[half:, half:]
                for_key = jnp.concatenate(
                    [product(upper, query), product(lower, query[half:])], axis=0
                )
                upper = across(key[:half], own_query).astype(LOW) * mask_back[:half, :]
                lower = across(key[half:], own_query[half:]).astype(LOW) * mask_back[half:, half:]
                for_value = jnp.concatenate(
                    [product(upper, numerator), product(lower, numerator[half:])], axis=0
                )
                grads.append((for_query, for_key, for_value))
            for_query, for_key, for_value = [
                jnp.where(first, one, two) for one, two in zip(*grads, strict=True)
            ]
            keep, tail = images.keep, images.tail
            for_query = for_query + keep * (
                across(numerator, unpack_pair(memory[i])) + slant * sums[i, 0:1]
            )
            square = unpack_pair(update[i])
            for_key = for_key + tail * (across(value, square) + key_update[i, 0:1])
            for_value = for_value + product(key * tail.astype(LOW), square)
            broad[:, at[0]] = (for_query * jnp.minimum(query.astype(FULL), 1.0)).astype(LOW)
            broad[:, at[1]] = (for_key * jnp.minimum(key.astype(FULL), 1.0)).astype(LOW)
            broad[:, at[2]] = for_value.astype(LOW)

    def first_norm():
        loads[8].wait()

        @pl.loop(0, length // 128, unroll=2)
        def _(i):
            rows = tile(i, 128)
            value, _ = statistics(cotangent[rows, :].astype(FULL))
            normed[rows, :] = (value * gains[0:1, :] + gains[1:2, :]).astype(LOW)

    def in_gradient(j):
        chunks[(6, 7, 3)[j]].release()
        weight_gradient(
            j,
            lambda columns: normed[:, columns],
            lambda: broad[:, 1024 * j : 1024 * j + 1024],
        )

    total = Sum(p, stages, landed, sum_send, sum_recv)

    def token_gradient():
        @pl.loop(0, length // 128, unroll=2)
        def _(i):
            rows = tile(i, 128)
            value, gain, shift = norm_gradient(rows, cotangent[rows, :].astype(FULL), gains[0:1, :])
            stages[0, 0:1, :] += fold(gain)
            stages[0, 1:2, :] += fold(shift)
            grad_middle[rows, :] += value

        save(grad_middle, outputs[4])
        total.step(0)

    do = functools.partial
    work = {
        1: [do(active_gradient, 0), do(active_gradient, 1), do(active_gradient, 2)],
        2: [do(active_gradient, 3), second_norm, do(up_gradient, 0)],
        3: [do(up_gradient, 1), do(up_gradient, 2), do(inner_gradient, 4, 0)],
        4: [do(inner_gradient, 4, 1), do(inner_gradient, 4, 2), do(inner_gradient, 4, 3)],
        5: [do(up_gradient, 3), middle_gradient, mixed_gradient],
        6: [output_gradient, numerator_gradient],
        7: [lambda: None, do(attend, 0, 1), do(attend, 1, 3)],
        8: [do(attend, 3, 5), do(attend, 5, 7), do(attend, 7, 8)],
        9: [do(in_gradient, 1), do(in_gradient, 2), do(inner_gradient, 9, 0)],
        10: [
            do(inner_gradient, 9, 1),
            do(inner_gradient, 9, 2),
            token_gradient,
        ],
        11: [lambda: None, do(total.step, 1)],
        12: [lambda: None, do(total.step, 2)],
        13: [lambda: None, do(total.step, 3)],
    }
    for tick in range(12 + 6):
        todo = work.get(tick, []) + [lambda: None] * 3
        if tick == 9:
            in_gradient(0)
        event(tick, 0)
        event(tick - 1, 1)
        todo[0]()
        event(tick - 2, 2)
        todo[1]()
        event(tick - 3, 3)
        event(tick - 6, 4)
        todo[2]()
    total_value = total.result()
    landed[0] = total_value
    group = (p.dp * 8 + p.seq) // 4
    mine = landed[0, :, tile(group, 128)]
    mine = pltpu.roll(mine, (128 - 32 * (p.seq % 4)) % 128, 1)
    outputs[5][...] = mine
    total.finish()
    for copy in state:
        copy.wait_send()
    for chunk in chunks:
        chunk.finish()
    for copy in stores:
        copy.wait()


def backward_pass(*inputs):
    length, width = inputs[0].shape
    shape = jax.ShapeDtypeStruct
    vmem = pltpu.VMEM
    tall = scatter_buffers(4, 128, 256)
    wide = scatter_buffers(8, 32, 1024)[1:]

    def body(*refs):
        backward_kernel(refs[:16], refs[16:22], refs[22:29], refs[29:35], refs[35:])

    return pl.pallas_call(
        body,
        out_shape=[
            shape((32, 3072), FULL),
            shape((32, 1024), FULL),
            shape((32, 4096), FULL),
            shape((128, 1024), FULL),
            shape((length, width), FULL),
            shape((8, 128), FULL),
        ],
        in_specs=[
            pl.BlockSpec(memory_space=pltpu.SMEM if i == 2 else pl.ANY) for i in range(16)
        ],
        out_specs=[pl.BlockSpec(memory_space=pl.ANY)] * 5
        + [pl.BlockSpec(memory_space=pltpu.VMEM)],
        scratch_shapes=[
            *tall,
            *wide,
            vmem((length, width), LOW),
            vmem((length, width), LOW),
            vmem((2, width, width), LOW),
            vmem((length, 4 * width), LOW),
            vmem((length, width), FULL),
            vmem((length, width), FULL),
            vmem((length, width), FULL),
            vmem((length, width), FULL),
            vmem((8, HEAD, 128), LOW),
            vmem((8, 8, 128), FULL),
            vmem((16, width), FULL),
            vmem((length, length), LOW),
            vmem((length, length), LOW),
            vmem((3, 2, 2, 4, 2, 32, 1024), LOW),
            vmem((32, 3072), FULL),
            vmem((32, 1024), FULL),
            vmem((32, 4096), FULL),
            vmem((128, 1024), FULL),
            vmem((4, 8, width), FULL),
            vmem((6, 8, width), FULL),
            vmem((8, HEAD + 16, 128), LOW),
            vmem((2, 8, HEAD + 16, 128), LOW),
            vmem((8, HEAD, 128), LOW),
            vmem((8, 8, 128), FULL),
            pltpu.SemaphoreType.DMA((12, 9)),
            pltpu.SemaphoreType.DMA((12, 8)),
            pltpu.SemaphoreType.DMA((6,)),
            pltpu.SemaphoreType.DMA((6,)),
            pltpu.SemaphoreType.DMA((2,)),
            pltpu.SemaphoreType.DMA((2,)),
            pltpu.SemaphoreType.DMA((12,)),
            pltpu.SemaphoreType.DMA((12,)),
            pltpu.SemaphoreType.DMA((13,)),
        ],
        compiler_params=pltpu.CompilerParams(
            collective_id=1, has_side_effects=True, vmem_limit_bytes=62 << 20
        ),
        name="backward_pass",
    )(*inputs)


def hand_over(*values):
    large = len(values) - 1

    def body(*refs):
        inputs, vectors, outputs = refs[:large], refs[large], refs[large + 1 : 2 * large + 1]
        small, held, sems = refs[2 * large + 1 : 2 * large + 5], refs[2 * large + 5 : -1], refs[-1]
        copies = [
            (
                pltpu.make_async_copy(inputs[i], held[i], sems.at[0, i]),
                pltpu.make_async_copy(held[i], outputs[i], sems.at[1, i]),
            )
            for i in range(large)
        ]
        for load, _ in copies:
            load.start()
        for k in range(4):
            small[k][...] = vectors[k : k + 1, 0:32]
        for load, store in copies:
            load.wait()
            store.start()
        for _, store in copies:
            store.wait()

    anywhere, near = pl.BlockSpec(memory_space=pl.ANY), pl.BlockSpec(memory_space=pltpu.VMEM)
    return pl.pallas_call(
        body,
        out_shape=[jax.ShapeDtypeStruct(value.shape, value.dtype) for value in values[:large]]
        + [jax.ShapeDtypeStruct((1, 32), FULL)] * 4,
        in_specs=[anywhere] * large + [near],
        out_specs=[anywhere] * large + [near] * 4,
        scratch_shapes=[pltpu.VMEM(value.shape, value.dtype) for value in values[:large]]
        + [pltpu.SemaphoreType.DMA((2, large))],
        name="hand_over",
    )(*values)


def on_device(
    tokens,
    starts,
    query_key_value_weight,
    attention_output_weight,
    up_projection_weight,
    down_projection_weight,
    first_gain,
    first_shift,
    second_gain,
    second_shift,
    cotangent,
):
    mine = lax.axis_index("dp") * 8 + lax.axis_index("seq")
    pack = jnp.stack([first_gain, first_shift, second_gain, second_shift]).astype(FULL)
    pack = jnp.roll(jnp.pad(pack, ((0, 12), (0, 96))), 32 * (mine % 4), axis=1).astype(LOW)
    in_full, out_full, up_full, down_full, grad_down, result, *saved = forward_pass(
        tokens[0],
        cotangent[0],
        starts,
        query_key_value_weight,
        attention_output_weight,
        up_projection_weight,
        down_projection_weight,
        pack,
    )
    grads = backward_pass(
        tokens[0],
        cotangent[0],
        starts,
        in_full.reshape(1024, 3072),
        out_full.reshape(1024, 1024),
        up_full.reshape(1024, 4096),
        down_full.reshape(4096, 1024),
        grad_down,
        *saved,
    )
    result, *grads = hand_over(result, *grads)
    vectors = [grad.reshape(32) for grad in grads[5:]]
    return (result[None], grads[4][None], *grads[:4], *vectors)


def solution(mesh):

    fast = dict(mesh.shape) == {"dp": 4, "seq": 8}
    return jax.shard_map(
        on_device if fast else on_device_general,
        mesh=mesh,
        in_specs=(
            P("dp", "seq", None),
            P("dp", None),
            P(("dp", "seq"), None),
            P(("dp", "seq"), None),
            P(("dp", "seq"), None),
            P(("dp", "seq"), None),
            P(("dp", "seq")),
            P(("dp", "seq")),
            P(("dp", "seq")),
            P(("dp", "seq")),
            P("dp", "seq", None),
        ),
        out_specs=(
            P("dp", "seq", None),
            P("dp", "seq", None),
            P(("dp", "seq"), None),
            P(("dp", "seq"), None),
            P(("dp", "seq"), None),
            P(("dp", "seq"), None),
            P(("dp", "seq")),
            P(("dp", "seq")),
            P(("dp", "seq")),
            P(("dp", "seq")),
        ),
        check_vma=False,
    )
```

```python
import functools

import jax
import jax.numpy as jnp
from jax import lax
from jax.experimental import pallas as pl
from jax.experimental.pallas import tpu as pltpu
from jax.sharding import PartitionSpec as P

HEAD = 64
BLOCK = 512


def prefix(value, axis, combine, identity, reverse):
    size, mine = (lax.axis_size(axis), lax.axis_index(axis))
    everything = jax.tree.map(
        lambda part, kind: lax.all_gather(part.astype(kind), axis),
        value,
        jax.tree.map(lambda a: jnp.bfloat16 if a.dtype == jnp.float32 else a.dtype, value),
    )
    start = jax.tree.map(
        lambda part, zero: jnp.broadcast_to(jnp.asarray(zero, part.dtype), part.shape),
        value,
        identity,
    )

    def lap(k, before):
        at = size - 1 - k if reverse else k
        reached = at > mine if reverse else at < mine
        new = combine(
            before, jax.tree.map(lambda part, own: part[at].astype(own.dtype), everything, value)
        )
        return jax.tree.map(lambda a, b: jnp.where(reached, a, b), new, before)

    return lax.fori_loop(0, size, lap, start)


def layer_norm(values, norm_gain, norm_shift):
    average = jnp.mean(values, axis=-1, keepdims=True)
    centred = values - average
    spread = jnp.mean(centred * centred, axis=-1, keepdims=True)
    return centred * lax.rsqrt(spread + 1e-05) * norm_gain + norm_shift


def feature(values):
    return jax.nn.elu(values) + 1.0


def combine(former, latter):
    return (
        former[0] * latter[0],
        latter[0] * former[1] + latter[1],
        latter[0] * former[2] + latter[2],
    )


def rows_product(factor_one, factor_two):
    return lax.dot_general(
        factor_one, factor_two, (((0,), (0,)), ((), ())), preferred_element_type=jnp.float32
    )


def cols_product(factor_one, factor_two):
    return lax.dot_general(
        factor_one, factor_two, (((1,), (1,)), ((), ())), preferred_element_type=jnp.float32
    )


def on_device_general(
    tokens,
    starts,
    query_key_value_weight,
    attention_output_weight,
    up_projection_weight,
    down_projection_weight,
    first_gain,
    first_shift,
    second_gain,
    second_shift,
    cotangent,
):
    local_len = tokens.shape[1]
    model_width = tokens.shape[2]
    head_count = model_width // HEAD
    block_count = local_len // BLOCK
    block_shape = (block_count, BLOCK, head_count, HEAD)
    zero_low = jnp.zeros((), jnp.bfloat16)
    input_tokens = tokens[0].astype(jnp.float32)
    first_pos = lax.axis_index("seq") * local_len
    positions = first_pos + jnp.arange(local_len, dtype=jnp.int32)
    pack_starts = starts[0]
    image_ids = jnp.sum((pack_starts[None, :] <= positions[:, None]).astype(jnp.int32), axis=1) - 1
    before_id = jnp.sum((pack_starts <= first_pos - 1).astype(jnp.int32)) - 1
    causal = jnp.arange(BLOCK)[:, None] >= jnp.arange(BLOCK)[None, :]
    attn_set = (
        lax.all_gather(query_key_value_weight, ("dp", "seq"), axis=0, tiled=True),
        lax.all_gather(attention_output_weight, ("dp", "seq"), axis=0, tiled=True),
        lax.all_gather(first_gain, ("dp", "seq"), axis=0, tiled=True),
        lax.all_gather(first_shift, ("dp", "seq"), axis=0, tiled=True),
    )
    in_full = attn_set[0]
    out_full = attn_set[1]
    gain_one = attn_set[2].astype(jnp.float32)
    shift_one = attn_set[3].astype(jnp.float32)
    first_normed_tokens = layer_norm(input_tokens, gain_one, shift_one)
    normed_low = first_normed_tokens.astype(jnp.bfloat16)
    projected_tokens = jnp.dot(normed_low, in_full, preferred_element_type=jnp.float32)
    queries = projected_tokens[:, :model_width]
    keys_raw = projected_tokens[:, model_width : 2 * model_width]
    values_raw = projected_tokens[:, 2 * model_width :]
    feat_query = feature(queries).astype(jnp.bfloat16).reshape(block_shape)
    feat_key = feature(keys_raw).astype(jnp.bfloat16).reshape(block_shape)
    value_low = values_raw.astype(jnp.bfloat16).reshape(block_shape)
    block_number = 0
    last_id = image_ids[-1]
    tail_mask = image_ids == last_id
    tail_key = jnp.where(tail_mask[:, None, None], feat_key[block_number], zero_low)
    keep_list = [image_ids == before_id]
    tail_list = [tail_mask]
    flag_list = [(last_id == before_id).astype(jnp.float32)]
    same_list = [causal & (image_ids[:, None] == image_ids[None, :])]
    update_list = [
        jnp.einsum(
            "jhe,jhf->hef", tail_key, value_low[block_number], preferred_element_type=jnp.float32
        )
    ]
    total_list = [jnp.sum(tail_key.astype(jnp.float32), axis=0)]
    identity = (
        jnp.ones((), jnp.float32),
        jnp.zeros((head_count, HEAD, HEAD), jnp.float32),
        jnp.zeros((head_count, HEAD), jnp.float32),
    )
    combined = identity
    block_number = 0
    combined = combine(
        combined, (flag_list[block_number], update_list[block_number], total_list[block_number])
    )
    entering = prefix(combined, "seq", combine, identity, False)
    memory = entering[1]
    key_sum = entering[2]
    block_number = 0
    query_block = feat_query[block_number]
    keep_float = keep_list[block_number].astype(jnp.float32)
    memory_low = memory.astype(jnp.bfloat16)
    raw_scores = jnp.einsum(
        "the,jhe->htj", query_block, feat_key[block_number], preferred_element_type=jnp.float32
    )
    masked = jnp.where(same_list[block_number][None], raw_scores, 0.0)
    scores_low = masked.astype(jnp.bfloat16)
    carried = (
        jnp.einsum("the,hef->thf", query_block, memory_low, preferred_element_type=jnp.float32)
        * keep_float[:, None, None]
    )
    numerator = (
        jnp.einsum(
            "htj,jhf->thf", scores_low, value_low[block_number], preferred_element_type=jnp.float32
        )
        + carried
    )
    denominator = jnp.transpose(jnp.sum(masked, axis=2)) + keep_float[:, None] * jnp.sum(
        query_block.astype(jnp.float32) * key_sum[None], axis=2
    )
    memory_list = [memory_low]
    keysum_list = [key_sum]
    numer_list = [numerator]
    denom_list = [denominator]
    ratio_list = numerator / denominator[:, :, None]
    mixed_low = ratio_list.reshape(local_len, model_width).astype(jnp.bfloat16)
    middle_tokens = input_tokens + jnp.dot(mixed_low, out_full, preferred_element_type=jnp.float32)
    mlp_set = (
        lax.all_gather(up_projection_weight, ("dp", "seq"), axis=0, tiled=True),
        lax.all_gather(down_projection_weight, ("dp", "seq"), axis=0, tiled=True),
        lax.all_gather(second_gain, ("dp", "seq"), axis=0, tiled=True),
        lax.all_gather(second_shift, ("dp", "seq"), axis=0, tiled=True),
    )
    up_full = mlp_set[0]
    down_full = mlp_set[1]
    gain_two = mlp_set[2].astype(jnp.float32)
    shift_two = mlp_set[3].astype(jnp.float32)
    normed_two_low = layer_norm(middle_tokens, gain_two, shift_two).astype(jnp.bfloat16)
    upper_hidden = jnp.dot(normed_two_low, up_full, preferred_element_type=jnp.float32)
    active_low = jax.nn.gelu(upper_hidden).astype(jnp.bfloat16)
    result = middle_tokens + jnp.dot(active_low, down_full, preferred_element_type=jnp.float32)
    result_tokens = result.astype(jnp.bfloat16).reshape(1, local_len, model_width)
    grad_out = cotangent[0].astype(jnp.float32)
    mlp_again = (
        lax.all_gather(up_projection_weight, ("dp", "seq"), axis=0, tiled=True),
        lax.all_gather(down_projection_weight, ("dp", "seq"), axis=0, tiled=True),
        lax.all_gather(second_gain, ("dp", "seq"), axis=0, tiled=True),
        lax.all_gather(second_shift, ("dp", "seq"), axis=0, tiled=True),
    )
    up_back = mlp_again[0]
    down_back = mlp_again[1]
    grad_out_low = cotangent[0]
    grad_down = rows_product(active_low, grad_out_low)
    d_active = cols_product(grad_out_low, down_back)
    gelu_value, gelu_back = jax.vjp(jax.nn.gelu, upper_hidden)
    g_upper = gelu_back(d_active)[0].astype(jnp.bfloat16)
    grad_up = rows_product(normed_two_low, g_upper)
    d_normed_two = cols_product(g_upper, up_back)
    norm_value, norm_back = jax.vjp(layer_norm, middle_tokens, gain_two, shift_two)
    middle_part, grad_gain_two, grad_shift_two = norm_back(d_normed_two)
    g_middle = grad_out + middle_part
    attn_again = (
        lax.all_gather(query_key_value_weight, ("dp", "seq"), axis=0, tiled=True),
        lax.all_gather(attention_output_weight, ("dp", "seq"), axis=0, tiled=True),
        lax.all_gather(first_gain, ("dp", "seq"), axis=0, tiled=True),
        lax.all_gather(first_shift, ("dp", "seq"), axis=0, tiled=True),
    )
    in_back = attn_again[0]
    out_back = attn_again[1]
    g_middle_low = g_middle.astype(jnp.bfloat16)
    grad_out_weight = rows_product(mixed_low, g_middle_low)
    d_mixed = cols_product(g_middle_low, out_back).reshape(block_shape)
    block_number = 0
    query_block = feat_query[block_number]
    denominator = denom_list[block_number]
    g_numerator = (d_mixed[block_number] / denominator[:, :, None]).astype(jnp.bfloat16)
    g_denominator = -jnp.sum(d_mixed[block_number] * numer_list[block_number], axis=2) / (
        denominator * denominator
    )
    kept_query = jnp.where(keep_list[block_number][:, None, None], query_block, zero_low)
    gnum_list = [g_numerator]
    gden_list = [g_denominator]
    local_list = [
        jnp.einsum("the,thf->hef", kept_query, g_numerator, preferred_element_type=jnp.float32)
    ]
    localkey_list = [jnp.sum(kept_query.astype(jnp.float32) * g_denominator[:, :, None], axis=0)]
    combined = identity
    for block_number in reversed(range(block_count)):
        combined = combine(
            combined,
            (flag_list[block_number], local_list[block_number], localkey_list[block_number]),
        )
    leaving = prefix(combined, "seq", combine, identity, True)
    g_memory = leaving[1]
    g_key_sum = leaving[2]
    gq_list = []
    gk_list = []
    gv_list = []
    for block_number in reversed(range(block_count)):
        query_block = feat_query[block_number]
        key_block = feat_key[block_number]
        value_block = value_low[block_number]
        keep_float = keep_list[block_number].astype(jnp.float32)
        tail_float = tail_list[block_number].astype(jnp.float32)
        g_numerator = gnum_list[block_number]
        g_denominator = gden_list[block_number]
        g_update = g_memory.astype(jnp.bfloat16)
        raw_scores = jnp.einsum(
            "the,jhe->htj", query_block, key_block, preferred_element_type=jnp.float32
        )
        scores_low = jnp.where(same_list[block_number][None], raw_scores, 0.0).astype(jnp.bfloat16)
        g_scores = (
            jnp.einsum("thf,jhf->htj", g_numerator, value_block, preferred_element_type=jnp.float32)
            + jnp.transpose(g_denominator)[:, :, None]
        )
        g_scores_low = jnp.where(
            same_list[block_number][None], g_scores.astype(jnp.bfloat16), zero_low
        )
        query_grad = jnp.einsum(
            "htj,jhe->the", g_scores_low, key_block, preferred_element_type=jnp.float32
        )
        query_grad = query_grad + keep_float[:, None, None] * (
            jnp.einsum(
                "thf,hef->the",
                g_numerator,
                memory_list[block_number],
                preferred_element_type=jnp.float32,
            )
            + g_denominator[:, :, None] * keysum_list[block_number][None]
        )
        key_grad = jnp.einsum(
            "htj,the->jhe", g_scores_low, query_block, preferred_element_type=jnp.float32
        )
        key_grad = key_grad + tail_float[:, None, None] * (
            jnp.einsum("jhf,hef->jhe", value_block, g_update, preferred_element_type=jnp.float32)
            + g_key_sum[None]
        )
        tail_key = jnp.where(tail_list[block_number][:, None, None], key_block, zero_low)
        value_grad = jnp.einsum(
            "htj,thf->jhf", scores_low, g_numerator, preferred_element_type=jnp.float32
        )
        value_grad = value_grad + jnp.einsum(
            "jhe,hef->jhf", tail_key, g_update, preferred_element_type=jnp.float32
        )
        gq_list.append(query_grad)
        gk_list.append(key_grad)
        gv_list.append(value_grad)
        g_memory = local_list[block_number] + flag_list[block_number] * g_memory
        g_key_sum = localkey_list[block_number] + flag_list[block_number] * g_key_sum
    d_feat_query = jnp.concatenate(gq_list[::-1], axis=0).reshape(local_len, model_width)
    d_feat_key = jnp.concatenate(gk_list[::-1], axis=0).reshape(local_len, model_width)
    d_value = jnp.concatenate(gv_list[::-1], axis=0).reshape(local_len, model_width)
    query_value, query_back = jax.vjp(feature, queries)
    key_value, key_back = jax.vjp(feature, keys_raw)
    g_projected = jnp.concatenate(
        [query_back(d_feat_query)[0], key_back(d_feat_key)[0], d_value], axis=1
    ).astype(jnp.bfloat16)
    grad_in_weight = rows_product(normed_low, g_projected)
    d_normed = cols_product(g_projected, in_back)
    first_value, first_back = jax.vjp(layer_norm, input_tokens, gain_one, shift_one)
    input_part, grad_gain_one, grad_shift_one = first_back(d_normed)
    grad_tokens = (g_middle + input_part).reshape(1, local_len, model_width)
    summed = (
        lax.psum_scatter(grad_in_weight, ("dp", "seq"), scatter_dimension=0, tiled=True),
        lax.psum_scatter(grad_out_weight, ("dp", "seq"), scatter_dimension=0, tiled=True),
        lax.psum_scatter(grad_up, ("dp", "seq"), scatter_dimension=0, tiled=True),
        lax.psum_scatter(grad_down, ("dp", "seq"), scatter_dimension=0, tiled=True),
        lax.psum_scatter(grad_gain_one, ("dp", "seq"), scatter_dimension=0, tiled=True),
        lax.psum_scatter(grad_shift_one, ("dp", "seq"), scatter_dimension=0, tiled=True),
        lax.psum_scatter(grad_gain_two, ("dp", "seq"), scatter_dimension=0, tiled=True),
        lax.psum_scatter(grad_shift_two, ("dp", "seq"), scatter_dimension=0, tiled=True),
    )
    return (
        result_tokens,
        grad_tokens,
        summed[0],
        summed[1],
        summed[2],
        summed[3],
        summed[4],
        summed[5],
        summed[6],
        summed[7],
    )


MESH = pl.DeviceIdType.MESH
LOW = jnp.bfloat16
FULL = jnp.float32


class Place:
    def __init__(self):
        dp, seq = lax.axis_index("dp"), lax.axis_index("seq")
        self.y, self.x = dp // 2, dp % 2
        self.z, self.c = seq // 2, seq % 2
        self.dp, self.seq = dp, seq
        self.over_x = (self.y * 2 + 1 - self.x, seq)
        self.over_y = ((1 - self.y) * 2 + self.x, seq)
        self.sibling = (dp, self.z * 2 + 1 - self.c)
        self.following = [(dp, (seq + 1) % 8), (dp, (seq + 2) % 8)]
        self.preceding = [(dp, (seq + 7) % 8), (dp, (seq + 6) % 8)]
        self.over_end = (dp, (seq + 2 * self.c + 7) % 8)
        self.along_z = [(dp, (self.z + d) % 4 * 2 + self.c) for d in (1, 2, 3)]

    def meet(self):
        barrier = pltpu.get_barrier_semaphore()
        everyone = [self.over_x, self.over_y, self.sibling, self.over_end, *self.along_z]
        for device in everyone:
            pl.semaphore_signal(barrier, inc=1, device_id=device, device_id_type=MESH)
        pl.semaphore_wait(barrier, len(everyone))


def remote(source, target, send, recv, device):
    return pltpu.make_async_remote_copy(
        src_ref=source,
        dst_ref=target,
        send_sem=send,
        recv_sem=recv,
        device_id=device,
        device_id_type=MESH,
    )


class Gather:
    def __init__(self, place, full, send, recv):
        p = place
        half = full.shape[4] // 2
        low, high = pl.ds(0, half), pl.ds(half, half)
        own = full.at[p.y, p.x, p.z, p.c]
        parts = [(own, device) for device in p.along_z]
        parts.append((full.at[p.y, p.x, :, p.c, low], p.over_x))
        parts.append((full.at[p.y, p.x, :, p.c, high], p.over_y))
        parts.append((full.at[p.y, :, :, p.c, low], p.over_y))
        parts.append((full.at[:, p.x, :, p.c, high], p.over_x))
        for y, x in ((p.y, p.x), (p.y, 1 - p.x), (1 - p.y, p.x), (1 - p.y, 1 - p.x)):
            parts.append((full.at[y, x, :, p.c], p.sibling))
        self.copies = [
            remote(ref, ref, send.at[i], recv.at[i], device)
            for i, (ref, device) in enumerate(parts)
        ]

    def start(self, *which):
        for i in which:
            self.copies[i].start()

    def arrive(self, *which):
        for i in which:
            self.copies[i].wait_recv()

    def step(self, number):
        if number == 0:
            self.start(0, 1, 2)
        elif number == 1:
            self.arrive(0, 1, 2)
            self.start(3, 4, 7)
        elif number == 2:
            self.arrive(3, 4)
            self.start(5, 6)
        elif number == 3:
            self.arrive(5, 6)
            self.start(8, 9, 10)
        else:
            self.arrive(7, 8, 9, 10)

    def finish(self):
        for copy in self.copies:
            copy.wait_send()


class Scatter:
    def __init__(self, place, own, total, pair, first_a, first_b, second_a, second_b, last, send, recv, outside):
        p = place
        self.outside, self.released = outside, False
        half = own.shape[4] // 2
        self.place, self.half = p, half
        self.own, self.total, self.pair = own, total, pair
        self.first_a, self.first_b = first_a, first_b
        self.second_a, self.second_b = second_a, second_b
        self.last = last
        low, high = pl.ds(0, half), pl.ds(half, half)
        parts = [
            (own.at[:, :, :, 1 - p.c], pair, p.sibling),
            (total.at[1 - p.y, :, :, low], first_a, p.over_y),
            (total.at[:, 1 - p.x, :, high], first_b, p.over_x),
            (total.at[p.y, 1 - p.x, :, low], second_a, p.over_x),
            (total.at[1 - p.y, p.x, :, high], second_b, p.over_y),
        ]
        if outside:
            self.keep = pltpu.make_async_copy(own.at[:, :, :, p.c], total, send.at[8])
        for d in (1, 2, 3):
            parts.append((total.at[p.y, p.x, (p.z + d) % 4], last.at[d - 1], p.along_z[d - 1]))
        self.copies = [
            remote(source, target, send.at[i], recv.at[i], device)
            for i, (source, target, device) in enumerate(parts)
        ]

    def step(self, number):
        p, half = self.place, self.half
        low, high = slice(0, half), slice(half, 2 * half)
        total = self.total
        if number == 0:
            self.copies[0].start()
            if self.outside:
                self.keep.start()
        elif number == 1:
            if self.outside:
                self.keep.wait()
            self.copies[0].wait_recv()

            @pl.loop(0, 4)
            def _(i):
                y, x = i // 2, i % 2
                mine = total[y, x] if self.outside else self.own[y, x, :, p.c]
                total[y, x] = mine + self.pair[y, x]

            self.copies[1].start()
            self.copies[2].start()
        elif number == 2:
            self.copies[1].wait_recv()
            self.copies[2].wait_recv()
            for i in range(2):
                total[p.y, i, :, low] += self.first_a[i]
                total[i, p.x, :, high] += self.first_b[i]
            self.copies[3].start()
            self.copies[4].start()
        elif number == 3:
            self.copies[3].wait_recv()
            self.copies[4].wait_recv()
            total[p.y, p.x, :, low] += self.second_a[...]
            total[p.y, p.x, :, high] += self.second_b[...]
            for i in (5, 6, 7):
                self.copies[i].start()

    def result(self):
        for i in (5, 6, 7):
            self.copies[i].wait_recv()
        p = self.place
        value = self.total[p.y, p.x, p.z].astype(FULL)
        for d in range(3):
            value = value + self.last[d].astype(FULL)
        return value

    def release(self):
        self.copies[0].wait_send()
        self.released = True

    def finish(self):
        for copy in self.copies[1 if self.released else 0 :]:
            copy.wait_send()


class SmallGather(Gather):
    def __init__(self, place, full, send, recv):
        p = place
        own = full.at[p.y, p.x, p.z, p.c]
        parts = [(own, device) for device in p.along_z]
        parts.append((full.at[p.y, p.x, :, p.c], p.over_x))
        parts.append((full.at[p.y, :, :, p.c], p.over_y))
        for y in range(2):
            for x in range(2):
                parts.append((full.at[y, x, :, p.c], p.sibling))
        self.copies = [
            remote(ref, ref, send.at[i], recv.at[i], device)
            for i, (ref, device) in enumerate(parts)
        ]

    def step(self, number):
        if number == 0:
            self.start(0, 1, 2)
        elif number == 1:
            self.arrive(0, 1, 2)
            self.start(3)
        elif number == 2:
            self.arrive(3)
            self.start(4)
        elif number == 3:
            self.arrive(4)
            self.start(5, 6, 7, 8)
        else:
            self.arrive(5, 6, 7, 8)


def product(one, two):
    return jnp.dot(one, two, preferred_element_type=FULL)


def across(one, two):
    return lax.dot_general(one, two, (((1,), (1,)), ((), ())), preferred_element_type=FULL)


def down_rows(one, two):
    return lax.dot_general(one, two, (((0,), (0,)), ((), ())), preferred_element_type=FULL)


def tile(i, size):
    return pl.ds(pl.multiple_of(i * size, size), size)


def image_count(starts, at):
    total = jnp.where(starts[0, 0] <= at, 1, 0)
    for k in range(1, starts.shape[1]):
        total = total + jnp.where(starts[0, k] <= at, 1, 0)
    return total


class Images:
    def __init__(self, starts, seq, length):
        first = seq * length
        self.length = length
        self.column = image_count(starts, first + lax.broadcasted_iota(jnp.int32, (length, 128), 0))
        self.row = image_count(starts, first + lax.broadcasted_iota(jnp.int32, (8, length), 1))
        before = image_count(starts, first - 1)
        last = image_count(starts, first + length - 1)
        earlier = image_count(starts, first - length - 1)
        later = image_count(starts, first + 2 * length - 1)
        self.keep = jnp.where(self.column == before, 1.0, 0.0)
        self.tail = jnp.where(self.column == last, 1.0, 0.0)
        self.flag_before = jnp.where(before == earlier, 1.0, 0.0)
        self.flag_after = jnp.where(later == last, 1.0, 0.0)


def same_mask(images, rows, columns, transposed):
    shape = (images.length, images.length)
    down = lax.broadcasted_iota(jnp.int32, shape, 0)
    along = lax.broadcasted_iota(jnp.int32, shape, 1)
    order = down <= along if transposed else down >= along
    equal = images.column[:, :1] == images.row[:1, :]
    return jnp.where(order & equal, 1.0, 0.0).astype(LOW)


def head_lanes(rows):
    return lax.broadcasted_iota(jnp.int32, (rows, 128), 1) < HEAD


def own_block():
    return jnp.where(
        (lax.broadcasted_iota(jnp.int32, (128, 128), 0) < HEAD)
        == (lax.broadcasted_iota(jnp.int32, (128, 128), 1) < HEAD),
        1.0,
        0.0,
    ).astype(LOW)


def pack_pair(square):
    return jnp.where(head_lanes(HEAD), square[:HEAD], square[HEAD:])


def unpack_pair(packed):
    lanes = head_lanes(HEAD)
    zero = jnp.zeros_like(packed)
    return jnp.concatenate([jnp.where(lanes, packed, zero), jnp.where(lanes, zero, packed)], axis=0)


def statistics(values):
    average = jnp.mean(values, axis=-1, keepdims=True)
    centred = values - average
    spread = jnp.mean(centred * centred, axis=-1, keepdims=True)
    scale = lax.rsqrt(spread + 1e-05)
    return centred * scale, scale


def gelu_both(values):
    root = 0.7978845608028654
    square = values * values
    angle = jnp.tanh(root * values * (1.0 + 0.044715 * square))
    half = 0.5 + 0.5 * angle
    slope = half + 0.5 * values * (1.0 - angle * angle) * (root * (1.0 + 0.134145 * square))
    return values * half, slope


def forward_kernel(inputs, outputs, scratch):
    tokens_in, cotangent_in, starts, in_weight, out_weight, up_weight, down_weight, pack_in = inputs
    (
        in_full,
        out_full,
        up_full,
        down_full,
        grad_down_out,
        result_out,
        heads_out,
        mixed_out,
        inverse_out,
        middle_out,
        slope_out,
        memory_out,
        sums_out,
        gains_out,
    ) = outputs
    (
        wide,
        tall,
        pack,
        tokens,
        cotangent,
        gains,
        normed,
        heads,
        mask,
        mixed,
        mixed_low,
        inverse,
        middle,
        active,
        slope,
        grad_down,
        result,
        outgoing,
        incoming,
        memory,
        sums,
        send,
        recv,
        small_send,
        small_recv,
        state_send,
        state_recv,
        local,
        store,
    ) = scratch
    p = Place()
    length, width = tokens.shape
    loads = []
    for j in range(8):
        source = in_weight if j < 3 else (out_weight if j == 3 else up_weight)
        column = j if j < 3 else (0 if j == 3 else j - 4)
        loads.append((source.at[:, pl.ds(column * 1024, 1024)], wide.at[j, p.y, p.x, p.z, p.c]))
    for j in range(4):
        loads.append((down_weight.at[:, pl.ds(256 * j, 256)], tall.at[j, p.y, p.x, p.z, p.c]))
    loads.append((pack_in, pack.at[p.y, p.x, p.z, p.c]))
    loads.append((tokens_in, tokens))
    loads.append((cotangent_in, cotangent))
    loads = [pltpu.make_async_copy(a, b, local.at[i]) for i, (a, b) in enumerate(loads)]
    for i in (12, 0, 1, 2, 13, 3, 4, 5, 6, 7, 8, 9, 10, 11, 14):
        loads[i].start()
    stores = []

    def save(source, target):
        copy = pltpu.make_async_copy(source, target, store.at[len(stores)])
        copy.start()
        stores.append(copy)

    p.meet()
    small = SmallGather(p, pack, small_send, small_recv)
    chunks = [Gather(p, wide.at[j], send.at[j], recv.at[j]) for j in range(8)]
    chunks += [Gather(p, tall.at[j], send.at[8 + j], recv.at[8 + j]) for j in range(4)]

    def event(j, number):
        if not 0 <= j < 12:
            return
        if number == 0:
            loads[j].wait()
        chunks[j].step(number)
        if number == 4:
            if j < 8:
                target = in_full if j < 3 else (out_full if j == 3 else up_full)
                column = j if j < 3 else (0 if j == 3 else j - 4)
                save(wide.at[j], target.at[:, :, :, :, :, pl.ds(column * 1024, 1024)])
            else:
                save(tall.at[j - 8], down_full.at[:, :, :, :, :, pl.ds(256 * (j - 8), 256)])

    def weight(j, columns):
        return wide[j, :, :, :, :, :, columns].reshape(width, columns.size)

    images = Images(starts, p.seq, length)

    def first_norm():
        for y in range(2):
            for x in range(2):
                for k in range(2):
                    value = pack[y, x, 2 * k : 2 * k + 2].astype(FULL)
                    value = (value[0, 0] + value[0, 1]) + (value[1, 0] + value[1, 1])
                    at = 128 * ((y * 2 + x) * 2 + k)
                    gains[:, at : at + 128] = value
        save(gains, gains_out)
        loads[13].wait()

        @pl.loop(0, length // 128, unroll=2)
        def _(i):
            rows = tile(i, 128)
            value, _ = statistics(tokens[rows, :].astype(FULL))
            normed[rows, :] = (value * gains[0:1, :] + gains[1:2, :]).astype(LOW)

        mask[...] = same_mask(images, length, length, False)

    def project(j):
        @pl.loop(0, 2, unroll=2)
        def _(i):
            value = product(normed[...], weight(j, tile(i, 512)))
            if j < 2:
                value = jnp.where(value > 0, value + 1.0, jnp.exp(jnp.minimum(value, 0.0)))
            heads[j, :, tile(i, 512)] = value.astype(LOW)

    def update():
        tail = images.tail.astype(LOW)

        @pl.loop(0, 8, unroll=2)
        def _(i):
            lanes = tile(i, 128)
            key = heads[1, :, lanes] * tail
            square = down_rows(key, heads[2, :, lanes])
            outgoing[i, 0:HEAD] = pack_pair(square).astype(LOW)
            total = product(jnp.ones((16, length), LOW), key)
            outgoing[i, HEAD : HEAD + 16] = total.astype(LOW)

        save(heads, heads_out)
        for copy in state:
            copy.start()

    state = [
        remote(outgoing, incoming.at[d], state_send.at[d], state_recv.at[d], device)
        for d, device in enumerate(p.following)
    ]

    def enter():
        for copy in state:
            copy.wait_recv()

        @pl.loop(0, 8, unroll=2)
        def _(i):
            value = incoming[0, i].astype(FULL) + images.flag_before * incoming[1, i].astype(FULL)
            memory[i] = value[0:HEAD].astype(LOW)
            sums[i] = value[HEAD : HEAD + 8]

        save(memory, memory_out)
        save(sums, sums_out)

    def attend(begin, end):
        lanes_column = head_lanes(length)
        blocks = own_block()
        keep = images.keep.astype(LOW)
        half = length // 2
        identity = jnp.where(
            lax.broadcasted_iota(jnp.int32, (128, 128), 0)
            == lax.broadcasted_iota(jnp.int32, (128, 128), 1),
            1.0,
            0.0,
        )
        ones = jnp.ones((length, 128), LOW)

        @pl.loop(begin, end, unroll=2)
        def _(i):
            lanes = tile(i, 128)
            query, key, value = heads[0, :, lanes], heads[1, :, lanes], heads[2, :, lanes]
            wider = jnp.concatenate([value, ones], axis=1)
            parts = []
            for h in range(2):
                mine = lanes_column if h == 0 else ~lanes_column
                own = jnp.where(mine, query, jnp.zeros_like(query))
                upper = across(own[:half], key[:half]).astype(LOW) * mask[:half, :half]
                lower = across(own[half:], key).astype(LOW) * mask[half:, :]
                parts.append(
                    jnp.concatenate([product(upper, wider[:half]), product(lower, wider)], axis=0)
                )
            diagonal = (identity * sums[i, 0:1]).astype(LOW)
            right = jnp.concatenate(
                [unpack_pair(memory[i]), product(diagonal, blocks).astype(LOW)], axis=1
            )
            carried = product(query * keep, right)
            numerator = jnp.where(lanes_column, parts[0][:, :128], parts[1][:, :128])
            denominator = jnp.where(lanes_column, parts[0][:, 128:], parts[1][:, 128:])
            over = 1.0 / (denominator + carried[:, 128:])
            value = (numerator + carried[:, :128]) * over
            inverse[:, lanes] = over
            mixed[:, lanes] = value
            mixed_low[:, lanes] = value.astype(LOW)

    def join():
        save(mixed, mixed_out)
        save(inverse, inverse_out)

        @pl.loop(0, 2, unroll=2)
        def _(i):
            columns = tile(i, 512)
            middle[:, columns] = tokens[:, columns].astype(FULL) + product(
                mixed_low[...], weight(3, columns)
            )

        save(middle, middle_out)

    def second_norm():
        @pl.loop(0, length // 128, unroll=2)
        def _(i):
            rows = tile(i, 128)
            value, _ = statistics(middle[rows, :])
            normed[rows, :] = (value * gains[2:3, :] + gains[3:4, :]).astype(LOW)

    def raise_up(j):
        @pl.loop(0, 4, unroll=4)
        def _(i):
            value = product(normed[...], weight(4 + j, tile(i, 256)))
            columns = pl.ds(pl.multiple_of(j * 1024 + i * 256, 256), 256)
            value, steep = gelu_both(value)
            active[:, columns] = value.astype(LOW)
            slope[:, columns] = steep.astype(LOW)

        if j == 3:
            save(slope, slope_out)

    def down_gradient(begin, end):
        if begin == 0:
            loads[14].wait()

        @pl.loop(begin, end, unroll=4)
        def _(i):
            value = down_rows(active[:, tile(i, 512)], cotangent[...]).astype(LOW)
            y, x, z = i // 4, i // 2 % 2, i % 2 * 2
            for j in range(4):
                part = value[:, 256 * j : 256 * j + 256].reshape(2, 2, 128, 256)
                grad_down[j, y, x, pl.ds(z, 2)] = part

        if end == 8:
            save(grad_down, grad_down_out)

    def lower(j):
        columns = slice(256 * j, 256 * j + 256)

        @pl.loop(0, 2, unroll=2)
        def _(i):
            rows = tile(i, 256)
            value = product(active[rows, :], tall[j].reshape(4 * width, 256))
            result[rows, columns] = (middle[rows, columns] + value).astype(LOW)

        save(result.at[:, pl.ds(256 * j, 256)], result_out.at[:, pl.ds(256 * j, 256)])

    do = functools.partial
    work = {
        4: [lambda: None, first_norm],
        5: [do(project, 0)],
        6: [do(project, 1)],
        7: [do(project, 2), update],
        8: [lambda: None, lambda: None, enter],
        9: [do(attend, 0, 4), do(attend, 4, 6), do(attend, 6, 8)],
        10: [join, second_norm, do(raise_up, 0)],
        11: [do(raise_up, 1), do(raise_up, 2)],
        12: [do(raise_up, 3), do(down_gradient, 0, 4), do(down_gradient, 4, 8)],
        13: [do(lower, 0)],
        14: [do(lower, 1)],
        15: [do(lower, 2)],
    }
    loads[12].wait()
    small.step(0)
    for tick in range(12 + 4):
        todo = work.get(tick, []) + [lambda: None] * 3
        event(tick, 0)
        event(tick - 1, 1)
        if 1 <= tick < 5:
            small.step(tick)
        todo[0]()
        event(tick - 2, 2)
        todo[1]()
        event(tick - 3, 3)
        event(tick - 4, 4)
        todo[2]()
    lower(3)
    small.finish()
    for copy in state:
        copy.wait_send()
    for chunk in chunks:
        chunk.finish()
    for copy in stores:
        copy.wait()


def forward_pass(tokens, cotangent, starts, in_weight, out_weight, up_weight, down_weight, pack):
    length, width = tokens.shape
    block = lambda rows, columns: jax.ShapeDtypeStruct((2, 2, 4, 2, rows, columns), LOW)
    shape = jax.ShapeDtypeStruct

    def body(*refs):
        forward_kernel(refs[:8], refs[8:22], refs[22:])

    return pl.pallas_call(
        body,
        out_shape=[
            block(32, 3072),
            block(32, 1024),
            block(32, 4096),
            block(128, 1024),
            shape((4, 2, 2, 4, 2, 128, 256), LOW),
            shape((length, width), LOW),
            shape((3, length, width), LOW),
            shape((length, width), FULL),
            shape((length, width), FULL),
            shape((length, width), FULL),
            shape((length, 4 * width), LOW),
            shape((8, HEAD, 128), LOW),
            shape((8, 8, 128), FULL),
            shape((16, width), FULL),
        ],
        in_specs=[
            pl.BlockSpec(memory_space=pltpu.SMEM if i == 2 else pl.ANY) for i in range(8)
        ],
        out_specs=[pl.BlockSpec(memory_space=pl.ANY)] * 14,
        scratch_shapes=[
            pltpu.VMEM((8, 2, 2, 4, 2, 32, 1024), LOW),
            pltpu.VMEM((4, 2, 2, 4, 2, 128, 256), LOW),
            pltpu.VMEM((2, 2, 4, 2, 16, 128), LOW),
            pltpu.VMEM((length, width), LOW),
            pltpu.VMEM((length, width), LOW),
            pltpu.VMEM((16, width), FULL),
            pltpu.VMEM((length, width), LOW),
            pltpu.VMEM((3, length, width), LOW),
            pltpu.VMEM((length, length), LOW),
            pltpu.VMEM((length, width), FULL),
            pltpu.VMEM((length, width), LOW),
            pltpu.VMEM((length, width), FULL),
            pltpu.VMEM((length, width), FULL),
            pltpu.VMEM((length, 4 * width), LOW),
            pltpu.VMEM((length, 4 * width), LOW),
            pltpu.VMEM((4, 2, 2, 4, 2, 128, 256), LOW),
            pltpu.VMEM((length, width), LOW),
            pltpu.VMEM((8, HEAD + 16, 128), LOW),
            pltpu.VMEM((2, 8, HEAD + 16, 128), LOW),
            pltpu.VMEM((8, HEAD, 128), LOW),
            pltpu.VMEM((8, 8, 128), FULL),
            pltpu.SemaphoreType.DMA((12, 11)),
            pltpu.SemaphoreType.DMA((12, 11)),
            pltpu.SemaphoreType.DMA((9,)),
            pltpu.SemaphoreType.DMA((9,)),
            pltpu.SemaphoreType.DMA((2,)),
            pltpu.SemaphoreType.DMA((2,)),
            pltpu.SemaphoreType.DMA((15,)),
            pltpu.SemaphoreType.DMA((26,)),
        ],
        compiler_params=pltpu.CompilerParams(
            collective_id=0, has_side_effects=True, vmem_limit_bytes=62 << 20
        ),
        name="forward_pass",
    )(tokens, cotangent, starts, in_weight, out_weight, up_weight, down_weight, pack)


def scatter_buffers(count, rows, columns):
    half = rows // 2
    shapes = [
        (2, 2, 4, rows, columns),
        (2, 2, 4, rows, columns),
        (2, 4, half, columns),
        (2, 4, half, columns),
        (4, half, columns),
        (4, half, columns),
        (3, rows, columns),
    ]
    return [pltpu.VMEM((count, *shape), LOW) for shape in shapes]


class Sum:
    def __init__(self, place, stages, landed, send, recv):
        p = place
        devices = [p.sibling, p.over_x, p.over_y, *p.along_z]
        self.stages, self.landed = stages, landed
        self.copies = [
            remote(stages.at[min(i, 3)], landed.at[i], send.at[i], recv.at[i], device)
            for i, device in enumerate(devices)
        ]

    def step(self, number):
        stages, landed = self.stages, self.landed
        if 1 <= number <= 3:
            self.copies[number - 1].wait_recv()
            stages[number] = stages[number - 1] + landed[number - 1]
        if number < 3:
            self.copies[number].start()
        elif number == 3:
            for i in (3, 4, 5):
                self.copies[i].start()

    def result(self):
        for i in (3, 4, 5):
            self.copies[i].wait_recv()
        return (self.stages[3] + self.landed[3]) + (self.landed[4] + self.landed[5])

    def finish(self):
        for copy in self.copies:
            copy.wait_send()


def backward_kernel(inputs, outputs, tall, wide, scratch):
    (
        tokens_in,
        cotangent_in,
        starts,
        in_full,
        out_full,
        up_full,
        down_full,
        grad_down_in,
        heads_in,
        mixed_in,
        inverse_in,
        middle_in,
        slope_in,
        memory_in,
        sums_in,
        gains_in,
    ) = inputs
    (
        cotangent,
        normed,
        slab,
        broad,
        grad_middle,
        inner,
        mixed,
        inverse,
        memory,
        sums,
        gains,
        mask,
        mask_back,
        parts,
        done_in,
        done_out,
        done_up,
        done_down,
        stages,
        landed,
        outgoing,
        incoming,
        update,
        key_update,
        send,
        recv,
        sum_send,
        sum_recv,
        state_send,
        state_recv,
        local,
        stream,
        store,
    ) = scratch
    p = Place()
    length, width = cotangent.shape

    pairs = [
        (cotangent_in, cotangent),
        (slope_in, broad),
        (middle_in, grad_middle),
        (gains_in, gains),
        (memory_in, memory),
        (sums_in, sums),
        (mixed_in, mixed),
        (inverse_in, inverse),
        (tokens_in, cotangent),
    ]
    pairs += [(heads_in.at[k], broad.at[:, pl.ds(1024 * k, 1024)]) for k in range(3)]
    loads = [pltpu.make_async_copy(a, b, local.at[i]) for i, (a, b) in enumerate(pairs)]
    slabs = [down_full.at[pl.ds(1024 * j, 1024), :] for j in range(4)]
    slabs += [up_full.at[:, pl.ds(1024 * j, 1024)] for j in range(4)]
    slabs += [out_full]
    slabs += [in_full.at[:, pl.ds(1024 * j, 1024)] for j in range(3)]
    slabs = [
        pltpu.make_async_copy(source, slab.at[i % 2], stream.at[i]) for i, source in enumerate(slabs)
    ]
    order = [8, 9, 10, 11, 4, 5, 6, 7, 3, 0, 1, 2]
    room = {4: 0, 5: 1, 6: 2, 7: 0, 3: 1, 0: 2, 1: 0, 2: 1}
    chunks = []
    for j in range(12):
        if j < 8:
            first, *others = [ref.at[j] for ref in wide]
            buffers = [first, first, *others]
            own = parts.at[room[j]]
        else:
            buffers = [ref.at[j - 8] for ref in tall]
            own = grad_down_in.at[j - 8]
        chunks.append(Scatter(p, own, *buffers, send.at[j], recv.at[j], j >= 8))

    p.meet()
    chunks[8].step(0)
    for i in range(4):
        loads[i].start()
    slabs[0].start()
    slabs[1].start()
    for i in range(4, 8):
        loads[i].start()
    stores = []

    def save(source, target):
        copy = pltpu.make_async_copy(source, target, store.at[len(stores)])
        copy.start()
        stores.append(copy)

    def event(position, number):
        if not 0 <= position < 12:
            return
        j = order[position]
        if number < 4:
            if (j, number) != (8, 0):
                chunks[j].step(number)
            return
        if j < 8:
            target, k = (done_in, j) if j < 3 else ((done_out, 0) if j == 3 else (done_up, j - 4))
            size = 1024
        else:
            target, k, size = done_down, j - 8, 256
        where = outputs[0 if j < 3 else 1 if j == 3 else 2 if j < 8 else 3]
        target[:, size * k : size * k + size] = chunks[j].result()
        save(target.at[:, pl.ds(size * k, size)], where.at[:, pl.ds(size * k, size)])

    images = Images(starts, p.seq, length)

    def second_norm():
        loads[2].wait()
        loads[3].wait()

        @pl.loop(0, length // 128, unroll=2)
        def _(i):
            rows = tile(i, 128)
            value, _ = statistics(grad_middle[rows, :])
            normed[rows, :] = (value * gains[2:3, :] + gains[3:4, :]).astype(LOW)

    def active_gradient(j):
        if j == 0:
            loads[0].wait()
            loads[1].wait()
        slabs[j].wait()

        @pl.loop(0, 4, unroll=4)
        def _(i):
            columns = pl.ds(pl.multiple_of(1024 * j + 256 * i, 256), 256)
            value = across(cotangent[...], slab[j % 2, tile(i, 256), :])
            broad[:, columns] = (value * broad[:, columns].astype(FULL)).astype(LOW)

        slabs[j + 2].start()

    def weight_gradient(j, left, right):
        at = room[j]

        @pl.loop(0, 4, unroll=4)
        def _(i):
            value = down_rows(left(tile(i, 256)), right()).astype(LOW)
            parts[at, i // 2, i % 2] = value.reshape(4, 2, 32, 1024)

    def up_gradient(j):
        if j == 3:
            chunks[4].release()
        weight_gradient(
            4 + j,
            lambda columns: normed[:, columns],
            lambda: broad[:, 1024 * j : 1024 * j + 1024],
        )
        if j == 3:
            for k in range(9, 12):
                loads[k].start()

    def inner_gradient(first, j):
        slabs[first + j].wait()

        @pl.loop(0, 4, unroll=4)
        def _(i):
            columns = tile(i, 256)
            value = across(
                broad[:, 1024 * j : 1024 * j + 1024], slab[(first + j) % 2, columns, :]
            )
            if j > 0:
                value = value + inner[:, columns]
            inner[:, columns] = value

        if first + j + 2 < 12:
            slabs[first + j + 2].start()

    def norm_gradient(rows, values, gain):
        unit, scale = statistics(values)
        given = inner[rows, :]
        scaled = given * gain
        one = jnp.mean(scaled, axis=-1, keepdims=True)
        two = jnp.mean(scaled * unit, axis=-1, keepdims=True)
        return scale * (scaled - one - unit * two), given * unit, given

    def fold(values):
        return jnp.sum(values, axis=0, keepdims=True)

    def middle_gradient():
        stages[0] = jnp.zeros((8, width), FULL)

        @pl.loop(0, length // 128, unroll=2)
        def _(i):
            rows = tile(i, 128)
            value, gain, shift = norm_gradient(rows, grad_middle[rows, :], gains[2:3, :])
            stages[0, 2:3, :] += fold(gain)
            stages[0, 3:4, :] += fold(shift)
            value = value + cotangent[rows, :].astype(FULL)
            grad_middle[rows, :] = value
            cotangent[rows, :] = value.astype(LOW)

    def output_gradient():
        loads[6].wait()
        chunks[5].release()
        weight_gradient(
            3, lambda columns: mixed[:, columns].astype(LOW), lambda: cotangent[...]
        )
        loads[8].start()

    def mixed_gradient():
        slabs[8].wait()

        @pl.loop(0, 4, unroll=4)
        def _(i):
            columns = tile(i, 256)
            inner[:, columns] = across(cotangent[...], slab[0, columns, :])

        slabs[10].start()

    state = [
        remote(outgoing, incoming.at[d], state_send.at[d], state_recv.at[d], device)
        for d, device in enumerate(p.preceding)
    ]

    def numerator_gradient():
        for i in (4, 5, 7, 9, 10, 11):
            loads[i].wait()
        blocks = own_block()
        doubled = jnp.concatenate([blocks, blocks], axis=0)

        @pl.loop(0, 8, unroll=2)
        def _(i):
            lanes = tile(i, 128)
            given, over = inner[:, lanes], inverse[:, lanes]
            numerator = (given * over).astype(LOW)
            each = given * mixed[:, lanes]
            high = each.astype(LOW)
            rest = (each - high.astype(FULL)).astype(LOW)
            slant = product(jnp.concatenate([high, rest], axis=1), doubled) * over * -1.0
            mixed[:, lanes] = slant
            broad[:, pl.ds(pl.multiple_of(3072 + 128 * i, 128), 128)] = numerator
            kept = broad[:, lanes].astype(FULL) * images.keep
            square = down_rows(kept.astype(LOW), numerator)
            outgoing[i, 0:HEAD] = pack_pair(square).astype(LOW)
            total = fold(kept * slant)
            outgoing[i, HEAD : HEAD + 16] = jnp.broadcast_to(total, (16, 128)).astype(LOW)

        for copy in state:
            copy.start()
        mask[...] = same_mask(images, length, length, False)
        mask_back[...] = same_mask(images, length, length, True)

    def enter():
        for copy in state:
            copy.wait_recv()
        flag = jnp.where(p.seq == 7, 0.0, images.flag_after)

        @pl.loop(0, 8, unroll=2)
        def _(i):
            value = incoming[0, i].astype(FULL) + flag * incoming[1, i].astype(FULL)
            update[i] = value[0:HEAD].astype(LOW)
            key_update[i] = value[HEAD : HEAD + 8]

    def attend(begin, end):
        if begin == 0:
            enter()
        if end == 8:
            first_norm()
        first = head_lanes(length)
        lane = lax.broadcasted_iota(jnp.int32, (length, 128), 1)
        ones = jnp.ones((length, 128), LOW)
        zero = jnp.zeros((length, 128), LOW)
        half = length // 2

        @pl.loop(begin, end)
        def _(i):
            at = [pl.ds(pl.multiple_of(1024 * k + 128 * i, 128), 128) for k in range(4)]
            query, key, value, numerator = [broad[:, lanes] for lanes in at]
            slant = mixed[:, at[0]]
            high = slant.astype(LOW)
            rest = (slant - high.astype(FULL)).astype(LOW)
            right = jnp.concatenate([value, ones], axis=1)
            grads = []
            for h in range(2):
                mine = first if h == 0 else ~first
                own_query = jnp.where(mine, query, zero)
                left = jnp.concatenate(
                    [
                        jnp.where(mine, numerator, zero),
                        jnp.where(
                            lane == HEAD * h, high, jnp.where(lane == HEAD * h + 1, rest, zero)
                        ),
                    ],
                    axis=1,
                )
                upper = across(left[:half], right[:half]).astype(LOW) * mask[:half, :half]
                lower = across(left[half:], right).astype(LOW) * mask[half:, :]
                for_query = jnp.concatenate([product(upper, key[:half]), product(lower, key)], axis=0)
                upper = across(right[:half], left).astype(LOW) * mask_back[:half, :]
                lower = across(right[half:], left[half:]).astype(LOW) * mask_back[half:, half:]
                for_key = jnp.concatenate(
                    [product(upper, query), product(lower, query[half:])], axis=0
                )
                upper = across(key[:half], own_query).astype(LOW) * mask_back[:half, :]
                lower = across(key[half:], own_query[half:]).astype(LOW) * mask_back[half:, half:]
                for_value = jnp.concatenate(
                    [product(upper, numerator), product(lower, numerator[half:])], axis=0
                )
                grads.append((for_query, for_key, for_value))
            for_query, for_key, for_value = [
                jnp.where(first, one, two) for one, two in zip(*grads, strict=True)
            ]
            keep, tail = images.keep, images.tail
            for_query = for_query + keep * (
                across(numerator, unpack_pair(memory[i])) + slant * sums[i, 0:1]
            )
            square = unpack_pair(update[i])
            for_key = for_key + tail * (across(value, square) + key_update[i, 0:1])
            for_value = for_value + product(key * tail.astype(LOW), square)
            broad[:, at[0]] = (for_query * jnp.minimum(query.astype(FULL), 1.0)).astype(LOW)
            broad[:, at[1]] = (for_key * jnp.minimum(key.astype(FULL), 1.0)).astype(LOW)
            broad[:, at[2]] = for_value.astype(LOW)

    def first_norm():
        loads[8].wait()

        @pl.loop(0, length // 128, unroll=2)
        def _(i):
            rows = tile(i, 128)
            value, _ = statistics(cotangent[rows, :].astype(FULL))
            normed[rows, :] = (value * gains[0:1, :] + gains[1:2, :]).astype(LOW)

    def in_gradient(j):
        chunks[(6, 7, 3)[j]].release()
        weight_gradient(
            j,
            lambda columns: normed[:, columns],
            lambda: broad[:, 1024 * j : 1024 * j + 1024],
        )

    total = Sum(p, stages, landed, sum_send, sum_recv)

    def token_gradient():
        @pl.loop(0, length // 128, unroll=2)
        def _(i):
            rows = tile(i, 128)
            value, gain, shift = norm_gradient(rows, cotangent[rows, :].astype(FULL), gains[0:1, :])
            stages[0, 0:1, :] += fold(gain)
            stages[0, 1:2, :] += fold(shift)
            grad_middle[rows, :] += value

        save(grad_middle, outputs[4])
        total.step(0)

    do = functools.partial
    work = {
        1: [do(active_gradient, 0), do(active_gradient, 1), do(active_gradient, 2)],
        2: [do(active_gradient, 3), second_norm, do(up_gradient, 0)],
        3: [do(up_gradient, 1), do(up_gradient, 2), do(inner_gradient, 4, 0)],
        4: [do(inner_gradient, 4, 1), do(inner_gradient, 4, 2), do(inner_gradient, 4, 3)],
        5: [do(up_gradient, 3), middle_gradient, mixed_gradient],
        6: [output_gradient, numerator_gradient],
        7: [lambda: None, do(attend, 0, 1), do(attend, 1, 3)],
        8: [do(attend, 3, 5), do(attend, 5, 7), do(attend, 7, 8)],
        9: [do(in_gradient, 1), do(in_gradient, 2), do(inner_gradient, 9, 0)],
        10: [
            do(inner_gradient, 9, 1),
            do(inner_gradient, 9, 2),
            token_gradient,
        ],
        11: [lambda: None, do(total.step, 1)],
        12: [lambda: None, do(total.step, 2)],
        13: [lambda: None, do(total.step, 3)],
    }
    for tick in range(12 + 6):
        todo = work.get(tick, []) + [lambda: None] * 3
        if tick == 9:
            in_gradient(0)
        event(tick, 0)
        event(tick - 1, 1)
        todo[0]()
        event(tick - 2, 2)
        todo[1]()
        event(tick - 3, 3)
        event(tick - 6, 4)
        todo[2]()
    total_value = total.result()
    landed[0] = total_value
    group = (p.dp * 8 + p.seq) // 4
    mine = landed[0, :, tile(group, 128)]
    mine = pltpu.roll(mine, (128 - 32 * (p.seq % 4)) % 128, 1)
    for k in range(4):
        outputs[5 + k][...] = mine[k : k + 1, 0:32]
    total.finish()
    for copy in state:
        copy.wait_send()
    for chunk in chunks:
        chunk.finish()
    for copy in stores:
        copy.wait()


def backward_pass(*inputs):
    length, width = inputs[0].shape
    shape = jax.ShapeDtypeStruct
    vmem = pltpu.VMEM
    tall = scatter_buffers(4, 128, 256)
    wide = scatter_buffers(8, 32, 1024)[1:]

    def body(*refs):
        backward_kernel(refs[:16], refs[16:25], refs[25:32], refs[32:38], refs[38:])

    return pl.pallas_call(
        body,
        out_shape=[
            shape((32, 3072), FULL),
            shape((32, 1024), FULL),
            shape((32, 4096), FULL),
            shape((128, 1024), FULL),
            shape((length, width), FULL),
            *[shape((1, 32), FULL)] * 4,
        ],
        in_specs=[
            pl.BlockSpec(memory_space=pltpu.SMEM if i == 2 else pl.ANY) for i in range(16)
        ],
        out_specs=[pl.BlockSpec(memory_space=pl.ANY)] * 5
        + [pl.BlockSpec(memory_space=pltpu.VMEM)] * 4,
        scratch_shapes=[
            *tall,
            *wide,
            vmem((length, width), LOW),
            vmem((length, width), LOW),
            vmem((2, width, width), LOW),
            vmem((length, 4 * width), LOW),
            vmem((length, width), FULL),
            vmem((length, width), FULL),
            vmem((length, width), FULL),
            vmem((length, width), FULL),
            vmem((8, HEAD, 128), LOW),
            vmem((8, 8, 128), FULL),
            vmem((16, width), FULL),
            vmem((length, length), LOW),
            vmem((length, length), LOW),
            vmem((3, 2, 2, 4, 2, 32, 1024), LOW),
            vmem((32, 3072), FULL),
            vmem((32, 1024), FULL),
            vmem((32, 4096), FULL),
            vmem((128, 1024), FULL),
            vmem((4, 8, width), FULL),
            vmem((6, 8, width), FULL),
            vmem((8, HEAD + 16, 128), LOW),
            vmem((2, 8, HEAD + 16, 128), LOW),
            vmem((8, HEAD, 128), LOW),
            vmem((8, 8, 128), FULL),
            pltpu.SemaphoreType.DMA((12, 9)),
            pltpu.SemaphoreType.DMA((12, 8)),
            pltpu.SemaphoreType.DMA((6,)),
            pltpu.SemaphoreType.DMA((6,)),
            pltpu.SemaphoreType.DMA((2,)),
            pltpu.SemaphoreType.DMA((2,)),
            pltpu.SemaphoreType.DMA((12,)),
            pltpu.SemaphoreType.DMA((12,)),
            pltpu.SemaphoreType.DMA((13,)),
        ],
        compiler_params=pltpu.CompilerParams(
            collective_id=1, has_side_effects=True, vmem_limit_bytes=62 << 20
        ),
        name="backward_pass",
    )(*inputs)


def on_device(
    tokens,
    starts,
    query_key_value_weight,
    attention_output_weight,
    up_projection_weight,
    down_projection_weight,
    first_gain,
    first_shift,
    second_gain,
    second_shift,
    cotangent,
):
    mine = lax.axis_index("dp") * 8 + lax.axis_index("seq")
    pack = jnp.stack([first_gain, first_shift, second_gain, second_shift]).astype(FULL)
    pack = jnp.roll(jnp.pad(pack, ((0, 12), (0, 96))), 32 * (mine % 4), axis=1).astype(LOW)
    in_full, out_full, up_full, down_full, grad_down, result, *saved = forward_pass(
        tokens[0],
        cotangent[0],
        starts,
        query_key_value_weight,
        attention_output_weight,
        up_projection_weight,
        down_projection_weight,
        pack,
    )
    grads = backward_pass(
        tokens[0],
        cotangent[0],
        starts,
        in_full.reshape(1024, 3072),
        out_full.reshape(1024, 1024),
        up_full.reshape(1024, 4096),
        down_full.reshape(4096, 1024),
        grad_down,
        *saved,
    )
    vectors = [grad.reshape(32) for grad in grads[5:]]
    return (result[None], grads[4][None], *grads[:4], *vectors)


def solution(mesh):

    fast = dict(mesh.shape) == {"dp": 4, "seq": 8}
    return jax.shard_map(
        on_device if fast else on_device_general,
        mesh=mesh,
        in_specs=(
            P("dp", "seq", None),
            P("dp", None),
            P(("dp", "seq"), None),
            P(("dp", "seq"), None),
            P(("dp", "seq"), None),
            P(("dp", "seq"), None),
            P(("dp", "seq")),
            P(("dp", "seq")),
            P(("dp", "seq")),
            P(("dp", "seq")),
            P("dp", "seq", None),
        ),
        out_specs=(
            P("dp", "seq", None),
            P("dp", "seq", None),
            P(("dp", "seq"), None),
            P(("dp", "seq"), None),
            P(("dp", "seq"), None),
            P(("dp", "seq"), None),
            P(("dp", "seq")),
            P(("dp", "seq")),
            P(("dp", "seq")),
            P(("dp", "seq")),
        ),
        check_vma=False,
    )
```

```python
import functools

import jax
import jax.numpy as jnp
from jax import lax
from jax.experimental import pallas as pl
from jax.experimental.pallas import tpu as pltpu
from jax.sharding import PartitionSpec as P

HEAD = 64
BLOCK = 512


def prefix(value, axis, combine, identity, reverse):
    size, mine = (lax.axis_size(axis), lax.axis_index(axis))
    everything = jax.tree.map(
        lambda part, kind: lax.all_gather(part.astype(kind), axis),
        value,
        jax.tree.map(lambda a: jnp.bfloat16 if a.dtype == jnp.float32 else a.dtype, value),
    )
    start = jax.tree.map(
        lambda part, zero: jnp.broadcast_to(jnp.asarray(zero, part.dtype), part.shape),
        value,
        identity,
    )

    def lap(k, before):
        at = size - 1 - k if reverse else k
        reached = at > mine if reverse else at < mine
        new = combine(
            before, jax.tree.map(lambda part, own: part[at].astype(own.dtype), everything, value)
        )
        return jax.tree.map(lambda a, b: jnp.where(reached, a, b), new, before)

    return lax.fori_loop(0, size, lap, start)


def layer_norm(values, norm_gain, norm_shift):
    average = jnp.mean(values, axis=-1, keepdims=True)
    centred = values - average
    spread = jnp.mean(centred * centred, axis=-1, keepdims=True)
    return centred * lax.rsqrt(spread + 1e-05) * norm_gain + norm_shift


def feature(values):
    return jax.nn.elu(values) + 1.0


def combine(former, latter):
    return (
        former[0] * latter[0],
        latter[0] * former[1] + latter[1],
        latter[0] * former[2] + latter[2],
    )


def rows_product(factor_one, factor_two):
    return lax.dot_general(
        factor_one, factor_two, (((0,), (0,)), ((), ())), preferred_element_type=jnp.float32
    )


def cols_product(factor_one, factor_two):
    return lax.dot_general(
        factor_one, factor_two, (((1,), (1,)), ((), ())), preferred_element_type=jnp.float32
    )


def on_device_general(
    tokens,
    starts,
    query_key_value_weight,
    attention_output_weight,
    up_projection_weight,
    down_projection_weight,
    first_gain,
    first_shift,
    second_gain,
    second_shift,
    cotangent,
):
    local_len = tokens.shape[1]
    model_width = tokens.shape[2]
    head_count = model_width // HEAD
    block_count = local_len // BLOCK
    block_shape = (block_count, BLOCK, head_count, HEAD)
    zero_low = jnp.zeros((), jnp.bfloat16)
    input_tokens = tokens[0].astype(jnp.float32)
    first_pos = lax.axis_index("seq") * local_len
    positions = first_pos + jnp.arange(local_len, dtype=jnp.int32)
    pack_starts = starts[0]
    image_ids = jnp.sum((pack_starts[None, :] <= positions[:, None]).astype(jnp.int32), axis=1) - 1
    before_id = jnp.sum((pack_starts <= first_pos - 1).astype(jnp.int32)) - 1
    causal = jnp.arange(BLOCK)[:, None] >= jnp.arange(BLOCK)[None, :]
    attn_set = (
        lax.all_gather(query_key_value_weight, ("dp", "seq"), axis=0, tiled=True),
        lax.all_gather(attention_output_weight, ("dp", "seq"), axis=0, tiled=True),
        lax.all_gather(first_gain, ("dp", "seq"), axis=0, tiled=True),
        lax.all_gather(first_shift, ("dp", "seq"), axis=0, tiled=True),
    )
    in_full = attn_set[0]
    out_full = attn_set[1]
    gain_one = attn_set[2].astype(jnp.float32)
    shift_one = attn_set[3].astype(jnp.float32)
    first_normed_tokens = layer_norm(input_tokens, gain_one, shift_one)
    normed_low = first_normed_tokens.astype(jnp.bfloat16)
    projected_tokens = jnp.dot(normed_low, in_full, preferred_element_type=jnp.float32)
    queries = projected_tokens[:, :model_width]
    keys_raw = projected_tokens[:, model_width : 2 * model_width]
    values_raw = projected_tokens[:, 2 * model_width :]
    feat_query = feature(queries).astype(jnp.bfloat16).reshape(block_shape)
    feat_key = feature(keys_raw).astype(jnp.bfloat16).reshape(block_shape)
    value_low = values_raw.astype(jnp.bfloat16).reshape(block_shape)
    block_number = 0
    last_id = image_ids[-1]
    tail_mask = image_ids == last_id
    tail_key = jnp.where(tail_mask[:, None, None], feat_key[block_number], zero_low)
    keep_list = [image_ids == before_id]
    tail_list = [tail_mask]
    flag_list = [(last_id == before_id).astype(jnp.float32)]
    same_list = [causal & (image_ids[:, None] == image_ids[None, :])]
    update_list = [
        jnp.einsum(
            "jhe,jhf->hef", tail_key, value_low[block_number], preferred_element_type=jnp.float32
        )
    ]
    total_list = [jnp.sum(tail_key.astype(jnp.float32), axis=0)]
    identity = (
        jnp.ones((), jnp.float32),
        jnp.zeros((head_count, HEAD, HEAD), jnp.float32),
        jnp.zeros((head_count, HEAD), jnp.float32),
    )
    combined = identity
    block_number = 0
    combined = combine(
        combined, (flag_list[block_number], update_list[block_number], total_list[block_number])
    )
    entering = prefix(combined, "seq", combine, identity, False)
    memory = entering[1]
    key_sum = entering[2]
    block_number = 0
    query_block = feat_query[block_number]
    keep_float = keep_list[block_number].astype(jnp.float32)
    memory_low = memory.astype(jnp.bfloat16)
    raw_scores = jnp.einsum(
        "the,jhe->htj", query_block, feat_key[block_number], preferred_element_type=jnp.float32
    )
    masked = jnp.where(same_list[block_number][None], raw_scores, 0.0)
    scores_low = masked.astype(jnp.bfloat16)
    carried = (
        jnp.einsum("the,hef->thf", query_block, memory_low, preferred_element_type=jnp.float32)
        * keep_float[:, None, None]
    )
    numerator = (
        jnp.einsum(
            "htj,jhf->thf", scores_low, value_low[block_number], preferred_element_type=jnp.float32
        )
        + carried
    )
    denominator = jnp.transpose(jnp.sum(masked, axis=2)) + keep_float[:, None] * jnp.sum(
        query_block.astype(jnp.float32) * key_sum[None], axis=2
    )
    memory_list = [memory_low]
    keysum_list = [key_sum]
    numer_list = [numerator]
    denom_list = [denominator]
    ratio_list = numerator / denominator[:, :, None]
    mixed_low = ratio_list.reshape(local_len, model_width).astype(jnp.bfloat16)
    middle_tokens = input_tokens + jnp.dot(mixed_low, out_full, preferred_element_type=jnp.float32)
    mlp_set = (
        lax.all_gather(up_projection_weight, ("dp", "seq"), axis=0, tiled=True),
        lax.all_gather(down_projection_weight, ("dp", "seq"), axis=0, tiled=True),
        lax.all_gather(second_gain, ("dp", "seq"), axis=0, tiled=True),
        lax.all_gather(second_shift, ("dp", "seq"), axis=0, tiled=True),
    )
    up_full = mlp_set[0]
    down_full = mlp_set[1]
    gain_two = mlp_set[2].astype(jnp.float32)
    shift_two = mlp_set[3].astype(jnp.float32)
    normed_two_low = layer_norm(middle_tokens, gain_two, shift_two).astype(jnp.bfloat16)
    upper_hidden = jnp.dot(normed_two_low, up_full, preferred_element_type=jnp.float32)
    active_low = jax.nn.gelu(upper_hidden).astype(jnp.bfloat16)
    result = middle_tokens + jnp.dot(active_low, down_full, preferred_element_type=jnp.float32)
    result_tokens = result.astype(jnp.bfloat16).reshape(1, local_len, model_width)
    grad_out = cotangent[0].astype(jnp.float32)
    mlp_again = (
        lax.all_gather(up_projection_weight, ("dp", "seq"), axis=0, tiled=True),
        lax.all_gather(down_projection_weight, ("dp", "seq"), axis=0, tiled=True),
        lax.all_gather(second_gain, ("dp", "seq"), axis=0, tiled=True),
        lax.all_gather(second_shift, ("dp", "seq"), axis=0, tiled=True),
    )
    up_back = mlp_again[0]
    down_back = mlp_again[1]
    grad_out_low = cotangent[0]
    grad_down = rows_product(active_low, grad_out_low)
    d_active = cols_product(grad_out_low, down_back)
    gelu_value, gelu_back = jax.vjp(jax.nn.gelu, upper_hidden)
    g_upper = gelu_back(d_active)[0].astype(jnp.bfloat16)
    grad_up = rows_product(normed_two_low, g_upper)
    d_normed_two = cols_product(g_upper, up_back)
    norm_value, norm_back = jax.vjp(layer_norm, middle_tokens, gain_two, shift_two)
    middle_part, grad_gain_two, grad_shift_two = norm_back(d_normed_two)
    g_middle = grad_out + middle_part
    attn_again = (
        lax.all_gather(query_key_value_weight, ("dp", "seq"), axis=0, tiled=True),
        lax.all_gather(attention_output_weight, ("dp", "seq"), axis=0, tiled=True),
        lax.all_gather(first_gain, ("dp", "seq"), axis=0, tiled=True),
        lax.all_gather(first_shift, ("dp", "seq"), axis=0, tiled=True),
    )
    in_back = attn_again[0]
    out_back = attn_again[1]
    g_middle_low = g_middle.astype(jnp.bfloat16)
    grad_out_weight = rows_product(mixed_low, g_middle_low)
    d_mixed = cols_product(g_middle_low, out_back).reshape(block_shape)
    block_number = 0
    query_block = feat_query[block_number]
    denominator = denom_list[block_number]
    g_numerator = (d_mixed[block_number] / denominator[:, :, None]).astype(jnp.bfloat16)
    g_denominator = -jnp.sum(d_mixed[block_number] * numer_list[block_number], axis=2) / (
        denominator * denominator
    )
    kept_query = jnp.where(keep_list[block_number][:, None, None], query_block, zero_low)
    gnum_list = [g_numerator]
    gden_list = [g_denominator]
    local_list = [
        jnp.einsum("the,thf->hef", kept_query, g_numerator, preferred_element_type=jnp.float32)
    ]
    localkey_list = [jnp.sum(kept_query.astype(jnp.float32) * g_denominator[:, :, None], axis=0)]
    combined = identity
    for block_number in reversed(range(block_count)):
        combined = combine(
            combined,
            (flag_list[block_number], local_list[block_number], localkey_list[block_number]),
        )
    leaving = prefix(combined, "seq", combine, identity, True)
    g_memory = leaving[1]
    g_key_sum = leaving[2]
    gq_list = []
    gk_list = []
    gv_list = []
    for block_number in reversed(range(block_count)):
        query_block = feat_query[block_number]
        key_block = feat_key[block_number]
        value_block = value_low[block_number]
        keep_float = keep_list[block_number].astype(jnp.float32)
        tail_float = tail_list[block_number].astype(jnp.float32)
        g_numerator = gnum_list[block_number]
        g_denominator = gden_list[block_number]
        g_update = g_memory.astype(jnp.bfloat16)
        raw_scores = jnp.einsum(
            "the,jhe->htj", query_block, key_block, preferred_element_type=jnp.float32
        )
        scores_low = jnp.where(same_list[block_number][None], raw_scores, 0.0).astype(jnp.bfloat16)
        g_scores = (
            jnp.einsum("thf,jhf->htj", g_numerator, value_block, preferred_element_type=jnp.float32)
            + jnp.transpose(g_denominator)[:, :, None]
        )
        g_scores_low = jnp.where(
            same_list[block_number][None], g_scores.astype(jnp.bfloat16), zero_low
        )
        query_grad = jnp.einsum(
            "htj,jhe->the", g_scores_low, key_block, preferred_element_type=jnp.float32
        )
        query_grad = query_grad + keep_float[:, None, None] * (
            jnp.einsum(
                "thf,hef->the",
                g_numerator,
                memory_list[block_number],
                preferred_element_type=jnp.float32,
            )
            + g_denominator[:, :, None] * keysum_list[block_number][None]
        )
        key_grad = jnp.einsum(
            "htj,the->jhe", g_scores_low, query_block, preferred_element_type=jnp.float32
        )
        key_grad = key_grad + tail_float[:, None, None] * (
            jnp.einsum("jhf,hef->jhe", value_block, g_update, preferred_element_type=jnp.float32)
            + g_key_sum[None]
        )
        tail_key = jnp.where(tail_list[block_number][:, None, None], key_block, zero_low)
        value_grad = jnp.einsum(
            "htj,thf->jhf", scores_low, g_numerator, preferred_element_type=jnp.float32
        )
        value_grad = value_grad + jnp.einsum(
            "jhe,hef->jhf", tail_key, g_update, preferred_element_type=jnp.float32
        )
        gq_list.append(query_grad)
        gk_list.append(key_grad)
        gv_list.append(value_grad)
        g_memory = local_list[block_number] + flag_list[block_number] * g_memory
        g_key_sum = localkey_list[block_number] + flag_list[block_number] * g_key_sum
    d_feat_query = jnp.concatenate(gq_list[::-1], axis=0).reshape(local_len, model_width)
    d_feat_key = jnp.concatenate(gk_list[::-1], axis=0).reshape(local_len, model_width)
    d_value = jnp.concatenate(gv_list[::-1], axis=0).reshape(local_len, model_width)
    query_value, query_back = jax.vjp(feature, queries)
    key_value, key_back = jax.vjp(feature, keys_raw)
    g_projected = jnp.concatenate(
        [query_back(d_feat_query)[0], key_back(d_feat_key)[0], d_value], axis=1
    ).astype(jnp.bfloat16)
    grad_in_weight = rows_product(normed_low, g_projected)
    d_normed = cols_product(g_projected, in_back)
    first_value, first_back = jax.vjp(layer_norm, input_tokens, gain_one, shift_one)
    input_part, grad_gain_one, grad_shift_one = first_back(d_normed)
    grad_tokens = (g_middle + input_part).reshape(1, local_len, model_width)
    summed = (
        lax.psum_scatter(grad_in_weight, ("dp", "seq"), scatter_dimension=0, tiled=True),
        lax.psum_scatter(grad_out_weight, ("dp", "seq"), scatter_dimension=0, tiled=True),
        lax.psum_scatter(grad_up, ("dp", "seq"), scatter_dimension=0, tiled=True),
        lax.psum_scatter(grad_down, ("dp", "seq"), scatter_dimension=0, tiled=True),
        lax.psum_scatter(grad_gain_one, ("dp", "seq"), scatter_dimension=0, tiled=True),
        lax.psum_scatter(grad_shift_one, ("dp", "seq"), scatter_dimension=0, tiled=True),
        lax.psum_scatter(grad_gain_two, ("dp", "seq"), scatter_dimension=0, tiled=True),
        lax.psum_scatter(grad_shift_two, ("dp", "seq"), scatter_dimension=0, tiled=True),
    )
    return (
        result_tokens,
        grad_tokens,
        summed[0],
        summed[1],
        summed[2],
        summed[3],
        summed[4],
        summed[5],
        summed[6],
        summed[7],
    )


MESH = pl.DeviceIdType.MESH
LOW = jnp.bfloat16
FULL = jnp.float32


class Place:
    def __init__(self):
        dp, seq = lax.axis_index("dp"), lax.axis_index("seq")
        self.y, self.x = dp // 2, dp % 2
        self.z, self.c = seq // 2, seq % 2
        self.dp, self.seq = dp, seq
        self.over_x = (self.y * 2 + 1 - self.x, seq)
        self.over_y = ((1 - self.y) * 2 + self.x, seq)
        self.sibling = (dp, self.z * 2 + 1 - self.c)
        self.following = [(dp, (seq + 1) % 8), (dp, (seq + 2) % 8)]
        self.preceding = [(dp, (seq + 7) % 8), (dp, (seq + 6) % 8)]
        self.over_end = (dp, (seq + 2 * self.c + 7) % 8)
        self.along_z = [(dp, (self.z + d) % 4 * 2 + self.c) for d in (1, 2, 3)]

    def meet(self):
        barrier = pltpu.get_barrier_semaphore()
        everyone = [self.over_x, self.over_y, self.sibling, self.over_end, *self.along_z]
        for device in everyone:
            pl.semaphore_signal(barrier, inc=1, device_id=device, device_id_type=MESH)
        pl.semaphore_wait(barrier, len(everyone))


def remote(source, target, send, recv, device):
    return pltpu.make_async_remote_copy(
        src_ref=source,
        dst_ref=target,
        send_sem=send,
        recv_sem=recv,
        device_id=device,
        device_id_type=MESH,
    )


class Gather:
    def __init__(self, place, full, send, recv):
        p = place
        half = full.shape[4] // 2
        low, high = pl.ds(0, half), pl.ds(half, half)
        own = full.at[p.y, p.x, p.z, p.c]
        parts = [(own, device) for device in p.along_z]
        parts.append((full.at[p.y, p.x, :, p.c, low], p.over_x))
        parts.append((full.at[p.y, p.x, :, p.c, high], p.over_y))
        parts.append((full.at[p.y, :, :, p.c, low], p.over_y))
        parts.append((full.at[:, p.x, :, p.c, high], p.over_x))
        for y, x in ((p.y, p.x), (p.y, 1 - p.x), (1 - p.y, p.x), (1 - p.y, 1 - p.x)):
            parts.append((full.at[y, x, :, p.c], p.sibling))
        self.copies = [
            remote(ref, ref, send.at[i], recv.at[i], device)
            for i, (ref, device) in enumerate(parts)
        ]

    def start(self, *which):
        for i in which:
            self.copies[i].start()

    def arrive(self, *which):
        for i in which:
            self.copies[i].wait_recv()

    def step(self, number):
        if number == 0:
            self.start(0, 1, 2)
        elif number == 1:
            self.arrive(0, 1, 2)
            self.start(3, 4, 7)
        elif number == 2:
            self.arrive(3, 4)
            self.start(5, 6)
        elif number == 3:
            self.arrive(5, 6)
            self.start(8, 9, 10)
        else:
            self.arrive(7, 8, 9, 10)

    def finish(self):
        for copy in self.copies:
            copy.wait_send()


class Scatter:
    def __init__(self, place, own, total, pair, first_a, first_b, second_a, second_b, last, send, recv, outside):
        p = place
        self.outside, self.released = outside, False
        half = own.shape[4] // 2
        self.place, self.half = p, half
        self.own, self.total, self.pair = own, total, pair
        self.first_a, self.first_b = first_a, first_b
        self.second_a, self.second_b = second_a, second_b
        self.last = last
        low, high = pl.ds(0, half), pl.ds(half, half)
        parts = [
            (own.at[:, :, :, 1 - p.c], pair, p.sibling),
            (total.at[1 - p.y, :, :, low], first_a, p.over_y),
            (total.at[:, 1 - p.x, :, high], first_b, p.over_x),
            (total.at[p.y, 1 - p.x, :, low], second_a, p.over_x),
            (total.at[1 - p.y, p.x, :, high], second_b, p.over_y),
        ]
        if outside:
            self.keep = pltpu.make_async_copy(own.at[:, :, :, p.c], total, send.at[8])
        for d in (1, 2, 3):
            parts.append((total.at[p.y, p.x, (p.z + d) % 4], last.at[d - 1], p.along_z[d - 1]))
        self.copies = [
            remote(source, target, send.at[i], recv.at[i], device)
            for i, (source, target, device) in enumerate(parts)
        ]

    def step(self, number):
        p, half = self.place, self.half
        low, high = slice(0, half), slice(half, 2 * half)
        total = self.total
        if number == 0:
            self.copies[0].start()
            if self.outside:
                self.keep.start()
        elif number == 1:
            if self.outside:
                self.keep.wait()
            self.copies[0].wait_recv()

            @pl.loop(0, 4)
            def _(i):
                y, x = i // 2, i % 2
                mine = total[y, x] if self.outside else self.own[y, x, :, p.c]
                total[y, x] = mine + self.pair[y, x]

            self.copies[1].start()
            self.copies[2].start()
        elif number == 2:
            self.copies[1].wait_recv()
            self.copies[2].wait_recv()
            for i in range(2):
                total[p.y, i, :, low] += self.first_a[i]
                total[i, p.x, :, high] += self.first_b[i]
            self.copies[3].start()
            self.copies[4].start()
        elif number == 3:
            self.copies[3].wait_recv()
            self.copies[4].wait_recv()
            total[p.y, p.x, :, low] += self.second_a[...]
            total[p.y, p.x, :, high] += self.second_b[...]
            for i in (5, 6, 7):
                self.copies[i].start()

    def result(self):
        for i in (5, 6, 7):
            self.copies[i].wait_recv()
        p = self.place
        value = self.total[p.y, p.x, p.z].astype(FULL)
        for d in range(3):
            value = value + self.last[d].astype(FULL)
        return value

    def release(self):
        self.copies[0].wait_send()
        self.released = True

    def finish(self):
        for copy in self.copies[1 if self.released else 0 :]:
            copy.wait_send()


class SmallGather(Gather):
    def __init__(self, place, full, send, recv):
        p = place
        own = full.at[p.y, p.x, p.z, p.c]
        parts = [(own, device) for device in p.along_z]
        parts.append((full.at[p.y, p.x, :, p.c], p.over_x))
        parts.append((full.at[p.y, :, :, p.c], p.over_y))
        for y in range(2):
            for x in range(2):
                parts.append((full.at[y, x, :, p.c], p.sibling))
        self.copies = [
            remote(ref, ref, send.at[i], recv.at[i], device)
            for i, (ref, device) in enumerate(parts)
        ]

    def step(self, number):
        if number == 0:
            self.start(0, 1, 2)
        elif number == 1:
            self.arrive(0, 1, 2)
            self.start(3)
        elif number == 2:
            self.arrive(3)
            self.start(4)
        elif number == 3:
            self.arrive(4)
            self.start(5, 6, 7, 8)
        else:
            self.arrive(5, 6, 7, 8)


def product(one, two):
    return jnp.dot(one, two, preferred_element_type=FULL)


def across(one, two):
    return lax.dot_general(one, two, (((1,), (1,)), ((), ())), preferred_element_type=FULL)


def down_rows(one, two):
    return lax.dot_general(one, two, (((0,), (0,)), ((), ())), preferred_element_type=FULL)


def tile(i, size):
    return pl.ds(pl.multiple_of(i * size, size), size)


def image_count(starts, at):
    total = jnp.where(starts[0, 0] <= at, 1, 0)
    for k in range(1, starts.shape[1]):
        total = total + jnp.where(starts[0, k] <= at, 1, 0)
    return total


class Images:
    def __init__(self, starts, seq, length):
        first = seq * length
        self.length = length
        self.column = image_count(starts, first + lax.broadcasted_iota(jnp.int32, (length, 128), 0))
        self.row = image_count(starts, first + lax.broadcasted_iota(jnp.int32, (8, length), 1))
        before = image_count(starts, first - 1)
        last = image_count(starts, first + length - 1)
        earlier = image_count(starts, first - length - 1)
        later = image_count(starts, first + 2 * length - 1)
        self.keep = jnp.where(self.column == before, 1.0, 0.0)
        self.tail = jnp.where(self.column == last, 1.0, 0.0)
        self.flag_before = jnp.where(before == earlier, 1.0, 0.0)
        self.flag_after = jnp.where(later == last, 1.0, 0.0)


def same_mask(images, rows, columns, transposed):
    shape = (images.length, images.length)
    down = lax.broadcasted_iota(jnp.int32, shape, 0)
    along = lax.broadcasted_iota(jnp.int32, shape, 1)
    order = down <= along if transposed else down >= along
    equal = images.column[:, :1] == images.row[:1, :]
    return jnp.where(order & equal, 1.0, 0.0).astype(LOW)


def head_lanes(rows):
    return lax.broadcasted_iota(jnp.int32, (rows, 128), 1) < HEAD


def own_block():
    return jnp.where(
        (lax.broadcasted_iota(jnp.int32, (128, 128), 0) < HEAD)
        == (lax.broadcasted_iota(jnp.int32, (128, 128), 1) < HEAD),
        1.0,
        0.0,
    ).astype(LOW)


def pack_pair(square):
    return jnp.where(head_lanes(HEAD), square[:HEAD], square[HEAD:])


def unpack_pair(packed):
    lanes = head_lanes(HEAD)
    zero = jnp.zeros_like(packed)
    return jnp.concatenate([jnp.where(lanes, packed, zero), jnp.where(lanes, zero, packed)], axis=0)


def statistics(values):
    average = jnp.mean(values, axis=-1, keepdims=True)
    centred = values - average
    spread = jnp.mean(centred * centred, axis=-1, keepdims=True)
    scale = lax.rsqrt(spread + 1e-05)
    return centred * scale, scale


def gelu_both(values):
    root = 0.7978845608028654
    square = values * values
    angle = jnp.tanh(root * values * (1.0 + 0.044715 * square))
    half = 0.5 + 0.5 * angle
    slope = half + 0.5 * values * (1.0 - angle * angle) * (root * (1.0 + 0.134145 * square))
    return values * half, slope


def forward_kernel(inputs, outputs, scratch):
    tokens_in, cotangent_in, starts, in_weight, out_weight, up_weight, down_weight, pack_in = inputs
    (
        in_full,
        out_full,
        up_full,
        down_full,
        grad_down_out,
        result_out,
        heads_out,
        mixed_out,
        inverse_out,
        middle_out,
        slope_out,
        memory_out,
        sums_out,
        gains_out,
    ) = outputs
    (
        wide,
        tall,
        pack,
        tokens,
        cotangent,
        gains,
        normed,
        heads,
        mask,
        mixed,
        mixed_low,
        inverse,
        middle,
        active,
        slope,
        grad_down,
        result,
        outgoing,
        incoming,
        memory,
        sums,
        send,
        recv,
        small_send,
        small_recv,
        state_send,
        state_recv,
        local,
        store,
    ) = scratch
    p = Place()
    length, width = tokens.shape
    loads = []
    for j in range(8):
        source = in_weight if j < 3 else (out_weight if j == 3 else up_weight)
        column = j if j < 3 else (0 if j == 3 else j - 4)
        loads.append((source.at[:, pl.ds(column * 1024, 1024)], wide.at[j, p.y, p.x, p.z, p.c]))
    for j in range(4):
        loads.append((down_weight.at[:, pl.ds(256 * j, 256)], tall.at[j, p.y, p.x, p.z, p.c]))
    loads.append((pack_in, pack.at[p.y, p.x, p.z, p.c]))
    loads.append((tokens_in, tokens))
    loads.append((cotangent_in, cotangent))
    loads = [pltpu.make_async_copy(a, b, local.at[i]) for i, (a, b) in enumerate(loads)]
    for i in (12, 0, 1, 2, 13, 3, 4, 5, 6, 7, 8, 9, 10, 11, 14):
        loads[i].start()
    stores = []

    def save(source, target):
        copy = pltpu.make_async_copy(source, target, store.at[len(stores)])
        copy.start()
        stores.append(copy)

    p.meet()
    small = SmallGather(p, pack, small_send, small_recv)
    chunks = [Gather(p, wide.at[j], send.at[j], recv.at[j]) for j in range(8)]
    chunks += [Gather(p, tall.at[j], send.at[8 + j], recv.at[8 + j]) for j in range(4)]

    def event(j, number):
        if not 0 <= j < 12:
            return
        if number == 0:
            loads[j].wait()
        chunks[j].step(number)
        if number == 4:
            if j < 8:
                target = in_full if j < 3 else (out_full if j == 3 else up_full)
                column = j if j < 3 else (0 if j == 3 else j - 4)
                save(wide.at[j], target.at[:, :, :, :, :, pl.ds(column * 1024, 1024)])
            else:
                save(tall.at[j - 8], down_full.at[:, :, :, :, :, pl.ds(256 * (j - 8), 256)])

    def weight(j, columns):
        return wide[j, :, :, :, :, :, columns].reshape(width, columns.size)

    images = Images(starts, p.seq, length)

    def first_norm():
        for y in range(2):
            for x in range(2):
                for k in range(2):
                    value = pack[y, x, 2 * k : 2 * k + 2].astype(FULL)
                    value = (value[0, 0] + value[0, 1]) + (value[1, 0] + value[1, 1])
                    at = 128 * ((y * 2 + x) * 2 + k)
                    gains[:, at : at + 128] = value
        save(gains, gains_out)
        loads[13].wait()

        @pl.loop(0, length // 128)
        def _(i):
            rows = tile(i, 128)
            value, _ = statistics(tokens[rows, :].astype(FULL))
            normed[rows, :] = (value * gains[0:1, :] + gains[1:2, :]).astype(LOW)

        mask[...] = same_mask(images, length, length, False)

    def project(j):
        @pl.loop(0, 2)
        def _(i):
            value = product(normed[...], weight(j, tile(i, 512)))
            if j < 2:
                value = jnp.where(value > 0, value + 1.0, jnp.exp(jnp.minimum(value, 0.0)))
            heads[j, :, tile(i, 512)] = value.astype(LOW)

    def update():
        tail = images.tail.astype(LOW)

        @pl.loop(0, 8)
        def _(i):
            lanes = tile(i, 128)
            key = heads[1, :, lanes] * tail
            square = down_rows(key, heads[2, :, lanes])
            outgoing[i, 0:HEAD] = pack_pair(square).astype(LOW)
            total = product(jnp.ones((16, length), LOW), key)
            outgoing[i, HEAD : HEAD + 16] = total.astype(LOW)

        save(heads, heads_out)
        for copy in state:
            copy.start()

    state = [
        remote(outgoing, incoming.at[d], state_send.at[d], state_recv.at[d], device)
        for d, device in enumerate(p.following)
    ]

    def enter():
        for copy in state:
            copy.wait_recv()

        @pl.loop(0, 8)
        def _(i):
            value = incoming[0, i].astype(FULL) + images.flag_before * incoming[1, i].astype(FULL)
            memory[i] = value[0:HEAD].astype(LOW)
            sums[i] = value[HEAD : HEAD + 8]

        save(memory, memory_out)
        save(sums, sums_out)

    def attend(begin, end):
        lanes_column = head_lanes(length)
        blocks = own_block()
        keep = images.keep.astype(LOW)
        half = length // 2
        identity = jnp.where(
            lax.broadcasted_iota(jnp.int32, (128, 128), 0)
            == lax.broadcasted_iota(jnp.int32, (128, 128), 1),
            1.0,
            0.0,
        )
        ones = jnp.ones((length, 128), LOW)

        @pl.loop(begin, end)
        def _(i):
            lanes = tile(i, 128)
            query, key, value = heads[0, :, lanes], heads[1, :, lanes], heads[2, :, lanes]
            wider = jnp.concatenate([value, ones], axis=1)
            parts = []
            for h in range(2):
                mine = lanes_column if h == 0 else ~lanes_column
                own = jnp.where(mine, query, jnp.zeros_like(query))
                upper = across(own[:half], key[:half]).astype(LOW) * mask[:half, :half]
                lower = across(own[half:], key).astype(LOW) * mask[half:, :]
                parts.append(
                    jnp.concatenate([product(upper, wider[:half]), product(lower, wider)], axis=0)
                )
            diagonal = (identity * sums[i, 0:1]).astype(LOW)
            right = jnp.concatenate(
                [unpack_pair(memory[i]), product(diagonal, blocks).astype(LOW)], axis=1
            )
            carried = product(query * keep, right)
            numerator = jnp.where(lanes_column, parts[0][:, :128], parts[1][:, :128])
            denominator = jnp.where(lanes_column, parts[0][:, 128:], parts[1][:, 128:])
            over = 1.0 / (denominator + carried[:, 128:])
            value = (numerator + carried[:, :128]) * over
            inverse[:, lanes] = over
            mixed[:, lanes] = value
            mixed_low[:, lanes] = value.astype(LOW)

    def join():
        save(mixed, mixed_out)
        save(inverse, inverse_out)

        @pl.loop(0, 2)
        def _(i):
            columns = tile(i, 512)
            middle[:, columns] = tokens[:, columns].astype(FULL) + product(
                mixed_low[...], weight(3, columns)
            )

        save(middle, middle_out)

    def second_norm():
        @pl.loop(0, length // 128)
        def _(i):
            rows = tile(i, 128)
            value, _ = statistics(middle[rows, :])
            normed[rows, :] = (value * gains[2:3, :] + gains[3:4, :]).astype(LOW)

    def raise_up(j):
        @pl.loop(0, 4)
        def _(i):
            value = product(normed[...], weight(4 + j, tile(i, 256)))
            columns = pl.ds(pl.multiple_of(j * 1024 + i * 256, 256), 256)
            value, steep = gelu_both(value)
            active[:, columns] = value.astype(LOW)
            slope[:, columns] = steep.astype(LOW)

        if j == 3:
            save(slope, slope_out)

    def down_gradient(begin, end):
        if begin == 0:
            loads[14].wait()

        @pl.loop(begin, end)
        def _(i):
            value = down_rows(active[:, tile(i, 512)], cotangent[...]).astype(LOW)
            y, x, z = i // 4, i // 2 % 2, i % 2 * 2
            for j in range(4):
                part = value[:, 256 * j : 256 * j + 256].reshape(2, 2, 128, 256)
                grad_down[j, y, x, pl.ds(z, 2)] = part

        if end == 8:
            save(grad_down, grad_down_out)

    def lower(j):
        columns = slice(256 * j, 256 * j + 256)

        @pl.loop(0, 2)
        def _(i):
            rows = tile(i, 256)
            value = product(active[rows, :], tall[j].reshape(4 * width, 256))
            result[rows, columns] = (middle[rows, columns] + value).astype(LOW)

        save(result.at[:, pl.ds(256 * j, 256)], result_out.at[:, pl.ds(256 * j, 256)])

    do = functools.partial
    work = {
        4: [lambda: None, first_norm],
        5: [do(project, 0)],
        6: [do(project, 1)],
        7: [do(project, 2), update],
        8: [lambda: None, lambda: None, enter],
        9: [do(attend, 0, 4), do(attend, 4, 6), do(attend, 6, 8)],
        10: [join, second_norm, do(raise_up, 0)],
        11: [do(raise_up, 1), do(raise_up, 2)],
        12: [do(raise_up, 3), do(down_gradient, 0, 4), do(down_gradient, 4, 8)],
        13: [do(lower, 0)],
        14: [do(lower, 1)],
        15: [do(lower, 2)],
    }
    loads[12].wait()
    small.step(0)
    for tick in range(12 + 4):
        todo = work.get(tick, []) + [lambda: None] * 3
        event(tick, 0)
        event(tick - 1, 1)
        if 1 <= tick < 5:
            small.step(tick)
        todo[0]()
        event(tick - 2, 2)
        todo[1]()
        event(tick - 3, 3)
        event(tick - 4, 4)
        todo[2]()
    lower(3)
    small.finish()
    for copy in state:
        copy.wait_send()
    for chunk in chunks:
        chunk.finish()
    for copy in stores:
        copy.wait()


def forward_pass(tokens, cotangent, starts, in_weight, out_weight, up_weight, down_weight, pack):
    length, width = tokens.shape
    block = lambda rows, columns: jax.ShapeDtypeStruct((2, 2, 4, 2, rows, columns), LOW)
    shape = jax.ShapeDtypeStruct

    def body(*refs):
        forward_kernel(refs[:8], refs[8:22], refs[22:])

    return pl.pallas_call(
        body,
        out_shape=[
            block(32, 3072),
            block(32, 1024),
            block(32, 4096),
            block(128, 1024),
            shape((4, 2, 2, 4, 2, 128, 256), LOW),
            shape((length, width), LOW),
            shape((3, length, width), LOW),
            shape((length, width), FULL),
            shape((length, width), FULL),
            shape((length, width), FULL),
            shape((length, 4 * width), LOW),
            shape((8, HEAD, 128), LOW),
            shape((8, 8, 128), FULL),
            shape((16, width), FULL),
        ],
        in_specs=[
            pl.BlockSpec(memory_space=pltpu.SMEM if i == 2 else pl.ANY) for i in range(8)
        ],
        out_specs=[pl.BlockSpec(memory_space=pl.ANY)] * 14,
        scratch_shapes=[
            pltpu.VMEM((8, 2, 2, 4, 2, 32, 1024), LOW),
            pltpu.VMEM((4, 2, 2, 4, 2, 128, 256), LOW),
            pltpu.VMEM((2, 2, 4, 2, 16, 128), LOW),
            pltpu.VMEM((length, width), LOW),
            pltpu.VMEM((length, width), LOW),
            pltpu.VMEM((16, width), FULL),
            pltpu.VMEM((length, width), LOW),
            pltpu.VMEM((3, length, width), LOW),
            pltpu.VMEM((length, length), LOW),
            pltpu.VMEM((length, width), FULL),
            pltpu.VMEM((length, width), LOW),
            pltpu.VMEM((length, width), FULL),
            pltpu.VMEM((length, width), FULL),
            pltpu.VMEM((length, 4 * width), LOW),
            pltpu.VMEM((length, 4 * width), LOW),
            pltpu.VMEM((4, 2, 2, 4, 2, 128, 256), LOW),
            pltpu.VMEM((length, width), LOW),
            pltpu.VMEM((8, HEAD + 16, 128), LOW),
            pltpu.VMEM((2, 8, HEAD + 16, 128), LOW),
            pltpu.VMEM((8, HEAD, 128), LOW),
            pltpu.VMEM((8, 8, 128), FULL),
            pltpu.SemaphoreType.DMA((12, 11)),
            pltpu.SemaphoreType.DMA((12, 11)),
            pltpu.SemaphoreType.DMA((9,)),
            pltpu.SemaphoreType.DMA((9,)),
            pltpu.SemaphoreType.DMA((2,)),
            pltpu.SemaphoreType.DMA((2,)),
            pltpu.SemaphoreType.DMA((15,)),
            pltpu.SemaphoreType.DMA((26,)),
        ],
        compiler_params=pltpu.CompilerParams(
            collective_id=0, has_side_effects=True, vmem_limit_bytes=62 << 20
        ),
        name="forward_pass",
    )(tokens, cotangent, starts, in_weight, out_weight, up_weight, down_weight, pack)


def scatter_buffers(count, rows, columns):
    half = rows // 2
    shapes = [
        (2, 2, 4, rows, columns),
        (2, 2, 4, rows, columns),
        (2, 4, half, columns),
        (2, 4, half, columns),
        (4, half, columns),
        (4, half, columns),
        (3, rows, columns),
    ]
    return [pltpu.VMEM((count, *shape), LOW) for shape in shapes]


class Sum:
    def __init__(self, place, stages, landed, send, recv):
        p = place
        devices = [p.sibling, p.over_x, p.over_y, *p.along_z]
        self.stages, self.landed = stages, landed
        self.copies = [
            remote(stages.at[min(i, 3)], landed.at[i], send.at[i], recv.at[i], device)
            for i, device in enumerate(devices)
        ]

    def step(self, number):
        stages, landed = self.stages, self.landed
        if 1 <= number <= 3:
            self.copies[number - 1].wait_recv()
            stages[number] = stages[number - 1] + landed[number - 1]
        if number < 3:
            self.copies[number].start()
        elif number == 3:
            for i in (3, 4, 5):
                self.copies[i].start()

    def result(self):
        for i in (3, 4, 5):
            self.copies[i].wait_recv()
        return (self.stages[3] + self.landed[3]) + (self.landed[4] + self.landed[5])

    def finish(self):
        for copy in self.copies:
            copy.wait_send()


def backward_kernel(inputs, outputs, tall, wide, scratch):
    (
        tokens_in,
        cotangent_in,
        starts,
        in_full,
        out_full,
        up_full,
        down_full,
        grad_down_in,
        heads_in,
        mixed_in,
        inverse_in,
        middle_in,
        slope_in,
        memory_in,
        sums_in,
        gains_in,
    ) = inputs
    (
        cotangent,
        normed,
        slab,
        broad,
        grad_middle,
        inner,
        mixed,
        inverse,
        memory,
        sums,
        gains,
        mask,
        mask_back,
        parts,
        done_in,
        done_out,
        done_up,
        done_down,
        stages,
        landed,
        outgoing,
        incoming,
        update,
        key_update,
        send,
        recv,
        sum_send,
        sum_recv,
        state_send,
        state_recv,
        local,
        stream,
        store,
    ) = scratch
    p = Place()
    length, width = cotangent.shape

    pairs = [
        (cotangent_in, cotangent),
        (slope_in, broad),
        (middle_in, grad_middle),
        (gains_in, gains),
        (memory_in, memory),
        (sums_in, sums),
        (mixed_in, mixed),
        (inverse_in, inverse),
        (tokens_in, cotangent),
    ]
    pairs += [(heads_in.at[k], broad.at[:, pl.ds(1024 * k, 1024)]) for k in range(3)]
    loads = [pltpu.make_async_copy(a, b, local.at[i]) for i, (a, b) in enumerate(pairs)]
    slabs = [down_full.at[pl.ds(1024 * j, 1024), :] for j in range(4)]
    slabs += [up_full.at[:, pl.ds(1024 * j, 1024)] for j in range(4)]
    slabs += [out_full]
    slabs += [in_full.at[:, pl.ds(1024 * j, 1024)] for j in range(3)]
    slabs = [
        pltpu.make_async_copy(source, slab.at[i % 2], stream.at[i]) for i, source in enumerate(slabs)
    ]
    order = [8, 9, 10, 11, 4, 5, 6, 7, 3, 0, 1, 2]
    room = {4: 0, 5: 1, 6: 2, 7: 0, 3: 1, 0: 2, 1: 0, 2: 1}
    chunks = []
    for j in range(12):
        if j < 8:
            first, *others = [ref.at[j] for ref in wide]
            buffers = [first, first, *others]
            own = parts.at[room[j]]
        else:
            buffers = [ref.at[j - 8] for ref in tall]
            own = grad_down_in.at[j - 8]
        chunks.append(Scatter(p, own, *buffers, send.at[j], recv.at[j], j >= 8))

    p.meet()
    chunks[8].step(0)
    for i in range(4):
        loads[i].start()
    slabs[0].start()
    slabs[1].start()
    for i in range(4, 8):
        loads[i].start()
    stores = []

    def save(source, target):
        copy = pltpu.make_async_copy(source, target, store.at[len(stores)])
        copy.start()
        stores.append(copy)

    def event(position, number):
        if not 0 <= position < 12:
            return
        j = order[position]
        if number < 4:
            if (j, number) != (8, 0):
                chunks[j].step(number)
            return
        if j < 8:
            target, k = (done_in, j) if j < 3 else ((done_out, 0) if j == 3 else (done_up, j - 4))
            size = 1024
        else:
            target, k, size = done_down, j - 8, 256
        where = outputs[0 if j < 3 else 1 if j == 3 else 2 if j < 8 else 3]
        target[:, size * k : size * k + size] = chunks[j].result()
        save(target.at[:, pl.ds(size * k, size)], where.at[:, pl.ds(size * k, size)])

    images = Images(starts, p.seq, length)

    def second_norm():
        loads[2].wait()
        loads[3].wait()

        @pl.loop(0, length // 128)
        def _(i):
            rows = tile(i, 128)
            value, _ = statistics(grad_middle[rows, :])
            normed[rows, :] = (value * gains[2:3, :] + gains[3:4, :]).astype(LOW)

    def active_gradient(j):
        if j == 0:
            loads[0].wait()
            loads[1].wait()
        slabs[j].wait()

        @pl.loop(0, 4)
        def _(i):
            columns = pl.ds(pl.multiple_of(1024 * j + 256 * i, 256), 256)
            value = across(cotangent[...], slab[j % 2, tile(i, 256), :])
            broad[:, columns] = (value * broad[:, columns].astype(FULL)).astype(LOW)

        slabs[j + 2].start()

    def weight_gradient(j, left, right):
        at = room[j]

        @pl.loop(0, 4)
        def _(i):
            value = down_rows(left(tile(i, 256)), right()).astype(LOW)
            parts[at, i // 2, i % 2] = value.reshape(4, 2, 32, 1024)

    def up_gradient(j):
        if j == 3:
            chunks[4].release()
        weight_gradient(
            4 + j,
            lambda columns: normed[:, columns],
            lambda: broad[:, 1024 * j : 1024 * j + 1024],
        )
        if j == 3:
            for k in range(9, 12):
                loads[k].start()

    def inner_gradient(first, j):
        slabs[first + j].wait()

        @pl.loop(0, 4)
        def _(i):
            columns = tile(i, 256)
            value = across(
                broad[:, 1024 * j : 1024 * j + 1024], slab[(first + j) % 2, columns, :]
            )
            if j > 0:
                value = value + inner[:, columns]
            inner[:, columns] = value

        if first + j + 2 < 12:
            slabs[first + j + 2].start()

    def norm_gradient(rows, values, gain):
        unit, scale = statistics(values)
        given = inner[rows, :]
        scaled = given * gain
        one = jnp.mean(scaled, axis=-1, keepdims=True)
        two = jnp.mean(scaled * unit, axis=-1, keepdims=True)
        return scale * (scaled - one - unit * two), given * unit, given

    def fold(values):
        return jnp.sum(values, axis=0, keepdims=True)

    def middle_gradient():
        stages[0] = jnp.zeros((8, width), FULL)

        @pl.loop(0, length // 128)
        def _(i):
            rows = tile(i, 128)
            value, gain, shift = norm_gradient(rows, grad_middle[rows, :], gains[2:3, :])
            stages[0, 2:3, :] += fold(gain)
            stages[0, 3:4, :] += fold(shift)
            value = value + cotangent[rows, :].astype(FULL)
            grad_middle[rows, :] = value
            cotangent[rows, :] = value.astype(LOW)

    def output_gradient():
        loads[6].wait()
        chunks[5].release()
        weight_gradient(
            3, lambda columns: mixed[:, columns].astype(LOW), lambda: cotangent[...]
        )
        loads[8].start()

    def mixed_gradient():
        slabs[8].wait()

        @pl.loop(0, 4)
        def _(i):
            columns = tile(i, 256)
            inner[:, columns] = across(cotangent[...], slab[0, columns, :])

        slabs[10].start()

    state = [
        remote(outgoing, incoming.at[d], state_send.at[d], state_recv.at[d], device)
        for d, device in enumerate(p.preceding)
    ]

    def numerator_gradient():
        for i in (4, 5, 7, 9, 10, 11):
            loads[i].wait()
        blocks = own_block()
        doubled = jnp.concatenate([blocks, blocks], axis=0)

        @pl.loop(0, 8)
        def _(i):
            lanes = tile(i, 128)
            given, over = inner[:, lanes], inverse[:, lanes]
            numerator = (given * over).astype(LOW)
            each = given * mixed[:, lanes]
            high = each.astype(LOW)
            rest = (each - high.astype(FULL)).astype(LOW)
            slant = product(jnp.concatenate([high, rest], axis=1), doubled) * over * -1.0
            mixed[:, lanes] = slant
            broad[:, pl.ds(pl.multiple_of(3072 + 128 * i, 128), 128)] = numerator
            kept = broad[:, lanes].astype(FULL) * images.keep
            square = down_rows(kept.astype(LOW), numerator)
            outgoing[i, 0:HEAD] = pack_pair(square).astype(LOW)
            total = fold(kept * slant)
            outgoing[i, HEAD : HEAD + 16] = jnp.broadcast_to(total, (16, 128)).astype(LOW)

        for copy in state:
            copy.start()
        mask[...] = same_mask(images, length, length, False)
        mask_back[...] = same_mask(images, length, length, True)

    def enter():
        for copy in state:
            copy.wait_recv()
        flag = jnp.where(p.seq == 7, 0.0, images.flag_after)

        @pl.loop(0, 8)
        def _(i):
            value = incoming[0, i].astype(FULL) + flag * incoming[1, i].astype(FULL)
            update[i] = value[0:HEAD].astype(LOW)
            key_update[i] = value[HEAD : HEAD + 8]

    def attend(begin, end):
        if begin == 0:
            enter()
        if end == 8:
            first_norm()
        first = head_lanes(length)
        lane = lax.broadcasted_iota(jnp.int32, (length, 128), 1)
        ones = jnp.ones((length, 128), LOW)
        zero = jnp.zeros((length, 128), LOW)
        half = length // 2

        @pl.loop(begin, end)
        def _(i):
            at = [pl.ds(pl.multiple_of(1024 * k + 128 * i, 128), 128) for k in range(4)]
            query, key, value, numerator = [broad[:, lanes] for lanes in at]
            slant = mixed[:, at[0]]
            high = slant.astype(LOW)
            rest = (slant - high.astype(FULL)).astype(LOW)
            right = jnp.concatenate([value, ones], axis=1)
            grads = []
            for h in range(2):
                mine = first if h == 0 else ~first
                own_query = jnp.where(mine, query, zero)
                left = jnp.concatenate(
                    [
                        jnp.where(mine, numerator, zero),
                        jnp.where(
                            lane == HEAD * h, high, jnp.where(lane == HEAD * h + 1, rest, zero)
                        ),
                    ],
                    axis=1,
                )
                upper = across(left[:half], right[:half]).astype(LOW) * mask[:half, :half]
                lower = across(left[half:], right).astype(LOW) * mask[half:, :]
                for_query = jnp.concatenate([product(upper, key[:half]), product(lower, key)], axis=0)
                upper = across(right[:half], left).astype(LOW) * mask_back[:half, :]
                lower = across(right[half:], left[half:]).astype(LOW) * mask_back[half:, half:]
                for_key = jnp.concatenate(
                    [product(upper, query), product(lower, query[half:])], axis=0
                )
                upper = across(key[:half], own_query).astype(LOW) * mask_back[:half, :]
                lower = across(key[half:], own_query[half:]).astype(LOW) * mask_back[half:, half:]
                for_value = jnp.concatenate(
                    [product(upper, numerator), product(lower, numerator[half:])], axis=0
                )
                grads.append((for_query, for_key, for_value))
            for_query, for_key, for_value = [
                jnp.where(first, one, two) for one, two in zip(*grads, strict=True)
            ]
            keep, tail = images.keep, images.tail
            for_query = for_query + keep * (
                across(numerator, unpack_pair(memory[i])) + slant * sums[i, 0:1]
            )
            square = unpack_pair(update[i])
            for_key = for_key + tail * (across(value, square) + key_update[i, 0:1])
            for_value = for_value + product(key * tail.astype(LOW), square)
            broad[:, at[0]] = (for_query * jnp.minimum(query.astype(FULL), 1.0)).astype(LOW)
            broad[:, at[1]] = (for_key * jnp.minimum(key.astype(FULL), 1.0)).astype(LOW)
            broad[:, at[2]] = for_value.astype(LOW)

    def first_norm():
        loads[8].wait()

        @pl.loop(0, length // 128)
        def _(i):
            rows = tile(i, 128)
            value, _ = statistics(cotangent[rows, :].astype(FULL))
            normed[rows, :] = (value * gains[0:1, :] + gains[1:2, :]).astype(LOW)

    def in_gradient(j):
        chunks[(6, 7, 3)[j]].release()
        weight_gradient(
            j,
            lambda columns: normed[:, columns],
            lambda: broad[:, 1024 * j : 1024 * j + 1024],
        )

    total = Sum(p, stages, landed, sum_send, sum_recv)

    def token_gradient():
        @pl.loop(0, length // 128)
        def _(i):
            rows = tile(i, 128)
            value, gain, shift = norm_gradient(rows, cotangent[rows, :].astype(FULL), gains[0:1, :])
            stages[0, 0:1, :] += fold(gain)
            stages[0, 1:2, :] += fold(shift)
            grad_middle[rows, :] += value

        save(grad_middle, outputs[4])
        total.step(0)

    do = functools.partial
    work = {
        1: [do(active_gradient, 0), do(active_gradient, 1), do(active_gradient, 2)],
        2: [do(active_gradient, 3), second_norm, do(up_gradient, 0)],
        3: [do(up_gradient, 1), do(up_gradient, 2), do(inner_gradient, 4, 0)],
        4: [do(inner_gradient, 4, 1), do(inner_gradient, 4, 2), do(inner_gradient, 4, 3)],
        5: [do(up_gradient, 3), middle_gradient, mixed_gradient],
        6: [output_gradient, numerator_gradient],
        7: [lambda: None, do(attend, 0, 1), do(attend, 1, 3)],
        8: [do(attend, 3, 5), do(attend, 5, 7), do(attend, 7, 8)],
        9: [do(in_gradient, 1), do(in_gradient, 2), do(inner_gradient, 9, 0)],
        10: [
            do(inner_gradient, 9, 1),
            do(inner_gradient, 9, 2),
            token_gradient,
        ],
        11: [lambda: None, do(total.step, 1)],
        12: [lambda: None, do(total.step, 2)],
        13: [lambda: None, do(total.step, 3)],
    }
    for tick in range(12 + 6):
        todo = work.get(tick, []) + [lambda: None] * 3
        if tick == 9:
            in_gradient(0)
        event(tick, 0)
        event(tick - 1, 1)
        todo[0]()
        event(tick - 2, 2)
        todo[1]()
        event(tick - 3, 3)
        event(tick - 6, 4)
        todo[2]()
    total_value = total.result()
    landed[0] = total_value
    group = (p.dp * 8 + p.seq) // 4
    mine = landed[0, :, tile(group, 128)]
    mine = pltpu.roll(mine, (128 - 32 * (p.seq % 4)) % 128, 1)
    outputs[5][...] = mine
    total.finish()
    for copy in state:
        copy.wait_send()
    for chunk in chunks:
        chunk.finish()
    for copy in stores:
        copy.wait()


def backward_pass(*inputs):
    length, width = inputs[0].shape
    shape = jax.ShapeDtypeStruct
    vmem = pltpu.VMEM
    tall = scatter_buffers(4, 128, 256)
    wide = scatter_buffers(8, 32, 1024)[1:]

    def body(*refs):
        backward_kernel(refs[:16], refs[16:22], refs[22:29], refs[29:35], refs[35:])

    return pl.pallas_call(
        body,
        out_shape=[
            shape((32, 3072), FULL),
            shape((32, 1024), FULL),
            shape((32, 4096), FULL),
            shape((128, 1024), FULL),
            shape((length, width), FULL),
            shape((8, 128), FULL),
        ],
        in_specs=[
            pl.BlockSpec(memory_space=pltpu.SMEM if i == 2 else pl.ANY) for i in range(16)
        ],
        out_specs=[pl.BlockSpec(memory_space=pl.ANY)] * 5
        + [pl.BlockSpec(memory_space=pltpu.VMEM)],
        scratch_shapes=[
            *tall,
            *wide,
            vmem((length, width), LOW),
            vmem((length, width), LOW),
            vmem((2, width, width), LOW),
            vmem((length, 4 * width), LOW),
            vmem((length, width), FULL),
            vmem((length, width), FULL),
            vmem((length, width), FULL),
            vmem((length, width), FULL),
            vmem((8, HEAD, 128), LOW),
            vmem((8, 8, 128), FULL),
            vmem((16, width), FULL),
            vmem((length, length), LOW),
            vmem((length, length), LOW),
            vmem((3, 2, 2, 4, 2, 32, 1024), LOW),
            vmem((32, 3072), FULL),
            vmem((32, 1024), FULL),
            vmem((32, 4096), FULL),
            vmem((128, 1024), FULL),
            vmem((4, 8, width), FULL),
            vmem((6, 8, width), FULL),
            vmem((8, HEAD + 16, 128), LOW),
            vmem((2, 8, HEAD + 16, 128), LOW),
            vmem((8, HEAD, 128), LOW),
            vmem((8, 8, 128), FULL),
            pltpu.SemaphoreType.DMA((12, 9)),
            pltpu.SemaphoreType.DMA((12, 8)),
            pltpu.SemaphoreType.DMA((6,)),
            pltpu.SemaphoreType.DMA((6,)),
            pltpu.SemaphoreType.DMA((2,)),
            pltpu.SemaphoreType.DMA((2,)),
            pltpu.SemaphoreType.DMA((12,)),
            pltpu.SemaphoreType.DMA((12,)),
            pltpu.SemaphoreType.DMA((13,)),
        ],
        compiler_params=pltpu.CompilerParams(
            collective_id=1, has_side_effects=True, vmem_limit_bytes=62 << 20
        ),
        name="backward_pass",
    )(*inputs)


def hand_over(*values):
    large = len(values) - 1

    def body(*refs):
        inputs, vectors, outputs = refs[:large], refs[large], refs[large + 1 : 2 * large + 1]
        small, held, sems = refs[2 * large + 1 : 2 * large + 5], refs[2 * large + 5 : -1], refs[-1]
        copies = [
            (
                pltpu.make_async_copy(inputs[i], held[i], sems.at[0, i]),
                pltpu.make_async_copy(held[i], outputs[i], sems.at[1, i]),
            )
            for i in range(large)
        ]
        for load, _ in copies:
            load.start()
        for k in range(4):
            small[k][...] = vectors[k : k + 1, 0:32]
        for load, store in copies:
            load.wait()
            store.start()
        for _, store in copies:
            store.wait()

    anywhere, near = pl.BlockSpec(memory_space=pl.ANY), pl.BlockSpec(memory_space=pltpu.VMEM)
    return pl.pallas_call(
        body,
        out_shape=[jax.ShapeDtypeStruct(value.shape, value.dtype) for value in values[:large]]
        + [jax.ShapeDtypeStruct((1, 32), FULL)] * 4,
        in_specs=[anywhere] * large + [near],
        out_specs=[anywhere] * large + [near] * 4,
        scratch_shapes=[pltpu.VMEM(value.shape, value.dtype) for value in values[:large]]
        + [pltpu.SemaphoreType.DMA((2, large))],
        name="hand_over",
    )(*values)


def on_device(
    tokens,
    starts,
    query_key_value_weight,
    attention_output_weight,
    up_projection_weight,
    down_projection_weight,
    first_gain,
    first_shift,
    second_gain,
    second_shift,
    cotangent,
):
    mine = lax.axis_index("dp") * 8 + lax.axis_index("seq")
    pack = jnp.stack([first_gain, first_shift, second_gain, second_shift]).astype(FULL)
    pack = jnp.roll(jnp.pad(pack, ((0, 12), (0, 96))), 32 * (mine % 4), axis=1).astype(LOW)
    in_full, out_full, up_full, down_full, grad_down, result, *saved = forward_pass(
        tokens[0],
        cotangent[0],
        starts,
        query_key_value_weight,
        attention_output_weight,
        up_projection_weight,
        down_projection_weight,
        pack,
    )
    grads = backward_pass(
        tokens[0],
        cotangent[0],
        starts,
        in_full.reshape(1024, 3072),
        out_full.reshape(1024, 1024),
        up_full.reshape(1024, 4096),
        down_full.reshape(4096, 1024),
        grad_down,
        *saved,
    )
    result, *grads = hand_over(result, *grads)
    vectors = [grad.reshape(32) for grad in grads[5:]]
    return (result[None], grads[4][None], *grads[:4], *vectors)


def solution(mesh):

    fast = dict(mesh.shape) == {"dp": 4, "seq": 8}
    return jax.shard_map(
        on_device if fast else on_device_general,
        mesh=mesh,
        in_specs=(
            P("dp", "seq", None),
            P("dp", None),
            P(("dp", "seq"), None),
            P(("dp", "seq"), None),
            P(("dp", "seq"), None),
            P(("dp", "seq"), None),
            P(("dp", "seq")),
            P(("dp", "seq")),
            P(("dp", "seq")),
            P(("dp", "seq")),
            P("dp", "seq", None),
        ),
        out_specs=(
            P("dp", "seq", None),
            P("dp", "seq", None),
            P(("dp", "seq"), None),
            P(("dp", "seq"), None),
            P(("dp", "seq"), None),
            P(("dp", "seq"), None),
            P(("dp", "seq")),
            P(("dp", "seq")),
            P(("dp", "seq")),
            P(("dp", "seq")),
        ),
        check_vma=False,
    )
```

```python
import functools

import jax
import jax.numpy as jnp
from jax import lax
from jax.experimental import pallas as pl
from jax.experimental.pallas import tpu as pltpu
from jax.sharding import PartitionSpec as P

HEAD = 64
BLOCK = 512


def prefix(value, axis, combine, identity, reverse):
    size, mine = (lax.axis_size(axis), lax.axis_index(axis))
    everything = jax.tree.map(
        lambda part, kind: lax.all_gather(part.astype(kind), axis),
        value,
        jax.tree.map(lambda a: jnp.bfloat16 if a.dtype == jnp.float32 else a.dtype, value),
    )
    start = jax.tree.map(
        lambda part, zero: jnp.broadcast_to(jnp.asarray(zero, part.dtype), part.shape),
        value,
        identity,
    )

    def lap(k, before):
        at = size - 1 - k if reverse else k
        reached = at > mine if reverse else at < mine
        new = combine(
            before, jax.tree.map(lambda part, own: part[at].astype(own.dtype), everything, value)
        )
        return jax.tree.map(lambda a, b: jnp.where(reached, a, b), new, before)

    return lax.fori_loop(0, size, lap, start)


def layer_norm(values, norm_gain, norm_shift):
    average = jnp.mean(values, axis=-1, keepdims=True)
    centred = values - average
    spread = jnp.mean(centred * centred, axis=-1, keepdims=True)
    return centred * lax.rsqrt(spread + 1e-05) * norm_gain + norm_shift


def feature(values):
    return jax.nn.elu(values) + 1.0


def combine(former, latter):
    return (
        former[0] * latter[0],
        latter[0] * former[1] + latter[1],
        latter[0] * former[2] + latter[2],
    )


def rows_product(factor_one, factor_two):
    return lax.dot_general(
        factor_one, factor_two, (((0,), (0,)), ((), ())), preferred_element_type=jnp.float32
    )


def cols_product(factor_one, factor_two):
    return lax.dot_general(
        factor_one, factor_two, (((1,), (1,)), ((), ())), preferred_element_type=jnp.float32
    )


def on_device_general(
    tokens,
    starts,
    query_key_value_weight,
    attention_output_weight,
    up_projection_weight,
    down_projection_weight,
    first_gain,
    first_shift,
    second_gain,
    second_shift,
    cotangent,
):
    local_len = tokens.shape[1]
    model_width = tokens.shape[2]
    head_count = model_width // HEAD
    block_count = local_len // BLOCK
    block_shape = (block_count, BLOCK, head_count, HEAD)
    zero_low = jnp.zeros((), jnp.bfloat16)
    input_tokens = tokens[0].astype(jnp.float32)
    first_pos = lax.axis_index("seq") * local_len
    positions = first_pos + jnp.arange(local_len, dtype=jnp.int32)
    pack_starts = starts[0]
    image_ids = jnp.sum((pack_starts[None, :] <= positions[:, None]).astype(jnp.int32), axis=1) - 1
    before_id = jnp.sum((pack_starts <= first_pos - 1).astype(jnp.int32)) - 1
    causal = jnp.arange(BLOCK)[:, None] >= jnp.arange(BLOCK)[None, :]
    attn_set = (
        lax.all_gather(query_key_value_weight, ("dp", "seq"), axis=0, tiled=True),
        lax.all_gather(attention_output_weight, ("dp", "seq"), axis=0, tiled=True),
        lax.all_gather(first_gain, ("dp", "seq"), axis=0, tiled=True),
        lax.all_gather(first_shift, ("dp", "seq"), axis=0, tiled=True),
    )
    in_full = attn_set[0]
    out_full = attn_set[1]
    gain_one = attn_set[2].astype(jnp.float32)
    shift_one = attn_set[3].astype(jnp.float32)
    first_normed_tokens = layer_norm(input_tokens, gain_one, shift_one)
    normed_low = first_normed_tokens.astype(jnp.bfloat16)
    projected_tokens = jnp.dot(normed_low, in_full, preferred_element_type=jnp.float32)
    queries = projected_tokens[:, :model_width]
    keys_raw = projected_tokens[:, model_width : 2 * model_width]
    values_raw = projected_tokens[:, 2 * model_width :]
    feat_query = feature(queries).astype(jnp.bfloat16).reshape(block_shape)
    feat_key = feature(keys_raw).astype(jnp.bfloat16).reshape(block_shape)
    value_low = values_raw.astype(jnp.bfloat16).reshape(block_shape)
    block_number = 0
    last_id = image_ids[-1]
    tail_mask = image_ids == last_id
    tail_key = jnp.where(tail_mask[:, None, None], feat_key[block_number], zero_low)
    keep_list = [image_ids == before_id]
    tail_list = [tail_mask]
    flag_list = [(last_id == before_id).astype(jnp.float32)]
    same_list = [causal & (image_ids[:, None] == image_ids[None, :])]
    update_list = [
        jnp.einsum(
            "jhe,jhf->hef", tail_key, value_low[block_number], preferred_element_type=jnp.float32
        )
    ]
    total_list = [jnp.sum(tail_key.astype(jnp.float32), axis=0)]
    identity = (
        jnp.ones((), jnp.float32),
        jnp.zeros((head_count, HEAD, HEAD), jnp.float32),
        jnp.zeros((head_count, HEAD), jnp.float32),
    )
    combined = identity
    block_number = 0
    combined = combine(
        combined, (flag_list[block_number], update_list[block_number], total_list[block_number])
    )
    entering = prefix(combined, "seq", combine, identity, False)
    memory = entering[1]
    key_sum = entering[2]
    block_number = 0
    query_block = feat_query[block_number]
    keep_float = keep_list[block_number].astype(jnp.float32)
    memory_low = memory.astype(jnp.bfloat16)
    raw_scores = jnp.einsum(
        "the,jhe->htj", query_block, feat_key[block_number], preferred_element_type=jnp.float32
    )
    masked = jnp.where(same_list[block_number][None], raw_scores, 0.0)
    scores_low = masked.astype(jnp.bfloat16)
    carried = (
        jnp.einsum("the,hef->thf", query_block, memory_low, preferred_element_type=jnp.float32)
        * keep_float[:, None, None]
    )
    numerator = (
        jnp.einsum(
            "htj,jhf->thf", scores_low, value_low[block_number], preferred_element_type=jnp.float32
        )
        + carried
    )
    denominator = jnp.transpose(jnp.sum(masked, axis=2)) + keep_float[:, None] * jnp.sum(
        query_block.astype(jnp.float32) * key_sum[None], axis=2
    )
    memory_list = [memory_low]
    keysum_list = [key_sum]
    numer_list = [numerator]
    denom_list = [denominator]
    ratio_list = numerator / denominator[:, :, None]
    mixed_low = ratio_list.reshape(local_len, model_width).astype(jnp.bfloat16)
    middle_tokens = input_tokens + jnp.dot(mixed_low, out_full, preferred_element_type=jnp.float32)
    mlp_set = (
        lax.all_gather(up_projection_weight, ("dp", "seq"), axis=0, tiled=True),
        lax.all_gather(down_projection_weight, ("dp", "seq"), axis=0, tiled=True),
        lax.all_gather(second_gain, ("dp", "seq"), axis=0, tiled=True),
        lax.all_gather(second_shift, ("dp", "seq"), axis=0, tiled=True),
    )
    up_full = mlp_set[0]
    down_full = mlp_set[1]
    gain_two = mlp_set[2].astype(jnp.float32)
    shift_two = mlp_set[3].astype(jnp.float32)
    normed_two_low = layer_norm(middle_tokens, gain_two, shift_two).astype(jnp.bfloat16)
    upper_hidden = jnp.dot(normed_two_low, up_full, preferred_element_type=jnp.float32)
    active_low = jax.nn.gelu(upper_hidden).astype(jnp.bfloat16)
    result = middle_tokens + jnp.dot(active_low, down_full, preferred_element_type=jnp.float32)
    result_tokens = result.astype(jnp.bfloat16).reshape(1, local_len, model_width)
    grad_out = cotangent[0].astype(jnp.float32)
    mlp_again = (
        lax.all_gather(up_projection_weight, ("dp", "seq"), axis=0, tiled=True),
        lax.all_gather(down_projection_weight, ("dp", "seq"), axis=0, tiled=True),
        lax.all_gather(second_gain, ("dp", "seq"), axis=0, tiled=True),
        lax.all_gather(second_shift, ("dp", "seq"), axis=0, tiled=True),
    )
    up_back = mlp_again[0]
    down_back = mlp_again[1]
    grad_out_low = cotangent[0]
    grad_down = rows_product(active_low, grad_out_low)
    d_active = cols_product(grad_out_low, down_back)
    gelu_value, gelu_back = jax.vjp(jax.nn.gelu, upper_hidden)
    g_upper = gelu_back(d_active)[0].astype(jnp.bfloat16)
    grad_up = rows_product(normed_two_low, g_upper)
    d_normed_two = cols_product(g_upper, up_back)
    norm_value, norm_back = jax.vjp(layer_norm, middle_tokens, gain_two, shift_two)
    middle_part, grad_gain_two, grad_shift_two = norm_back(d_normed_two)
    g_middle = grad_out + middle_part
    attn_again = (
        lax.all_gather(query_key_value_weight, ("dp", "seq"), axis=0, tiled=True),
        lax.all_gather(attention_output_weight, ("dp", "seq"), axis=0, tiled=True),
        lax.all_gather(first_gain, ("dp", "seq"), axis=0, tiled=True),
        lax.all_gather(first_shift, ("dp", "seq"), axis=0, tiled=True),
    )
    in_back = attn_again[0]
    out_back = attn_again[1]
    g_middle_low = g_middle.astype(jnp.bfloat16)
    grad_out_weight = rows_product(mixed_low, g_middle_low)
    d_mixed = cols_product(g_middle_low, out_back).reshape(block_shape)
    block_number = 0
    query_block = feat_query[block_number]
    denominator = denom_list[block_number]
    g_numerator = (d_mixed[block_number] / denominator[:, :, None]).astype(jnp.bfloat16)
    g_denominator = -jnp.sum(d_mixed[block_number] * numer_list[block_number], axis=2) / (
        denominator * denominator
    )
    kept_query = jnp.where(keep_list[block_number][:, None, None], query_block, zero_low)
    gnum_list = [g_numerator]
    gden_list = [g_denominator]
    local_list = [
        jnp.einsum("the,thf->hef", kept_query, g_numerator, preferred_element_type=jnp.float32)
    ]
    localkey_list = [jnp.sum(kept_query.astype(jnp.float32) * g_denominator[:, :, None], axis=0)]
    combined = identity
    for block_number in reversed(range(block_count)):
        combined = combine(
            combined,
            (flag_list[block_number], local_list[block_number], localkey_list[block_number]),
        )
    leaving = prefix(combined, "seq", combine, identity, True)
    g_memory = leaving[1]
    g_key_sum = leaving[2]
    gq_list = []
    gk_list = []
    gv_list = []
    for block_number in reversed(range(block_count)):
        query_block = feat_query[block_number]
        key_block = feat_key[block_number]
        value_block = value_low[block_number]
        keep_float = keep_list[block_number].astype(jnp.float32)
        tail_float = tail_list[block_number].astype(jnp.float32)
        g_numerator = gnum_list[block_number]
        g_denominator = gden_list[block_number]
        g_update = g_memory.astype(jnp.bfloat16)
        raw_scores = jnp.einsum(
            "the,jhe->htj", query_block, key_block, preferred_element_type=jnp.float32
        )
        scores_low = jnp.where(same_list[block_number][None], raw_scores, 0.0).astype(jnp.bfloat16)
        g_scores = (
            jnp.einsum("thf,jhf->htj", g_numerator, value_block, preferred_element_type=jnp.float32)
            + jnp.transpose(g_denominator)[:, :, None]
        )
        g_scores_low = jnp.where(
            same_list[block_number][None], g_scores.astype(jnp.bfloat16), zero_low
        )
        query_grad = jnp.einsum(
            "htj,jhe->the", g_scores_low, key_block, preferred_element_type=jnp.float32
        )
        query_grad = query_grad + keep_float[:, None, None] * (
            jnp.einsum(
                "thf,hef->the",
                g_numerator,
                memory_list[block_number],
                preferred_element_type=jnp.float32,
            )
            + g_denominator[:, :, None] * keysum_list[block_number][None]
        )
        key_grad = jnp.einsum(
            "htj,the->jhe", g_scores_low, query_block, preferred_element_type=jnp.float32
        )
        key_grad = key_grad + tail_float[:, None, None] * (
            jnp.einsum("jhf,hef->jhe", value_block, g_update, preferred_element_type=jnp.float32)
            + g_key_sum[None]
        )
        tail_key = jnp.where(tail_list[block_number][:, None, None], key_block, zero_low)
        value_grad = jnp.einsum(
            "htj,thf->jhf", scores_low, g_numerator, preferred_element_type=jnp.float32
        )
        value_grad = value_grad + jnp.einsum(
            "jhe,hef->jhf", tail_key, g_update, preferred_element_type=jnp.float32
        )
        gq_list.append(query_grad)
        gk_list.append(key_grad)
        gv_list.append(value_grad)
        g_memory = local_list[block_number] + flag_list[block_number] * g_memory
        g_key_sum = localkey_list[block_number] + flag_list[block_number] * g_key_sum
    d_feat_query = jnp.concatenate(gq_list[::-1], axis=0).reshape(local_len, model_width)
    d_feat_key = jnp.concatenate(gk_list[::-1], axis=0).reshape(local_len, model_width)
    d_value = jnp.concatenate(gv_list[::-1], axis=0).reshape(local_len, model_width)
    query_value, query_back = jax.vjp(feature, queries)
    key_value, key_back = jax.vjp(feature, keys_raw)
    g_projected = jnp.concatenate(
        [query_back(d_feat_query)[0], key_back(d_feat_key)[0], d_value], axis=1
    ).astype(jnp.bfloat16)
    grad_in_weight = rows_product(normed_low, g_projected)
    d_normed = cols_product(g_projected, in_back)
    first_value, first_back = jax.vjp(layer_norm, input_tokens, gain_one, shift_one)
    input_part, grad_gain_one, grad_shift_one = first_back(d_normed)
    grad_tokens = (g_middle + input_part).reshape(1, local_len, model_width)
    summed = (
        lax.psum_scatter(grad_in_weight, ("dp", "seq"), scatter_dimension=0, tiled=True),
        lax.psum_scatter(grad_out_weight, ("dp", "seq"), scatter_dimension=0, tiled=True),
        lax.psum_scatter(grad_up, ("dp", "seq"), scatter_dimension=0, tiled=True),
        lax.psum_scatter(grad_down, ("dp", "seq"), scatter_dimension=0, tiled=True),
        lax.psum_scatter(grad_gain_one, ("dp", "seq"), scatter_dimension=0, tiled=True),
        lax.psum_scatter(grad_shift_one, ("dp", "seq"), scatter_dimension=0, tiled=True),
        lax.psum_scatter(grad_gain_two, ("dp", "seq"), scatter_dimension=0, tiled=True),
        lax.psum_scatter(grad_shift_two, ("dp", "seq"), scatter_dimension=0, tiled=True),
    )
    return (
        result_tokens,
        grad_tokens,
        summed[0],
        summed[1],
        summed[2],
        summed[3],
        summed[4],
        summed[5],
        summed[6],
        summed[7],
    )


MESH = pl.DeviceIdType.MESH
LOW = jnp.bfloat16
FULL = jnp.float32


class Place:
    def __init__(self):
        dp, seq = lax.axis_index("dp"), lax.axis_index("seq")
        self.y, self.x = dp // 2, dp % 2
        self.z, self.c = seq // 2, seq % 2
        self.dp, self.seq = dp, seq
        self.over_x = (self.y * 2 + 1 - self.x, seq)
        self.over_y = ((1 - self.y) * 2 + self.x, seq)
        self.sibling = (dp, self.z * 2 + 1 - self.c)
        self.following = [(dp, (seq + 1) % 8), (dp, (seq + 2) % 8)]
        self.preceding = [(dp, (seq + 7) % 8), (dp, (seq + 6) % 8)]
        self.over_end = (dp, (seq + 2 * self.c + 7) % 8)
        self.along_z = [(dp, (self.z + d) % 4 * 2 + self.c) for d in (1, 2, 3)]

    def meet(self):
        barrier = pltpu.get_barrier_semaphore()
        everyone = [self.over_x, self.over_y, self.sibling, self.over_end, *self.along_z]
        for device in everyone:
            pl.semaphore_signal(barrier, inc=1, device_id=device, device_id_type=MESH)
        pl.semaphore_wait(barrier, len(everyone))


def remote(source, target, send, recv, device):
    return pltpu.make_async_remote_copy(
        src_ref=source,
        dst_ref=target,
        send_sem=send,
        recv_sem=recv,
        device_id=device,
        device_id_type=MESH,
    )


class Gather:
    def __init__(self, place, full, send, recv):
        p = place
        half = full.shape[4] // 2
        low, high = pl.ds(0, half), pl.ds(half, half)
        own = full.at[p.y, p.x, p.z, p.c]
        parts = [(own, device) for device in p.along_z]
        parts.append((full.at[p.y, p.x, :, p.c, low], p.over_x))
        parts.append((full.at[p.y, p.x, :, p.c, high], p.over_y))
        parts.append((full.at[p.y, :, :, p.c, low], p.over_y))
        parts.append((full.at[:, p.x, :, p.c, high], p.over_x))
        for y, x in ((p.y, p.x), (p.y, 1 - p.x), (1 - p.y, p.x), (1 - p.y, 1 - p.x)):
            parts.append((full.at[y, x, :, p.c], p.sibling))
        self.copies = [
            remote(ref, ref, send.at[i], recv.at[i], device)
            for i, (ref, device) in enumerate(parts)
        ]

    def start(self, *which):
        for i in which:
            self.copies[i].start()

    def arrive(self, *which):
        for i in which:
            self.copies[i].wait_recv()

    def step(self, number):
        if number == 0:
            self.start(0, 1, 2)
        elif number == 1:
            self.arrive(0, 1, 2)
            self.start(3, 4, 7)
        elif number == 2:
            self.arrive(3, 4)
            self.start(5, 6)
        elif number == 3:
            self.arrive(5, 6)
            self.start(8, 9, 10)
        else:
            self.arrive(7, 8, 9, 10)

    def finish(self):
        for copy in self.copies:
            copy.wait_send()


class Scatter:
    def __init__(self, place, own, total, pair, first_a, first_b, second_a, second_b, last, send, recv, outside):
        p = place
        self.outside, self.released = outside, False
        half = own.shape[4] // 2
        self.place, self.half = p, half
        self.own, self.total, self.pair = own, total, pair
        self.first_a, self.first_b = first_a, first_b
        self.second_a, self.second_b = second_a, second_b
        self.last = last
        low, high = pl.ds(0, half), pl.ds(half, half)
        parts = [
            (own.at[:, :, :, 1 - p.c], pair, p.sibling),
            (total.at[1 - p.y, :, :, low], first_a, p.over_y),
            (total.at[:, 1 - p.x, :, high], first_b, p.over_x),
            (total.at[p.y, 1 - p.x, :, low], second_a, p.over_x),
            (total.at[1 - p.y, p.x, :, high], second_b, p.over_y),
        ]
        if outside:
            self.keep = pltpu.make_async_copy(own.at[:, :, :, p.c], total, send.at[8])
        for d in (1, 2, 3):
            parts.append((total.at[p.y, p.x, (p.z + d) % 4], last.at[d - 1], p.along_z[d - 1]))
        self.copies = [
            remote(source, target, send.at[i], recv.at[i], device)
            for i, (source, target, device) in enumerate(parts)
        ]

    def step(self, number):
        p, half = self.place, self.half
        low, high = slice(0, half), slice(half, 2 * half)
        total = self.total
        if number == 0:
            self.copies[0].start()
            if self.outside:
                self.keep.start()
        elif number == 1:
            if self.outside:
                self.keep.wait()
            self.copies[0].wait_recv()

            @pl.loop(0, 4)
            def _(i):
                y, x = i // 2, i % 2
                mine = total[y, x] if self.outside else self.own[y, x, :, p.c]
                total[y, x] = mine + self.pair[y, x]

            self.copies[1].start()
            self.copies[2].start()
        elif number == 2:
            self.copies[1].wait_recv()
            self.copies[2].wait_recv()
            for i in range(2):
                total[p.y, i, :, low] += self.first_a[i]
                total[i, p.x, :, high] += self.first_b[i]
            self.copies[3].start()
            self.copies[4].start()
        elif number == 3:
            self.copies[3].wait_recv()
            self.copies[4].wait_recv()
            total[p.y, p.x, :, low] += self.second_a[...]
            total[p.y, p.x, :, high] += self.second_b[...]
            for i in (5, 6, 7):
                self.copies[i].start()

    def result(self):
        for i in (5, 6, 7):
            self.copies[i].wait_recv()
        p = self.place
        value = self.total[p.y, p.x, p.z].astype(FULL)
        for d in range(3):
            value = value + self.last[d].astype(FULL)
        return value

    def release(self):
        self.copies[0].wait_send()
        self.released = True

    def finish(self):
        for copy in self.copies[1 if self.released else 0 :]:
            copy.wait_send()


class SmallGather(Gather):
    def __init__(self, place, full, send, recv):
        p = place
        own = full.at[p.y, p.x, p.z, p.c]
        parts = [(own, device) for device in p.along_z]
        parts.append((full.at[p.y, p.x, :, p.c], p.over_x))
        parts.append((full.at[p.y, :, :, p.c], p.over_y))
        for y in range(2):
            for x in range(2):
                parts.append((full.at[y, x, :, p.c], p.sibling))
        self.copies = [
            remote(ref, ref, send.at[i], recv.at[i], device)
            for i, (ref, device) in enumerate(parts)
        ]

    def step(self, number):
        if number == 0:
            self.start(0, 1, 2)
        elif number == 1:
            self.arrive(0, 1, 2)
            self.start(3)
        elif number == 2:
            self.arrive(3)
            self.start(4)
        elif number == 3:
            self.arrive(4)
            self.start(5, 6, 7, 8)
        else:
            self.arrive(5, 6, 7, 8)


def product(one, two):
    return jnp.dot(one, two, preferred_element_type=FULL)


def across(one, two):
    return lax.dot_general(one, two, (((1,), (1,)), ((), ())), preferred_element_type=FULL)


def down_rows(one, two):
    return lax.dot_general(one, two, (((0,), (0,)), ((), ())), preferred_element_type=FULL)


def tile(i, size):
    return pl.ds(pl.multiple_of(i * size, size), size)


def image_count(starts, at):
    total = jnp.where(starts[0, 0] <= at, 1, 0)
    for k in range(1, starts.shape[1]):
        total = total + jnp.where(starts[0, k] <= at, 1, 0)
    return total


class Images:
    def __init__(self, starts, seq, length):
        first = seq * length
        self.length = length
        self.column = image_count(starts, first + lax.broadcasted_iota(jnp.int32, (length, 128), 0))
        self.row = image_count(starts, first + lax.broadcasted_iota(jnp.int32, (8, length), 1))
        before = image_count(starts, first - 1)
        last = image_count(starts, first + length - 1)
        earlier = image_count(starts, first - length - 1)
        later = image_count(starts, first + 2 * length - 1)
        self.keep = jnp.where(self.column == before, 1.0, 0.0)
        self.tail = jnp.where(self.column == last, 1.0, 0.0)
        self.flag_before = jnp.where(before == earlier, 1.0, 0.0)
        self.flag_after = jnp.where(later == last, 1.0, 0.0)


def same_mask(images, rows, columns, transposed):
    shape = (images.length, images.length)
    down = lax.broadcasted_iota(jnp.int32, shape, 0)
    along = lax.broadcasted_iota(jnp.int32, shape, 1)
    order = down <= along if transposed else down >= along
    equal = images.column[:, :1] == images.row[:1, :]
    return jnp.where(order & equal, 1.0, 0.0).astype(LOW)


def head_lanes(rows):
    return lax.broadcasted_iota(jnp.int32, (rows, 128), 1) < HEAD


def own_block():
    return jnp.where(
        (lax.broadcasted_iota(jnp.int32, (128, 128), 0) < HEAD)
        == (lax.broadcasted_iota(jnp.int32, (128, 128), 1) < HEAD),
        1.0,
        0.0,
    ).astype(LOW)


def pack_pair(square):
    return jnp.where(head_lanes(HEAD), square[:HEAD], square[HEAD:])


def unpack_pair(packed):
    lanes = head_lanes(HEAD)
    zero = jnp.zeros_like(packed)
    return jnp.concatenate([jnp.where(lanes, packed, zero), jnp.where(lanes, zero, packed)], axis=0)


def statistics(values):
    average = jnp.mean(values, axis=-1, keepdims=True)
    centred = values - average
    spread = jnp.mean(centred * centred, axis=-1, keepdims=True)
    scale = lax.rsqrt(spread + 1e-05)
    return centred * scale, scale


def gelu_both(values):
    root = 0.7978845608028654
    square = values * values
    angle = jnp.tanh(root * values * (1.0 + 0.044715 * square))
    half = 0.5 + 0.5 * angle
    slope = half + 0.5 * values * (1.0 - angle * angle) * (root * (1.0 + 0.134145 * square))
    return values * half, slope


def forward_kernel(inputs, outputs, scratch):
    tokens_in, cotangent_in, starts, in_weight, out_weight, up_weight, down_weight, pack_in = inputs
    (
        in_full,
        out_full,
        up_full,
        down_full,
        grad_down_out,
        result_out,
        heads_out,
        mixed_out,
        inverse_out,
        middle_out,
        slope_out,
        memory_out,
        sums_out,
        gains_out,
    ) = outputs
    (
        wide,
        tall,
        pack,
        tokens,
        cotangent,
        gains,
        normed,
        heads,
        mask,
        mixed,
        mixed_low,
        inverse,
        middle,
        active,
        slope,
        grad_down,
        result,
        outgoing,
        incoming,
        memory,
        sums,
        send,
        recv,
        small_send,
        small_recv,
        state_send,
        state_recv,
        local,
        store,
    ) = scratch
    p = Place()
    length, width = tokens.shape
    loads = []
    for j in range(8):
        source = in_weight if j < 3 else (out_weight if j == 3 else up_weight)
        column = j if j < 3 else (0 if j == 3 else j - 4)
        loads.append((source.at[:, pl.ds(column * 1024, 1024)], wide.at[j, p.y, p.x, p.z, p.c]))
    for j in range(4):
        loads.append((down_weight.at[:, pl.ds(256 * j, 256)], tall.at[j, p.y, p.x, p.z, p.c]))
    loads.append((pack_in, pack.at[p.y, p.x, p.z, p.c]))
    loads.append((tokens_in, tokens))
    loads.append((cotangent_in, cotangent))
    loads = [pltpu.make_async_copy(a, b, local.at[i]) for i, (a, b) in enumerate(loads)]
    for i in (12, 0, 1, 2, 13, 3, 4, 5, 6, 7, 8, 9, 10, 11, 14):
        loads[i].start()
    stores = []

    def save(source, target):
        copy = pltpu.make_async_copy(source, target, store.at[len(stores)])
        copy.start()
        stores.append(copy)

    p.meet()
    small = SmallGather(p, pack, small_send, small_recv)
    chunks = [Gather(p, wide.at[j], send.at[j], recv.at[j]) for j in range(8)]
    chunks += [Gather(p, tall.at[j], send.at[8 + j], recv.at[8 + j]) for j in range(4)]

    def event(j, number):
        if not 0 <= j < 12:
            return
        if number == 0:
            loads[j].wait()
        chunks[j].step(number)
        if number == 4:
            if j < 8:
                target = in_full if j < 3 else (out_full if j == 3 else up_full)
                column = j if j < 3 else (0 if j == 3 else j - 4)
                save(wide.at[j], target.at[:, :, :, :, :, pl.ds(column * 1024, 1024)])
            else:
                save(tall.at[j - 8], down_full.at[:, :, :, :, :, pl.ds(256 * (j - 8), 256)])

    def weight(j, columns):
        return wide[j, :, :, :, :, :, columns].reshape(width, columns.size)

    images = Images(starts, p.seq, length)

    def first_norm():
        for y in range(2):
            for x in range(2):
                for k in range(2):
                    value = pack[y, x, 2 * k : 2 * k + 2].astype(FULL)
                    value = (value[0, 0] + value[0, 1]) + (value[1, 0] + value[1, 1])
                    at = 128 * ((y * 2 + x) * 2 + k)
                    gains[:, at : at + 128] = value
        save(gains, gains_out)
        loads[13].wait()

        @pl.loop(0, length // 128)
        def _(i):
            rows = tile(i, 128)
            value, _ = statistics(tokens[rows, :].astype(FULL))
            normed[rows, :] = (value * gains[0:1, :] + gains[1:2, :]).astype(LOW)

        mask[...] = same_mask(images, length, length, False)

    def project(j):
        @pl.loop(0, 2)
        def _(i):
            value = product(normed[...], weight(j, tile(i, 512)))
            if j < 2:
                value = jnp.where(value > 0, value + 1.0, jnp.exp(jnp.minimum(value, 0.0)))
            heads[j, :, tile(i, 512)] = value.astype(LOW)

    def update():
        tail = images.tail.astype(LOW)

        @pl.loop(0, 8)
        def _(i):
            lanes = tile(i, 128)
            key = heads[1, :, lanes] * tail
            square = down_rows(key, heads[2, :, lanes])
            outgoing[i, 0:HEAD] = pack_pair(square).astype(LOW)
            total = product(jnp.ones((16, length), LOW), key)
            outgoing[i, HEAD : HEAD + 16] = total.astype(LOW)

        save(heads, heads_out)
        for copy in state:
            copy.start()

    state = [
        remote(outgoing, incoming.at[d], state_send.at[d], state_recv.at[d], device)
        for d, device in enumerate(p.following)
    ]

    def enter():
        for copy in state:
            copy.wait_recv()

        @pl.loop(0, 8)
        def _(i):
            value = incoming[0, i].astype(FULL) + images.flag_before * incoming[1, i].astype(FULL)
            memory[i] = value[0:HEAD].astype(LOW)
            sums[i] = value[HEAD : HEAD + 8]

        save(memory, memory_out)
        save(sums, sums_out)

    def attend(begin, end):
        lanes_column = head_lanes(length)
        blocks = own_block()
        keep = images.keep.astype(LOW)
        half = length // 2
        identity = jnp.where(
            lax.broadcasted_iota(jnp.int32, (128, 128), 0)
            == lax.broadcasted_iota(jnp.int32, (128, 128), 1),
            1.0,
            0.0,
        )
        ones = jnp.ones((length, 128), LOW)

        @pl.loop(begin, end)
        def _(i):
            lanes = tile(i, 128)
            query, key, value = heads[0, :, lanes], heads[1, :, lanes], heads[2, :, lanes]
            wider = jnp.concatenate([value, ones], axis=1)
            parts = []
            for h in range(2):
                mine = lanes_column if h == 0 else ~lanes_column
                own = jnp.where(mine, query, jnp.zeros_like(query))
                upper = across(own[:half], key[:half]).astype(LOW) * mask[:half, :half]
                lower = across(own[half:], key).astype(LOW) * mask[half:, :]
                parts.append(
                    jnp.concatenate([product(upper, wider[:half]), product(lower, wider)], axis=0)
                )
            diagonal = (identity * sums[i, 0:1]).astype(LOW)
            right = jnp.concatenate(
                [unpack_pair(memory[i]), product(diagonal, blocks).astype(LOW)], axis=1
            )
            carried = product(query * keep, right)
            numerator = jnp.where(lanes_column, parts[0][:, :128], parts[1][:, :128])
            denominator = jnp.where(lanes_column, parts[0][:, 128:], parts[1][:, 128:])
            over = 1.0 / (denominator + carried[:, 128:])
            value = (numerator + carried[:, :128]) * over
            inverse[:, lanes] = over
            mixed[:, lanes] = value
            mixed_low[:, lanes] = value.astype(LOW)

    def join():
        save(mixed, mixed_out)
        save(inverse, inverse_out)

        @pl.loop(0, 2)
        def _(i):
            columns = tile(i, 512)
            middle[:, columns] = tokens[:, columns].astype(FULL) + product(
                mixed_low[...], weight(3, columns)
            )

        save(middle, middle_out)

    def second_norm():
        @pl.loop(0, length // 128)
        def _(i):
            rows = tile(i, 128)
            value, _ = statistics(middle[rows, :])
            normed[rows, :] = (value * gains[2:3, :] + gains[3:4, :]).astype(LOW)

    def raise_up(j):
        @pl.loop(0, 4)
        def _(i):
            value = product(normed[...], weight(4 + j, tile(i, 256)))
            columns = pl.ds(pl.multiple_of(j * 1024 + i * 256, 256), 256)
            value, steep = gelu_both(value)
            active[:, columns] = value.astype(LOW)
            slope[:, columns] = steep.astype(LOW)

        if j == 3:
            save(slope, slope_out)

    def down_gradient(begin, end):
        if begin == 0:
            loads[14].wait()

        @pl.loop(begin, end)
        def _(i):
            value = down_rows(active[:, tile(i, 512)], cotangent[...]).astype(LOW)
            y, x, z = i // 4, i // 2 % 2, i % 2 * 2
            for j in range(4):
                part = value[:, 256 * j : 256 * j + 256].reshape(2, 2, 128, 256)
                grad_down[j, y, x, pl.ds(z, 2)] = part

        if end == 8:
            save(grad_down, grad_down_out)

    def lower(j):
        columns = slice(256 * j, 256 * j + 256)

        @pl.loop(0, 2)
        def _(i):
            rows = tile(i, 256)
            value = product(active[rows, :], tall[j].reshape(4 * width, 256))
            result[rows, columns] = (middle[rows, columns] + value).astype(LOW)

        save(result.at[:, pl.ds(256 * j, 256)], result_out.at[:, pl.ds(256 * j, 256)])

    do = functools.partial
    work = {
        4: [lambda: None, first_norm],
        5: [do(project, 0)],
        6: [do(project, 1)],
        7: [do(project, 2), update],
        8: [lambda: None, lambda: None, enter],
        9: [do(attend, 0, 4), do(attend, 4, 6), do(attend, 6, 8)],
        10: [join, second_norm, do(raise_up, 0)],
        11: [do(raise_up, 1), do(raise_up, 2)],
        12: [do(raise_up, 3), do(down_gradient, 0, 4), do(down_gradient, 4, 8)],
        13: [do(lower, 0)],
        14: [do(lower, 1)],
        15: [do(lower, 2)],
    }
    loads[12].wait()
    small.step(0)
    for tick in range(12 + 4):
        todo = work.get(tick, []) + [lambda: None] * 3
        event(tick, 0)
        event(tick - 1, 1)
        if 1 <= tick < 5:
            small.step(tick)
        todo[0]()
        event(tick - 2, 2)
        todo[1]()
        event(tick - 3, 3)
        event(tick - 4, 4)
        todo[2]()
    lower(3)
    small.finish()
    for copy in state:
        copy.wait_send()
    for chunk in chunks:
        chunk.finish()
    for copy in stores:
        copy.wait()


def forward_pass(tokens, cotangent, starts, in_weight, out_weight, up_weight, down_weight, pack):
    length, width = tokens.shape
    block = lambda rows, columns: jax.ShapeDtypeStruct((2, 2, 4, 2, rows, columns), LOW)
    shape = jax.ShapeDtypeStruct

    def body(*refs):
        forward_kernel(refs[:8], refs[8:22], refs[22:])

    return pl.pallas_call(
        body,
        out_shape=[
            block(32, 3072),
            block(32, 1024),
            block(32, 4096),
            block(128, 1024),
            shape((4, 2, 2, 4, 2, 128, 256), LOW),
            shape((length, width), LOW),
            shape((3, length, width), LOW),
            shape((length, width), FULL),
            shape((length, width), FULL),
            shape((length, width), FULL),
            shape((length, 4 * width), LOW),
            shape((8, HEAD, 128), LOW),
            shape((8, 8, 128), FULL),
            shape((16, width), FULL),
        ],
        in_specs=[
            pl.BlockSpec(memory_space=pltpu.SMEM if i == 2 else pl.ANY) for i in range(8)
        ],
        out_specs=[pl.BlockSpec(memory_space=pl.ANY)] * 14,
        scratch_shapes=[
            pltpu.VMEM((8, 2, 2, 4, 2, 32, 1024), LOW),
            pltpu.VMEM((4, 2, 2, 4, 2, 128, 256), LOW),
            pltpu.VMEM((2, 2, 4, 2, 16, 128), LOW),
            pltpu.VMEM((length, width), LOW),
            pltpu.VMEM((length, width), LOW),
            pltpu.VMEM((16, width), FULL),
            pltpu.VMEM((length, width), LOW),
            pltpu.VMEM((3, length, width), LOW),
            pltpu.VMEM((length, length), LOW),
            pltpu.VMEM((length, width), FULL),
            pltpu.VMEM((length, width), LOW),
            pltpu.VMEM((length, width), FULL),
            pltpu.VMEM((length, width), FULL),
            pltpu.VMEM((length, 4 * width), LOW),
            pltpu.VMEM((length, 4 * width), LOW),
            pltpu.VMEM((4, 2, 2, 4, 2, 128, 256), LOW),
            pltpu.VMEM((length, width), LOW),
            pltpu.VMEM((8, HEAD + 16, 128), LOW),
            pltpu.VMEM((2, 8, HEAD + 16, 128), LOW),
            pltpu.VMEM((8, HEAD, 128), LOW),
            pltpu.VMEM((8, 8, 128), FULL),
            pltpu.SemaphoreType.DMA((12, 11)),
            pltpu.SemaphoreType.DMA((12, 11)),
            pltpu.SemaphoreType.DMA((9,)),
            pltpu.SemaphoreType.DMA((9,)),
            pltpu.SemaphoreType.DMA((2,)),
            pltpu.SemaphoreType.DMA((2,)),
            pltpu.SemaphoreType.DMA((15,)),
            pltpu.SemaphoreType.DMA((26,)),
        ],
        compiler_params=pltpu.CompilerParams(
            collective_id=0, has_side_effects=True, vmem_limit_bytes=62 << 20
        ),
        name="forward_pass",
    )(tokens, cotangent, starts, in_weight, out_weight, up_weight, down_weight, pack)


def scatter_buffers(count, rows, columns):
    half = rows // 2
    shapes = [
        (2, 2, 4, rows, columns),
        (2, 2, 4, rows, columns),
        (2, 4, half, columns),
        (2, 4, half, columns),
        (4, half, columns),
        (4, half, columns),
        (3, rows, columns),
    ]
    return [pltpu.VMEM((count, *shape), LOW) for shape in shapes]


class Sum:
    def __init__(self, place, stages, landed, send, recv):
        p = place
        devices = [p.sibling, p.over_x, p.over_y, *p.along_z]
        self.stages, self.landed = stages, landed
        self.copies = [
            remote(stages.at[min(i, 3)], landed.at[i], send.at[i], recv.at[i], device)
            for i, device in enumerate(devices)
        ]

    def step(self, number):
        stages, landed = self.stages, self.landed
        if 1 <= number <= 3:
            self.copies[number - 1].wait_recv()
            stages[number] = stages[number - 1] + landed[number - 1]
        if number < 3:
            self.copies[number].start()
        elif number == 3:
            for i in (3, 4, 5):
                self.copies[i].start()

    def result(self):
        for i in (3, 4, 5):
            self.copies[i].wait_recv()
        return (self.stages[3] + self.landed[3]) + (self.landed[4] + self.landed[5])

    def finish(self):
        for copy in self.copies:
            copy.wait_send()


def backward_kernel(inputs, outputs, tall, wide, scratch):
    (
        tokens_in,
        cotangent_in,
        starts,
        in_full,
        out_full,
        up_full,
        down_full,
        grad_down_in,
        heads_in,
        mixed_in,
        inverse_in,
        middle_in,
        slope_in,
        memory_in,
        sums_in,
        gains_in,
    ) = inputs
    (
        cotangent,
        normed,
        slab,
        broad,
        grad_middle,
        inner,
        mixed,
        inverse,
        memory,
        sums,
        gains,
        mask,
        mask_back,
        parts,
        done_in,
        done_out,
        done_up,
        done_down,
        stages,
        landed,
        outgoing,
        incoming,
        update,
        key_update,
        send,
        recv,
        sum_send,
        sum_recv,
        state_send,
        state_recv,
        local,
        stream,
        store,
    ) = scratch
    p = Place()
    length, width = cotangent.shape

    pairs = [
        (cotangent_in, cotangent),
        (slope_in, broad),
        (middle_in, grad_middle),
        (gains_in, gains),
        (memory_in, memory),
        (sums_in, sums),
        (mixed_in, mixed),
        (inverse_in, inverse),
        (tokens_in, cotangent),
    ]
    pairs += [(heads_in.at[k], broad.at[:, pl.ds(1024 * k, 1024)]) for k in range(3)]
    loads = [pltpu.make_async_copy(a, b, local.at[i]) for i, (a, b) in enumerate(pairs)]
    slabs = [down_full.at[pl.ds(1024 * j, 1024), :] for j in range(4)]
    slabs += [up_full.at[:, pl.ds(1024 * j, 1024)] for j in range(4)]
    slabs += [out_full]
    slabs += [in_full.at[:, pl.ds(1024 * j, 1024)] for j in range(3)]
    slabs = [
        pltpu.make_async_copy(source, slab.at[i % 2], stream.at[i]) for i, source in enumerate(slabs)
    ]
    order = [8, 9, 10, 11, 4, 5, 6, 7, 3, 0, 1, 2]
    room = {4: 0, 5: 1, 6: 2, 7: 0, 3: 1, 0: 2, 1: 0, 2: 1}
    chunks = []
    for j in range(12):
        if j < 8:
            first, *others = [ref.at[j] for ref in wide]
            buffers = [first, first, *others]
            own = parts.at[room[j]]
        else:
            buffers = [ref.at[j - 8] for ref in tall]
            own = grad_down_in.at[j - 8]
        chunks.append(Scatter(p, own, *buffers, send.at[j], recv.at[j], j >= 8))

    p.meet()
    chunks[8].step(0)
    for i in range(4):
        loads[i].start()
    slabs[0].start()
    slabs[1].start()
    for i in range(4, 8):
        loads[i].start()
    stores = []

    def save(source, target):
        copy = pltpu.make_async_copy(source, target, store.at[len(stores)])
        copy.start()
        stores.append(copy)

    def event(position, number):
        if not 0 <= position < 12:
            return
        j = order[position]
        if number < 4:
            if (j, number) != (8, 0):
                chunks[j].step(number)
            return
        if j < 8:
            target, k = (done_in, j) if j < 3 else ((done_out, 0) if j == 3 else (done_up, j - 4))
            size = 1024
        else:
            target, k, size = done_down, j - 8, 256
        where = outputs[0 if j < 3 else 1 if j == 3 else 2 if j < 8 else 3]
        target[:, size * k : size * k + size] = chunks[j].result()
        save(target.at[:, pl.ds(size * k, size)], where.at[:, pl.ds(size * k, size)])

    images = Images(starts, p.seq, length)

    def second_norm():
        loads[2].wait()
        loads[3].wait()

        @pl.loop(0, length // 128)
        def _(i):
            rows = tile(i, 128)
            value, _ = statistics(grad_middle[rows, :])
            normed[rows, :] = (value * gains[2:3, :] + gains[3:4, :]).astype(LOW)

    def active_gradient(j):
        if j == 0:
            loads[0].wait()
            loads[1].wait()
        slabs[j].wait()

        @pl.loop(0, 4, unroll=2)
        def _(i):
            columns = pl.ds(pl.multiple_of(1024 * j + 256 * i, 256), 256)
            value = across(cotangent[...], slab[j % 2, tile(i, 256), :])
            broad[:, columns] = (value * broad[:, columns].astype(FULL)).astype(LOW)

        slabs[j + 2].start()

    def weight_gradient(j, left, right):
        at = room[j]

        @pl.loop(0, 4, unroll=2)
        def _(i):
            value = down_rows(left(tile(i, 256)), right()).astype(LOW)
            parts[at, i // 2, i % 2] = value.reshape(4, 2, 32, 1024)

    def up_gradient(j):
        if j == 3:
            chunks[4].release()
        weight_gradient(
            4 + j,
            lambda columns: normed[:, columns],
            lambda: broad[:, 1024 * j : 1024 * j + 1024],
        )
        if j == 3:
            for k in range(9, 12):
                loads[k].start()

    def inner_gradient(first, j):
        slabs[first + j].wait()

        @pl.loop(0, 4, unroll=2)
        def _(i):
            columns = tile(i, 256)
            value = across(
                broad[:, 1024 * j : 1024 * j + 1024], slab[(first + j) % 2, columns, :]
            )
            if j > 0:
                value = value + inner[:, columns]
            inner[:, columns] = value

        if first + j + 2 < 12:
            slabs[first + j + 2].start()

    def norm_gradient(rows, values, gain):
        unit, scale = statistics(values)
        given = inner[rows, :]
        scaled = given * gain
        one = jnp.mean(scaled, axis=-1, keepdims=True)
        two = jnp.mean(scaled * unit, axis=-1, keepdims=True)
        return scale * (scaled - one - unit * two), given * unit, given

    def fold(values):
        return jnp.sum(values, axis=0, keepdims=True)

    def middle_gradient():
        stages[0] = jnp.zeros((8, width), FULL)

        @pl.loop(0, length // 128)
        def _(i):
            rows = tile(i, 128)
            value, gain, shift = norm_gradient(rows, grad_middle[rows, :], gains[2:3, :])
            stages[0, 2:3, :] += fold(gain)
            stages[0, 3:4, :] += fold(shift)
            value = value + cotangent[rows, :].astype(FULL)
            grad_middle[rows, :] = value
            cotangent[rows, :] = value.astype(LOW)

    def output_gradient():
        loads[6].wait()
        chunks[5].release()
        weight_gradient(
            3, lambda columns: mixed[:, columns].astype(LOW), lambda: cotangent[...]
        )
        loads[8].start()

    def mixed_gradient():
        slabs[8].wait()

        @pl.loop(0, 4)
        def _(i):
            columns = tile(i, 256)
            inner[:, columns] = across(cotangent[...], slab[0, columns, :])

        slabs[10].start()

    state = [
        remote(outgoing, incoming.at[d], state_send.at[d], state_recv.at[d], device)
        for d, device in enumerate(p.preceding)
    ]

    def numerator_gradient():
        for i in (4, 5, 7, 9, 10, 11):
            loads[i].wait()
        blocks = own_block()
        doubled = jnp.concatenate([blocks, blocks], axis=0)

        @pl.loop(0, 8)
        def _(i):
            lanes = tile(i, 128)
            given, over = inner[:, lanes], inverse[:, lanes]
            numerator = (given * over).astype(LOW)
            each = given * mixed[:, lanes]
            high = each.astype(LOW)
            rest = (each - high.astype(FULL)).astype(LOW)
            slant = product(jnp.concatenate([high, rest], axis=1), doubled) * over * -1.0
            mixed[:, lanes] = slant
            broad[:, pl.ds(pl.multiple_of(3072 + 128 * i, 128), 128)] = numerator
            kept = broad[:, lanes].astype(FULL) * images.keep
            square = down_rows(kept.astype(LOW), numerator)
            outgoing[i, 0:HEAD] = pack_pair(square).astype(LOW)
            total = fold(kept * slant)
            outgoing[i, HEAD : HEAD + 16] = jnp.broadcast_to(total, (16, 128)).astype(LOW)

        for copy in state:
            copy.start()
        mask[...] = same_mask(images, length, length, False)
        mask_back[...] = same_mask(images, length, length, True)

    def enter():
        for copy in state:
            copy.wait_recv()
        flag = jnp.where(p.seq == 7, 0.0, images.flag_after)

        @pl.loop(0, 8)
        def _(i):
            value = incoming[0, i].astype(FULL) + flag * incoming[1, i].astype(FULL)
            update[i] = value[0:HEAD].astype(LOW)
            key_update[i] = value[HEAD : HEAD + 8]

    def attend(begin, end):
        if begin == 0:
            enter()
        if end == 8:
            first_norm()
        first = head_lanes(length)
        lane = lax.broadcasted_iota(jnp.int32, (length, 128), 1)
        ones = jnp.ones((length, 128), LOW)
        zero = jnp.zeros((length, 128), LOW)
        half = length // 2

        @pl.loop(begin, end)
        def _(i):
            at = [pl.ds(pl.multiple_of(1024 * k + 128 * i, 128), 128) for k in range(4)]
            query, key, value, numerator = [broad[:, lanes] for lanes in at]
            slant = mixed[:, at[0]]
            high = slant.astype(LOW)
            rest = (slant - high.astype(FULL)).astype(LOW)
            right = jnp.concatenate([value, ones], axis=1)
            grads = []
            for h in range(2):
                mine = first if h == 0 else ~first
                own_query = jnp.where(mine, query, zero)
                left = jnp.concatenate(
                    [
                        jnp.where(mine, numerator, zero),
                        jnp.where(
                            lane == HEAD * h, high, jnp.where(lane == HEAD * h + 1, rest, zero)
                        ),
                    ],
                    axis=1,
                )
                upper = across(left[:half], right[:half]).astype(LOW) * mask[:half, :half]
                lower = across(left[half:], right).astype(LOW) * mask[half:, :]
                for_query = jnp.concatenate([product(upper, key[:half]), product(lower, key)], axis=0)
                upper = across(right[:half], left).astype(LOW) * mask_back[:half, :]
                lower = across(right[half:], left[half:]).astype(LOW) * mask_back[half:, half:]
                for_key = jnp.concatenate(
                    [product(upper, query), product(lower, query[half:])], axis=0
                )
                upper = across(key[:half], own_query).astype(LOW) * mask_back[:half, :]
                lower = across(key[half:], own_query[half:]).astype(LOW) * mask_back[half:, half:]
                for_value = jnp.concatenate(
                    [product(upper, numerator), product(lower, numerator[half:])], axis=0
                )
                grads.append((for_query, for_key, for_value))
            for_query, for_key, for_value = [
                jnp.where(first, one, two) for one, two in zip(*grads, strict=True)
            ]
            keep, tail = images.keep, images.tail
            for_query = for_query + keep * (
                across(numerator, unpack_pair(memory[i])) + slant * sums[i, 0:1]
            )
            square = unpack_pair(update[i])
            for_key = for_key + tail * (across(value, square) + key_update[i, 0:1])
            for_value = for_value + product(key * tail.astype(LOW), square)
            broad[:, at[0]] = (for_query * jnp.minimum(query.astype(FULL), 1.0)).astype(LOW)
            broad[:, at[1]] = (for_key * jnp.minimum(key.astype(FULL), 1.0)).astype(LOW)
            broad[:, at[2]] = for_value.astype(LOW)

    def first_norm():
        loads[8].wait()

        @pl.loop(0, length // 128)
        def _(i):
            rows = tile(i, 128)
            value, _ = statistics(cotangent[rows, :].astype(FULL))
            normed[rows, :] = (value * gains[0:1, :] + gains[1:2, :]).astype(LOW)

    def in_gradient(j):
        chunks[(6, 7, 3)[j]].release()
        weight_gradient(
            j,
            lambda columns: normed[:, columns],
            lambda: broad[:, 1024 * j : 1024 * j + 1024],
        )

    total = Sum(p, stages, landed, sum_send, sum_recv)

    def token_gradient():
        @pl.loop(0, length // 128)
        def _(i):
            rows = tile(i, 128)
            value, gain, shift = norm_gradient(rows, cotangent[rows, :].astype(FULL), gains[0:1, :])
            stages[0, 0:1, :] += fold(gain)
            stages[0, 1:2, :] += fold(shift)
            grad_middle[rows, :] += value

        save(grad_middle, outputs[4])
        total.step(0)

    do = functools.partial
    work = {
        1: [do(active_gradient, 0), do(active_gradient, 1), do(active_gradient, 2)],
        2: [do(active_gradient, 3), second_norm, do(up_gradient, 0)],
        3: [do(up_gradient, 1), do(up_gradient, 2), do(inner_gradient, 4, 0)],
        4: [do(inner_gradient, 4, 1), do(inner_gradient, 4, 2), do(inner_gradient, 4, 3)],
        5: [do(up_gradient, 3), middle_gradient, mixed_gradient],
        6: [output_gradient, numerator_gradient],
        7: [lambda: None, do(attend, 0, 1), do(attend, 1, 3)],
        8: [do(attend, 3, 5), do(attend, 5, 7), do(attend, 7, 8)],
        9: [do(in_gradient, 1), do(in_gradient, 2), do(inner_gradient, 9, 0)],
        10: [
            do(inner_gradient, 9, 1),
            do(inner_gradient, 9, 2),
            token_gradient,
        ],
        11: [lambda: None, do(total.step, 1)],
        12: [lambda: None, do(total.step, 2)],
        13: [lambda: None, do(total.step, 3)],
    }
    for tick in range(12 + 6):
        todo = work.get(tick, []) + [lambda: None] * 3
        if tick == 9:
            in_gradient(0)
        event(tick, 0)
        event(tick - 1, 1)
        todo[0]()
        event(tick - 2, 2)
        todo[1]()
        event(tick - 3, 3)
        event(tick - 6, 4)
        todo[2]()
    total_value = total.result()
    landed[0] = total_value
    group = (p.dp * 8 + p.seq) // 4
    mine = landed[0, :, tile(group, 128)]
    mine = pltpu.roll(mine, (128 - 32 * (p.seq % 4)) % 128, 1)
    outputs[5][...] = mine
    total.finish()
    for copy in state:
        copy.wait_send()
    for chunk in chunks:
        chunk.finish()
    for copy in stores:
        copy.wait()


def backward_pass(*inputs):
    length, width = inputs[0].shape
    shape = jax.ShapeDtypeStruct
    vmem = pltpu.VMEM
    tall = scatter_buffers(4, 128, 256)
    wide = scatter_buffers(8, 32, 1024)[1:]

    def body(*refs):
        backward_kernel(refs[:16], refs[16:22], refs[22:29], refs[29:35], refs[35:])

    return pl.pallas_call(
        body,
        out_shape=[
            shape((32, 3072), FULL),
            shape((32, 1024), FULL),
            shape((32, 4096), FULL),
            shape((128, 1024), FULL),
            shape((length, width), FULL),
            shape((8, 128), FULL),
        ],
        in_specs=[
            pl.BlockSpec(memory_space=pltpu.SMEM if i == 2 else pl.ANY) for i in range(16)
        ],
        out_specs=[pl.BlockSpec(memory_space=pl.ANY)] * 5
        + [pl.BlockSpec(memory_space=pltpu.VMEM)],
        scratch_shapes=[
            *tall,
            *wide,
            vmem((length, width), LOW),
            vmem((length, width), LOW),
            vmem((2, width, width), LOW),
            vmem((length, 4 * width), LOW),
            vmem((length, width), FULL),
            vmem((length, width), FULL),
            vmem((length, width), FULL),
            vmem((length, width), FULL),
            vmem((8, HEAD, 128), LOW),
            vmem((8, 8, 128), FULL),
            vmem((16, width), FULL),
            vmem((length, length), LOW),
            vmem((length, length), LOW),
            vmem((3, 2, 2, 4, 2, 32, 1024), LOW),
            vmem((32, 3072), FULL),
            vmem((32, 1024), FULL),
            vmem((32, 4096), FULL),
            vmem((128, 1024), FULL),
            vmem((4, 8, width), FULL),
            vmem((6, 8, width), FULL),
            vmem((8, HEAD + 16, 128), LOW),
            vmem((2, 8, HEAD + 16, 128), LOW),
            vmem((8, HEAD, 128), LOW),
            vmem((8, 8, 128), FULL),
            pltpu.SemaphoreType.DMA((12, 9)),
            pltpu.SemaphoreType.DMA((12, 8)),
            pltpu.SemaphoreType.DMA((6,)),
            pltpu.SemaphoreType.DMA((6,)),
            pltpu.SemaphoreType.DMA((2,)),
            pltpu.SemaphoreType.DMA((2,)),
            pltpu.SemaphoreType.DMA((12,)),
            pltpu.SemaphoreType.DMA((12,)),
            pltpu.SemaphoreType.DMA((13,)),
        ],
        compiler_params=pltpu.CompilerParams(
            collective_id=1, has_side_effects=True, vmem_limit_bytes=62 << 20
        ),
        name="backward_pass",
    )(*inputs)


def hand_over(*values):
    large = len(values) - 1

    def body(*refs):
        inputs, vectors, outputs = refs[:large], refs[large], refs[large + 1 : 2 * large + 1]
        small, held, sems = refs[2 * large + 1 : 2 * large + 5], refs[2 * large + 5 : -1], refs[-1]
        copies = [
            (
                pltpu.make_async_copy(inputs[i], held[i], sems.at[0, i]),
                pltpu.make_async_copy(held[i], outputs[i], sems.at[1, i]),
            )
            for i in range(large)
        ]
        for load, _ in copies:
            load.start()
        for k in range(4):
            small[k][...] = vectors[k : k + 1, 0:32]
        for load, store in copies:
            load.wait()
            store.start()
        for _, store in copies:
            store.wait()

    anywhere, near = pl.BlockSpec(memory_space=pl.ANY), pl.BlockSpec(memory_space=pltpu.VMEM)
    return pl.pallas_call(
        body,
        out_shape=[jax.ShapeDtypeStruct(value.shape, value.dtype) for value in values[:large]]
        + [jax.ShapeDtypeStruct((1, 32), FULL)] * 4,
        in_specs=[anywhere] * large + [near],
        out_specs=[anywhere] * large + [near] * 4,
        scratch_shapes=[pltpu.VMEM(value.shape, value.dtype) for value in values[:large]]
        + [pltpu.SemaphoreType.DMA((2, large))],
        name="hand_over",
    )(*values)


def on_device(
    tokens,
    starts,
    query_key_value_weight,
    attention_output_weight,
    up_projection_weight,
    down_projection_weight,
    first_gain,
    first_shift,
    second_gain,
    second_shift,
    cotangent,
):
    mine = lax.axis_index("dp") * 8 + lax.axis_index("seq")
    pack = jnp.stack([first_gain, first_shift, second_gain, second_shift]).astype(FULL)
    pack = jnp.roll(jnp.pad(pack, ((0, 12), (0, 96))), 32 * (mine % 4), axis=1).astype(LOW)
    in_full, out_full, up_full, down_full, grad_down, result, *saved = forward_pass(
        tokens[0],
        cotangent[0],
        starts,
        query_key_value_weight,
        attention_output_weight,
        up_projection_weight,
        down_projection_weight,
        pack,
    )
    grads = backward_pass(
        tokens[0],
        cotangent[0],
        starts,
        in_full.reshape(1024, 3072),
        out_full.reshape(1024, 1024),
        up_full.reshape(1024, 4096),
        down_full.reshape(4096, 1024),
        grad_down,
        *saved,
    )
    result, *grads = hand_over(result, *grads)
    vectors = [grad.reshape(32) for grad in grads[5:]]
    return (result[None], grads[4][None], *grads[:4], *vectors)


def solution(mesh):

    fast = dict(mesh.shape) == {"dp": 4, "seq": 8}
    return jax.shard_map(
        on_device if fast else on_device_general,
        mesh=mesh,
        in_specs=(
            P("dp", "seq", None),
            P("dp", None),
            P(("dp", "seq"), None),
            P(("dp", "seq"), None),
            P(("dp", "seq"), None),
            P(("dp", "seq"), None),
            P(("dp", "seq")),
            P(("dp", "seq")),
            P(("dp", "seq")),
            P(("dp", "seq")),
            P("dp", "seq", None),
        ),
        out_specs=(
            P("dp", "seq", None),
            P("dp", "seq", None),
            P(("dp", "seq"), None),
            P(("dp", "seq"), None),
            P(("dp", "seq"), None),
            P(("dp", "seq"), None),
            P(("dp", "seq")),
            P(("dp", "seq")),
            P(("dp", "seq")),
            P(("dp", "seq")),
        ),
        check_vma=False,
    )
```
